32 devices in a mesh: section: 2 (over x), seq: 4 (over y, core), shard: 4 (over z).
Axes of the slice: x: 2, y: 2, z: 4, core: 2. Of those that a mesh axis runs over, the one named last changes fastest.
Arguments:
- inputs: bfloat16 [2, 4, 512, 1024], P(None, 'shard', 'seq'), may hold values from -6 to 6
- segment_ids: int32 [2, 4, 512], P(None, 'shard'), may hold values from 0 to 3, never falling along the last dimension, each value on 1 to 256 neighbouring positions
- cotangent: bfloat16 [2, 4, 512, 1024], P(None, 'shard', 'seq'), may hold values from -6 to 6
- w_mix: bfloat16 [2, 1024, 4096], P('section', 'shard'), may hold values from -0.1875 to 0.1875
- w_out: bfloat16 [2, 1024, 1024], P('section', 'shard'), may hold values from -0.375 to 0.375
- w_gu: bfloat16 [2, 1024, 5632], P('section', 'shard'), may hold values from -0.1875 to 0.1875
- w_down: bfloat16 [2, 2816, 1024], P('section', 'shard'), may hold values from -0.109375 to 0.109375
- norm_gains: bfloat16 [2, 1024, 2], P('section', 'shard'), may hold values from 0.25 to 1.75
- persist_kv: bfloat16 [2, 2, 16, 1024], P('section', None, None, 'seq'), may hold values from -6 to 6
- memory_decay: float32 [2, 8], P('section', 'seq'), may hold values from 0.00048828125 to 0.05
Outputs:
- section_outputs: bfloat16 [2, 2, 4, 512, 1024], P('section', None, 'shard', 'seq')
- section_grads: float32 [2, 2, 4, 512, 1024], P('section', None, 'shard', 'seq')
- grad_w_mix: float32 [2, 1024, 4096], P('section', 'shard')
- grad_w_out: float32 [2, 1024, 1024], P('section', 'shard')
- grad_w_gu: float32 [2, 1024, 5632], P('section', 'shard')
- grad_w_down: float32 [2, 2816, 1024], P('section', 'shard')
- grad_gains: float32 [2, 1024, 2], P('section', 'shard')
- grad_persist: float32 [2, 2, 16, 1024], P('section', None, None, 'seq')
- grad_decay: float32 [2, 8], P('section', 'seq')
The draws below stay inside these ranges and needn't reach their ends.
Inputs may be any that keep to these rules, and one draw needn't show every extreme that they name: `segment_ids`: within one sequence the ids never fall; equal ids mark one document.
All inputs are finite; a program needn't handle non-finite values.
Results may differ from the reference program's by a relative error of at most 0.033.
Values may be sent and summed in bfloat16 or wider, within the bound.
A program may use at most 256 MiB of HBM per device.

```python
import math
import jax
import jax.numpy as jnp
import numpy as np
from jax import lax

D = 1024
H = 8
HD = 128
FF = 2816
NP = 16
MICRO = 2
SEQ_LEN = 512
SEQS = 4
LAYERS = 2


def block_levels(stream_key, shape, shards, least, largest):
    loudness = 1.0
    for position, shards_of in shards:
        heights = jax.random.uniform(jax.random.fold_in(jax.random.fold_in(stream_key, 6), position), (shards_of,), jnp.float32, least / len(shards), largest / len(shards))
        loudness = loudness * jnp.repeat(jnp.exp(heights), shape[position] // shards_of).reshape((-1,) + (1,) * (len(shape) - 1 - position))
    return loudness


def length_profile(number_of, total, most, slope):
    portions = [(1 << 20) // math.isqrt(rank ** slope) + 1 for rank in range(2, number_of + 1)]
    spare, given = total - most - (number_of - 1), [1] * (number_of - 1)
    while spare > 0:
        candidates = [i for i in range(number_of - 1) if given[i] < most]
        pool, budget = sum([portions[i] for i in candidates]), spare
        for i in candidates:
            addition = min(most - given[i], max(1, budget * portions[i] // pool), spare)
            given[i] = given[i] + addition
            spare = spare - addition
    return np.array([most] + given)


def uneven(own_key, count, total, bound, lean):
    if count == 2:
        one = jax.random.randint(own_key, (), max(1, total - bound), min(bound, total - 1) + 1)
        return jnp.stack([one, total - one])
    tallies = jnp.asarray(length_profile(count, total, bound, lean), jnp.int32)
    pairs = (count - 1) // 2
    giver, sink = tallies[1:1 + 2 * pairs:2], tallies[2:2 + 2 * pairs:2]
    slack = jnp.minimum(giver - 1, bound - sink)
    moved = jax.random.randint(jax.random.fold_in(own_key, 1), (pairs,), 0, 1 << 20) % (slack + 1)
    tallies = tallies.at[1:1 + 2 * pairs:2].set(giver - moved).at[2:2 + 2 * pairs:2].set(sink + moved)
    return tallies[jax.random.permutation(jax.random.fold_in(own_key, 2), count)]


def scatter_about(own_key, dims, scale, reach, shards=(), kind=jnp.bfloat16):
    factor_of = block_levels(own_key, dims, shards, -0.22, 0.18) if shards else 1.0
    result = jax.random.normal(own_key, dims, jnp.float32) * scale * factor_of
    return jnp.minimum(jnp.maximum(result, -reach), reach).astype(kind)


def setup_inputs(seed: int = 0) -> dict:
    streams_of = jax.random.split(jax.random.key(seed), 11)
    inputs = scatter_about(streams_of[0], (MICRO, SEQS, SEQ_LEN, D), 1.0, 6.0, ((1, 4), (2, 4)))
    segment_ids = jax.vmap(lambda own: jnp.searchsorted(jnp.cumsum(uneven(own, max(4, SEQ_LEN // 128), SEQ_LEN, SEQ_LEN // 2, 2)), jnp.arange(SEQ_LEN), side="right"))(jax.random.split(streams_of[1], MICRO * SEQS)).reshape((MICRO, SEQS, SEQ_LEN)).astype(jnp.int32)
    cotangent = scatter_about(streams_of[2], (MICRO, SEQS, SEQ_LEN, D), 1.0, 6.0, ((1, 4), (2, 4)))
    w_mix = scatter_about(streams_of[3], (LAYERS, D, 4 * D), D ** -0.5, 0.1875, ((0, 2), (1, 4)))
    w_out = scatter_about(streams_of[4], (LAYERS, D, D), (D // 4) ** -0.5, 0.375, ((0, 2), (1, 4)))
    w_gu = scatter_about(streams_of[5], (LAYERS, D, 2 * FF), D ** -0.5, 0.1875, ((0, 2), (1, 4)))
    w_down = scatter_about(streams_of[6], (LAYERS, FF, D), FF ** -0.5, 0.109375, ((0, 2), (1, 4)))
    norm_gains = jnp.clip(1.0 + 0.15 * jax.random.normal(streams_of[7], (LAYERS, D, 2), jnp.float32), 0.25, 1.75).astype(jnp.bfloat16)
    persist_kv = scatter_about(streams_of[8], (LAYERS, 2, NP, D), 1.0, 6.0, ((0, 2), (3, 4)))
    memory_decay = jnp.clip(jnp.exp(math.log(0.05) - 4.6288867 * jax.random.uniform(streams_of[9], (LAYERS, H), jnp.float32) ** block_levels(streams_of[9], (LAYERS, H), ((0, 2), (1, 4)), -0.2, 0.2)), 0.00048828125, 0.05)
    return {"inputs": inputs, "segment_ids": segment_ids, "cotangent": cotangent, "w_mix": w_mix, "w_out": w_out, "w_gu": w_gu, "w_down": w_down, "norm_gains": norm_gains, "persist_kv": persist_kv, "memory_decay": memory_decay}


@jax.custom_vjp
def low(v):
    return lax.optimization_barrier(v.astype(jnp.bfloat16)).astype(jnp.float32)

@jax.custom_vjp
def low_back(v):
    return v

def low_keep(v):
    return (low(v), None)

def low_pass(kept, grad):
    return (grad,)

def back_keep(v):
    return (v, None)

def back_low(kept, grad):
    return (low(grad),)
low.defvjp(low_keep, low_pass)
low_back.defvjp(back_keep, back_low)

def rms_scale(values):
    return lax.rsqrt(lax.optimization_barrier(jnp.mean(values * values, axis=-1, keepdims=True)) + 1e-06)

def mixer_head(query, keys, values, pkeys, pvalues, rate, seg_ids):
    length = query.shape[0]
    scale = 1.0 / math.sqrt(HD)
    places = jnp.arange(length, dtype=jnp.int32)
    allowed = (seg_ids[:, None] == seg_ids[None, :]) & (places[None, :] <= places[:, None])
    inner = jnp.dot(query, keys.T, precision=lax.Precision.HIGHEST)
    seq_scores = jnp.where(allowed, low_back(inner * scale), -jnp.inf)
    per_scores = low_back(jnp.dot(query, pkeys.T, precision=lax.Precision.HIGHEST) * scale)
    scores = jnp.concatenate([per_scores, seq_scores], axis=1)
    probs = low(jax.nn.softmax(scores, axis=-1))
    both_values = jnp.concatenate([pvalues, values], axis=0)
    attended = jnp.dot(probs, both_values, precision=lax.Precision.HIGHEST)
    distance = jnp.maximum(places[:, None] - places[None, :], 0).astype(jnp.float32)
    decay_w = jnp.where(allowed, jnp.exp(-rate * distance), jnp.float32(0.0))
    memory_w = low(low_back(inner) * decay_w * (1.0 / HD))
    recalled = jnp.dot(memory_w, values, precision=lax.Precision.HIGHEST)
    return (low(low_back(attended)), low(low_back(recalled)))

def layer(rows_in, seg_ids, mix_w, out_w, gu_w, down_w, gains, pkv, rates):
    length = rows_in.shape[0]
    normed = low(rows_in * rms_scale(rows_in) * gains[:, 0])
    proj = low_back(jnp.dot(normed, mix_w, precision=lax.Precision.HIGHEST))
    qkv = low(proj[:, :3 * D]).reshape(length, 3, H, HD)
    gate = jax.nn.sigmoid(proj[:, 3 * D:])
    pkeys = pkv[0].reshape(NP, H, HD)
    pvalues = pkv[1].reshape(NP, H, HD)
    attended, recalled = jax.vmap(mixer_head, in_axes=(1, 1, 1, 1, 1, 0, None), out_axes=1)(qkv[:, 0], qkv[:, 1], qkv[:, 2], pkeys, pvalues, rates, seg_ids)
    combined = low(attended.reshape(length, D) + gate * recalled.reshape(length, D))
    mid = rows_in + low_back(jnp.dot(combined, out_w, precision=lax.Precision.HIGHEST))
    normed_two = low(mid * rms_scale(mid) * gains[:, 1])
    gate_up = low_back(jnp.dot(normed_two, gu_w, precision=lax.Precision.HIGHEST))
    hidden = low(jax.nn.silu(gate_up[:, :FF]) * gate_up[:, FF:])
    return mid + low_back(jnp.dot(hidden, down_w, precision=lax.Precision.HIGHEST))

def two_layers(rows_in, probe, weights, seg_ids):
    mix_w, out_w, gu_w, down_w, gains, pkv, rates = weights
    first_out = layer(rows_in, seg_ids, mix_w[0], out_w[0], gu_w[0], down_w[0], gains[0], pkv[0], rates[0])
    sent = low(low_back(first_out + probe))
    final = layer(sent, seg_ids, mix_w[1], out_w[1], gu_w[1], down_w[1], gains[1], pkv[1], rates[1])
    return (sent, final)

def reference(inputs, segment_ids, cotangent, w_mix, w_out, w_gu, w_down, norm_gains, persist_kv, memory_decay):
    weights = (w_mix.astype(jnp.float32), w_out.astype(jnp.float32), w_gu.astype(jnp.float32), w_down.astype(jnp.float32), norm_gains.astype(jnp.float32), persist_kv.astype(jnp.float32), memory_decay.astype(jnp.float32))
    count = MICRO * SEQS
    all_rows = inputs.reshape(count, SEQ_LEN, D).astype(jnp.float32)
    all_segs = segment_ids.reshape(count, SEQ_LEN).astype(jnp.int32)
    all_cots = cotangent.reshape(count, SEQ_LEN, D).astype(jnp.float32)

    def one_sequence(totals, item):
        rows_in, seg_ids, cot_rows = item

        def forward(first_in, probe, params):
            return two_layers(first_in, probe, params, seg_ids)
        (sent, final), pull = jax.vjp(forward, rows_in, jnp.zeros_like(rows_in), weights)
        grad_in, grad_probe, grad_weights = pull((jnp.zeros_like(sent), cot_rows))
        totals = jax.tree.map(jnp.add, totals, grad_weights)
        return (totals, (sent, final, grad_in, grad_probe))
    zeros = jax.tree.map(jnp.zeros_like, weights)
    totals, (sent, final, grad_in, grad_probe) = lax.scan(one_sequence, zeros, (all_rows, all_segs, all_cots))
    shape = (MICRO, SEQS, SEQ_LEN, D)
    section_outputs = jnp.stack([sent.reshape(shape), final.reshape(shape)]).astype(jnp.bfloat16)
    section_grads = jnp.stack([grad_in.reshape(shape), grad_probe.reshape(shape)])
    return (section_outputs, section_grads, totals[0], totals[1], totals[2], totals[3], totals[4], totals[5], totals[6])
```

```python
import functools
import math

import jax
import jax.numpy as jnp
from jax import lax
from jax.experimental import pallas as pl
from jax.experimental.pallas import tpu as pltpu
from jax.sharding import PartitionSpec as P

D = 1024
H = 8
HD = 128
FF = 2816


def shifted(value, axis, by):
    size = lax.axis_size(axis)
    pairs = [(i, i + by) for i in range(size) if 0 <= i + by < size]
    return lax.ppermute(value, axis, pairs)


def as_sent(value):
    return jax.tree.map(lambda a: a.astype(jnp.bfloat16) if a.dtype == jnp.float32 else a, value)


def rms_scale(values):
    return lax.rsqrt(jnp.mean(values * values, axis=-1, keepdims=True) + 1e-06)


def norm_back(grad_normed, scaled, inverse, gain):
    grad_scaled = grad_normed * gain
    grad_rows = inverse * (
        grad_scaled - scaled * jnp.mean(grad_scaled * scaled, axis=-1, keepdims=True)
    )
    return (grad_rows, jnp.sum(grad_normed * scaled, axis=0))


def block_terms(query_rows, key_rows, seg_ids, begin, reach, rate):
    inner = jnp.dot(query_rows, key_rows.T, preferred_element_type=jnp.float32)
    row_places = begin + jnp.arange(reach - begin, dtype=jnp.int32)
    col_places = jnp.arange(reach, dtype=jnp.int32)
    allowed = (seg_ids[begin:reach][:, None] == seg_ids[:reach][None, :]) & (
        col_places[None, :] <= row_places[:, None]
    )
    distance = jnp.maximum(row_places[:, None] - col_places[None, :], 0).astype(jnp.float32)
    decay_w = jnp.where(allowed, jnp.exp(-rate * distance), jnp.float32(0.0))
    return (inner, allowed, decay_w, distance)


def head_forward(query, keys, values, pkeys, pvalues, rate, seg_ids):
    length, width = query.shape
    block = min(512, length)
    scale = 1.0 / math.sqrt(width)
    attn_parts, memory_parts, lse_parts = ([], [], [])
    for begin in range(0, length, block):
        reach = begin + block
        query_rows = query[begin:reach]
        inner, allowed, decay_w, distance = block_terms(
            query_rows, keys[:reach], seg_ids, begin, reach, rate
        )
        per_scores = jnp.dot(query_rows, pkeys.T, preferred_element_type=jnp.float32) * scale
        seq_scores = jnp.where(allowed, inner * scale, -jnp.inf)
        top = jnp.maximum(
            jnp.max(per_scores, axis=1, keepdims=True), jnp.max(seq_scores, axis=1, keepdims=True)
        )
        per_exp = jnp.exp(per_scores - top)
        seq_exp = jnp.exp(seq_scores - top)
        denom = jnp.sum(per_exp, axis=1, keepdims=True) + jnp.sum(seq_exp, axis=1, keepdims=True)
        attended = jnp.dot(
            (per_exp / denom).astype(jnp.bfloat16), pvalues, preferred_element_type=jnp.float32
        )
        attended = attended + jnp.dot(
            (seq_exp / denom).astype(jnp.bfloat16),
            values[:reach],
            preferred_element_type=jnp.float32,
        )
        memory_w = (inner * decay_w * (1.0 / width)).astype(jnp.bfloat16)
        recalled = jnp.dot(memory_w, values[:reach], preferred_element_type=jnp.float32)
        attn_parts.append(attended)
        memory_parts.append(recalled)
        lse_parts.append(top[:, 0] + jnp.log(denom[:, 0]))
    return (
        jnp.concatenate(attn_parts, 0),
        jnp.concatenate(memory_parts, 0),
        jnp.concatenate(lse_parts, 0),
    )


def head_backward(query, keys, values, pkeys, pvalues, rate, seg_ids, lse, grad_attn, grad_memory):
    length, width = query.shape
    block = min(512, length)
    scale = 1.0 / math.sqrt(width)
    query_grads = []
    grad_keys = jnp.zeros((length, width), jnp.float32)
    grad_values = jnp.zeros((length, width), jnp.float32)
    grad_pkeys = jnp.zeros(pkeys.shape, jnp.float32)
    grad_pvalues = jnp.zeros(pvalues.shape, jnp.float32)
    grad_rate = jnp.float32(0.0)
    for begin in range(0, length, block):
        reach = begin + block
        query_rows = query[begin:reach]
        key_rows = keys[:reach]
        value_rows = values[:reach]
        inner, allowed, decay_w, distance = block_terms(
            query_rows, key_rows, seg_ids, begin, reach, rate
        )
        per_scores = jnp.dot(query_rows, pkeys.T, preferred_element_type=jnp.float32) * scale
        seq_scores = jnp.where(allowed, inner * scale, -jnp.inf)
        row_lse = lse[begin:reach][:, None]
        per_prob = jnp.exp(per_scores - row_lse)
        seq_prob = jnp.exp(seq_scores - row_lse)
        attn_rows = grad_attn[begin:reach]
        memory_rows = grad_memory[begin:reach]
        per_dp = jnp.dot(attn_rows, pvalues.T, preferred_element_type=jnp.float32)
        seq_dp = jnp.dot(attn_rows, value_rows.T, preferred_element_type=jnp.float32)
        delta = jnp.sum(per_prob * per_dp, axis=1, keepdims=True) + jnp.sum(
            seq_prob * seq_dp, axis=1, keepdims=True
        )
        per_ds = (per_prob * (per_dp - delta)).astype(jnp.bfloat16)
        seq_ds = (seq_prob * (seq_dp - delta)).astype(jnp.bfloat16)
        rows_grad = (
            jnp.dot(per_ds, pkeys, preferred_element_type=jnp.float32)
            + jnp.dot(seq_ds, key_rows, preferred_element_type=jnp.float32)
        ) * scale
        grad_pkeys = (
            grad_pkeys
            + jnp.einsum("qk,qd->kd", per_ds, query_rows, preferred_element_type=jnp.float32)
            * scale
        )
        grad_pvalues = grad_pvalues + jnp.einsum(
            "qk,qd->kd",
            per_prob.astype(jnp.bfloat16),
            attn_rows,
            preferred_element_type=jnp.float32,
        )
        key_part = (
            jnp.einsum("qk,qd->kd", seq_ds, query_rows, preferred_element_type=jnp.float32) * scale
        )
        value_part = jnp.einsum(
            "qk,qd->kd",
            seq_prob.astype(jnp.bfloat16),
            attn_rows,
            preferred_element_type=jnp.float32,
        )
        memory_w = (inner * decay_w * (1.0 / width)).astype(jnp.bfloat16)
        grad_mw = jnp.dot(memory_rows, value_rows.T, preferred_element_type=jnp.float32)
        value_part = value_part + jnp.einsum(
            "qk,qd->kd", memory_w, memory_rows, preferred_element_type=jnp.float32
        )
        grad_inner = (grad_mw * decay_w * (1.0 / width)).astype(jnp.bfloat16)
        rows_grad = rows_grad + jnp.dot(grad_inner, key_rows, preferred_element_type=jnp.float32)
        key_part = key_part + jnp.einsum(
            "qk,qd->kd", grad_inner, query_rows, preferred_element_type=jnp.float32
        )
        grad_rate = grad_rate - jnp.sum(grad_mw * inner * decay_w * (1.0 / width) * distance)
        grad_keys = grad_keys.at[:reach].add(key_part)
        grad_values = grad_values.at[:reach].add(value_part)
        query_grads.append(rows_grad)
    return (
        jnp.concatenate(query_grads, 0),
        grad_keys,
        grad_values,
        grad_pkeys,
        grad_pvalues,
        grad_rate,
    )


def layer_forward(rows_in, seg_ids, full, pkv, rates):
    mix_w, out_w, gu_w, down_w, gains = full
    tokens = rows_in.shape[0]
    gain_one = gains[:, 0].astype(jnp.float32)
    gain_two = gains[:, 1].astype(jnp.float32)
    inverse_one = rms_scale(rows_in)
    scaled_one = rows_in * inverse_one
    normed = (scaled_one * gain_one).astype(jnp.bfloat16)
    proj = jnp.dot(normed, mix_w, preferred_element_type=jnp.float32)
    qkv = proj[:, : 3 * D].astype(jnp.bfloat16).reshape(tokens, 3, H, HD)
    gate = jax.nn.sigmoid(proj[:, 3 * D :])
    grouped = lax.all_to_all(qkv, "seq", split_axis=2, concat_axis=0, tiled=True)
    attn_heads, memory_heads, lse_heads = ([], [], [])
    for head in range(grouped.shape[2]):
        cols = slice(head * HD, (head + 1) * HD)
        attended, recalled, lse = head_forward(
            grouped[:, 0, head],
            grouped[:, 1, head],
            grouped[:, 2, head],
            pkv[0][:, cols],
            pkv[1][:, cols],
            rates[head],
            seg_ids,
        )
        attn_heads.append(attended)
        memory_heads.append(recalled)
        lse_heads.append(lse)
    mixed = jnp.stack([jnp.stack(attn_heads, 1), jnp.stack(memory_heads, 1)], 1).astype(
        jnp.bfloat16
    )
    returned = lax.all_to_all(mixed, "seq", split_axis=0, concat_axis=2, tiled=True)
    attended = returned[:, 0].reshape(tokens, D).astype(jnp.float32)
    recalled = returned[:, 1].reshape(tokens, D).astype(jnp.float32)
    combined = (attended + gate * recalled).astype(jnp.bfloat16)
    mid = rows_in + jnp.dot(combined, out_w, preferred_element_type=jnp.float32)
    inverse_two = rms_scale(mid)
    scaled_two = mid * inverse_two
    normed_two = (scaled_two * gain_two).astype(jnp.bfloat16)
    gate_up = jnp.dot(normed_two, gu_w, preferred_element_type=jnp.float32)
    hidden = (jax.nn.silu(gate_up[:, :FF]) * gate_up[:, FF:]).astype(jnp.bfloat16)
    result = mid + jnp.dot(hidden, down_w, preferred_element_type=jnp.float32)
    kept = (
        seg_ids,
        inverse_one,
        scaled_one,
        normed,
        grouped,
        jnp.stack(lse_heads, 1),
        gate,
        recalled,
        combined,
        inverse_two,
        scaled_two,
        normed_two,
        gate_up,
        hidden,
    )
    return (result, kept)


def layer_backward(grad_out, kept, full, pkv, rates):
    (
        seg_ids,
        inverse_one,
        scaled_one,
        normed,
        grouped,
        lse_all,
        gate,
        recalled,
        combined,
        inverse_two,
        scaled_two,
        normed_two,
        gate_up,
        hidden,
    ) = kept
    mix_w, out_w, gu_w, down_w, gains = full
    tokens = grad_out.shape[0]
    gain_one = gains[:, 0].astype(jnp.float32)
    gain_two = gains[:, 1].astype(jnp.float32)
    grad_f = grad_out.astype(jnp.bfloat16)
    grad_down = jnp.einsum("tf,td->fd", hidden, grad_f, preferred_element_type=jnp.float32)
    grad_hidden = jnp.dot(grad_f, down_w.T, preferred_element_type=jnp.float32)
    gate_part = gate_up[:, :FF]
    up_part = gate_up[:, FF:]
    sig_part = jax.nn.sigmoid(gate_part)
    grad_gate_part = grad_hidden * up_part * sig_part * (1.0 + gate_part * (1.0 - sig_part))
    grad_up_part = grad_hidden * gate_part * sig_part
    grad_gate_up = jnp.concatenate([grad_gate_part, grad_up_part], 1).astype(jnp.bfloat16)
    grad_gu = jnp.einsum("td,tf->df", normed_two, grad_gate_up, preferred_element_type=jnp.float32)
    grad_normed_two = jnp.dot(grad_gate_up, gu_w.T, preferred_element_type=jnp.float32)
    grad_mid_norm, grad_gain_two = norm_back(grad_normed_two, scaled_two, inverse_two, gain_two)
    grad_mid = grad_out + grad_mid_norm
    grad_branch = grad_mid.astype(jnp.bfloat16)
    grad_out_w = jnp.einsum("td,te->de", combined, grad_branch, preferred_element_type=jnp.float32)
    grad_combined = jnp.dot(grad_branch, out_w.T, preferred_element_type=jnp.float32)
    grad_attended = grad_combined.astype(jnp.bfloat16).reshape(tokens, H, HD)
    grad_recalled = (grad_combined * gate).astype(jnp.bfloat16).reshape(tokens, H, HD)
    grad_gate_pre = grad_combined * recalled * gate * (1.0 - gate)
    outgoing = jnp.stack([grad_attended, grad_recalled], 1)
    headward = lax.all_to_all(outgoing, "seq", split_axis=2, concat_axis=0, tiled=True)
    head_grads, pkey_grads, pvalue_grads, rate_grads = ([], [], [], [])
    for head in range(grouped.shape[2]):
        cols = slice(head * HD, (head + 1) * HD)
        dq, dk, dv, dpk, dpv, drate = head_backward(
            grouped[:, 0, head],
            grouped[:, 1, head],
            grouped[:, 2, head],
            pkv[0][:, cols],
            pkv[1][:, cols],
            rates[head],
            seg_ids,
            lse_all[:, head],
            headward[:, 0, head],
            headward[:, 1, head],
        )
        head_grads.append(jnp.stack([dq, dk, dv], 1))
        pkey_grads.append(dpk)
        pvalue_grads.append(dpv)
        rate_grads.append(drate)
    grads_heads = jnp.stack(head_grads, 2).astype(jnp.bfloat16)
    tokenward = lax.all_to_all(grads_heads, "seq", split_axis=0, concat_axis=2, tiled=True)
    grad_proj = jnp.concatenate(
        [tokenward.reshape(tokens, 3 * D), grad_gate_pre.astype(jnp.bfloat16)], 1
    )
    grad_mix = jnp.einsum("td,tf->df", normed, grad_proj, preferred_element_type=jnp.float32)
    grad_normed = jnp.dot(grad_proj, mix_w.T, preferred_element_type=jnp.float32)
    grad_in_norm, grad_gain_one = norm_back(grad_normed, scaled_one, inverse_one, gain_one)
    grad_rows = grad_mid + grad_in_norm
    weight_terms = (
        grad_mix,
        grad_out_w,
        grad_gu,
        grad_down,
        jnp.stack([grad_gain_one, grad_gain_two], 1),
    )
    memory_terms = (
        jnp.stack([jnp.concatenate(pkey_grads, 1), jnp.concatenate(pvalue_grads, 1)], 0),
        jnp.stack(rate_grads, 0),
    )
    return (weight_terms, memory_terms, grad_rows)


def on_device(
    inputs, segment_ids, cotangent, w_mix, w_out, w_gu, w_down, norm_gains, persist_kv, memory_decay
):
    first = lax.axis_index("section") == 0
    own_weights = (w_mix[0], w_out[0], w_gu[0], w_down[0], norm_gains[0])
    pkv = persist_kv[0]
    rates = memory_decay[0]
    count = inputs.shape[0]
    tokens = inputs.shape[2]
    zero_rows = jnp.zeros((tokens, D), jnp.float32)
    received = jnp.zeros((tokens, D), jnp.bfloat16)
    kept_ticks, out_ticks = ([], [])
    for tick in range(count + 1):
        own_rows = inputs[tick, 0].astype(jnp.float32) if tick < count else zero_rows
        layer_in = jnp.where(first, own_rows, received.astype(jnp.float32))
        seg_ids = jnp.where(
            first, segment_ids[min(tick, count - 1), 0], segment_ids[max(tick - 1, 0), 0]
        )
        full = (
            lax.all_gather(own_weights[0], "shard", axis=0, tiled=True),
            lax.all_gather(own_weights[1], "shard", axis=0, tiled=True),
            lax.all_gather(own_weights[2], "shard", axis=0, tiled=True),
            lax.all_gather(own_weights[3], "shard", axis=0, tiled=True),
            lax.all_gather(own_weights[4], "shard", axis=0, tiled=True),
        )
        result, kept = layer_forward(layer_in, seg_ids, full, pkv, rates)
        result_low = result.astype(jnp.bfloat16)
        out_ticks.append(result_low)
        kept_ticks.append(kept)
        if tick < count:
            received = shifted(result_low, "section", 1)
    grad_weights = (
        jnp.zeros((D, 4 * D), jnp.float32),
        jnp.zeros((D, D), jnp.float32),
        jnp.zeros((D, 2 * FF), jnp.float32),
        jnp.zeros((FF, D), jnp.float32),
        jnp.zeros((D, 2), jnp.float32),
    )
    grad_memory = (
        jnp.zeros((2,) + pkv.shape[1:], jnp.float32),
        jnp.zeros(rates.shape, jnp.float32),
    )
    back_received = jnp.zeros((tokens, D), jnp.bfloat16)
    grad_ticks = []
    for tick in range(count + 1):
        lower = max(tick - 1, 0)
        upper = min(tick + 1, count)
        kept = jax.tree.map(
            lambda early, late: jnp.where(first, early, late), kept_ticks[lower], kept_ticks[upper]
        )
        given = cotangent[tick, 0].astype(jnp.float32) if tick < count else zero_rows
        grad_out = jnp.where(first, back_received.astype(jnp.float32), given)
        full = (
            lax.all_gather(own_weights[0], "shard", axis=0, tiled=True),
            lax.all_gather(own_weights[1], "shard", axis=0, tiled=True),
            lax.all_gather(own_weights[2], "shard", axis=0, tiled=True),
            lax.all_gather(own_weights[3], "shard", axis=0, tiled=True),
            lax.all_gather(own_weights[4], "shard", axis=0, tiled=True),
        )
        weight_terms, memory_terms, grad_rows = layer_backward(grad_out, kept, full, pkv, rates)
        grad_weights = jax.tree.map(jnp.add, grad_weights, weight_terms)
        grad_memory = jax.tree.map(jnp.add, grad_memory, memory_terms)
        grad_ticks.append(grad_rows)
        if tick < count:
            back_received = shifted(grad_rows.astype(jnp.bfloat16), "section", -1)
    section_out = jnp.stack(
        [jnp.where(first, out_ticks[batch], out_ticks[batch + 1]) for batch in range(count)], 0
    )
    section_grad = jnp.stack(
        [
            jnp.where(
                first,
                grad_ticks[batch + 1],
                grad_ticks[batch].astype(jnp.bfloat16).astype(jnp.float32),
            )
            for batch in range(count)
        ],
        0,
    )
    shares = jax.tree.map(
        lambda part: part.astype(jnp.float32),
        lax.psum_scatter(as_sent(grad_weights), "shard", scatter_dimension=0, tiled=True),
    )
    shares = jax.tree.map(lambda part: part.astype(jnp.float32), lax.psum(as_sent(shares), "seq"))
    memory_sums = lax.psum(grad_memory, "shard")
    return (
        section_out.reshape(1, count, 1, tokens, D),
        section_grad.reshape(1, count, 1, tokens, D),
        shares[0][None],
        shares[1][None],
        shares[2][None],
        shares[3][None],
        shares[4][None],
        memory_sums[0][None],
        memory_sums[1][None],
    )


MESH = pl.DeviceIdType.MESH
BF = jnp.bfloat16
F32 = jnp.float32


def here():
    return (lax.axis_index("section"), lax.axis_index("seq"), lax.axis_index("shard"))


def peer(place, chip, flip):
    x, s, z = place
    if chip % 2:
        x = 1 - x
    if chip // 2:
        s = (s + 2) % 4
    if flip:
        s = s + 1 - 2 * (s % 2)
    return (x, s, z)


def rows_of(device, size):
    x, s, _ = device
    return pl.ds(pl.multiple_of((s * 2 + x) * size, size), size)


class Gather:
    def __init__(self, full, batch, send, recv):
        self.place = here()
        self.full, self.batch, self.send, self.recv = full, batch, send, recv
        self.size = full.shape[1] // 8

    def copy(self, owner, target, sem):
        block = self.full.at[self.batch, rows_of(owner, self.size)]
        return pltpu.make_async_remote_copy(
            src_ref=block,
            dst_ref=block,
            send_sem=self.send.at[self.batch, sem],
            recv_sem=self.recv.at[self.batch, sem],
            device_id=target,
            device_id_type=MESH,
        )

    def start(self, value):
        self.full[self.batch, rows_of(self.place, self.size), :] = value
        for chip in (3, 1, 2, 0):
            self.copy(self.place, peer(self.place, chip, chip == 0), chip).start()

    def forward(self):
        other = peer(self.place, 0, True)
        for chip in (1, 2, 3):
            owner = peer(self.place, chip, False)
            self.copy(owner, owner, chip).wait_recv()
            self.copy(owner, other, 3 + chip).start()

    def finish(self):
        other = peer(self.place, 0, True)
        self.copy(other, other, 0).wait_recv()
        for chip in (1, 2, 3):
            owner = peer(self.place, chip, True)
            self.copy(owner, other, 3 + chip).wait_recv()
        for chip in (0, 1, 2, 3):
            self.copy(self.place, peer(self.place, chip, chip == 0), chip).wait_send()
        for chip in (1, 2, 3):
            self.copy(peer(self.place, chip, False), other, 3 + chip).wait_send()


class Scatter:
    def __init__(self, part, batch, pair, away, near, send, recv):
        self.place = here()
        self.part, self.batch, self.pair, self.away, self.near = part, batch, pair, away, near
        self.send, self.recv = send, recv
        self.size = part.shape[1] // 8

    def to_pair(self, chip):
        return pltpu.make_async_remote_copy(
            src_ref=self.part.at[self.batch, rows_of(peer(self.place, chip, True), self.size)],
            dst_ref=self.pair.at[self.batch, chip],
            send_sem=self.send.at[self.batch, chip],
            recv_sem=self.recv.at[self.batch, chip],
            device_id=peer(self.place, 0, True),
            device_id_type=MESH,
        )

    def to_chip(self, chip):
        return pltpu.make_async_remote_copy(
            src_ref=self.away.at[self.batch, chip - 1],
            dst_ref=self.near.at[self.batch, chip - 1],
            send_sem=self.send.at[self.batch, 3 + chip],
            recv_sem=self.recv.at[self.batch, 3 + chip],
            device_id=peer(self.place, chip, False),
            device_id_type=MESH,
        )

    def start(self):
        for chip in (3, 1, 2, 0):
            self.to_pair(chip).start()

    def chip_sum(self, chip):
        self.to_pair(chip).wait_recv()
        own = self.part[self.batch, rows_of(peer(self.place, chip, False), self.size), :]
        return own.astype(F32) + self.pair[self.batch, chip].astype(F32)

    def forward(self):
        for chip in (3, 1, 2):
            self.away[self.batch, chip - 1] = self.chip_sum(chip).astype(BF)
            self.to_chip(chip).start()

    def finish(self):
        total = self.chip_sum(0)
        for chip in (1, 2, 3):
            self.to_chip(chip).wait_recv()
            total = total + self.near[self.batch, chip - 1].astype(F32)
        for chip in (0, 1, 2, 3):
            self.to_pair(chip).wait_send()
        for chip in (1, 2, 3):
            self.to_chip(chip).wait_send()
        return total


def meet():
    place = here()
    barrier = pltpu.get_barrier_semaphore()
    for chip in (0, 1, 2, 3):
        pl.semaphore_signal(
            barrier, inc=1, device_id=peer(place, chip, chip == 0), device_id_type=MESH
        )
    pl.semaphore_wait(barrier, 4)


def start_kernel(rows_ref, gain_ref, full_ref, gsend, grecv):
    meet()
    gathers = [Gather(full_ref, batch, gsend, grecv) for batch in range(2)]
    for batch, gather in enumerate(gathers):
        rows = rows_ref[batch]
        gather.start((rows * rms_scale(rows) * gain_ref[...]).astype(BF))
    for gather in gathers:
        gather.forward()
    for gather in gathers:
        gather.finish()


def forward_kernel(low, last, part_ref, rows_ref, gain_ref, own_ref, *rest):
    if last:
        pair, away, near, ssend, srecv = rest
    else:
        full_ref, pair, away, near, ssend, srecv, gsend, grecv = rest
    meet()
    scatters = [Scatter(part_ref, b, pair, away, near, ssend, srecv) for b in range(2)]
    for scatter in scatters:
        scatter.start()
    for scatter in scatters:
        scatter.forward()
    gathers = []
    for batch, scatter in enumerate(scatters):
        own = (rows_ref[batch] + scatter.finish()).astype(own_ref.dtype)
        own_ref[batch] = own
        if not last:
            own = own.astype(F32)
            gather = Gather(full_ref, batch, gsend, grecv)
            gather.start((own * rms_scale(own) * gain_ref[...]).astype(BF))
            gathers.append(gather)
    for gather in gathers:
        gather.forward()
    for gather in gathers:
        gather.finish()


def backward_kernel(last, part_ref, rows_ref, gain_ref, grad_ref, own_ref, gains_ref, *rest):
    if last:
        pair, away, near, ssend, srecv = rest
    else:
        full_ref, pair, away, near, ssend, srecv, gsend, grecv = rest
    meet()
    scatters = [Scatter(part_ref, b, pair, away, near, ssend, srecv) for b in range(2)]
    for scatter in scatters:
        scatter.start()
    for scatter in scatters:
        scatter.forward()
    gathers = []
    sums = jnp.zeros((1, D), F32)
    for batch, scatter in enumerate(scatters):
        grad_normed = scatter.finish()
        rows = rows_ref[batch]
        inverse = rms_scale(rows)
        grad_rows, gain_sum = norm_back(grad_normed, rows * inverse, inverse, gain_ref[...])
        sums = sums + gain_sum[None]
        own = (grad_ref[batch] + grad_rows).astype(own_ref.dtype)
        own_ref[batch] = own
        if not last:
            gather = Gather(full_ref, batch, gsend, grecv)
            gather.start(own.astype(BF))
            gathers.append(gather)
    gains_ref[...] = sums
    for gather in gathers:
        gather.forward()
    for gather in gathers:
        gather.finish()


def plane_call(kernel, number, operands, outs, scatter, gather):
    _, length, width = outs["full"].shape
    size = length // 8
    scratch = []
    if scatter:
        scratch += [
            pltpu.VMEM((2, 4, size, width), BF),
            pltpu.VMEM((2, 3, size, width), BF),
            pltpu.VMEM((2, 3, size, width), BF),
            pltpu.SemaphoreType.DMA((2, 7)),
            pltpu.SemaphoreType.DMA((2, 7)),
        ]
    if gather:
        scratch += [pltpu.SemaphoreType.DMA((2, 7)), pltpu.SemaphoreType.DMA((2, 7))]
    else:
        outs = {name: out for name, out in outs.items() if name != "full"}
    vmem = pl.BlockSpec(memory_space=pltpu.VMEM)
    return pl.pallas_call(
        kernel,
        out_shape=list(outs.values()),
        in_specs=[vmem] * len(operands),
        out_specs=[vmem] * len(outs),
        scratch_shapes=scratch,
        compiler_params=pltpu.CompilerParams(
            collective_id=number, has_side_effects=True, vmem_limit_bytes=24 * 2**20
        ),
    )(*operands)


def tensor_parallel(
    inputs, segment_ids, cotangent, w_mix, w_out, w_gu, w_down, norm_gains, persist_kv, memory_decay
):
    x, s, z = here()
    nx, ns, nz = (lax.axis_size(a) for a in ("section", "seq", "shard"))
    width = nx * ns
    mine = x * ns + s
    other = (1 - x) * ns + s
    first = x == 0
    count, _, tokens, _ = inputs.shape
    length = tokens * ns
    size = length // width
    depth = w_mix.shape[1]
    unit = w_down.shape[1] // width

    heads = w_mix[0].reshape(depth, 4, H, HD)
    halves = w_gu[0].reshape(depth, 2, nz, width, unit)
    downs = w_down[0].reshape(width, unit, D)

    def pick(which):
        return (
            lax.dynamic_index_in_dim(heads, which, 2, keepdims=False).reshape(depth, 4 * HD),
            lax.dynamic_index_in_dim(halves, which, 3, keepdims=False).reshape(
                depth, 2 * nz * unit
            ),
            lax.dynamic_index_in_dim(downs, which, 0, keepdims=False),
        )

    def layers(own, got):
        return (jnp.where(first, own, got), jnp.where(first, got, own))

    swap = [(0, 1), (1, 0)]
    parts = [layers(o, lax.ppermute(g, "section", swap)) for o, g in zip(pick(mine), pick(other))]
    out_rows = lax.dynamic_index_in_dim(
        w_out[0].reshape(2, HD, D), lax.rem(s, 2), 0, keepdims=False
    )
    out_all = lax.all_gather(out_rows, "shard", axis=0)
    out_own = lax.dynamic_index_in_dim(out_all, mine // 2, 0, keepdims=False)
    out_got = lax.ppermute(
        lax.dynamic_index_in_dim(out_all, other // 2, 0, keepdims=False), "section", swap
    )
    out_w = layers(out_own, out_got)
    mix_w, gu_w, down_w = (
        [lax.all_gather(part[layer], "shard", axis=0, tiled=True) for layer in range(2)]
        for part in parts
    )

    small = jnp.concatenate([persist_kv[0].reshape(-1).astype(F32), memory_decay[0]])
    small = lax.all_gather(small, ("section", "seq"), axis=0)
    rates = small[:, -2:].reshape(2, H)[:, mine]
    persist = small[:, :-2].astype(BF).reshape(2, ns, 2, persist_kv.shape[2], 2, HD)
    persist = lax.dynamic_index_in_dim(persist, mine // 2, 1, keepdims=False)
    persist = lax.dynamic_index_in_dim(persist, lax.rem(mine, 2), 3, keepdims=False)
    gains = lax.all_gather(norm_gains[0], ("section", "shard"), axis=0, tiled=True)
    gains = gains.astype(F32).reshape(2, 1, D, 2)

    def own_rows(whole):
        return lax.dynamic_slice_in_dim(whole[:, 0], x * size, size, 1).astype(F32)

    full = jax.ShapeDtypeStruct((count, length, D), BF)
    own32 = jax.ShapeDtypeStruct((count, size, D), F32)
    own16 = jax.ShapeDtypeStruct((count, size, D), BF)
    sums = jax.ShapeDtypeStruct((1, D), F32)

    cot_full = lax.all_gather(cotangent[:, 0], "seq", axis=1, tiled=True)
    rows = own_rows(inputs)
    (normed,) = plane_call(
        start_kernel, 0, (rows, gains[0, :, :, 0]), {"full": full}, False, True
    )
    kept = []
    outputs = []
    flat = count * length
    for layer in range(2):
        proj = jnp.dot(normed.reshape(flat, D), mix_w[layer], preferred_element_type=F32)
        qkv = proj[:, : 3 * HD].astype(BF).reshape(count, length, 3, HD)
        gate = jax.nn.sigmoid(proj[:, 3 * HD :])
        results = [
            head_forward(
                qkv[b, :, 0],
                qkv[b, :, 1],
                qkv[b, :, 2],
                persist[layer, 0],
                persist[layer, 1],
                rates[layer],
                segment_ids[b, 0],
            )
            for b in range(count)
        ]
        attended = jnp.concatenate([r[0] for r in results], 0).astype(BF).astype(F32)
        recalled = jnp.concatenate([r[1] for r in results], 0).astype(BF).astype(F32)
        combined = (attended + gate * recalled).astype(BF)
        partial = jnp.dot(combined, out_w[layer], preferred_element_type=F32).astype(BF)
        mid, normed_two = plane_call(
            functools.partial(forward_kernel, False, False),
            1 + 2 * layer,
            (partial.reshape(count, length, D), rows, gains[layer, :, :, 1]),
            {"own": own32, "full": full},
            True,
            True,
        )
        gate_up = jnp.dot(normed_two.reshape(flat, D), gu_w[layer], preferred_element_type=F32)
        half = gate_up.shape[1] // 2
        hidden = (jax.nn.silu(gate_up[:, :half]) * gate_up[:, half:]).astype(BF)
        partial = jnp.dot(hidden, down_w[layer], preferred_element_type=F32).astype(BF)
        kept.append(
            (rows, normed, qkv, gate, [r[2] for r in results], recalled, combined, mid)
            + (normed_two, gate_up, hidden)
        )
        last = layer == 1
        found = plane_call(
            functools.partial(forward_kernel, True, last),
            2 + 2 * layer,
            (partial.reshape(count, length, D), mid, gains[1, :, :, 0]),
            {"own": own16, "full": full},
            True,
            not last,
        )
        outputs.append(found[0])
        if not last:
            rows = found[0].astype(F32)
            normed = found[1]

    grad_full = cot_full
    grad_own = own_rows(cotangent)
    pieces, gain_sums, memory_terms, grads = ([None] * 2, [None] * 2, [None] * 2, [None] * 2)
    for layer in (1, 0):
        (
            rows,
            normed,
            qkv,
            gate,
            lse,
            recalled,
            combined,
            mid,
            normed_two,
            gate_up,
            hidden,
        ) = kept[layer]
        grad_f = grad_full.reshape(flat, D)
        grad_hidden = jnp.dot(grad_f, down_w[layer].T, preferred_element_type=F32)
        half = gate_up.shape[1] // 2
        gate_part = gate_up[:, :half]
        up_part = gate_up[:, half:]
        sig_part = jax.nn.sigmoid(gate_part)
        grad_gate_up = jnp.concatenate(
            [
                grad_hidden * up_part * sig_part * (1.0 + gate_part * (1.0 - sig_part)),
                grad_hidden * gate_part * sig_part,
            ],
            1,
        ).astype(BF)
        partial = jnp.dot(grad_gate_up, gu_w[layer].T, preferred_element_type=F32).astype(BF)
        grad_down = jnp.einsum("tf,td->fd", hidden, grad_f, preferred_element_type=F32)
        grad_gu = jnp.einsum(
            "td,tf->df", normed_two.reshape(flat, D), grad_gate_up, preferred_element_type=F32
        )
        grad_mid, gain_two, branch = plane_call(
            functools.partial(backward_kernel, False),
            5 + 2 * (1 - layer),
            (partial.reshape(count, length, D), mid, gains[layer, :, :, 1], grad_own),
            {"own": own32, "sums": sums, "full": full},
            True,
            True,
        )
        branch = branch.reshape(flat, D)
        grad_combined = jnp.dot(branch, out_w[layer].T, preferred_element_type=F32)
        grad_out = jnp.einsum("td,te->de", combined, branch, preferred_element_type=F32)
        grad_attended = grad_combined.astype(BF).reshape(count, length, HD)
        grad_recalled = (grad_combined * gate).astype(BF).reshape(count, length, HD)
        grad_gate_pre = grad_combined * recalled * gate * (1.0 - gate)
        found = [
            head_backward(
                qkv[b, :, 0],
                qkv[b, :, 1],
                qkv[b, :, 2],
                persist[layer, 0],
                persist[layer, 1],
                rates[layer],
                segment_ids[b, 0],
                lse[b],
                grad_attended[b],
                grad_recalled[b],
            )
            for b in range(count)
        ]
        grad_heads = jnp.concatenate([jnp.concatenate(f[:3], 1) for f in found], 0)
        grad_proj = jnp.concatenate([grad_heads, grad_gate_pre], 1).astype(BF)
        memory_terms[layer] = (
            jnp.stack([sum(f[3] for f in found), sum(f[4] for f in found)], 0),
            sum(f[5] for f in found),
        )
        partial = jnp.dot(grad_proj, mix_w[layer].T, preferred_element_type=F32).astype(BF)
        grad_mix = jnp.einsum(
            "td,tf->df", normed.reshape(flat, D), grad_proj, preferred_element_type=F32
        )
        last = layer == 0
        found = plane_call(
            functools.partial(backward_kernel, last),
            6 + 2 * (1 - layer),
            (partial.reshape(count, length, D), rows, gains[layer, :, :, 0], grad_mid),
            {"own": own32 if last else own16, "sums": sums, "full": full},
            True,
            not last,
        )
        grads[layer] = found[0].astype(BF)
        gain_sums[layer] = jnp.stack([found[1][0], gain_two[0]], 1)
        if not last:
            grad_own = found[0].astype(F32)
            grad_full = found[2]
        owner = mine // 2 == jnp.arange(nz)
        grad_out = jnp.where(owner[:, None, None], grad_out[None], 0.0)
        pieces[layer] = [
            lax.psum_scatter(part.astype(BF), "shard", scatter_dimension=0, tiled=True)
            for part in (grad_mix, grad_gu, grad_down, grad_out.reshape(nz * HD, D))
        ]

    def to_section(of_layer):
        own = jnp.where(first, of_layer[0], of_layer[1])
        got = lax.ppermute(jnp.where(first, of_layer[1], of_layer[0]), "section", swap)
        return layers(own, got)

    def whole_rows(of_layer):
        return jnp.concatenate(to_section(of_layer), 1)[None, :, None]

    section_out = whole_rows(outputs)
    section_grad = whole_rows(grads).astype(F32)

    def collect(index):
        both = jnp.stack(to_section([pieces[layer][index] for layer in range(2)]), 0)
        return lax.all_gather(both, "seq", axis=0).astype(F32)

    mix_all = collect(0).reshape(ns, nx, depth, 4, HD)
    gu_all = collect(1).reshape(ns, nx, depth, 2, nz, unit)
    down_all = collect(2)
    out_all = collect(3)
    grad_mix = mix_all.transpose(2, 3, 1, 0, 4).reshape(1, depth, 4 * D)
    grad_gu = gu_all.transpose(2, 3, 4, 1, 0, 5).reshape(1, depth, 2 * FF)
    grad_down = down_all.transpose(1, 0, 2, 3).reshape(1, unit * width, D)
    out_all = lax.dynamic_index_in_dim(out_all, z // 2, 1, keepdims=False)
    grad_out = lax.dynamic_slice_in_dim(out_all, 2 * lax.rem(z, 2), 2, 0).reshape(1, 2 * HD, D)

    memory_all = jnp.stack([m[0] for m in memory_terms], 0)
    places = jnp.arange(width) == mine
    memory_all = jnp.where(places[None, None, None, :, None], memory_all[:, :, :, None, :], 0.0)
    rate_all = jnp.where(places[None], jnp.stack([m[1] for m in memory_terms])[:, None], 0.0)
    gain_all = jnp.stack(gain_sums, 0)
    packed = jnp.concatenate(
        [memory_all.reshape(-1), rate_all.reshape(-1), gain_all.reshape(-1)]
    )
    packed = lax.psum(packed, ("section", "seq", "shard"))
    cut = memory_all.size
    memory_all = packed[:cut].reshape(2, 2, -1, D)
    rate_all = packed[cut : cut + 2 * width].reshape(2, width)
    gain_all = packed[cut + 2 * width :].reshape(2, D, 2)
    own = lax.dynamic_index_in_dim
    grad_persist = lax.dynamic_slice_in_dim(
        own(memory_all, x, 0), s * 2 * HD, 2 * HD, 3
    )
    grad_rate = lax.dynamic_slice_in_dim(own(rate_all, x, 0), 2 * s, 2, 1)
    grad_gain = lax.dynamic_slice_in_dim(own(gain_all, x, 0), z * depth, depth, 1)
    return (
        section_out,
        section_grad,
        grad_mix,
        grad_out,
        grad_gu,
        grad_down,
        grad_gain,
        grad_persist,
        grad_rate,
    )


def solution(mesh):
    sizes = mesh.shape
    planar = (sizes["section"], sizes["seq"]) == (2, 4)
    placed = (
        P(None, "shard", "seq", None),
        P(None, "shard", None),
        P(None, "shard", "seq", None),
        P("section", "shard", None),
        P("section", "shard", None),
        P("section", "shard", None),
        P("section", "shard", None),
        P("section", "shard", None),
        P("section", None, None, "seq"),
        P("section", "seq"),
    )
    return jax.shard_map(
        tensor_parallel if planar else on_device,
        mesh=mesh,
        in_specs=placed,
        out_specs=(
            P("section", None, "shard", "seq", None),
            P("section", None, "shard", "seq", None),
            P("section", "shard", None),
            P("section", "shard", None),
            P("section", "shard", None),
            P("section", "shard", None),
            P("section", "shard", None),
            P("section", None, None, "seq"),
            P("section", "seq"),
        ),
        check_vma=False,
    )
```

```python
import functools
import math

import jax
import jax.numpy as jnp
from jax import lax
from jax.experimental import pallas as pl
from jax.experimental.pallas import tpu as pltpu
from jax.sharding import PartitionSpec as P

D = 1024
H = 8
HD = 128
FF = 2816


def shifted(value, axis, by):
    size = lax.axis_size(axis)
    pairs = [(i, i + by) for i in range(size) if 0 <= i + by < size]
    return lax.ppermute(value, axis, pairs)


def as_sent(value):
    return jax.tree.map(lambda a: a.astype(jnp.bfloat16) if a.dtype == jnp.float32 else a, value)


def rms_scale(values):
    return lax.rsqrt(jnp.mean(values * values, axis=-1, keepdims=True) + 1e-06)


def norm_back(grad_normed, scaled, inverse, gain):
    grad_scaled = grad_normed * gain
    grad_rows = inverse * (
        grad_scaled - scaled * jnp.mean(grad_scaled * scaled, axis=-1, keepdims=True)
    )
    return (grad_rows, jnp.sum(grad_normed * scaled, axis=0))


def block_terms(query_rows, key_rows, seg_ids, begin, reach, rate):
    inner = jnp.dot(query_rows, key_rows.T, preferred_element_type=jnp.float32)
    row_places = begin + jnp.arange(reach - begin, dtype=jnp.int32)
    col_places = jnp.arange(reach, dtype=jnp.int32)
    allowed = (seg_ids[begin:reach][:, None] == seg_ids[:reach][None, :]) & (
        col_places[None, :] <= row_places[:, None]
    )
    distance = jnp.maximum(row_places[:, None] - col_places[None, :], 0).astype(jnp.float32)
    decay_w = jnp.where(allowed, jnp.exp(-rate * distance), jnp.float32(0.0))
    return (inner, allowed, decay_w, distance)


def head_forward(query, keys, values, pkeys, pvalues, rate, seg_ids):
    length, width = query.shape
    block = min(512, length)
    scale = 1.0 / math.sqrt(width)
    attn_parts, memory_parts, lse_parts = ([], [], [])
    for begin in range(0, length, block):
        reach = begin + block
        query_rows = query[begin:reach]
        inner, allowed, decay_w, distance = block_terms(
            query_rows, keys[:reach], seg_ids, begin, reach, rate
        )
        per_scores = jnp.dot(query_rows, pkeys.T, preferred_element_type=jnp.float32) * scale
        seq_scores = jnp.where(allowed, inner * scale, -jnp.inf)
        top = jnp.maximum(
            jnp.max(per_scores, axis=1, keepdims=True), jnp.max(seq_scores, axis=1, keepdims=True)
        )
        per_exp = jnp.exp(per_scores - top)
        seq_exp = jnp.exp(seq_scores - top)
        denom = jnp.sum(per_exp, axis=1, keepdims=True) + jnp.sum(seq_exp, axis=1, keepdims=True)
        attended = jnp.dot(
            (per_exp / denom).astype(jnp.bfloat16), pvalues, preferred_element_type=jnp.float32
        )
        attended = attended + jnp.dot(
            (seq_exp / denom).astype(jnp.bfloat16),
            values[:reach],
            preferred_element_type=jnp.float32,
        )
        memory_w = (inner * decay_w * (1.0 / width)).astype(jnp.bfloat16)
        recalled = jnp.dot(memory_w, values[:reach], preferred_element_type=jnp.float32)
        attn_parts.append(attended)
        memory_parts.append(recalled)
        lse_parts.append(top[:, 0] + jnp.log(denom[:, 0]))
    return (
        jnp.concatenate(attn_parts, 0),
        jnp.concatenate(memory_parts, 0),
        jnp.concatenate(lse_parts, 0),
    )


def head_backward(query, keys, values, pkeys, pvalues, rate, seg_ids, lse, grad_attn, grad_memory):
    length, width = query.shape
    block = min(512, length)
    scale = 1.0 / math.sqrt(width)
    query_grads = []
    grad_keys = jnp.zeros((length, width), jnp.float32)
    grad_values = jnp.zeros((length, width), jnp.float32)
    grad_pkeys = jnp.zeros(pkeys.shape, jnp.float32)
    grad_pvalues = jnp.zeros(pvalues.shape, jnp.float32)
    grad_rate = jnp.float32(0.0)
    for begin in range(0, length, block):
        reach = begin + block
        query_rows = query[begin:reach]
        key_rows = keys[:reach]
        value_rows = values[:reach]
        inner, allowed, decay_w, distance = block_terms(
            query_rows, key_rows, seg_ids, begin, reach, rate
        )
        per_scores = jnp.dot(query_rows, pkeys.T, preferred_element_type=jnp.float32) * scale
        seq_scores = jnp.where(allowed, inner * scale, -jnp.inf)
        row_lse = lse[begin:reach][:, None]
        per_prob = jnp.exp(per_scores - row_lse)
        seq_prob = jnp.exp(seq_scores - row_lse)
        attn_rows = grad_attn[begin:reach]
        memory_rows = grad_memory[begin:reach]
        per_dp = jnp.dot(attn_rows, pvalues.T, preferred_element_type=jnp.float32)
        seq_dp = jnp.dot(attn_rows, value_rows.T, preferred_element_type=jnp.float32)
        delta = jnp.sum(per_prob * per_dp, axis=1, keepdims=True) + jnp.sum(
            seq_prob * seq_dp, axis=1, keepdims=True
        )
        per_ds = (per_prob * (per_dp - delta)).astype(jnp.bfloat16)
        seq_ds = (seq_prob * (seq_dp - delta)).astype(jnp.bfloat16)
        rows_grad = (
            jnp.dot(per_ds, pkeys, preferred_element_type=jnp.float32)
            + jnp.dot(seq_ds, key_rows, preferred_element_type=jnp.float32)
        ) * scale
        grad_pkeys = (
            grad_pkeys
            + jnp.einsum("qk,qd->kd", per_ds, query_rows, preferred_element_type=jnp.float32)
            * scale
        )
        grad_pvalues = grad_pvalues + jnp.einsum(
            "qk,qd->kd",
            per_prob.astype(jnp.bfloat16),
            attn_rows,
            preferred_element_type=jnp.float32,
        )
        key_part = (
            jnp.einsum("qk,qd->kd", seq_ds, query_rows, preferred_element_type=jnp.float32) * scale
        )
        value_part = jnp.einsum(
            "qk,qd->kd",
            seq_prob.astype(jnp.bfloat16),
            attn_rows,
            preferred_element_type=jnp.float32,
        )
        memory_w = (inner * decay_w * (1.0 / width)).astype(jnp.bfloat16)
        grad_mw = jnp.dot(memory_rows, value_rows.T, preferred_element_type=jnp.float32)
        value_part = value_part + jnp.einsum(
            "qk,qd->kd", memory_w, memory_rows, preferred_element_type=jnp.float32
        )
        grad_inner = (grad_mw * decay_w * (1.0 / width)).astype(jnp.bfloat16)
        rows_grad = rows_grad + jnp.dot(grad_inner, key_rows, preferred_element_type=jnp.float32)
        key_part = key_part + jnp.einsum(
            "qk,qd->kd", grad_inner, query_rows, preferred_element_type=jnp.float32
        )
        grad_rate = grad_rate - jnp.sum(grad_mw * inner * decay_w * (1.0 / width) * distance)
        grad_keys = grad_keys.at[:reach].add(key_part)
        grad_values = grad_values.at[:reach].add(value_part)
        query_grads.append(rows_grad)
    return (
        jnp.concatenate(query_grads, 0),
        grad_keys,
        grad_values,
        grad_pkeys,
        grad_pvalues,
        grad_rate,
    )


def layer_forward(rows_in, seg_ids, full, pkv, rates):
    mix_w, out_w, gu_w, down_w, gains = full
    tokens = rows_in.shape[0]
    gain_one = gains[:, 0].astype(jnp.float32)
    gain_two = gains[:, 1].astype(jnp.float32)
    inverse_one = rms_scale(rows_in)
    scaled_one = rows_in * inverse_one
    normed = (scaled_one * gain_one).astype(jnp.bfloat16)
    proj = jnp.dot(normed, mix_w, preferred_element_type=jnp.float32)
    qkv = proj[:, : 3 * D].astype(jnp.bfloat16).reshape(tokens, 3, H, HD)
    gate = jax.nn.sigmoid(proj[:, 3 * D :])
    grouped = lax.all_to_all(qkv, "seq", split_axis=2, concat_axis=0, tiled=True)
    attn_heads, memory_heads, lse_heads = ([], [], [])
    for head in range(grouped.shape[2]):
        cols = slice(head * HD, (head + 1) * HD)
        attended, recalled, lse = head_forward(
            grouped[:, 0, head],
            grouped[:, 1, head],
            grouped[:, 2, head],
            pkv[0][:, cols],
            pkv[1][:, cols],
            rates[head],
            seg_ids,
        )
        attn_heads.append(attended)
        memory_heads.append(recalled)
        lse_heads.append(lse)
    mixed = jnp.stack([jnp.stack(attn_heads, 1), jnp.stack(memory_heads, 1)], 1).astype(
        jnp.bfloat16
    )
    returned = lax.all_to_all(mixed, "seq", split_axis=0, concat_axis=2, tiled=True)
    attended = returned[:, 0].reshape(tokens, D).astype(jnp.float32)
    recalled = returned[:, 1].reshape(tokens, D).astype(jnp.float32)
    combined = (attended + gate * recalled).astype(jnp.bfloat16)
    mid = rows_in + jnp.dot(combined, out_w, preferred_element_type=jnp.float32)
    inverse_two = rms_scale(mid)
    scaled_two = mid * inverse_two
    normed_two = (scaled_two * gain_two).astype(jnp.bfloat16)
    gate_up = jnp.dot(normed_two, gu_w, preferred_element_type=jnp.float32)
    hidden = (jax.nn.silu(gate_up[:, :FF]) * gate_up[:, FF:]).astype(jnp.bfloat16)
    result = mid + jnp.dot(hidden, down_w, preferred_element_type=jnp.float32)
    kept = (
        seg_ids,
        inverse_one,
        scaled_one,
        normed,
        grouped,
        jnp.stack(lse_heads, 1),
        gate,
        recalled,
        combined,
        inverse_two,
        scaled_two,
        normed_two,
        gate_up,
        hidden,
    )
    return (result, kept)


def layer_backward(grad_out, kept, full, pkv, rates):
    (
        seg_ids,
        inverse_one,
        scaled_one,
        normed,
        grouped,
        lse_all,
        gate,
        recalled,
        combined,
        inverse_two,
        scaled_two,
        normed_two,
        gate_up,
        hidden,
    ) = kept
    mix_w, out_w, gu_w, down_w, gains = full
    tokens = grad_out.shape[0]
    gain_one = gains[:, 0].astype(jnp.float32)
    gain_two = gains[:, 1].astype(jnp.float32)
    grad_f = grad_out.astype(jnp.bfloat16)
    grad_down = jnp.einsum("tf,td->fd", hidden, grad_f, preferred_element_type=jnp.float32)
    grad_hidden = jnp.dot(grad_f, down_w.T, preferred_element_type=jnp.float32)
    gate_part = gate_up[:, :FF]
    up_part = gate_up[:, FF:]
    sig_part = jax.nn.sigmoid(gate_part)
    grad_gate_part = grad_hidden * up_part * sig_part * (1.0 + gate_part * (1.0 - sig_part))
    grad_up_part = grad_hidden * gate_part * sig_part
    grad_gate_up = jnp.concatenate([grad_gate_part, grad_up_part], 1).astype(jnp.bfloat16)
    grad_gu = jnp.einsum("td,tf->df", normed_two, grad_gate_up, preferred_element_type=jnp.float32)
    grad_normed_two = jnp.dot(grad_gate_up, gu_w.T, preferred_element_type=jnp.float32)
    grad_mid_norm, grad_gain_two = norm_back(grad_normed_two, scaled_two, inverse_two, gain_two)
    grad_mid = grad_out + grad_mid_norm
    grad_branch = grad_mid.astype(jnp.bfloat16)
    grad_out_w = jnp.einsum("td,te->de", combined, grad_branch, preferred_element_type=jnp.float32)
    grad_combined = jnp.dot(grad_branch, out_w.T, preferred_element_type=jnp.float32)
    grad_attended = grad_combined.astype(jnp.bfloat16).reshape(tokens, H, HD)
    grad_recalled = (grad_combined * gate).astype(jnp.bfloat16).reshape(tokens, H, HD)
    grad_gate_pre = grad_combined * recalled * gate * (1.0 - gate)
    outgoing = jnp.stack([grad_attended, grad_recalled], 1)
    headward = lax.all_to_all(outgoing, "seq", split_axis=2, concat_axis=0, tiled=True)
    head_grads, pkey_grads, pvalue_grads, rate_grads = ([], [], [], [])
    for head in range(grouped.shape[2]):
        cols = slice(head * HD, (head + 1) * HD)
        dq, dk, dv, dpk, dpv, drate = head_backward(
            grouped[:, 0, head],
            grouped[:, 1, head],
            grouped[:, 2, head],
            pkv[0][:, cols],
            pkv[1][:, cols],
            rates[head],
            seg_ids,
            lse_all[:, head],
            headward[:, 0, head],
            headward[:, 1, head],
        )
        head_grads.append(jnp.stack([dq, dk, dv], 1))
        pkey_grads.append(dpk)
        pvalue_grads.append(dpv)
        rate_grads.append(drate)
    grads_heads = jnp.stack(head_grads, 2).astype(jnp.bfloat16)
    tokenward = lax.all_to_all(grads_heads, "seq", split_axis=0, concat_axis=2, tiled=True)
    grad_proj = jnp.concatenate(
        [tokenward.reshape(tokens, 3 * D), grad_gate_pre.astype(jnp.bfloat16)], 1
    )
    grad_mix = jnp.einsum("td,tf->df", normed, grad_proj, preferred_element_type=jnp.float32)
    grad_normed = jnp.dot(grad_proj, mix_w.T, preferred_element_type=jnp.float32)
    grad_in_norm, grad_gain_one = norm_back(grad_normed, scaled_one, inverse_one, gain_one)
    grad_rows = grad_mid + grad_in_norm
    weight_terms = (
        grad_mix,
        grad_out_w,
        grad_gu,
        grad_down,
        jnp.stack([grad_gain_one, grad_gain_two], 1),
    )
    memory_terms = (
        jnp.stack([jnp.concatenate(pkey_grads, 1), jnp.concatenate(pvalue_grads, 1)], 0),
        jnp.stack(rate_grads, 0),
    )
    return (weight_terms, memory_terms, grad_rows)


def on_device(
    inputs, segment_ids, cotangent, w_mix, w_out, w_gu, w_down, norm_gains, persist_kv, memory_decay
):
    first = lax.axis_index("section") == 0
    own_weights = (w_mix[0], w_out[0], w_gu[0], w_down[0], norm_gains[0])
    pkv = persist_kv[0]
    rates = memory_decay[0]
    count = inputs.shape[0]
    tokens = inputs.shape[2]
    zero_rows = jnp.zeros((tokens, D), jnp.float32)
    received = jnp.zeros((tokens, D), jnp.bfloat16)
    kept_ticks, out_ticks = ([], [])
    for tick in range(count + 1):
        own_rows = inputs[tick, 0].astype(jnp.float32) if tick < count else zero_rows
        layer_in = jnp.where(first, own_rows, received.astype(jnp.float32))
        seg_ids = jnp.where(
            first, segment_ids[min(tick, count - 1), 0], segment_ids[max(tick - 1, 0), 0]
        )
        full = (
            lax.all_gather(own_weights[0], "shard", axis=0, tiled=True),
            lax.all_gather(own_weights[1], "shard", axis=0, tiled=True),
            lax.all_gather(own_weights[2], "shard", axis=0, tiled=True),
            lax.all_gather(own_weights[3], "shard", axis=0, tiled=True),
            lax.all_gather(own_weights[4], "shard", axis=0, tiled=True),
        )
        result, kept = layer_forward(layer_in, seg_ids, full, pkv, rates)
        result_low = result.astype(jnp.bfloat16)
        out_ticks.append(result_low)
        kept_ticks.append(kept)
        if tick < count:
            received = shifted(result_low, "section", 1)
    grad_weights = (
        jnp.zeros((D, 4 * D), jnp.float32),
        jnp.zeros((D, D), jnp.float32),
        jnp.zeros((D, 2 * FF), jnp.float32),
        jnp.zeros((FF, D), jnp.float32),
        jnp.zeros((D, 2), jnp.float32),
    )
    grad_memory = (
        jnp.zeros((2,) + pkv.shape[1:], jnp.float32),
        jnp.zeros(rates.shape, jnp.float32),
    )
    back_received = jnp.zeros((tokens, D), jnp.bfloat16)
    grad_ticks = []
    for tick in range(count + 1):
        lower = max(tick - 1, 0)
        upper = min(tick + 1, count)
        kept = jax.tree.map(
            lambda early, late: jnp.where(first, early, late), kept_ticks[lower], kept_ticks[upper]
        )
        given = cotangent[tick, 0].astype(jnp.float32) if tick < count else zero_rows
        grad_out = jnp.where(first, back_received.astype(jnp.float32), given)
        full = (
            lax.all_gather(own_weights[0], "shard", axis=0, tiled=True),
            lax.all_gather(own_weights[1], "shard", axis=0, tiled=True),
            lax.all_gather(own_weights[2], "shard", axis=0, tiled=True),
            lax.all_gather(own_weights[3], "shard", axis=0, tiled=True),
            lax.all_gather(own_weights[4], "shard", axis=0, tiled=True),
        )
        weight_terms, memory_terms, grad_rows = layer_backward(grad_out, kept, full, pkv, rates)
        grad_weights = jax.tree.map(jnp.add, grad_weights, weight_terms)
        grad_memory = jax.tree.map(jnp.add, grad_memory, memory_terms)
        grad_ticks.append(grad_rows)
        if tick < count:
            back_received = shifted(grad_rows.astype(jnp.bfloat16), "section", -1)
    section_out = jnp.stack(
        [jnp.where(first, out_ticks[batch], out_ticks[batch + 1]) for batch in range(count)], 0
    )
    section_grad = jnp.stack(
        [
            jnp.where(
                first,
                grad_ticks[batch + 1],
                grad_ticks[batch].astype(jnp.bfloat16).astype(jnp.float32),
            )
            for batch in range(count)
        ],
        0,
    )
    shares = jax.tree.map(
        lambda part: part.astype(jnp.float32),
        lax.psum_scatter(as_sent(grad_weights), "shard", scatter_dimension=0, tiled=True),
    )
    shares = jax.tree.map(lambda part: part.astype(jnp.float32), lax.psum(as_sent(shares), "seq"))
    memory_sums = lax.psum(grad_memory, "shard")
    return (
        section_out.reshape(1, count, 1, tokens, D),
        section_grad.reshape(1, count, 1, tokens, D),
        shares[0][None],
        shares[1][None],
        shares[2][None],
        shares[3][None],
        shares[4][None],
        memory_sums[0][None],
        memory_sums[1][None],
    )


MESH = pl.DeviceIdType.MESH
BF = jnp.bfloat16
F32 = jnp.float32


def here():
    return (lax.axis_index("section"), lax.axis_index("seq"), lax.axis_index("shard"))


def peer(place, chip, flip):
    x, s, z = place
    if chip % 2:
        x = 1 - x
    if chip // 2:
        s = (s + 2) % 4
    if flip:
        s = s + 1 - 2 * (s % 2)
    return (x, s, z)


def rows_of(device, size):
    x, s, _ = device
    return pl.ds(pl.multiple_of((s * 2 + x) * size, size), size)


class Gather:
    def __init__(self, full, batch, send, recv):
        self.place = here()
        self.full, self.batch, self.send, self.recv = full, batch, send, recv
        self.size = full.shape[1] // 8

    def copy(self, owner, target, sem):
        block = self.full.at[self.batch, rows_of(owner, self.size)]
        return pltpu.make_async_remote_copy(
            src_ref=block,
            dst_ref=block,
            send_sem=self.send.at[self.batch, sem],
            recv_sem=self.recv.at[self.batch, sem],
            device_id=target,
            device_id_type=MESH,
        )

    def start(self, value):
        self.full[self.batch, rows_of(self.place, self.size), :] = value
        for chip in (3, 1, 2, 0):
            self.copy(self.place, peer(self.place, chip, chip == 0), chip).start()

    def forward(self):
        other = peer(self.place, 0, True)
        for chip in (1, 2, 3):
            owner = peer(self.place, chip, False)
            self.copy(owner, owner, chip).wait_recv()
            self.copy(owner, other, 3 + chip).start()

    def finish(self):
        other = peer(self.place, 0, True)
        self.copy(other, other, 0).wait_recv()
        for chip in (1, 2, 3):
            owner = peer(self.place, chip, True)
            self.copy(owner, other, 3 + chip).wait_recv()
        for chip in (0, 1, 2, 3):
            self.copy(self.place, peer(self.place, chip, chip == 0), chip).wait_send()
        for chip in (1, 2, 3):
            self.copy(peer(self.place, chip, False), other, 3 + chip).wait_send()


class Scatter:
    def __init__(self, part, batch, pair, away, near, send, recv):
        self.place = here()
        self.part, self.batch, self.pair, self.away, self.near = part, batch, pair, away, near
        self.send, self.recv = send, recv
        self.size = part.shape[1] // 8

    def to_pair(self, chip):
        return pltpu.make_async_remote_copy(
            src_ref=self.part.at[self.batch, rows_of(peer(self.place, chip, True), self.size)],
            dst_ref=self.pair.at[self.batch, chip],
            send_sem=self.send.at[self.batch, chip],
            recv_sem=self.recv.at[self.batch, chip],
            device_id=peer(self.place, 0, True),
            device_id_type=MESH,
        )

    def to_chip(self, chip):
        return pltpu.make_async_remote_copy(
            src_ref=self.away.at[self.batch, chip - 1],
            dst_ref=self.near.at[self.batch, chip - 1],
            send_sem=self.send.at[self.batch, 3 + chip],
            recv_sem=self.recv.at[self.batch, 3 + chip],
            device_id=peer(self.place, chip, False),
            device_id_type=MESH,
        )

    def start(self):
        for chip in (3, 1, 2, 0):
            self.to_pair(chip).start()

    def chip_sum(self, chip):
        self.to_pair(chip).wait_recv()
        own = self.part[self.batch, rows_of(peer(self.place, chip, False), self.size), :]
        return own.astype(F32) + self.pair[self.batch, chip].astype(F32)

    def forward(self):
        for chip in (3, 1, 2):
            self.away[self.batch, chip - 1] = self.chip_sum(chip).astype(BF)
            self.to_chip(chip).start()

    def finish(self):
        total = self.chip_sum(0)
        for chip in (1, 2, 3):
            self.to_chip(chip).wait_recv()
            total = total + self.near[self.batch, chip - 1].astype(F32)
        for chip in (0, 1, 2, 3):
            self.to_pair(chip).wait_send()
        for chip in (1, 2, 3):
            self.to_chip(chip).wait_send()
        return total


class ColumnSum:
    def __init__(self, own, slots, out, send, recv, index):
        self.place = here()
        self.own, self.slots, self.out = own, slots, out
        self.send, self.recv, self.index = send, recv, index

    def copy(self, down, owner, source=None):
        x, s, z = self.place
        slot = owner if down else owner - 1
        target = (x, s, (z + 3) % 4 if down else (z + 1) % 4)
        landing = self.slots.at[down, slot]
        return pltpu.make_async_remote_copy(
            src_ref=landing if source is None else source,
            dst_ref=landing,
            send_sem=self.send.at[self.index, down, slot],
            recv_sem=self.recv.at[self.index, down, slot],
            device_id=target,
            device_id_type=MESH,
        )

    def start(self):
        z = self.place[2]
        for down in (0, 1):

            @pl.when(z == 3 * down)
            def _():
                for owner in (0, 1, 2) if down else (3, 2, 1):
                    self.copy(down, owner, self.own.at[owner]).start()

    def relay(self, down, owner, at):
        @pl.when(self.place[2] == at)
        def _():
            self.copy(down, owner).wait_recv()
            slot = owner if down else owner - 1
            self.slots[down, slot] = (
                self.slots[down, slot].astype(F32) + self.own[owner].astype(F32)
            ).astype(BF)
            self.copy(down, owner).start()

    def hop(self, number):
        if number == 1:
            self.relay(0, 3, 1)
            self.relay(1, 0, 2)
        else:
            self.relay(0, 2, 1)
            self.relay(1, 1, 2)
            self.relay(0, 3, 2)
            self.relay(1, 0, 1)

    def finish(self):
        z = self.place[2]
        for at in range(4):

            @pl.when(z == at)
            def _():
                total = self.own[at].astype(F32)
                if at > 0:
                    self.copy(0, at).wait_recv()
                    total = total + self.slots[0, at - 1].astype(F32)
                if at < 3:
                    self.copy(1, at).wait_recv()
                    total = total + self.slots[1, at].astype(F32)
                self.out[...] = total.astype(BF)
                for owner in range(at + 1, 4):
                    self.copy(0, owner).wait_send()
                for owner in range(at):
                    self.copy(1, owner).wait_send()


class RootSum:
    def __init__(self, own, slots, out, send, recv):
        self.place = here()
        x, s, _ = self.place
        self.root = 2 * x + s // 2
        self.own, self.slots, self.out = own, slots, out
        self.send, self.recv = send, recv

    def copy(self, down, source=None):
        x, s, z = self.place
        landing = self.slots.at[down]
        return pltpu.make_async_remote_copy(
            src_ref=landing if source is None else source,
            dst_ref=landing,
            send_sem=self.send.at[down],
            recv_sem=self.recv.at[down],
            device_id=(x, s, (z + 3) % 4 if down else (z + 1) % 4),
            device_id_type=MESH,
        )

    def sends(self, down):
        z = self.place[2]
        return z > self.root if down else z < self.root

    def start(self):
        for down in (0, 1):

            @pl.when((self.place[2] == 3 * down) & self.sends(down))
            def _():
                self.copy(down, self.own).start()

    def relay(self, down, at):
        @pl.when((self.place[2] == at) & self.sends(down))
        def _():
            self.copy(down).wait_recv()
            self.slots[down] = (self.slots[down].astype(F32) + self.own[...].astype(F32)).astype(BF)
            self.copy(down).start()

    def hop(self, number):
        self.relay(0, number)
        self.relay(1, 3 - number)

    def finish(self):
        z = self.place[2]
        self.out[...] = self.own[...]
        for down in (0, 1):

            @pl.when((z == self.root) & (z < 3 if down else z > 0))
            def _():
                self.copy(down).wait_recv()
                self.out[...] = (self.out[...].astype(F32) + self.slots[down].astype(F32)).astype(BF)

            @pl.when(self.sends(down))
            def _():
                self.copy(down).wait_send()


def meet(column=False):
    place = here()
    x, s, z = place
    others = [peer(place, chip, chip == 0) for chip in range(4)]
    if column:
        others += [(x, s, (z + 1) % 4), (x, s, (z + 3) % 4)]
    barrier = pltpu.get_barrier_semaphore()
    for other in others:
        pl.semaphore_signal(barrier, inc=1, device_id=other, device_id_type=MESH)
    pl.semaphore_wait(barrier, len(others))


def start_kernel(rows_ref, gain_ref, full_ref, gsend, grecv):
    meet()
    gathers = [Gather(full_ref, batch, gsend, grecv) for batch in range(2)]
    for batch, gather in enumerate(gathers):
        rows = rows_ref[batch]
        gather.start((rows * rms_scale(rows) * gain_ref[...]).astype(BF))
    for gather in gathers:
        gather.forward()
    for gather in gathers:
        gather.finish()


def forward_kernel(low, last, part_ref, rows_ref, gain_ref, own_ref, *rest):
    if last:
        pair, away, near, ssend, srecv = rest
    else:
        full_ref, pair, away, near, ssend, srecv, gsend, grecv = rest
    meet()
    scatters = [Scatter(part_ref, b, pair, away, near, ssend, srecv) for b in range(2)]
    for scatter in scatters:
        scatter.start()
    for scatter in scatters:
        scatter.forward()
    gathers = []
    for batch, scatter in enumerate(scatters):
        own = (rows_ref[batch] + scatter.finish()).astype(own_ref.dtype)
        own_ref[batch] = own
        if not last:
            own = own.astype(F32)
            gather = Gather(full_ref, batch, gsend, grecv)
            gather.start((own * rms_scale(own) * gain_ref[...]).astype(BF))
            gathers.append(gather)
    for gather in gathers:
        gather.forward()
    for gather in gathers:
        gather.finish()


def backward_kernel(last, rooted, *refs):
    part_ref, rows_ref, gain_ref, grad_ref, *refs = refs
    columns = 2
    owns, refs = refs[:columns], refs[columns:]
    own_ref, gains_ref, *refs = refs
    if not last:
        full_ref, *refs = refs
    outs, refs = refs[:columns], refs[columns:]
    pair, away, near, ssend, srecv, *refs = refs
    if not last:
        gsend, grecv, *refs = refs
    slots, refs = refs[:columns], refs[columns:]
    csend, crecv, *refs = refs
    sums_of = [ColumnSum(owns[0], slots[0], outs[0], csend, crecv, 0)]
    if rooted:
        sums_of.append(RootSum(owns[1], slots[1], outs[1], *refs))
    else:
        sums_of.append(ColumnSum(owns[1], slots[1], outs[1], csend, crecv, 1))
    meet(True)
    scatters = [Scatter(part_ref, b, pair, away, near, ssend, srecv) for b in range(2)]
    for scatter in scatters:
        scatter.start()
    for column in sums_of:
        column.start()
    for scatter in scatters:
        scatter.forward()
    gathers = []
    sums = jnp.zeros((1, D), F32)
    for batch, scatter in enumerate(scatters):
        grad_normed = scatter.finish()
        rows = rows_ref[batch]
        inverse = rms_scale(rows)
        grad_rows, gain_sum = norm_back(grad_normed, rows * inverse, inverse, gain_ref[...])
        sums = sums + gain_sum[None]
        own = (grad_ref[batch] + grad_rows).astype(own_ref.dtype)
        own_ref[batch] = own
        if not last:
            gather = Gather(full_ref, batch, gsend, grecv)
            gather.start(own.astype(BF))
            gathers.append(gather)
    gains_ref[...] = sums
    for column in sums_of:
        column.hop(1)
    for gather in gathers:
        gather.forward()
    for column in sums_of:
        column.hop(2)
    for gather in gathers:
        gather.finish()
    for column in sums_of:
        column.finish()


def final_kernel(*refs):
    place = here()
    x, s, z = place
    sibling, beside, partner = (peer(place, 0, True), peer(place, 2, False), peer(place, 1, False))
    across = peer(place, 3, False)
    by_layer = [refs[0:6], refs[6:12]]
    small_ref = refs[12]
    bufs = refs[13:16]
    out_buf, rows_buf, grads_buf, plane_buf = refs[16:20]
    column_buf, psend, precv, osend, orecv, rsend, rrecv, zsend, zrecv, ssend, srecv = refs[20:]

    def copy(source, landing, sems, index, target):
        return pltpu.make_async_remote_copy(
            src_ref=source,
            dst_ref=landing,
            send_sem=sems[0].at[index],
            recv_sem=sems[1].at[index],
            device_id=target,
            device_id_type=MESH,
        )

    flips = [(dx, ds) for dx in (0, 1) for ds in range(4) if dx or ds]
    plane = [((x + dx) % 2, (s + ds) % 4, z) for dx, ds in flips]
    column = [(x, s, (z + dz) % 4) for dz in (1, 2, 3)]
    barrier = pltpu.get_barrier_semaphore()
    for other in plane + column:
        pl.semaphore_signal(barrier, inc=1, device_id=other, device_id_type=MESH)
    pl.semaphore_wait(barrier, len(plane) + len(column))

    def to_plane_of(dz):
        target = (z + dz) % 4
        return copy(
            small_ref.at[target], column_buf.at[dz - 1], (zsend, zrecv), dz - 1, (x, s, target)
        )

    def to_plane(index):
        slot = plane_buf.at[x * 4 + s]
        return copy(slot, slot, (ssend, srecv), index, plane[index])

    for dz in (1, 2, 3):
        to_plane_of(dz).start()

    psems = [(psend.at[i], precv.at[i]) for i in range(3)]

    def piece(index, kind, slot, target, source=None):
        landing = bufs[index].at[slot]
        return copy(landing if source is None else source, landing, psems[index], kind, target)

    mine = (x, s)
    turned = (1 - x, s)
    for layer in (0, 1):
        own, theirs = by_layer[layer], by_layer[1 - layer]

        @pl.when(x == layer)
        def _():
            for index in range(3):
                piece(index, 2, mine, partner, theirs[index]).start()
                piece(index, 0, mine, beside, own[index]).start()
                piece(index, 1, mine, sibling, own[index]).start()
            copy(theirs[4], rows_buf, (rsend, rrecv), 0, partner).start()
            copy(theirs[5], grads_buf, (rsend, rrecv), 1, partner).start()
            for index in range(3):
                bufs[index][mine] = own[index][...]

    total = small_ref[z]
    for dz in (1, 2, 3):
        to_plane_of(dz).wait_recv()
        total = total + column_buf[dz - 1]
    plane_buf[x * 4 + s] = total
    for index in range(7):
        to_plane(index).start()

    core = s % 2
    root = z == 2 * x + s // 2
    of_root = (z // 2, 2 * (z % 2) + core)
    apart = 2 * ((x + of_root[0]) % 2) + (s // 2 + of_root[1] // 2) % 2

    def out_copy(index, target, source=None):
        landing = out_buf.at[core]
        return copy(landing if source is None else source, landing, (osend, orecv), index, target)

    for layer in (0, 1):

        @pl.when(root & (x == layer))
        def _():
            out_copy(1, beside, by_layer[layer][3]).start()
            out_copy(2, partner, by_layer[1 - layer][3]).start()
            out_copy(3, across, by_layer[1 - layer][3]).start()
            out_buf[core] = by_layer[layer][3][...]

    for apart_by in (1, 2, 3):

        @pl.when(apart == apart_by)
        def _():
            out_copy(apart_by, beside).wait_recv()

    out_copy(0, sibling).start()

    for index in range(3):
        piece(index, 2, turned, partner).wait_recv()
        piece(index, 3, turned, beside).start()
        piece(index, 4, turned, sibling).start()
    far = (x, (s + 2) % 4)
    far_turned = (1 - x, (s + 2) % 4)
    for index in range(3):
        piece(index, 0, far, beside).wait_recv()
        piece(index, 5, far, sibling).start()
    for index in range(3):
        piece(index, 3, far_turned, beside).wait_recv()
        piece(index, 6, far_turned, sibling).start()
    twin = sibling[1]
    far_twin = (twin + 2) % 4
    for index in range(3):
        piece(index, 1, (x, twin), sibling).wait_recv()
        piece(index, 4, (1 - x, twin), sibling).wait_recv()
        piece(index, 5, (x, far_twin), sibling).wait_recv()
        piece(index, 6, (1 - x, far_twin), sibling).wait_recv()
    other_out = out_buf.at[1 - core]
    copy(other_out, other_out, (osend, orecv), 0, sibling).wait_recv()
    for index in range(7):
        dx, ds = flips[index]
        slot = plane_buf.at[((x + dx) % 2) * 4 + (s + 4 - ds) % 4]
        copy(slot, slot, (ssend, srecv), index, plane[index]).wait_recv()
    for index in (0, 1):
        copy(rows_buf, rows_buf, (rsend, rrecv), index, partner).wait()
    for index in range(7):
        to_plane(index).wait_send()
    for dz in (1, 2, 3):
        to_plane_of(dz).wait_send()
    for index in range(3):
        for kind in range(7):
            piece(index, kind, mine, sibling).wait_send()
    out_copy(0, sibling).wait_send()

    @pl.when(root)
    def _():
        for index in (1, 2, 3):
            out_copy(index, sibling).wait_send()


def plane_call(kernel, number, operands, outs, scatter, gather, sums=(), root=None):
    _, length, width = outs["full"].shape
    size = length // 8
    scratch = []
    outs = dict(outs)
    if scatter:
        scratch += [
            pltpu.VMEM((2, 4, size, width), BF),
            pltpu.VMEM((2, 3, size, width), BF),
            pltpu.VMEM((2, 3, size, width), BF),
            pltpu.SemaphoreType.DMA((2, 7)),
            pltpu.SemaphoreType.DMA((2, 7)),
        ]
    if gather:
        scratch += [pltpu.SemaphoreType.DMA((2, 7)), pltpu.SemaphoreType.DMA((2, 7))]
    else:
        del outs["full"]
    outs = list(outs.values())
    for part in sums:
        outs.append(jax.ShapeDtypeStruct(part.shape[1:], BF))
        scratch.append(pltpu.VMEM((2, 3) + part.shape[1:], BF))
    if root is not None:
        outs.append(jax.ShapeDtypeStruct(root.shape, BF))
        scratch.append(pltpu.VMEM((2,) + root.shape, BF))
        sums = (*sums, root)
    if sums:
        scratch += [pltpu.SemaphoreType.DMA((2, 2, 3)), pltpu.SemaphoreType.DMA((2, 2, 3))]
    if root is not None:
        scratch += [pltpu.SemaphoreType.DMA((2,)), pltpu.SemaphoreType.DMA((2,))]
    operands = (*operands, *sums)
    vmem = pl.BlockSpec(memory_space=pltpu.VMEM)
    return pl.pallas_call(
        kernel,
        out_shape=outs,
        in_specs=[vmem] * len(operands),
        out_specs=[vmem] * len(outs),
        scratch_shapes=scratch,
        compiler_params=pltpu.CompilerParams(
            collective_id=number, has_side_effects=True, vmem_limit_bytes=40 * 2**20
        ),
    )(*operands)


def final_call(number, by_layer, small):
    operands = (*by_layer[0], *by_layer[1], small)
    outs = [jax.ShapeDtypeStruct((2, 4) + part.shape, BF) for part in by_layer[0][:3]]
    outs.append(jax.ShapeDtypeStruct((2,) + by_layer[0][3].shape, BF))
    outs += [jax.ShapeDtypeStruct(part.shape, BF) for part in by_layer[0][4:]]
    outs.append(jax.ShapeDtypeStruct((8,) + small.shape[1:], F32))
    sizes = [(3, 7), (4,), (2,), (3,), (7,)]
    scratch = [pltpu.VMEM((3,) + small.shape[1:], F32)]
    scratch += [pltpu.SemaphoreType.DMA(size) for size in sizes for _ in range(2)]
    vmem = pl.BlockSpec(memory_space=pltpu.VMEM)
    return pl.pallas_call(
        final_kernel,
        out_shape=outs,
        in_specs=[vmem] * len(operands),
        out_specs=[vmem] * len(outs),
        scratch_shapes=scratch,
        compiler_params=pltpu.CompilerParams(
            collective_id=number, has_side_effects=True, vmem_limit_bytes=40 * 2**20
        ),
    )(*operands)


def assemble_kernel(mix_buf, gu_buf, down_buf, mix_ref, gu_ref, down_ref):
    unit = down_buf.shape[2] // 2
    half = gu_buf.shape[3] // 2
    width = 4 * HD
    for which in range(8):
        slot = (which // 4, which % 4)
        mix = mix_buf[slot].astype(F32)
        for kind in range(4):
            begin = kind * D + which * HD
            mix_ref[0, :, begin : begin + HD] = mix[:, kind * HD : (kind + 1) * HD]
        part = gu_buf[slot].astype(F32)
        for side in range(2):
            for owner in range(half // unit):
                begin = side * FF + (owner * 8 + which) * unit
                source = side * half + owner * unit
                gu_ref[0, :, begin : begin + unit] = part[:, source : source + unit]
    for pair in range(2):
        down = down_buf[0, pair].astype(F32)
        down_ref[0, pair * unit : (pair + 1) * unit, :width] = down[:unit]
        down_ref[0, pair * unit : (pair + 1) * unit, width:] = down[unit:]


def assemble_call(mix_buf, gu_buf, down_buf):
    depth, unit = mix_buf.shape[2], down_buf.shape[2] // 2
    rows = depth // 4
    wide = gu_buf.shape[3] * 8
    return pl.pallas_call(
        assemble_kernel,
        grid=(4,),
        out_shape=[
            jax.ShapeDtypeStruct((1, depth, 4 * D), F32),
            jax.ShapeDtypeStruct((1, depth, wide), F32),
            jax.ShapeDtypeStruct((1, 8 * unit, D), F32),
        ],
        in_specs=[
            pl.BlockSpec((2, 4, rows, 4 * HD), lambda i: (0, 0, i, 0)),
            pl.BlockSpec((2, 4, rows, wide // 8), lambda i: (0, 0, i, 0)),
            pl.BlockSpec((1, 2, 2 * unit, D // 2), lambda i: (i // 2, i % 2, 0, 0)),
        ],
        out_specs=[
            pl.BlockSpec((1, rows, 4 * D), lambda i: (0, i, 0)),
            pl.BlockSpec((1, rows, wide), lambda i: (0, i, 0)),
            pl.BlockSpec((1, 2 * unit, D), lambda i: (0, i, 0)),
        ],
        compiler_params=pltpu.CompilerParams(vmem_limit_bytes=40 * 2**20),
    )(mix_buf, gu_buf, down_buf)


def tensor_parallel(
    inputs, segment_ids, cotangent, w_mix, w_out, w_gu, w_down, norm_gains, persist_kv, memory_decay
):
    x, s, z = here()
    nx, ns, nz = (lax.axis_size(a) for a in ("section", "seq", "shard"))
    width = nx * ns
    mine = x * ns + s
    other = (1 - x) * ns + s
    first = x == 0
    count, _, tokens, _ = inputs.shape
    length = tokens * ns
    size = length // width
    depth = w_mix.shape[1]
    unit = w_down.shape[1] // width

    heads = w_mix[0].reshape(depth, 4, H, HD)
    halves = w_gu[0].reshape(depth, 2, nz, width, unit)
    downs = w_down[0].reshape(width, unit, D)

    def pick(which):
        return (
            lax.dynamic_index_in_dim(heads, which, 2, keepdims=False).reshape(depth, 4 * HD),
            lax.dynamic_index_in_dim(halves, which, 3, keepdims=False).reshape(
                depth, 2 * nz * unit
            ),
            lax.dynamic_index_in_dim(downs, which, 0, keepdims=False),
        )

    def layers(own, got):
        return (jnp.where(first, own, got), jnp.where(first, got, own))

    swap = [(0, 1), (1, 0)]
    parts = [layers(o, lax.ppermute(g, "section", swap)) for o, g in zip(pick(mine), pick(other))]
    out_rows = lax.dynamic_index_in_dim(
        w_out[0].reshape(2, HD, D), lax.rem(s, 2), 0, keepdims=False
    )
    out_all = lax.all_gather(out_rows, "shard", axis=0)
    out_own = lax.dynamic_index_in_dim(out_all, mine // 2, 0, keepdims=False)
    out_got = lax.ppermute(
        lax.dynamic_index_in_dim(out_all, other // 2, 0, keepdims=False), "section", swap
    )
    out_w = layers(out_own, out_got)
    mix_w, gu_w, down_w = (
        [lax.all_gather(part[layer], "shard", axis=0, tiled=True) for layer in range(2)]
        for part in parts
    )

    small = jnp.concatenate([persist_kv[0].reshape(-1).astype(F32), memory_decay[0]])
    small = lax.all_gather(small, ("section", "seq"), axis=0)
    rates = small[:, -2:].reshape(2, H)[:, mine]
    persist = small[:, :-2].astype(BF).reshape(2, ns, 2, persist_kv.shape[2], 2, HD)
    persist = lax.dynamic_index_in_dim(persist, mine // 2, 1, keepdims=False)
    persist = lax.dynamic_index_in_dim(persist, lax.rem(mine, 2), 3, keepdims=False)
    gains = lax.all_gather(norm_gains[0], ("section", "shard"), axis=0, tiled=True)
    gains = gains.astype(F32).reshape(2, 1, D, 2)

    def own_rows(whole):
        return lax.dynamic_slice_in_dim(whole[:, 0], x * size, size, 1).astype(F32)

    full = jax.ShapeDtypeStruct((count, length, D), BF)
    own32 = jax.ShapeDtypeStruct((count, size, D), F32)
    own16 = jax.ShapeDtypeStruct((count, size, D), BF)
    sums = jax.ShapeDtypeStruct((1, D), F32)

    cot_full = lax.all_gather(cotangent[:, 0], "seq", axis=1, tiled=True)
    rows = own_rows(inputs)
    (normed,) = plane_call(
        start_kernel, 0, (rows, gains[0, :, :, 0]), {"full": full}, False, True
    )
    kept = []
    outputs = []
    flat = count * length
    for layer in range(2):
        proj = jnp.dot(normed.reshape(flat, D), mix_w[layer], preferred_element_type=F32)
        qkv = proj[:, : 3 * HD].astype(BF).reshape(count, length, 3, HD)
        gate = jax.nn.sigmoid(proj[:, 3 * HD :])
        results = [
            head_forward(
                qkv[b, :, 0],
                qkv[b, :, 1],
                qkv[b, :, 2],
                persist[layer, 0],
                persist[layer, 1],
                rates[layer],
                segment_ids[b, 0],
            )
            for b in range(count)
        ]
        attended = jnp.concatenate([r[0] for r in results], 0).astype(BF).astype(F32)
        recalled = jnp.concatenate([r[1] for r in results], 0).astype(BF).astype(F32)
        combined = (attended + gate * recalled).astype(BF)
        partial = jnp.dot(combined, out_w[layer], preferred_element_type=F32).astype(BF)
        mid, normed_two = plane_call(
            functools.partial(forward_kernel, False, False),
            1 + 2 * layer,
            (partial.reshape(count, length, D), rows, gains[layer, :, :, 1]),
            {"own": own32, "full": full},
            True,
            True,
        )
        gate_up = jnp.dot(normed_two.reshape(flat, D), gu_w[layer], preferred_element_type=F32)
        half = gate_up.shape[1] // 2
        hidden = (jax.nn.silu(gate_up[:, :half]) * gate_up[:, half:]).astype(BF)
        partial = jnp.dot(hidden, down_w[layer], preferred_element_type=F32).astype(BF)
        kept.append(
            (rows, normed, qkv, gate, [r[2] for r in results], recalled, combined, mid)
            + (normed_two, gate_up, hidden)
        )
        last = layer == 1
        found = plane_call(
            functools.partial(forward_kernel, True, last),
            2 + 2 * layer,
            (partial.reshape(count, length, D), mid, gains[1, :, :, 0]),
            {"own": own16, "full": full},
            True,
            not last,
        )
        outputs.append(found[0])
        if not last:
            rows = found[0].astype(F32)
            normed = found[1]

    grad_full = cot_full
    grad_own = own_rows(cotangent)
    pieces, gain_sums, memory_terms, grads = ([None] * 2, [None] * 2, [None] * 2, [None] * 2)
    for layer in (1, 0):
        (
            rows,
            normed,
            qkv,
            gate,
            lse,
            recalled,
            combined,
            mid,
            normed_two,
            gate_up,
            hidden,
        ) = kept[layer]
        grad_f = grad_full.reshape(flat, D)
        grad_hidden = jnp.dot(grad_f, down_w[layer].T, preferred_element_type=F32)
        half = gate_up.shape[1] // 2
        gate_part = gate_up[:, :half]
        up_part = gate_up[:, half:]
        sig_part = jax.nn.sigmoid(gate_part)
        grad_gate_up = jnp.concatenate(
            [
                grad_hidden * up_part * sig_part * (1.0 + gate_part * (1.0 - sig_part)),
                grad_hidden * gate_part * sig_part,
            ],
            1,
        ).astype(BF)
        partial = jnp.dot(grad_gate_up, gu_w[layer].T, preferred_element_type=F32).astype(BF)
        grad_down = jnp.einsum("tf,td->fd", hidden, grad_f, preferred_element_type=F32)
        grad_gu = jnp.einsum(
            "td,tf->df", normed_two.reshape(flat, D), grad_gate_up, preferred_element_type=F32
        )
        halves_of_down = grad_down.astype(BF).reshape(nz, unit, 2, D // 2)
        sent = (
            grad_gu.astype(BF).reshape(nz, depth, 2 * nz * unit),
            halves_of_down.transpose(0, 2, 1, 3).reshape(nz, 2 * unit, D // 2),
        )
        grad_mid, gain_two, branch, gu_sum, down_sum = plane_call(
            functools.partial(backward_kernel, False, False),
            5 + 2 * (1 - layer),
            (partial.reshape(count, length, D), mid, gains[layer, :, :, 1], grad_own),
            {"own": own32, "sums": sums, "full": full},
            True,
            True,
            sent,
        )
        branch = branch.reshape(flat, D)
        grad_combined = jnp.dot(branch, out_w[layer].T, preferred_element_type=F32)
        grad_out = jnp.einsum("td,te->de", combined, branch, preferred_element_type=F32)
        grad_attended = grad_combined.astype(BF).reshape(count, length, HD)
        grad_recalled = (grad_combined * gate).astype(BF).reshape(count, length, HD)
        grad_gate_pre = grad_combined * recalled * gate * (1.0 - gate)
        found = [
            head_backward(
                qkv[b, :, 0],
                qkv[b, :, 1],
                qkv[b, :, 2],
                persist[layer, 0],
                persist[layer, 1],
                rates[layer],
                segment_ids[b, 0],
                lse[b],
                grad_attended[b],
                grad_recalled[b],
            )
            for b in range(count)
        ]
        grad_heads = jnp.concatenate([jnp.concatenate(f[:3], 1) for f in found], 0)
        grad_proj = jnp.concatenate([grad_heads, grad_gate_pre], 1).astype(BF)
        memory_terms[layer] = (
            jnp.stack([sum(f[3] for f in found), sum(f[4] for f in found)], 0),
            sum(f[5] for f in found),
        )
        partial = jnp.dot(grad_proj, mix_w[layer].T, preferred_element_type=F32).astype(BF)
        grad_mix = jnp.einsum(
            "td,tf->df", normed.reshape(flat, D), grad_proj, preferred_element_type=F32
        )
        last = layer == 0
        found = plane_call(
            functools.partial(backward_kernel, last, True),
            6 + 2 * (1 - layer),
            (partial.reshape(count, length, D), rows, gains[layer, :, :, 0], grad_mid),
            {"own": own16, "sums": sums, "full": full},
            True,
            not last,
            (grad_mix.astype(BF).reshape(nz, depth, 4 * HD),),
            grad_out.astype(BF),
        )
        grads[layer] = found[0]
        gain_sums[layer] = jnp.concatenate([found[1], gain_two], 0)
        if not last:
            grad_own = found[0].astype(F32)
            grad_full = found[2]
        pieces[layer] = (found[-2], gu_sum, down_sum, found[-1])

    memory_all = jnp.stack([m[0] for m in memory_terms], 0).reshape(-1, HD)
    rate_all = jnp.pad(jnp.stack([m[1] for m in memory_terms])[None], ((0, 7), (0, HD - 2)))
    gain_all = jnp.stack(gain_sums, 0).reshape(4, nz, 2, HD).transpose(1, 0, 2, 3)
    memory_all = jnp.concatenate([memory_all, rate_all], 0)
    small = jnp.concatenate(
        [jnp.broadcast_to(memory_all[None], (nz,) + memory_all.shape), gain_all.reshape(nz, 8, HD)],
        1,
    )
    by_layer = [(*pieces[layer], outputs[layer], grads[layer]) for layer in range(2)]
    mix_all, gu_all, down_all, out_all, rows_got, grads_got, plane_all = final_call(
        9, by_layer, small
    )

    def whole_rows(of_layer, got):
        both = layers(jnp.where(first, of_layer[0], of_layer[1]), got)
        return jnp.concatenate(both, 1)[None, :, None]

    section_out = whole_rows(outputs, rows_got)
    section_grad = whole_rows(grads, grads_got).astype(F32)
    grad_mix, grad_gu, grad_down = assemble_call(mix_all, gu_all, down_all)
    grad_out = out_all.astype(F32).reshape(1, 2 * HD, D)

    heads_of = lax.dynamic_slice_in_dim(plane_all, 2 * s, 2, 0)
    of_layer = lax.dynamic_index_in_dim(
        heads_of[:, :64].reshape(2, 2, 2, -1, HD), x, 1, keepdims=False
    )
    grad_persist = of_layer.transpose(1, 2, 0, 3).reshape(1, 2, -1, 2 * HD)
    grad_rate = lax.dynamic_index_in_dim(heads_of[:, 64], x, 1, keepdims=False)[None]
    gain_all = jnp.sum(plane_all[:, 72:], 0).reshape(2, 2, depth)
    grad_gain = lax.dynamic_index_in_dim(gain_all, x, 0).transpose(0, 2, 1)
    return (
        section_out,
        section_grad,
        grad_mix,
        grad_out,
        grad_gu,
        grad_down,
        grad_gain,
        grad_persist,
        grad_rate,
    )


def solution(mesh):
    sizes = mesh.shape
    planar = (sizes["section"], sizes["seq"]) == (2, 4)
    placed = (
        P(None, "shard", "seq", None),
        P(None, "shard", None),
        P(None, "shard", "seq", None),
        P("section", "shard", None),
        P("section", "shard", None),
        P("section", "shard", None),
        P("section", "shard", None),
        P("section", "shard", None),
        P("section", None, None, "seq"),
        P("section", "seq"),
    )
    return jax.shard_map(
        tensor_parallel if planar else on_device,
        mesh=mesh,
        in_specs=placed,
        out_specs=(
            P("section", None, "shard", "seq", None),
            P("section", None, "shard", "seq", None),
            P("section", "shard", None),
            P("section", "shard", None),
            P("section", "shard", None),
            P("section", "shard", None),
            P("section", "shard", None),
            P("section", None, None, "seq"),
            P("section", "seq"),
        ),
        check_vma=False,
    )
```

```python
import functools
import math
import types
from typing import Any, NamedTuple

import jax
import jax.numpy as jnp
from jax import lax
from jax.experimental import pallas as pl
from jax.experimental.pallas import tpu as pltpu
from jax.sharding import PartitionSpec as P

D = 1024
H = 8
HD = 128
FF = 2816


def shifted(value, axis, by):
    size = lax.axis_size(axis)
    pairs = [(i, i + by) for i in range(size) if 0 <= i + by < size]
    return lax.ppermute(value, axis, pairs)


def as_sent(value):
    return jax.tree.map(lambda a: a.astype(jnp.bfloat16) if a.dtype == jnp.float32 else a, value)


def rms_scale(values):
    return lax.rsqrt(jnp.mean(values * values, axis=-1, keepdims=True) + 1e-06)


def norm_back(grad_normed, scaled, inverse, gain):
    grad_scaled = grad_normed * gain
    grad_rows = inverse * (
        grad_scaled - scaled * jnp.mean(grad_scaled * scaled, axis=-1, keepdims=True)
    )
    return (grad_rows, jnp.sum(grad_normed * scaled, axis=0))


def block_terms(query_rows, key_rows, seg_ids, begin, reach, rate):
    inner = jnp.dot(query_rows, key_rows.T, preferred_element_type=jnp.float32)
    row_places = begin + jnp.arange(reach - begin, dtype=jnp.int32)
    col_places = jnp.arange(reach, dtype=jnp.int32)
    allowed = (seg_ids[begin:reach][:, None] == seg_ids[:reach][None, :]) & (
        col_places[None, :] <= row_places[:, None]
    )
    distance = jnp.maximum(row_places[:, None] - col_places[None, :], 0).astype(jnp.float32)
    decay_w = jnp.where(allowed, jnp.exp(-rate * distance), jnp.float32(0.0))
    return (inner, allowed, decay_w, distance)


def head_forward(query, keys, values, pkeys, pvalues, rate, seg_ids):
    length, width = query.shape
    block = min(512, length)
    scale = 1.0 / math.sqrt(width)
    attn_parts, memory_parts, lse_parts = ([], [], [])
    for begin in range(0, length, block):
        reach = begin + block
        query_rows = query[begin:reach]
        inner, allowed, decay_w, distance = block_terms(
            query_rows, keys[:reach], seg_ids, begin, reach, rate
        )
        per_scores = jnp.dot(query_rows, pkeys.T, preferred_element_type=jnp.float32) * scale
        seq_scores = jnp.where(allowed, inner * scale, -jnp.inf)
        top = jnp.maximum(
            jnp.max(per_scores, axis=1, keepdims=True), jnp.max(seq_scores, axis=1, keepdims=True)
        )
        per_exp = jnp.exp(per_scores - top)
        seq_exp = jnp.exp(seq_scores - top)
        denom = jnp.sum(per_exp, axis=1, keepdims=True) + jnp.sum(seq_exp, axis=1, keepdims=True)
        attended = jnp.dot(
            (per_exp / denom).astype(jnp.bfloat16), pvalues, preferred_element_type=jnp.float32
        )
        attended = attended + jnp.dot(
            (seq_exp / denom).astype(jnp.bfloat16),
            values[:reach],
            preferred_element_type=jnp.float32,
        )
        memory_w = (inner * decay_w * (1.0 / width)).astype(jnp.bfloat16)
        recalled = jnp.dot(memory_w, values[:reach], preferred_element_type=jnp.float32)
        attn_parts.append(attended)
        memory_parts.append(recalled)
        lse_parts.append(top[:, 0] + jnp.log(denom[:, 0]))
    return (
        jnp.concatenate(attn_parts, 0),
        jnp.concatenate(memory_parts, 0),
        jnp.concatenate(lse_parts, 0),
    )


def head_backward(query, keys, values, pkeys, pvalues, rate, seg_ids, lse, grad_attn, grad_memory):
    length, width = query.shape
    block = min(512, length)
    scale = 1.0 / math.sqrt(width)
    query_grads = []
    grad_keys = jnp.zeros((length, width), jnp.float32)
    grad_values = jnp.zeros((length, width), jnp.float32)
    grad_pkeys = jnp.zeros(pkeys.shape, jnp.float32)
    grad_pvalues = jnp.zeros(pvalues.shape, jnp.float32)
    grad_rate = jnp.float32(0.0)
    for begin in range(0, length, block):
        reach = begin + block
        query_rows = query[begin:reach]
        key_rows = keys[:reach]
        value_rows = values[:reach]
        inner, allowed, decay_w, distance = block_terms(
            query_rows, key_rows, seg_ids, begin, reach, rate
        )
        per_scores = jnp.dot(query_rows, pkeys.T, preferred_element_type=jnp.float32) * scale
        seq_scores = jnp.where(allowed, inner * scale, -jnp.inf)
        row_lse = lse[begin:reach][:, None]
        per_prob = jnp.exp(per_scores - row_lse)
        seq_prob = jnp.exp(seq_scores - row_lse)
        attn_rows = grad_attn[begin:reach]
        memory_rows = grad_memory[begin:reach]
        per_dp = jnp.dot(attn_rows, pvalues.T, preferred_element_type=jnp.float32)
        seq_dp = jnp.dot(attn_rows, value_rows.T, preferred_element_type=jnp.float32)
        delta = jnp.sum(per_prob * per_dp, axis=1, keepdims=True) + jnp.sum(
            seq_prob * seq_dp, axis=1, keepdims=True
        )
        per_ds = (per_prob * (per_dp - delta)).astype(jnp.bfloat16)
        seq_ds = (seq_prob * (seq_dp - delta)).astype(jnp.bfloat16)
        rows_grad = (
            jnp.dot(per_ds, pkeys, preferred_element_type=jnp.float32)
            + jnp.dot(seq_ds, key_rows, preferred_element_type=jnp.float32)
        ) * scale
        grad_pkeys = (
            grad_pkeys
            + jnp.einsum("qk,qd->kd", per_ds, query_rows, preferred_element_type=jnp.float32)
            * scale
        )
        grad_pvalues = grad_pvalues + jnp.einsum(
            "qk,qd->kd",
            per_prob.astype(jnp.bfloat16),
            attn_rows,
            preferred_element_type=jnp.float32,
        )
        key_part = (
            jnp.einsum("qk,qd->kd", seq_ds, query_rows, preferred_element_type=jnp.float32) * scale
        )
        value_part = jnp.einsum(
            "qk,qd->kd",
            seq_prob.astype(jnp.bfloat16),
            attn_rows,
            preferred_element_type=jnp.float32,
        )
        memory_w = (inner * decay_w * (1.0 / width)).astype(jnp.bfloat16)
        grad_mw = jnp.dot(memory_rows, value_rows.T, preferred_element_type=jnp.float32)
        value_part = value_part + jnp.einsum(
            "qk,qd->kd", memory_w, memory_rows, preferred_element_type=jnp.float32
        )
        grad_inner = (grad_mw * decay_w * (1.0 / width)).astype(jnp.bfloat16)
        rows_grad = rows_grad + jnp.dot(grad_inner, key_rows, preferred_element_type=jnp.float32)
        key_part = key_part + jnp.einsum(
            "qk,qd->kd", grad_inner, query_rows, preferred_element_type=jnp.float32
        )
        grad_rate = grad_rate - jnp.sum(grad_mw * inner * decay_w * (1.0 / width) * distance)
        grad_keys = grad_keys.at[:reach].add(key_part)
        grad_values = grad_values.at[:reach].add(value_part)
        query_grads.append(rows_grad)
    return (
        jnp.concatenate(query_grads, 0),
        grad_keys,
        grad_values,
        grad_pkeys,
        grad_pvalues,
        grad_rate,
    )


def layer_forward(rows_in, seg_ids, full, pkv, rates):
    mix_w, out_w, gu_w, down_w, gains = full
    tokens = rows_in.shape[0]
    gain_one = gains[:, 0].astype(jnp.float32)
    gain_two = gains[:, 1].astype(jnp.float32)
    inverse_one = rms_scale(rows_in)
    scaled_one = rows_in * inverse_one
    normed = (scaled_one * gain_one).astype(jnp.bfloat16)
    proj = jnp.dot(normed, mix_w, preferred_element_type=jnp.float32)
    qkv = proj[:, : 3 * D].astype(jnp.bfloat16).reshape(tokens, 3, H, HD)
    gate = jax.nn.sigmoid(proj[:, 3 * D :])
    grouped = lax.all_to_all(qkv, "seq", split_axis=2, concat_axis=0, tiled=True)
    attn_heads, memory_heads, lse_heads = ([], [], [])
    for head in range(grouped.shape[2]):
        cols = slice(head * HD, (head + 1) * HD)
        attended, recalled, lse = head_forward(
            grouped[:, 0, head],
            grouped[:, 1, head],
            grouped[:, 2, head],
            pkv[0][:, cols],
            pkv[1][:, cols],
            rates[head],
            seg_ids,
        )
        attn_heads.append(attended)
        memory_heads.append(recalled)
        lse_heads.append(lse)
    mixed = jnp.stack([jnp.stack(attn_heads, 1), jnp.stack(memory_heads, 1)], 1).astype(
        jnp.bfloat16
    )
    returned = lax.all_to_all(mixed, "seq", split_axis=0, concat_axis=2, tiled=True)
    attended = returned[:, 0].reshape(tokens, D).astype(jnp.float32)
    recalled = returned[:, 1].reshape(tokens, D).astype(jnp.float32)
    combined = (attended + gate * recalled).astype(jnp.bfloat16)
    mid = rows_in + jnp.dot(combined, out_w, preferred_element_type=jnp.float32)
    inverse_two = rms_scale(mid)
    scaled_two = mid * inverse_two
    normed_two = (scaled_two * gain_two).astype(jnp.bfloat16)
    gate_up = jnp.dot(normed_two, gu_w, preferred_element_type=jnp.float32)
    hidden = (jax.nn.silu(gate_up[:, :FF]) * gate_up[:, FF:]).astype(jnp.bfloat16)
    result = mid + jnp.dot(hidden, down_w, preferred_element_type=jnp.float32)
    kept = (
        seg_ids,
        inverse_one,
        scaled_one,
        normed,
        grouped,
        jnp.stack(lse_heads, 1),
        gate,
        recalled,
        combined,
        inverse_two,
        scaled_two,
        normed_two,
        gate_up,
        hidden,
    )
    return (result, kept)


def layer_backward(grad_out, kept, full, pkv, rates):
    (
        seg_ids,
        inverse_one,
        scaled_one,
        normed,
        grouped,
        lse_all,
        gate,
        recalled,
        combined,
        inverse_two,
        scaled_two,
        normed_two,
        gate_up,
        hidden,
    ) = kept
    mix_w, out_w, gu_w, down_w, gains = full
    tokens = grad_out.shape[0]
    gain_one = gains[:, 0].astype(jnp.float32)
    gain_two = gains[:, 1].astype(jnp.float32)
    grad_f = grad_out.astype(jnp.bfloat16)
    grad_down = jnp.einsum("tf,td->fd", hidden, grad_f, preferred_element_type=jnp.float32)
    grad_hidden = jnp.dot(grad_f, down_w.T, preferred_element_type=jnp.float32)
    gate_part = gate_up[:, :FF]
    up_part = gate_up[:, FF:]
    sig_part = jax.nn.sigmoid(gate_part)
    grad_gate_part = grad_hidden * up_part * sig_part * (1.0 + gate_part * (1.0 - sig_part))
    grad_up_part = grad_hidden * gate_part * sig_part
    grad_gate_up = jnp.concatenate([grad_gate_part, grad_up_part], 1).astype(jnp.bfloat16)
    grad_gu = jnp.einsum("td,tf->df", normed_two, grad_gate_up, preferred_element_type=jnp.float32)
    grad_normed_two = jnp.dot(grad_gate_up, gu_w.T, preferred_element_type=jnp.float32)
    grad_mid_norm, grad_gain_two = norm_back(grad_normed_two, scaled_two, inverse_two, gain_two)
    grad_mid = grad_out + grad_mid_norm
    grad_branch = grad_mid.astype(jnp.bfloat16)
    grad_out_w = jnp.einsum("td,te->de", combined, grad_branch, preferred_element_type=jnp.float32)
    grad_combined = jnp.dot(grad_branch, out_w.T, preferred_element_type=jnp.float32)
    grad_attended = grad_combined.astype(jnp.bfloat16).reshape(tokens, H, HD)
    grad_recalled = (grad_combined * gate).astype(jnp.bfloat16).reshape(tokens, H, HD)
    grad_gate_pre = grad_combined * recalled * gate * (1.0 - gate)
    outgoing = jnp.stack([grad_attended, grad_recalled], 1)
    headward = lax.all_to_all(outgoing, "seq", split_axis=2, concat_axis=0, tiled=True)
    head_grads, pkey_grads, pvalue_grads, rate_grads = ([], [], [], [])
    for head in range(grouped.shape[2]):
        cols = slice(head * HD, (head + 1) * HD)
        dq, dk, dv, dpk, dpv, drate = head_backward(
            grouped[:, 0, head],
            grouped[:, 1, head],
            grouped[:, 2, head],
            pkv[0][:, cols],
            pkv[1][:, cols],
            rates[head],
            seg_ids,
            lse_all[:, head],
            headward[:, 0, head],
            headward[:, 1, head],
        )
        head_grads.append(jnp.stack([dq, dk, dv], 1))
        pkey_grads.append(dpk)
        pvalue_grads.append(dpv)
        rate_grads.append(drate)
    grads_heads = jnp.stack(head_grads, 2).astype(jnp.bfloat16)
    tokenward = lax.all_to_all(grads_heads, "seq", split_axis=0, concat_axis=2, tiled=True)
    grad_proj = jnp.concatenate(
        [tokenward.reshape(tokens, 3 * D), grad_gate_pre.astype(jnp.bfloat16)], 1
    )
    grad_mix = jnp.einsum("td,tf->df", normed, grad_proj, preferred_element_type=jnp.float32)
    grad_normed = jnp.dot(grad_proj, mix_w.T, preferred_element_type=jnp.float32)
    grad_in_norm, grad_gain_one = norm_back(grad_normed, scaled_one, inverse_one, gain_one)
    grad_rows = grad_mid + grad_in_norm
    weight_terms = (
        grad_mix,
        grad_out_w,
        grad_gu,
        grad_down,
        jnp.stack([grad_gain_one, grad_gain_two], 1),
    )
    memory_terms = (
        jnp.stack([jnp.concatenate(pkey_grads, 1), jnp.concatenate(pvalue_grads, 1)], 0),
        jnp.stack(rate_grads, 0),
    )
    return (weight_terms, memory_terms, grad_rows)


def on_device(
    inputs, segment_ids, cotangent, w_mix, w_out, w_gu, w_down, norm_gains, persist_kv, memory_decay
):
    first = lax.axis_index("section") == 0
    own_weights = (w_mix[0], w_out[0], w_gu[0], w_down[0], norm_gains[0])
    pkv = persist_kv[0]
    rates = memory_decay[0]
    count = inputs.shape[0]
    tokens = inputs.shape[2]
    zero_rows = jnp.zeros((tokens, D), jnp.float32)
    received = jnp.zeros((tokens, D), jnp.bfloat16)
    kept_ticks, out_ticks = ([], [])
    for tick in range(count + 1):
        own_rows = inputs[tick, 0].astype(jnp.float32) if tick < count else zero_rows
        layer_in = jnp.where(first, own_rows, received.astype(jnp.float32))
        seg_ids = jnp.where(
            first, segment_ids[min(tick, count - 1), 0], segment_ids[max(tick - 1, 0), 0]
        )
        full = (
            lax.all_gather(own_weights[0], "shard", axis=0, tiled=True),
            lax.all_gather(own_weights[1], "shard", axis=0, tiled=True),
            lax.all_gather(own_weights[2], "shard", axis=0, tiled=True),
            lax.all_gather(own_weights[3], "shard", axis=0, tiled=True),
            lax.all_gather(own_weights[4], "shard", axis=0, tiled=True),
        )
        result, kept = layer_forward(layer_in, seg_ids, full, pkv, rates)
        result_low = result.astype(jnp.bfloat16)
        out_ticks.append(result_low)
        kept_ticks.append(kept)
        if tick < count:
            received = shifted(result_low, "section", 1)
    grad_weights = (
        jnp.zeros((D, 4 * D), jnp.float32),
        jnp.zeros((D, D), jnp.float32),
        jnp.zeros((D, 2 * FF), jnp.float32),
        jnp.zeros((FF, D), jnp.float32),
        jnp.zeros((D, 2), jnp.float32),
    )
    grad_memory = (
        jnp.zeros((2,) + pkv.shape[1:], jnp.float32),
        jnp.zeros(rates.shape, jnp.float32),
    )
    back_received = jnp.zeros((tokens, D), jnp.bfloat16)
    grad_ticks = []
    for tick in range(count + 1):
        lower = max(tick - 1, 0)
        upper = min(tick + 1, count)
        kept = jax.tree.map(
            lambda early, late: jnp.where(first, early, late), kept_ticks[lower], kept_ticks[upper]
        )
        given = cotangent[tick, 0].astype(jnp.float32) if tick < count else zero_rows
        grad_out = jnp.where(first, back_received.astype(jnp.float32), given)
        full = (
            lax.all_gather(own_weights[0], "shard", axis=0, tiled=True),
            lax.all_gather(own_weights[1], "shard", axis=0, tiled=True),
            lax.all_gather(own_weights[2], "shard", axis=0, tiled=True),
            lax.all_gather(own_weights[3], "shard", axis=0, tiled=True),
            lax.all_gather(own_weights[4], "shard", axis=0, tiled=True),
        )
        weight_terms, memory_terms, grad_rows = layer_backward(grad_out, kept, full, pkv, rates)
        grad_weights = jax.tree.map(jnp.add, grad_weights, weight_terms)
        grad_memory = jax.tree.map(jnp.add, grad_memory, memory_terms)
        grad_ticks.append(grad_rows)
        if tick < count:
            back_received = shifted(grad_rows.astype(jnp.bfloat16), "section", -1)
    section_out = jnp.stack(
        [jnp.where(first, out_ticks[batch], out_ticks[batch + 1]) for batch in range(count)], 0
    )
    section_grad = jnp.stack(
        [
            jnp.where(
                first,
                grad_ticks[batch + 1],
                grad_ticks[batch].astype(jnp.bfloat16).astype(jnp.float32),
            )
            for batch in range(count)
        ],
        0,
    )
    shares = jax.tree.map(
        lambda part: part.astype(jnp.float32),
        lax.psum_scatter(as_sent(grad_weights), "shard", scatter_dimension=0, tiled=True),
    )
    shares = jax.tree.map(lambda part: part.astype(jnp.float32), lax.psum(as_sent(shares), "seq"))
    memory_sums = lax.psum(grad_memory, "shard")
    return (
        section_out.reshape(1, count, 1, tokens, D),
        section_grad.reshape(1, count, 1, tokens, D),
        shares[0][None],
        shares[1][None],
        shares[2][None],
        shares[3][None],
        shares[4][None],
        memory_sums[0][None],
        memory_sums[1][None],
    )


MESH = pl.DeviceIdType.MESH
BF = jnp.bfloat16
F32 = jnp.float32


def here():
    return (lax.axis_index("section"), lax.axis_index("seq"), lax.axis_index("shard"))


def peer(place, chip, flip):
    x, s, z = place
    if chip % 2:
        x = 1 - x
    if chip // 2:
        s = (s + 2) % 4
    if flip:
        s = s + 1 - 2 * (s % 2)
    return (x, s, z)


def rows_of(device, size):
    x, s, _ = device
    return pl.ds(pl.multiple_of((s * 2 + x) * size, size), size)


class Gather:
    def __init__(self, full, batch, send, recv):
        self.place = here()
        self.full, self.batch, self.send, self.recv = full, batch, send, recv
        self.size = full.shape[1] // 8

    def copy(self, owner, target, sem):
        block = self.full.at[self.batch, rows_of(owner, self.size)]
        return pltpu.make_async_remote_copy(
            src_ref=block,
            dst_ref=block,
            send_sem=self.send.at[self.batch, sem],
            recv_sem=self.recv.at[self.batch, sem],
            device_id=target,
            device_id_type=MESH,
        )

    def start(self, value):
        self.full[self.batch, rows_of(self.place, self.size), :] = value
        for chip in (3, 1, 2, 0):
            self.copy(self.place, peer(self.place, chip, chip == 0), chip).start()

    def forward(self):
        other = peer(self.place, 0, True)
        for chip in (1, 2, 3):
            owner = peer(self.place, chip, False)
            self.copy(owner, owner, chip).wait_recv()
            self.copy(owner, other, 3 + chip).start()

    def finish(self):
        other = peer(self.place, 0, True)
        self.copy(other, other, 0).wait_recv()
        for chip in (1, 2, 3):
            owner = peer(self.place, chip, True)
            self.copy(owner, other, 3 + chip).wait_recv()
        for chip in (0, 1, 2, 3):
            self.copy(self.place, peer(self.place, chip, chip == 0), chip).wait_send()
        for chip in (1, 2, 3):
            self.copy(peer(self.place, chip, False), other, 3 + chip).wait_send()


class Scatter:
    def __init__(self, part, batch, pair, away, near, send, recv):
        self.place = here()
        self.part, self.batch, self.pair, self.away, self.near = part, batch, pair, away, near
        self.send, self.recv = send, recv
        self.size = part.shape[1] // 8

    def to_pair(self, chip):
        return pltpu.make_async_remote_copy(
            src_ref=self.part.at[self.batch, rows_of(peer(self.place, chip, True), self.size)],
            dst_ref=self.pair.at[self.batch, chip],
            send_sem=self.send.at[self.batch, chip],
            recv_sem=self.recv.at[self.batch, chip],
            device_id=peer(self.place, 0, True),
            device_id_type=MESH,
        )

    def to_chip(self, chip):
        return pltpu.make_async_remote_copy(
            src_ref=self.away.at[self.batch, chip - 1],
            dst_ref=self.near.at[self.batch, chip - 1],
            send_sem=self.send.at[self.batch, 3 + chip],
            recv_sem=self.recv.at[self.batch, 3 + chip],
            device_id=peer(self.place, chip, False),
            device_id_type=MESH,
        )

    def start(self):
        for chip in (3, 1, 2, 0):
            self.to_pair(chip).start()

    def chip_sum(self, chip):
        self.to_pair(chip).wait_recv()
        own = self.part[self.batch, rows_of(peer(self.place, chip, False), self.size), :]
        return own.astype(F32) + self.pair[self.batch, chip].astype(F32)

    def forward(self):
        for chip in (3, 1, 2):
            self.away[self.batch, chip - 1] = self.chip_sum(chip).astype(BF)
            self.to_chip(chip).start()

    def finish(self):
        total = self.chip_sum(0)
        for chip in (1, 2, 3):
            self.to_chip(chip).wait_recv()
            total = total + self.near[self.batch, chip - 1].astype(F32)
        for chip in (0, 1, 2, 3):
            self.to_pair(chip).wait_send()
        for chip in (1, 2, 3):
            self.to_chip(chip).wait_send()
        return total


class ColumnSum:
    def __init__(self, own, slots, out, send, recv, index):
        self.place = here()
        self.own, self.slots, self.out = own, slots, out
        self.send, self.recv, self.index = send, recv, index

    def copy(self, down, owner, source=None):
        x, s, z = self.place
        slot = owner if down else owner - 1
        target = (x, s, (z + 3) % 4 if down else (z + 1) % 4)
        landing = self.slots.at[down, slot]
        return pltpu.make_async_remote_copy(
            src_ref=landing if source is None else source,
            dst_ref=landing,
            send_sem=self.send.at[self.index, down, slot],
            recv_sem=self.recv.at[self.index, down, slot],
            device_id=target,
            device_id_type=MESH,
        )

    def start(self):
        z = self.place[2]
        for down in (0, 1):

            @pl.when(z == 3 * down)
            def _():
                for owner in (0, 1, 2) if down else (3, 2, 1):
                    self.copy(down, owner, self.own.at[owner]).start()

    def relay(self, down, owner, at):
        @pl.when(self.place[2] == at)
        def _():
            self.copy(down, owner).wait_recv()
            slot = owner if down else owner - 1
            self.slots[down, slot] = (
                self.slots[down, slot].astype(F32) + self.own[owner].astype(F32)
            ).astype(BF)
            self.copy(down, owner).start()

    def hop(self, number):
        if number == 1:
            self.relay(0, 3, 1)
            self.relay(1, 0, 2)
        else:
            self.relay(0, 2, 1)
            self.relay(1, 1, 2)
            self.relay(0, 3, 2)
            self.relay(1, 0, 1)

    def finish(self):
        z = self.place[2]
        for at in range(4):

            @pl.when(z == at)
            def _():
                total = self.own[at].astype(F32)
                if at > 0:
                    self.copy(0, at).wait_recv()
                    total = total + self.slots[0, at - 1].astype(F32)
                if at < 3:
                    self.copy(1, at).wait_recv()
                    total = total + self.slots[1, at].astype(F32)
                self.out[...] = total.astype(BF)
                for owner in range(at + 1, 4):
                    self.copy(0, owner).wait_send()
                for owner in range(at):
                    self.copy(1, owner).wait_send()


class RootSum:
    def __init__(self, own, slots, out, send, recv):
        self.place = here()
        x, s, _ = self.place
        self.root = 2 * x + s // 2
        self.own, self.slots, self.out = own, slots, out
        self.send, self.recv = send, recv

    def copy(self, down, source=None):
        x, s, z = self.place
        landing = self.slots.at[down]
        return pltpu.make_async_remote_copy(
            src_ref=landing if source is None else source,
            dst_ref=landing,
            send_sem=self.send.at[down],
            recv_sem=self.recv.at[down],
            device_id=(x, s, (z + 3) % 4 if down else (z + 1) % 4),
            device_id_type=MESH,
        )

    def sends(self, down):
        z = self.place[2]
        return z > self.root if down else z < self.root

    def start(self):
        for down in (0, 1):

            @pl.when((self.place[2] == 3 * down) & self.sends(down))
            def _():
                self.copy(down, self.own).start()

    def relay(self, down, at):
        @pl.when((self.place[2] == at) & self.sends(down))
        def _():
            self.copy(down).wait_recv()
            self.slots[down] = (self.slots[down].astype(F32) + self.own[...].astype(F32)).astype(BF)
            self.copy(down).start()

    def hop(self, number):
        self.relay(0, number)
        self.relay(1, 3 - number)

    def finish(self):
        z = self.place[2]
        self.out[...] = self.own[...]
        for down in (0, 1):

            @pl.when((z == self.root) & (z < 3 if down else z > 0))
            def _():
                self.copy(down).wait_recv()
                self.out[...] = (self.out[...].astype(F32) + self.slots[down].astype(F32)).astype(BF)

            @pl.when(self.sends(down))
            def _():
                self.copy(down).wait_send()


def meet(column=False):
    place = here()
    x, s, z = place
    others = [peer(place, chip, chip == 0) for chip in range(4)]
    if column:
        others += [(x, s, (z + 1) % 4), (x, s, (z + 3) % 4)]
    barrier = pltpu.get_barrier_semaphore()
    for other in others:
        pl.semaphore_signal(barrier, inc=1, device_id=other, device_id_type=MESH)
    pl.semaphore_wait(barrier, len(others))


def nn(left, right):
    return jnp.dot(left, right, preferred_element_type=F32)


def nt(left, right):
    return lax.dot_general(left, right, (((1,), (1,)), ((), ())), preferred_element_type=F32)


def tn(left, right):
    return lax.dot_general(left, right, (((0,), (0,)), ((), ())), preferred_element_type=F32)


def in_blocks(length, size, body):
    def step(index, carry):
        body(pl.ds(pl.multiple_of(index * size, size), size), index * size)
        return carry

    lax.fori_loop(0, length // size, step, 0)


def weights_of_scores(query, keys, pkeys, seg_rows, seg_cols, begin, rate):
    scale = 1.0 / math.sqrt(HD)
    inner = nt(query, keys)
    per_scores = nt(query, pkeys) * scale
    row_places = begin + lax.broadcasted_iota(jnp.int32, inner.shape, 0)
    col_places = lax.broadcasted_iota(jnp.int32, inner.shape, 1)
    allowed = (seg_rows == seg_cols) & (col_places <= row_places)
    distance = jnp.maximum(row_places - col_places, 0).astype(F32)
    decay_w = jnp.where(allowed, jnp.exp(-rate * distance) * (1.0 / HD), 0.0)
    seq_scores = jnp.where(allowed, inner * scale, -jnp.inf)
    top = jnp.maximum(
        jnp.max(per_scores, axis=1, keepdims=True), jnp.max(seq_scores, axis=1, keepdims=True)
    )
    per_exp = jnp.exp(per_scores - top)
    seq_exp = jnp.exp(seq_scores - top)
    denom = jnp.sum(per_exp, axis=1, keepdims=True) + jnp.sum(seq_exp, axis=1, keepdims=True)
    share = 1.0 / denom
    return inner, decay_w, distance, seq_exp * share, per_exp * share


def start_kernel(rows_ref, gain_ref, full_ref, gsend, grecv):
    meet()
    gathers = [Gather(full_ref, batch, gsend, grecv) for batch in range(2)]
    for batch, gather in enumerate(gathers):
        rows = rows_ref[batch]
        gather.start((rows * rms_scale(rows) * gain_ref[...]).astype(BF))
    for gather in gathers:
        gather.forward()
    for gather in gathers:
        gather.finish()


class ForwardIn(NamedTuple):
    normed: Any
    rows: Any
    gain_two: Any
    gain_next: Any
    gu: Any
    down: Any
    mix: Any
    out: Any
    pkeys: Any
    pvalues: Any
    rate: Any
    seg_rows: Any
    seg_cols: Any


class ForwardOut(NamedTuple):
    qkv: Any
    gate: Any
    recalled: Any
    combined: Any
    mid: Any
    normed_two: Any
    gate_up: Any
    hidden: Any
    out_rows: Any
    normed_next: Any


class BackwardIn(NamedTuple):
    grad_full: Any
    grad_rows: Any
    rows: Any
    normed: Any
    gain_one: Any
    gain_two: Any
    gu: Any
    down: Any
    mix: Any
    out: Any
    pkeys: Any
    pvalues: Any
    rate: Any
    seg_rows: Any
    seg_cols: Any
    qkv: Any
    gate: Any
    recalled: Any
    combined: Any
    mid: Any
    normed_two: Any
    gate_up: Any
    hidden: Any


class BackwardOut(NamedTuple):
    grad_mix: Any
    grad_out: Any
    gains: Any
    grad_persist: Any
    grad_rate: Any
    gu_sum: Any
    down_sum: Any
    grad_h: Any


class PlaneScratch(NamedTuple):
    part: Any
    pair: Any
    away: Any
    near: Any
    ssend: Any
    srecv: Any
    gsend: Any
    grecv: Any


class BackwardScratch(NamedTuple):
    grad_gu: Any
    grad_proj: Any
    grad_keys: Any
    grad_values: Any
    own_gu: Any
    own_down: Any
    branch: Any
    grad_mid: Any
    gu_slots: Any
    down_slots: Any
    csend: Any
    crecv: Any


class EarlyIn(NamedTuple):
    early_mix: Any
    early_out: Any


class EarlyOut(NamedTuple):
    mix_sum: Any
    out_sum: Any


class EarlyScratch(NamedTuple):
    mix_slots: Any
    root_slots: Any
    rsend: Any
    rrecv: Any


class NextOut(NamedTuple):
    grad_next: Any


def fields(*kinds):
    return tuple(name for kind in kinds for name in kind._fields)


def named(names, refs):
    return types.SimpleNamespace(**dict(zip(names, refs, strict=True)))


def forward_layer(ins, outs, *refs):
    r = named(ins + outs + fields(PlaneScratch), refs)
    length = r.part.shape[1]
    last = not hasattr(r, "normed_next")

    def project(batch):
        def block(rows, begin):
            proj = nn(r.normed[batch, rows, :], r.mix[...])
            r.qkv[batch, rows, :] = proj[:, : 3 * HD].astype(BF)
            r.gate[batch, rows, :] = jax.nn.sigmoid(proj[:, 3 * HD :])

        in_blocks(length, 256, block)

    def mixer(batch):
        def block(rows, begin):
            values = r.qkv[batch, :, 2 * HD :]
            inner, decay_w, _, probs, per_probs = weights_of_scores(
                r.qkv[batch, rows, :HD],
                r.qkv[batch, :, HD : 2 * HD],
                r.pkeys[...],
                r.seg_rows[batch, rows, :],
                r.seg_cols[batch],
                begin,
                r.rate[...],
            )
            attended = nn(probs.astype(BF), values) + nn(per_probs.astype(BF), r.pvalues[...])
            recalled = nn((inner * decay_w).astype(BF), values).astype(BF)
            r.recalled[batch, rows, :] = recalled
            combined = attended.astype(BF).astype(F32)
            combined = combined + r.gate[batch, rows, :] * recalled.astype(F32)
            combined = combined.astype(BF)
            r.combined[batch, rows, :] = combined
            r.part[batch, rows, :] = nn(combined, r.out[...]).astype(BF)

        in_blocks(length, 128, block)

    def feed(batch):
        def block(rows, begin):
            gate_up = nn(r.normed_two[batch, rows, :], r.gu[...])
            r.gate_up[batch, rows, :] = gate_up
            half = gate_up.shape[1] // 2
            hidden = (jax.nn.silu(gate_up[:, :half]) * gate_up[:, half:]).astype(BF)
            r.hidden[batch, rows, :] = hidden
            r.part[batch, rows, :] = nn(hidden, r.down[...]).astype(BF)

        in_blocks(length, 256, block)

    def scatter(batch):
        return Scatter(r.part, batch, r.pair, r.away, r.near, r.ssend, r.srecv)

    def send_normed(batch, own, gain, full):
        gather = Gather(full, batch, r.gsend, r.grecv)
        gather.start((own * rms_scale(own) * gain[...]).astype(BF))
        return gather

    meet()
    first, second = (scatter(batch) for batch in range(2))
    project(0)
    mixer(0)
    first.start()
    first.forward()
    project(1)
    mixer(1)
    second.start()
    second.forward()
    gathers = []
    for batch, part in enumerate((first, second)):
        mid = r.rows[batch] + part.finish()
        r.mid[batch] = mid
        gathers.append(send_normed(batch, mid, r.gain_two, r.normed_two))
    first, second = (scatter(batch) for batch in range(2))
    for batch, part in enumerate((first, second)):
        gathers[batch].forward()
        gathers[batch].finish()
        feed(batch)
        part.start()
        part.forward()
    gathers = []
    for batch, part in enumerate((first, second)):
        own = (r.mid[batch] + part.finish()).astype(BF)
        r.out_rows[batch] = own
        if not last:
            gathers.append(
                send_normed(batch, own.astype(F32), r.gain_next, r.normed_next)
            )
    for gather in gathers:
        gather.forward()
    for gather in gathers:
        gather.finish()


def backward_layer(ins, outs, *refs):
    scratch = fields(PlaneScratch, BackwardScratch)
    earlier = len(outs) == len(fields(BackwardOut, EarlyOut))
    if earlier:
        scratch += fields(EarlyScratch)
    r = named(ins + outs + scratch, refs)
    length = r.part.shape[1]
    last = not hasattr(r, "grad_next")
    sums = [
        ColumnSum(r.own_gu, r.gu_slots, r.gu_sum, r.csend, r.crecv, 0),
        ColumnSum(r.own_down, r.down_slots, r.down_sum, r.csend, r.crecv, 1),
    ]
    early = []
    if earlier:
        early = [
            ColumnSum(r.early_mix, r.mix_slots, r.mix_sum, r.csend, r.crecv, 2),
            RootSum(r.early_out, r.root_slots, r.out_sum, r.rsend, r.rrecv),
        ]

    def feed_back(batch):
        def block(rows, begin):
            grad_hidden = nt(r.grad_full[batch, rows, :], r.down[...])
            half = grad_hidden.shape[1]
            gate_part = r.gate_up[batch, rows, :half]
            up_part = r.gate_up[batch, rows, half:]
            sig_part = jax.nn.sigmoid(gate_part)
            silu = gate_part * sig_part
            grad_gate = grad_hidden * up_part * (sig_part + silu * (1.0 - sig_part))
            r.grad_gu[batch, rows, :half] = grad_gate.astype(BF)
            r.grad_gu[batch, rows, half:] = (grad_hidden * silu).astype(BF)
            r.part[batch, rows, :] = nt(r.grad_gu[batch, rows, :], r.gu[...]).astype(BF)

        in_blocks(length, 256, block)

    def feed_weights():
        def down(cols, begin):
            grad = tn(r.hidden[0], r.grad_full[0, :, cols])
            grad = grad + tn(r.hidden[1], r.grad_full[1, :, cols])
            grad = grad.reshape(4, grad.shape[0] // 4, grad.shape[1])
            r.own_down[:, :, cols] = grad.astype(BF)

        in_blocks(D, 256, down)
        product(r.own_gu, r.normed_two, r.grad_gu)

    def product(out, left, right):
        for owner in range(4):
            cols = slice(owner * (D // 4), (owner + 1) * (D // 4))
            grad = tn(left[0, :, cols], right[0]) + tn(left[1, :, cols], right[1])
            out[owner] = grad.astype(BF)

    def mixer_back(batch):
        scale = 1.0 / math.sqrt(HD)
        r.grad_keys[...] = jnp.zeros_like(r.grad_keys)
        r.grad_values[...] = jnp.zeros_like(r.grad_values)

        def block(rows, begin):
            grad_combined = nt(r.branch[batch, rows, :], r.out[...])
            gate = r.gate[batch, rows, :]
            recalled = r.recalled[batch, rows, :].astype(F32)
            attn_rows = grad_combined.astype(BF)
            memory_rows = (grad_combined * gate).astype(BF)
            grad_pre = grad_combined * recalled * gate * (1.0 - gate)
            r.grad_proj[batch, rows, 3 * HD :] = grad_pre.astype(BF)
            query = r.qkv[batch, rows, :HD]
            keys = r.qkv[batch, :, HD : 2 * HD]
            values = r.qkv[batch, :, 2 * HD :]
            inner, decay_w, distance, probs, per_probs = weights_of_scores(
                query,
                keys,
                r.pkeys[...],
                r.seg_rows[batch, rows, :],
                r.seg_cols[batch],
                begin,
                r.rate[...],
            )
            per_dp = nt(attn_rows, r.pvalues[...])
            seq_dp = nt(attn_rows, values)
            delta = jnp.sum(per_probs * per_dp, axis=1, keepdims=True) + jnp.sum(
                probs * seq_dp, axis=1, keepdims=True
            )
            per_ds = (per_probs * (per_dp - delta)).astype(BF)
            seq_ds = (probs * (seq_dp - delta)).astype(BF)
            weighted = nt(memory_rows, values) * decay_w
            grad_inner = weighted.astype(BF)
            memory = inner * decay_w
            rate_terms = weighted * inner * distance
            r.grad_rate[...] -= jnp.sum(rate_terms, axis=0, keepdims=True)
            grad_query = (nn(per_ds, r.pkeys[...]) + nn(seq_ds, keys)) * scale
            grad_query = grad_query + nn(grad_inner, keys)
            r.grad_proj[batch, rows, :HD] = grad_query.astype(BF)
            r.grad_keys[...] += tn(seq_ds, query) * scale + tn(grad_inner, query)
            r.grad_values[...] += tn(probs.astype(BF), attn_rows) + tn(
                memory.astype(BF), memory_rows
            )
            r.grad_persist[0] += tn(per_ds, query) * scale
            r.grad_persist[1] += tn(per_probs.astype(BF), attn_rows)

        in_blocks(length, 128, block)
        r.grad_proj[batch, :, HD : 2 * HD] = r.grad_keys[...].astype(BF)
        r.grad_proj[batch, :, 2 * HD : 3 * HD] = r.grad_values[...].astype(BF)

        def back(rows, begin):
            r.part[batch, rows, :] = nt(r.grad_proj[batch, rows, :], r.mix[...]).astype(BF)

        in_blocks(length, 256, back)

    def scatter(batch):
        return Scatter(r.part, batch, r.pair, r.away, r.near, r.ssend, r.srecv)

    def through_norm(batch, part, rows, gain):
        grad_normed = part.finish()
        inverse = rms_scale(rows)
        return norm_back(grad_normed, rows * inverse, inverse, gain[...])

    meet(True)
    r.grad_rate[...] = jnp.zeros_like(r.grad_rate)
    r.grad_persist[...] = jnp.zeros_like(r.grad_persist)
    for column in early:
        column.start()
    first, second = (scatter(batch) for batch in range(2))
    for batch, part in enumerate((first, second)):
        feed_back(batch)
        part.start()
        part.forward()
    feed_weights()
    gathers = []
    gain_sums = []
    for batch, part in enumerate((first, second)):
        grad_mid, gain_sum = through_norm(batch, part, r.mid[batch], r.gain_two)
        gain_sums.append(gain_sum[None])
        grad_mid = grad_mid + r.grad_rows[batch]
        r.grad_mid[batch] = grad_mid
        gather = Gather(r.branch, batch, r.gsend, r.grecv)
        gather.start(grad_mid.astype(BF))
        gathers.append(gather)
    r.gains[1:2] = gain_sums[0] + gain_sums[1]
    for column in early:
        column.hop(1)
    for column in early:
        column.hop(2)
    for column in sums:
        column.start()
    first, second = (scatter(batch) for batch in range(2))
    for batch, part in enumerate((first, second)):
        gathers[batch].forward()
        gathers[batch].finish()
        mixer_back(batch)
        part.start()
        part.forward()
        if batch == 0:
            for column in early:
                column.finish()
            for column in sums:
                column.hop(1)
    product(r.grad_mix, r.normed, r.grad_proj)
    grad_out = tn(r.combined[0], r.branch[0]) + tn(r.combined[1], r.branch[1])
    r.grad_out[...] = grad_out.astype(BF)
    gathers = []
    gain_sums = []
    for batch, part in enumerate((first, second)):
        grad_h, gain_sum = through_norm(batch, part, r.rows[batch], r.gain_one)
        gain_sums.append(gain_sum[None])
        grad_h = (grad_h + r.grad_mid[batch]).astype(BF)
        r.grad_h[batch] = grad_h
        if not last:
            gather = Gather(r.grad_next, batch, r.gsend, r.grecv)
            gather.start(grad_h)
            gathers.append(gather)
    r.gains[0:1] = gain_sums[0] + gain_sums[1]
    for column in sums:
        column.hop(2)
    for gather in gathers:
        gather.forward()
    for gather in gathers:
        gather.finish()
    for column in sums:
        column.finish()


def final_kernel(*refs):
    place = here()
    x, s, z = place
    sibling, beside, partner = (peer(place, 0, True), peer(place, 2, False), peer(place, 1, False))
    across = peer(place, 3, False)
    by_layer = [list(refs[0:6]), list(refs[6:12])]
    small_ref = refs[12]
    bufs = refs[13:16]
    out_buf, rows_buf, grads_buf, plane_buf = refs[16:20]
    column_buf, mix_sum, out_sum, mix_slots, root_slots, *sems = refs[20:]
    psend, precv, osend, orecv, rsend, rrecv, zsend, zrecv, ssend, srecv, *sems = sems
    csend, crecv, hsend, hrecv = sems
    columns = [
        ColumnSum(by_layer[0][0], mix_slots, mix_sum, csend, crecv, 0),
        RootSum(by_layer[0][3], root_slots, out_sum, hsend, hrecv),
    ]
    by_layer[0][0], by_layer[0][3] = mix_sum, out_sum

    def copy(source, landing, sems, index, target):
        return pltpu.make_async_remote_copy(
            src_ref=source,
            dst_ref=landing,
            send_sem=sems[0].at[index],
            recv_sem=sems[1].at[index],
            device_id=target,
            device_id_type=MESH,
        )

    flips = [(dx, ds) for dx in (0, 1) for ds in range(4) if dx or ds]
    plane = [((x + dx) % 2, (s + ds) % 4, z) for dx, ds in flips]
    column = [(x, s, (z + dz) % 4) for dz in (1, 2, 3)]
    barrier = pltpu.get_barrier_semaphore()
    for other in plane + column:
        pl.semaphore_signal(barrier, inc=1, device_id=other, device_id_type=MESH)
    pl.semaphore_wait(barrier, len(plane) + len(column))

    def to_plane_of(dz):
        target = (z + dz) % 4
        return copy(
            small_ref.at[target], column_buf.at[dz - 1], (zsend, zrecv), dz - 1, (x, s, target)
        )

    def to_plane(index):
        slot = plane_buf.at[x * 4 + s]
        return copy(slot, slot, (ssend, srecv), index, plane[index])

    for dz in (1, 2, 3):
        to_plane_of(dz).start()

    psems = [(psend.at[i], precv.at[i]) for i in range(3)]

    def piece(index, kind, slot, target, source=None):
        landing = bufs[index].at[slot]
        return copy(landing if source is None else source, landing, psems[index], kind, target)

    mine = (x, s)
    turned = (1 - x, s)

    def send(indices):
        for layer in (0, 1):
            own, theirs = by_layer[layer], by_layer[1 - layer]

            @pl.when(x == layer)
            def _():
                for index in indices:
                    piece(index, 2, mine, partner, theirs[index]).start()
                    piece(index, 0, mine, beside, own[index]).start()
                    piece(index, 1, mine, sibling, own[index]).start()
                for index in indices:
                    bufs[index][mine] = own[index][...]

    def turn(indices):
        for index in indices:
            piece(index, 2, turned, partner).wait_recv()
            piece(index, 3, turned, beside).start()
            piece(index, 4, turned, sibling).start()

    for column in columns:
        column.start()
    send((1, 2))
    for layer in (0, 1):

        @pl.when(x == layer)
        def _():
            copy(by_layer[1 - layer][4], rows_buf, (rsend, rrecv), 0, partner).start()
            copy(by_layer[1 - layer][5], grads_buf, (rsend, rrecv), 1, partner).start()

    total = small_ref[z]
    for dz in (1, 2, 3):
        to_plane_of(dz).wait_recv()
        total = total + column_buf[dz - 1]
    plane_buf[x * 4 + s] = total
    for index in range(7):
        to_plane(index).start()
    for column in columns:
        column.hop(1)
    for column in columns:
        column.hop(2)
    turn((1, 2))
    for column in columns:
        column.finish()
    send((0,))

    core = s % 2
    root = z == 2 * x + s // 2
    of_root = (z // 2, 2 * (z % 2) + core)
    apart = 2 * ((x + of_root[0]) % 2) + (s // 2 + of_root[1] // 2) % 2

    def out_copy(index, target, source=None):
        landing = out_buf.at[core]
        return copy(landing if source is None else source, landing, (osend, orecv), index, target)

    for layer in (0, 1):

        @pl.when(root & (x == layer))
        def _():
            out_copy(1, beside, by_layer[layer][3]).start()
            out_copy(2, partner, by_layer[1 - layer][3]).start()
            out_copy(3, across, by_layer[1 - layer][3]).start()
            out_buf[core] = by_layer[layer][3][...]

    for apart_by in (1, 2, 3):

        @pl.when(apart == apart_by)
        def _():
            out_copy(apart_by, beside).wait_recv()

    out_copy(0, sibling).start()

    turn((0,))
    far = (x, (s + 2) % 4)
    far_turned = (1 - x, (s + 2) % 4)
    for index in (1, 2, 0):
        piece(index, 0, far, beside).wait_recv()
        piece(index, 5, far, sibling).start()
    for index in (1, 2, 0):
        piece(index, 3, far_turned, beside).wait_recv()
        piece(index, 6, far_turned, sibling).start()
    twin = sibling[1]
    far_twin = (twin + 2) % 4
    for index in range(3):
        piece(index, 1, (x, twin), sibling).wait_recv()
        piece(index, 4, (1 - x, twin), sibling).wait_recv()
        piece(index, 5, (x, far_twin), sibling).wait_recv()
        piece(index, 6, (1 - x, far_twin), sibling).wait_recv()
    other_out = out_buf.at[1 - core]
    copy(other_out, other_out, (osend, orecv), 0, sibling).wait_recv()
    for index in range(7):
        dx, ds = flips[index]
        slot = plane_buf.at[((x + dx) % 2) * 4 + (s + 4 - ds) % 4]
        copy(slot, slot, (ssend, srecv), index, plane[index]).wait_recv()
    for index in (0, 1):
        copy(rows_buf, rows_buf, (rsend, rrecv), index, partner).wait()
    for index in range(7):
        to_plane(index).wait_send()
    for dz in (1, 2, 3):
        to_plane_of(dz).wait_send()
    for index in range(3):
        for kind in range(7):
            piece(index, kind, mine, sibling).wait_send()
    out_copy(0, sibling).wait_send()

    @pl.when(root)
    def _():
        for index in (1, 2, 3):
            out_copy(index, sibling).wait_send()


def kernel_call(kernel, number, operands, outs, scratch):
    vmem = pl.BlockSpec(memory_space=pltpu.VMEM)
    return pl.pallas_call(
        kernel,
        out_shape=outs,
        in_specs=[vmem] * len(operands),
        out_specs=[vmem] * len(outs),
        scratch_shapes=scratch,
        compiler_params=pltpu.CompilerParams(
            collective_id=number, has_side_effects=True, vmem_limit_bytes=58 * 2**20
        ),
    )(*operands)


def pairs_of(*sizes):
    return [pltpu.SemaphoreType.DMA(size) for size in sizes for _ in range(2)]


def scatter_scratch(length):
    size = length // 8
    return [
        pltpu.VMEM((2, length, D), BF),
        pltpu.VMEM((2, 4, size, D), BF),
        pltpu.VMEM((2, 3, size, D), BF),
        pltpu.VMEM((2, 3, size, D), BF),
        *pairs_of((2, 7), (2, 7)),
    ]


def forward_call(number, given, last):
    count, length, _ = given.normed.shape
    half = given.down.shape[0]
    shape = jax.ShapeDtypeStruct
    outs = dict(
        qkv=shape((count, length, 3 * HD), BF),
        gate=shape((count, length, HD), F32),
        recalled=shape((count, length, HD), BF),
        combined=shape((count, length, HD), BF),
        mid=shape((count, length // 8, D), F32),
        normed_two=shape((count, length, D), BF),
        gate_up=shape((count, length, 2 * half), F32),
        hidden=shape((count, length, half), BF),
        out_rows=shape((count, length // 8, D), BF),
        normed_next=shape((count, length, D), BF),
    )
    if last:
        del outs[ForwardOut._fields[-1]]
    operands = [getattr(given, name) for name in ForwardIn._fields]
    kernel = functools.partial(forward_layer, ForwardIn._fields, tuple(outs))
    found = kernel_call(kernel, number, operands, list(outs.values()), scatter_scratch(length))
    return named(outs, found)


def backward_call(number, given, last):
    count, length, _ = given.normed.shape
    half = given.down.shape[0]
    depth = D // 4
    shape = jax.ShapeDtypeStruct
    outs = dict(
        grad_mix=shape((4, depth, 4 * HD), BF),
        grad_out=shape((HD, D), BF),
        gains=shape((2, D), F32),
        grad_persist=shape((2,) + given.pkeys.shape, F32),
        grad_rate=shape((1, length), F32),
        gu_sum=shape((depth, 2 * half), BF),
        down_sum=shape((half // 4, D), BF),
        grad_h=shape((count, length // 8, D), BF),
    )
    ins = BackwardIn._fields
    if last:
        ins += EarlyIn._fields
        outs |= dict(mix_sum=shape((depth, 4 * HD), BF), out_sum=shape((HD, D), BF))
    else:
        outs |= dict(grad_next=shape((count, length, D), BF))
    scratch = scatter_scratch(length) + [
        pltpu.VMEM((count, length, 2 * half), BF),
        pltpu.VMEM((count, length, 4 * HD), BF),
        pltpu.VMEM((length, HD), F32),
        pltpu.VMEM((length, HD), F32),
        pltpu.VMEM((4, depth, 2 * half), BF),
        pltpu.VMEM((4, half // 4, D), BF),
        pltpu.VMEM((count, length, D), BF),
        pltpu.VMEM((count, length // 8, D), F32),
        pltpu.VMEM((2, 3, depth, 2 * half), BF),
        pltpu.VMEM((2, 3, half // 4, D), BF),
        *pairs_of((3, 2, 3)),
    ]
    if last:
        scratch += [
            pltpu.VMEM((2, 3, depth, 4 * HD), BF),
            pltpu.VMEM((2, HD, D), BF),
            *pairs_of((2,)),
        ]
    kernel = functools.partial(backward_layer, ins, tuple(outs))
    operands = [getattr(given, name) for name in ins]
    found = kernel_call(kernel, number, operands, list(outs.values()), scratch)
    return named(outs, found)


def final_call(number, by_layer, small):
    operands = (*by_layer[0], *by_layer[1], small)
    mix, gu, down, out, *rows = by_layer[1]
    outs = [jax.ShapeDtypeStruct((2, 4) + part.shape, BF) for part in (mix, gu, down)]
    outs.append(jax.ShapeDtypeStruct((2,) + out.shape, BF))
    outs += [jax.ShapeDtypeStruct(part.shape, BF) for part in rows]
    outs.append(jax.ShapeDtypeStruct((8,) + small.shape[1:], F32))
    scratch = [
        pltpu.VMEM((3,) + small.shape[1:], F32),
        pltpu.VMEM(mix.shape, BF),
        pltpu.VMEM(out.shape, BF),
        pltpu.VMEM((2, 3) + mix.shape, BF),
        pltpu.VMEM((2,) + out.shape, BF),
        *pairs_of((3, 7), (4,), (2,), (3,), (7,), (1, 2, 3), (2,)),
    ]
    return kernel_call(final_kernel, number, operands, outs, scratch)


def assemble_kernel(unit, mix_buf, gu_buf, down_buf, mix_ref, gu_ref, down_ref):
    padded = down_buf.shape[2]
    half = gu_buf.shape[3] // 2
    for which in range(8):
        slot = (which // 4, which % 4)
        mix = mix_buf[slot].astype(F32)
        for kind in range(4):
            begin = kind * D + which * HD
            mix_ref[0, :, begin : begin + HD] = mix[:, kind * HD : (kind + 1) * HD]
        part = gu_buf[slot].astype(F32)
        for side in range(2):
            for owner in range(half // padded):
                begin = side * FF + (owner * 8 + which) * unit
                source = side * half + owner * padded
                gu_ref[0, :, begin : begin + unit] = part[:, source : source + unit]
    for pair in range(2):
        down = down_buf[0, pair].astype(F32)
        down_ref[0, pair * unit : (pair + 1) * unit, :] = down[:unit]


def assemble_call(unit, mix_buf, gu_buf, down_buf):
    depth, padded = mix_buf.shape[2], down_buf.shape[2]
    rows = depth // 4
    return pl.pallas_call(
        functools.partial(assemble_kernel, unit),
        grid=(4,),
        out_shape=[
            jax.ShapeDtypeStruct((1, depth, 4 * D), F32),
            jax.ShapeDtypeStruct((1, depth, 2 * FF), F32),
            jax.ShapeDtypeStruct((1, 8 * unit, D), F32),
        ],
        in_specs=[
            pl.BlockSpec((2, 4, rows, 4 * HD), lambda i: (0, 0, i, 0)),
            pl.BlockSpec((2, 4, rows, gu_buf.shape[3]), lambda i: (0, 0, i, 0)),
            pl.BlockSpec((1, 2, padded, D), lambda i: (i // 2, i % 2, 0, 0)),
        ],
        out_specs=[
            pl.BlockSpec((1, rows, 4 * D), lambda i: (0, i, 0)),
            pl.BlockSpec((1, rows, 2 * FF), lambda i: (0, i, 0)),
            pl.BlockSpec((1, 2 * unit, D), lambda i: (0, i, 0)),
        ],
        compiler_params=pltpu.CompilerParams(vmem_limit_bytes=40 * 2**20),
    )(mix_buf, gu_buf, down_buf)


def tensor_parallel(
    inputs, segment_ids, cotangent, w_mix, w_out, w_gu, w_down, norm_gains, persist_kv, memory_decay
):
    x, s, z = here()
    nx, ns, nz = (lax.axis_size(a) for a in ("section", "seq", "shard"))
    width = nx * ns
    mine = x * ns + s
    other = (1 - x) * ns + s
    first = x == 0
    count, _, tokens, _ = inputs.shape
    length = tokens * ns
    size = length // width
    depth = w_mix.shape[1]
    unit = w_down.shape[1] // width

    heads = w_mix[0].reshape(depth, 4, H, HD)
    halves = w_gu[0].reshape(depth, 2, nz, width, unit)
    downs = w_down[0].reshape(width, unit, D)
    more = -unit % 32

    def pick(which):
        both = lax.dynamic_index_in_dim(halves, which, 3, keepdims=False)
        both = jnp.pad(both, ((0, 0), (0, 0), (0, 0), (0, more)))
        down = lax.dynamic_index_in_dim(downs, which, 0, keepdims=False)
        return (
            lax.dynamic_index_in_dim(heads, which, 2, keepdims=False).reshape(depth, 4 * HD),
            both.reshape(depth, 2 * nz * (unit + more)),
            jnp.pad(down, ((0, more), (0, 0))),
        )

    def layers(own, got):
        return (jnp.where(first, own, got), jnp.where(first, got, own))

    swap = [(0, 1), (1, 0)]
    parts = [layers(o, lax.ppermute(g, "section", swap)) for o, g in zip(pick(mine), pick(other))]
    out_rows = lax.dynamic_index_in_dim(
        w_out[0].reshape(2, HD, D), lax.rem(s, 2), 0, keepdims=False
    )
    out_all = lax.all_gather(out_rows, "shard", axis=0)
    out_own = lax.dynamic_index_in_dim(out_all, mine // 2, 0, keepdims=False)
    out_got = lax.ppermute(
        lax.dynamic_index_in_dim(out_all, other // 2, 0, keepdims=False), "section", swap
    )
    out_w = layers(out_own, out_got)
    mix_w, gu_w, down_w = (
        [lax.all_gather(part[layer], "shard", axis=0, tiled=True) for layer in range(2)]
        for part in parts
    )

    small = jnp.concatenate([persist_kv[0].reshape(-1).astype(F32), memory_decay[0]])
    small = lax.all_gather(small, ("section", "seq"), axis=0)
    rates = small[:, -2:].reshape(2, H)[:, mine]
    persist = small[:, :-2].astype(BF).reshape(2, ns, 2, persist_kv.shape[2], 2, HD)
    persist = lax.dynamic_index_in_dim(persist, mine // 2, 1, keepdims=False)
    persist = lax.dynamic_index_in_dim(persist, lax.rem(mine, 2), 3, keepdims=False)
    gains = lax.all_gather(norm_gains[0], ("section", "shard"), axis=0, tiled=True)
    gains = gains.astype(F32).reshape(2, 1, D, 2)

    def own_rows(whole):
        return lax.dynamic_slice_in_dim(whole[:, 0], x * size, size, 1).astype(F32)

    cot_full = lax.all_gather(cotangent[:, 0], "seq", axis=1, tiled=True)
    rows = own_rows(inputs)
    full = jax.ShapeDtypeStruct((count, length, D), BF)
    (normed,) = kernel_call(
        start_kernel, 0, (rows, gains[0, :, :, 0]), [full], pairs_of((2, 7))
    )
    of_layer = [
        dict(
            mix=mix_w[layer],
            out=out_w[layer],
            gu=gu_w[layer],
            down=down_w[layer],
            gain_one=gains[layer, :, :, 0],
            gain_two=gains[layer, :, :, 1],
            gain_next=gains[1, :, :, 0],
            pkeys=persist[layer, 0],
            pvalues=persist[layer, 1],
            rate=rates[layer].reshape(1, 1),
            seg_rows=segment_ids[:, 0, :, None],
            seg_cols=segment_ids,
        )
        for layer in range(2)
    ]
    outputs = []
    for layer in range(2):
        of_layer[layer] |= dict(normed=normed, rows=rows)
        found = forward_call(1 + layer, types.SimpleNamespace(**of_layer[layer]), layer == 1)
        of_layer[layer] |= vars(found)
        outputs.append(found.out_rows)
        if layer == 0:
            normed = found.normed_next
            rows = found.out_rows.astype(F32)
    given = dict(of_layer[1], grad_full=cot_full, grad_rows=own_rows(cotangent))
    later = backward_call(3, types.SimpleNamespace(**given), False)
    given = dict(
        of_layer[0],
        grad_full=later.grad_next,
        grad_rows=later.grad_h.astype(F32),
        early_mix=later.grad_mix,
        early_out=later.grad_out,
    )
    earlier = backward_call(4, types.SimpleNamespace(**given), True)
    by_layer = [
        (earlier.grad_mix, earlier.gu_sum, earlier.down_sum, earlier.grad_out),
        (earlier.mix_sum, later.gu_sum, later.down_sum, earlier.out_sum),
    ]
    both = (earlier, later)
    grads = [found.grad_h for found in both]
    gain_sums = [found.gains for found in both]

    memory_all = jnp.stack([found.grad_persist for found in both], 0).reshape(-1, HD)
    rate_all = jnp.stack([jnp.sum(found.grad_rate) for found in both])
    rate_all = jnp.pad(rate_all[None], ((0, 7), (0, HD - 2)))
    gain_all = jnp.stack(gain_sums, 0).reshape(4, nz, 2, HD).transpose(1, 0, 2, 3)
    memory_all = jnp.concatenate([memory_all, rate_all], 0)
    small = jnp.concatenate(
        [jnp.broadcast_to(memory_all[None], (nz,) + memory_all.shape), gain_all.reshape(nz, 8, HD)],
        1,
    )
    by_layer = [(*by_layer[layer], outputs[layer], grads[layer]) for layer in range(2)]
    mix_all, gu_all, down_all, out_all, rows_got, grads_got, plane_all = final_call(
        5, by_layer, small
    )

    def whole_rows(of_layer, got):
        both = layers(jnp.where(first, of_layer[0], of_layer[1]), got)
        return jnp.concatenate(both, 1)[None, :, None]

    section_out = whole_rows(outputs, rows_got)
    section_grad = whole_rows(grads, grads_got).astype(F32)
    grad_mix, grad_gu, grad_down = assemble_call(unit, mix_all, gu_all, down_all)
    grad_out = out_all.astype(F32).reshape(1, 2 * HD, D)

    heads_of = lax.dynamic_slice_in_dim(plane_all, 2 * s, 2, 0)
    of_section = lax.dynamic_index_in_dim(
        heads_of[:, :64].reshape(2, 2, 2, -1, HD), x, 1, keepdims=False
    )
    grad_persist = of_section.transpose(1, 2, 0, 3).reshape(1, 2, -1, 2 * HD)
    grad_rate = lax.dynamic_index_in_dim(heads_of[:, 64], x, 1, keepdims=False)[None]
    gain_all = jnp.sum(plane_all[:, 72:], 0).reshape(2, 2, depth)
    grad_gain = lax.dynamic_index_in_dim(gain_all, x, 0).transpose(0, 2, 1)
    return (
        section_out,
        section_grad,
        grad_mix,
        grad_out,
        grad_gu,
        grad_down,
        grad_gain,
        grad_persist,
        grad_rate,
    )


def solution(mesh):
    sizes = mesh.shape
    planar = (sizes["section"], sizes["seq"]) == (2, 4)
    placed = (
        P(None, "shard", "seq", None),
        P(None, "shard", None),
        P(None, "shard", "seq", None),
        P("section", "shard", None),
        P("section", "shard", None),
        P("section", "shard", None),
        P("section", "shard", None),
        P("section", "shard", None),
        P("section", None, None, "seq"),
        P("section", "seq"),
    )
    return jax.shard_map(
        tensor_parallel if planar else on_device,
        mesh=mesh,
        in_specs=placed,
        out_specs=(
            P("section", None, "shard", "seq", None),
            P("section", None, "shard", "seq", None),
            P("section", "shard", None),
            P("section", "shard", None),
            P("section", "shard", None),
            P("section", "shard", None),
            P("section", "shard", None),
            P("section", None, None, "seq"),
            P("section", "seq"),
        ),
        check_vma=False,
    )
```

```python
import functools
import math
import types
from typing import Any, NamedTuple

import jax
import jax.numpy as jnp
from jax import lax
from jax.experimental import pallas as pl
from jax.experimental.pallas import tpu as pltpu
from jax.sharding import PartitionSpec as P

D = 1024
H = 8
HD = 128
FF = 2816


def shifted(value, axis, by):
    size = lax.axis_size(axis)
    pairs = [(i, i + by) for i in range(size) if 0 <= i + by < size]
    return lax.ppermute(value, axis, pairs)


def as_sent(value):
    return jax.tree.map(lambda a: a.astype(jnp.bfloat16) if a.dtype == jnp.float32 else a, value)


def rms_scale(values):
    return lax.rsqrt(jnp.mean(values * values, axis=-1, keepdims=True) + 1e-06)


def norm_back(grad_normed, scaled, inverse, gain):
    grad_scaled = grad_normed * gain
    grad_rows = inverse * (
        grad_scaled - scaled * jnp.mean(grad_scaled * scaled, axis=-1, keepdims=True)
    )
    return (grad_rows, jnp.sum(grad_normed * scaled, axis=0))


def block_terms(query_rows, key_rows, seg_ids, begin, reach, rate):
    inner = jnp.dot(query_rows, key_rows.T, preferred_element_type=jnp.float32)
    row_places = begin + jnp.arange(reach - begin, dtype=jnp.int32)
    col_places = jnp.arange(reach, dtype=jnp.int32)
    allowed = (seg_ids[begin:reach][:, None] == seg_ids[:reach][None, :]) & (
        col_places[None, :] <= row_places[:, None]
    )
    distance = jnp.maximum(row_places[:, None] - col_places[None, :], 0).astype(jnp.float32)
    decay_w = jnp.where(allowed, jnp.exp(-rate * distance), jnp.float32(0.0))
    return (inner, allowed, decay_w, distance)


def head_forward(query, keys, values, pkeys, pvalues, rate, seg_ids):
    length, width = query.shape
    block = min(512, length)
    scale = 1.0 / math.sqrt(width)
    attn_parts, memory_parts, lse_parts = ([], [], [])
    for begin in range(0, length, block):
        reach = begin + block
        query_rows = query[begin:reach]
        inner, allowed, decay_w, distance = block_terms(
            query_rows, keys[:reach], seg_ids, begin, reach, rate
        )
        per_scores = jnp.dot(query_rows, pkeys.T, preferred_element_type=jnp.float32) * scale
        seq_scores = jnp.where(allowed, inner * scale, -jnp.inf)
        top = jnp.maximum(
            jnp.max(per_scores, axis=1, keepdims=True), jnp.max(seq_scores, axis=1, keepdims=True)
        )
        per_exp = jnp.exp(per_scores - top)
        seq_exp = jnp.exp(seq_scores - top)
        denom = jnp.sum(per_exp, axis=1, keepdims=True) + jnp.sum(seq_exp, axis=1, keepdims=True)
        attended = jnp.dot(
            (per_exp / denom).astype(jnp.bfloat16), pvalues, preferred_element_type=jnp.float32
        )
        attended = attended + jnp.dot(
            (seq_exp / denom).astype(jnp.bfloat16),
            values[:reach],
            preferred_element_type=jnp.float32,
        )
        memory_w = (inner * decay_w * (1.0 / width)).astype(jnp.bfloat16)
        recalled = jnp.dot(memory_w, values[:reach], preferred_element_type=jnp.float32)
        attn_parts.append(attended)
        memory_parts.append(recalled)
        lse_parts.append(top[:, 0] + jnp.log(denom[:, 0]))
    return (
        jnp.concatenate(attn_parts, 0),
        jnp.concatenate(memory_parts, 0),
        jnp.concatenate(lse_parts, 0),
    )


def head_backward(query, keys, values, pkeys, pvalues, rate, seg_ids, lse, grad_attn, grad_memory):
    length, width = query.shape
    block = min(512, length)
    scale = 1.0 / math.sqrt(width)
    query_grads = []
    grad_keys = jnp.zeros((length, width), jnp.float32)
    grad_values = jnp.zeros((length, width), jnp.float32)
    grad_pkeys = jnp.zeros(pkeys.shape, jnp.float32)
    grad_pvalues = jnp.zeros(pvalues.shape, jnp.float32)
    grad_rate = jnp.float32(0.0)
    for begin in range(0, length, block):
        reach = begin + block
        query_rows = query[begin:reach]
        key_rows = keys[:reach]
        value_rows = values[:reach]
        inner, allowed, decay_w, distance = block_terms(
            query_rows, key_rows, seg_ids, begin, reach, rate
        )
        per_scores = jnp.dot(query_rows, pkeys.T, preferred_element_type=jnp.float32) * scale
        seq_scores = jnp.where(allowed, inner * scale, -jnp.inf)
        row_lse = lse[begin:reach][:, None]
        per_prob = jnp.exp(per_scores - row_lse)
        seq_prob = jnp.exp(seq_scores - row_lse)
        attn_rows = grad_attn[begin:reach]
        memory_rows = grad_memory[begin:reach]
        per_dp = jnp.dot(attn_rows, pvalues.T, preferred_element_type=jnp.float32)
        seq_dp = jnp.dot(attn_rows, value_rows.T, preferred_element_type=jnp.float32)
        delta = jnp.sum(per_prob * per_dp, axis=1, keepdims=True) + jnp.sum(
            seq_prob * seq_dp, axis=1, keepdims=True
        )
        per_ds = (per_prob * (per_dp - delta)).astype(jnp.bfloat16)
        seq_ds = (seq_prob * (seq_dp - delta)).astype(jnp.bfloat16)
        rows_grad = (
            jnp.dot(per_ds, pkeys, preferred_element_type=jnp.float32)
            + jnp.dot(seq_ds, key_rows, preferred_element_type=jnp.float32)
        ) * scale
        grad_pkeys = (
            grad_pkeys
            + jnp.einsum("qk,qd->kd", per_ds, query_rows, preferred_element_type=jnp.float32)
            * scale
        )
        grad_pvalues = grad_pvalues + jnp.einsum(
            "qk,qd->kd",
            per_prob.astype(jnp.bfloat16),
            attn_rows,
            preferred_element_type=jnp.float32,
        )
        key_part = (
            jnp.einsum("qk,qd->kd", seq_ds, query_rows, preferred_element_type=jnp.float32) * scale
        )
        value_part = jnp.einsum(
            "qk,qd->kd",
            seq_prob.astype(jnp.bfloat16),
            attn_rows,
            preferred_element_type=jnp.float32,
        )
        memory_w = (inner * decay_w * (1.0 / width)).astype(jnp.bfloat16)
        grad_mw = jnp.dot(memory_rows, value_rows.T, preferred_element_type=jnp.float32)
        value_part = value_part + jnp.einsum(
            "qk,qd->kd", memory_w, memory_rows, preferred_element_type=jnp.float32
        )
        grad_inner = (grad_mw * decay_w * (1.0 / width)).astype(jnp.bfloat16)
        rows_grad = rows_grad + jnp.dot(grad_inner, key_rows, preferred_element_type=jnp.float32)
        key_part = key_part + jnp.einsum(
            "qk,qd->kd", grad_inner, query_rows, preferred_element_type=jnp.float32
        )
        grad_rate = grad_rate - jnp.sum(grad_mw * inner * decay_w * (1.0 / width) * distance)
        grad_keys = grad_keys.at[:reach].add(key_part)
        grad_values = grad_values.at[:reach].add(value_part)
        query_grads.append(rows_grad)
    return (
        jnp.concatenate(query_grads, 0),
        grad_keys,
        grad_values,
        grad_pkeys,
        grad_pvalues,
        grad_rate,
    )


def layer_forward(rows_in, seg_ids, full, pkv, rates):
    mix_w, out_w, gu_w, down_w, gains = full
    tokens = rows_in.shape[0]
    gain_one = gains[:, 0].astype(jnp.float32)
    gain_two = gains[:, 1].astype(jnp.float32)
    inverse_one = rms_scale(rows_in)
    scaled_one = rows_in * inverse_one
    normed = (scaled_one * gain_one).astype(jnp.bfloat16)
    proj = jnp.dot(normed, mix_w, preferred_element_type=jnp.float32)
    qkv = proj[:, : 3 * D].astype(jnp.bfloat16).reshape(tokens, 3, H, HD)
    gate = jax.nn.sigmoid(proj[:, 3 * D :])
    grouped = lax.all_to_all(qkv, "seq", split_axis=2, concat_axis=0, tiled=True)
    attn_heads, memory_heads, lse_heads = ([], [], [])
    for head in range(grouped.shape[2]):
        cols = slice(head * HD, (head + 1) * HD)
        attended, recalled, lse = head_forward(
            grouped[:, 0, head],
            grouped[:, 1, head],
            grouped[:, 2, head],
            pkv[0][:, cols],
            pkv[1][:, cols],
            rates[head],
            seg_ids,
        )
        attn_heads.append(attended)
        memory_heads.append(recalled)
        lse_heads.append(lse)
    mixed = jnp.stack([jnp.stack(attn_heads, 1), jnp.stack(memory_heads, 1)], 1).astype(
        jnp.bfloat16
    )
    returned = lax.all_to_all(mixed, "seq", split_axis=0, concat_axis=2, tiled=True)
    attended = returned[:, 0].reshape(tokens, D).astype(jnp.float32)
    recalled = returned[:, 1].reshape(tokens, D).astype(jnp.float32)
    combined = (attended + gate * recalled).astype(jnp.bfloat16)
    mid = rows_in + jnp.dot(combined, out_w, preferred_element_type=jnp.float32)
    inverse_two = rms_scale(mid)
    scaled_two = mid * inverse_two
    normed_two = (scaled_two * gain_two).astype(jnp.bfloat16)
    gate_up = jnp.dot(normed_two, gu_w, preferred_element_type=jnp.float32)
    hidden = (jax.nn.silu(gate_up[:, :FF]) * gate_up[:, FF:]).astype(jnp.bfloat16)
    result = mid + jnp.dot(hidden, down_w, preferred_element_type=jnp.float32)
    kept = (
        seg_ids,
        inverse_one,
        scaled_one,
        normed,
        grouped,
        jnp.stack(lse_heads, 1),
        gate,
        recalled,
        combined,
        inverse_two,
        scaled_two,
        normed_two,
        gate_up,
        hidden,
    )
    return (result, kept)


def layer_backward(grad_out, kept, full, pkv, rates):
    (
        seg_ids,
        inverse_one,
        scaled_one,
        normed,
        grouped,
        lse_all,
        gate,
        recalled,
        combined,
        inverse_two,
        scaled_two,
        normed_two,
        gate_up,
        hidden,
    ) = kept
    mix_w, out_w, gu_w, down_w, gains = full
    tokens = grad_out.shape[0]
    gain_one = gains[:, 0].astype(jnp.float32)
    gain_two = gains[:, 1].astype(jnp.float32)
    grad_f = grad_out.astype(jnp.bfloat16)
    grad_down = jnp.einsum("tf,td->fd", hidden, grad_f, preferred_element_type=jnp.float32)
    grad_hidden = jnp.dot(grad_f, down_w.T, preferred_element_type=jnp.float32)
    gate_part = gate_up[:, :FF]
    up_part = gate_up[:, FF:]
    sig_part = jax.nn.sigmoid(gate_part)
    grad_gate_part = grad_hidden * up_part * sig_part * (1.0 + gate_part * (1.0 - sig_part))
    grad_up_part = grad_hidden * gate_part * sig_part
    grad_gate_up = jnp.concatenate([grad_gate_part, grad_up_part], 1).astype(jnp.bfloat16)
    grad_gu = jnp.einsum("td,tf->df", normed_two, grad_gate_up, preferred_element_type=jnp.float32)
    grad_normed_two = jnp.dot(grad_gate_up, gu_w.T, preferred_element_type=jnp.float32)
    grad_mid_norm, grad_gain_two = norm_back(grad_normed_two, scaled_two, inverse_two, gain_two)
    grad_mid = grad_out + grad_mid_norm
    grad_branch = grad_mid.astype(jnp.bfloat16)
    grad_out_w = jnp.einsum("td,te->de", combined, grad_branch, preferred_element_type=jnp.float32)
    grad_combined = jnp.dot(grad_branch, out_w.T, preferred_element_type=jnp.float32)
    grad_attended = grad_combined.astype(jnp.bfloat16).reshape(tokens, H, HD)
    grad_recalled = (grad_combined * gate).astype(jnp.bfloat16).reshape(tokens, H, HD)
    grad_gate_pre = grad_combined * recalled * gate * (1.0 - gate)
    outgoing = jnp.stack([grad_attended, grad_recalled], 1)
    headward = lax.all_to_all(outgoing, "seq", split_axis=2, concat_axis=0, tiled=True)
    head_grads, pkey_grads, pvalue_grads, rate_grads = ([], [], [], [])
    for head in range(grouped.shape[2]):
        cols = slice(head * HD, (head + 1) * HD)
        dq, dk, dv, dpk, dpv, drate = head_backward(
            grouped[:, 0, head],
            grouped[:, 1, head],
            grouped[:, 2, head],
            pkv[0][:, cols],
            pkv[1][:, cols],
            rates[head],
            seg_ids,
            lse_all[:, head],
            headward[:, 0, head],
            headward[:, 1, head],
        )
        head_grads.append(jnp.stack([dq, dk, dv], 1))
        pkey_grads.append(dpk)
        pvalue_grads.append(dpv)
        rate_grads.append(drate)
    grads_heads = jnp.stack(head_grads, 2).astype(jnp.bfloat16)
    tokenward = lax.all_to_all(grads_heads, "seq", split_axis=0, concat_axis=2, tiled=True)
    grad_proj = jnp.concatenate(
        [tokenward.reshape(tokens, 3 * D), grad_gate_pre.astype(jnp.bfloat16)], 1
    )
    grad_mix = jnp.einsum("td,tf->df", normed, grad_proj, preferred_element_type=jnp.float32)
    grad_normed = jnp.dot(grad_proj, mix_w.T, preferred_element_type=jnp.float32)
    grad_in_norm, grad_gain_one = norm_back(grad_normed, scaled_one, inverse_one, gain_one)
    grad_rows = grad_mid + grad_in_norm
    weight_terms = (
        grad_mix,
        grad_out_w,
        grad_gu,
        grad_down,
        jnp.stack([grad_gain_one, grad_gain_two], 1),
    )
    memory_terms = (
        jnp.stack([jnp.concatenate(pkey_grads, 1), jnp.concatenate(pvalue_grads, 1)], 0),
        jnp.stack(rate_grads, 0),
    )
    return (weight_terms, memory_terms, grad_rows)


def on_device(
    inputs, segment_ids, cotangent, w_mix, w_out, w_gu, w_down, norm_gains, persist_kv, memory_decay
):
    first = lax.axis_index("section") == 0
    own_weights = (w_mix[0], w_out[0], w_gu[0], w_down[0], norm_gains[0])
    pkv = persist_kv[0]
    rates = memory_decay[0]
    count = inputs.shape[0]
    tokens = inputs.shape[2]
    zero_rows = jnp.zeros((tokens, D), jnp.float32)
    received = jnp.zeros((tokens, D), jnp.bfloat16)
    kept_ticks, out_ticks = ([], [])
    for tick in range(count + 1):
        own_rows = inputs[tick, 0].astype(jnp.float32) if tick < count else zero_rows
        layer_in = jnp.where(first, own_rows, received.astype(jnp.float32))
        seg_ids = jnp.where(
            first, segment_ids[min(tick, count - 1), 0], segment_ids[max(tick - 1, 0), 0]
        )
        full = (
            lax.all_gather(own_weights[0], "shard", axis=0, tiled=True),
            lax.all_gather(own_weights[1], "shard", axis=0, tiled=True),
            lax.all_gather(own_weights[2], "shard", axis=0, tiled=True),
            lax.all_gather(own_weights[3], "shard", axis=0, tiled=True),
            lax.all_gather(own_weights[4], "shard", axis=0, tiled=True),
        )
        result, kept = layer_forward(layer_in, seg_ids, full, pkv, rates)
        result_low = result.astype(jnp.bfloat16)
        out_ticks.append(result_low)
        kept_ticks.append(kept)
        if tick < count:
            received = shifted(result_low, "section", 1)
    grad_weights = (
        jnp.zeros((D, 4 * D), jnp.float32),
        jnp.zeros((D, D), jnp.float32),
        jnp.zeros((D, 2 * FF), jnp.float32),
        jnp.zeros((FF, D), jnp.float32),
        jnp.zeros((D, 2), jnp.float32),
    )
    grad_memory = (
        jnp.zeros((2,) + pkv.shape[1:], jnp.float32),
        jnp.zeros(rates.shape, jnp.float32),
    )
    back_received = jnp.zeros((tokens, D), jnp.bfloat16)
    grad_ticks = []
    for tick in range(count + 1):
        lower = max(tick - 1, 0)
        upper = min(tick + 1, count)
        kept = jax.tree.map(
            lambda early, late: jnp.where(first, early, late), kept_ticks[lower], kept_ticks[upper]
        )
        given = cotangent[tick, 0].astype(jnp.float32) if tick < count else zero_rows
        grad_out = jnp.where(first, back_received.astype(jnp.float32), given)
        full = (
            lax.all_gather(own_weights[0], "shard", axis=0, tiled=True),
            lax.all_gather(own_weights[1], "shard", axis=0, tiled=True),
            lax.all_gather(own_weights[2], "shard", axis=0, tiled=True),
            lax.all_gather(own_weights[3], "shard", axis=0, tiled=True),
            lax.all_gather(own_weights[4], "shard", axis=0, tiled=True),
        )
        weight_terms, memory_terms, grad_rows = layer_backward(grad_out, kept, full, pkv, rates)
        grad_weights = jax.tree.map(jnp.add, grad_weights, weight_terms)
        grad_memory = jax.tree.map(jnp.add, grad_memory, memory_terms)
        grad_ticks.append(grad_rows)
        if tick < count:
            back_received = shifted(grad_rows.astype(jnp.bfloat16), "section", -1)
    section_out = jnp.stack(
        [jnp.where(first, out_ticks[batch], out_ticks[batch + 1]) for batch in range(count)], 0
    )
    section_grad = jnp.stack(
        [
            jnp.where(
                first,
                grad_ticks[batch + 1],
                grad_ticks[batch].astype(jnp.bfloat16).astype(jnp.float32),
            )
            for batch in range(count)
        ],
        0,
    )
    shares = jax.tree.map(
        lambda part: part.astype(jnp.float32),
        lax.psum_scatter(as_sent(grad_weights), "shard", scatter_dimension=0, tiled=True),
    )
    shares = jax.tree.map(lambda part: part.astype(jnp.float32), lax.psum(as_sent(shares), "seq"))
    memory_sums = lax.psum(grad_memory, "shard")
    return (
        section_out.reshape(1, count, 1, tokens, D),
        section_grad.reshape(1, count, 1, tokens, D),
        shares[0][None],
        shares[1][None],
        shares[2][None],
        shares[3][None],
        shares[4][None],
        memory_sums[0][None],
        memory_sums[1][None],
    )


MESH = pl.DeviceIdType.MESH
BF = jnp.bfloat16
F32 = jnp.float32


def here():
    return (lax.axis_index("section"), lax.axis_index("seq"), lax.axis_index("shard"))


def peer(place, chip, flip):
    x, s, z = place
    if chip % 2:
        x = 1 - x
    if chip // 2:
        s = (s + 2) % 4
    if flip:
        s = s + 1 - 2 * (s % 2)
    return (x, s, z)


def rows_of(device, size):
    x, s, _ = device
    return pl.ds(pl.multiple_of((s * 2 + x) * size, size), size)


class Gather:
    def __init__(self, full, batch, send, recv):
        self.place = here()
        self.full, self.batch, self.send, self.recv = full, batch, send, recv
        self.size = full.shape[1] // 8

    def copy(self, owner, target, sem):
        block = self.full.at[self.batch, rows_of(owner, self.size)]
        return pltpu.make_async_remote_copy(
            src_ref=block,
            dst_ref=block,
            send_sem=self.send.at[self.batch, sem],
            recv_sem=self.recv.at[self.batch, sem],
            device_id=target,
            device_id_type=MESH,
        )

    def start(self, value):
        self.full[self.batch, rows_of(self.place, self.size), :] = value
        for chip in (3, 1, 2, 0):
            self.copy(self.place, peer(self.place, chip, chip == 0), chip).start()

    def forward(self):
        other = peer(self.place, 0, True)
        for chip in (1, 2, 3):
            owner = peer(self.place, chip, False)
            self.copy(owner, owner, chip).wait_recv()
            self.copy(owner, other, 3 + chip).start()

    def finish(self):
        other = peer(self.place, 0, True)
        self.copy(other, other, 0).wait_recv()
        for chip in (1, 2, 3):
            owner = peer(self.place, chip, True)
            self.copy(owner, other, 3 + chip).wait_recv()
        for chip in (0, 1, 2, 3):
            self.copy(self.place, peer(self.place, chip, chip == 0), chip).wait_send()
        for chip in (1, 2, 3):
            self.copy(peer(self.place, chip, False), other, 3 + chip).wait_send()


class Scatter:
    def __init__(self, part, batch, pair, away, near, send, recv):
        self.place = here()
        self.part, self.batch, self.pair, self.away, self.near = part, batch, pair, away, near
        self.send, self.recv = send, recv
        self.size = part.shape[1] // 8

    def to_pair(self, chip):
        return pltpu.make_async_remote_copy(
            src_ref=self.part.at[self.batch, rows_of(peer(self.place, chip, True), self.size)],
            dst_ref=self.pair.at[self.batch, chip],
            send_sem=self.send.at[self.batch, chip],
            recv_sem=self.recv.at[self.batch, chip],
            device_id=peer(self.place, 0, True),
            device_id_type=MESH,
        )

    def to_chip(self, chip):
        return pltpu.make_async_remote_copy(
            src_ref=self.away.at[self.batch, chip - 1],
            dst_ref=self.near.at[self.batch, chip - 1],
            send_sem=self.send.at[self.batch, 3 + chip],
            recv_sem=self.recv.at[self.batch, 3 + chip],
            device_id=peer(self.place, chip, False),
            device_id_type=MESH,
        )

    def start(self):
        for chip in (3, 1, 2, 0):
            self.to_pair(chip).start()

    def chip_sum(self, chip):
        self.to_pair(chip).wait_recv()
        own = self.part[self.batch, rows_of(peer(self.place, chip, False), self.size), :]
        return own.astype(F32) + self.pair[self.batch, chip].astype(F32)

    def forward(self):
        for chip in (3, 1, 2):
            self.away[self.batch, chip - 1] = self.chip_sum(chip).astype(BF)
            self.to_chip(chip).start()

    def finish(self):
        total = self.chip_sum(0)
        for chip in (1, 2, 3):
            self.to_chip(chip).wait_recv()
            total = total + self.near[self.batch, chip - 1].astype(F32)
        for chip in (0, 1, 2, 3):
            self.to_pair(chip).wait_send()
        for chip in (1, 2, 3):
            self.to_chip(chip).wait_send()
        return total


class ColumnSum:
    def __init__(self, own, slots, out, send, recv, index):
        self.place = here()
        self.own, self.slots, self.out = own, slots, out
        self.send, self.recv, self.index = send, recv, index

    def copy(self, down, owner, source=None):
        x, s, z = self.place
        slot = owner if down else owner - 1
        target = (x, s, (z + 3) % 4 if down else (z + 1) % 4)
        landing = self.slots.at[down, slot]
        return pltpu.make_async_remote_copy(
            src_ref=landing if source is None else source,
            dst_ref=landing,
            send_sem=self.send.at[self.index, down, slot],
            recv_sem=self.recv.at[self.index, down, slot],
            device_id=target,
            device_id_type=MESH,
        )

    def start(self):
        z = self.place[2]
        for down in (0, 1):

            @pl.when(z == 3 * down)
            def _():
                for owner in (0, 1, 2) if down else (3, 2, 1):
                    self.copy(down, owner, self.own.at[owner]).start()

    def relay(self, down, owner, at):
        @pl.when(self.place[2] == at)
        def _():
            self.copy(down, owner).wait_recv()
            slot = owner if down else owner - 1
            self.slots[down, slot] = (
                self.slots[down, slot].astype(F32) + self.own[owner].astype(F32)
            ).astype(BF)
            self.copy(down, owner).start()

    def hop(self, number):
        if number == 1:
            self.relay(0, 3, 1)
            self.relay(1, 0, 2)
        else:
            self.relay(0, 2, 1)
            self.relay(1, 1, 2)
            self.relay(0, 3, 2)
            self.relay(1, 0, 1)

    def finish(self):
        z = self.place[2]
        for at in range(4):

            @pl.when(z == at)
            def _():
                total = self.own[at].astype(F32)
                if at > 0:
                    self.copy(0, at).wait_recv()
                    total = total + self.slots[0, at - 1].astype(F32)
                if at < 3:
                    self.copy(1, at).wait_recv()
                    total = total + self.slots[1, at].astype(F32)
                self.out[...] = total.astype(BF)
                for owner in range(at + 1, 4):
                    self.copy(0, owner).wait_send()
                for owner in range(at):
                    self.copy(1, owner).wait_send()


class RootSum:
    def __init__(self, own, slots, out, send, recv):
        self.place = here()
        x, s, _ = self.place
        self.root = 2 * x + s // 2
        self.own, self.slots, self.out = own, slots, out
        self.send, self.recv = send, recv

    def copy(self, down, source=None):
        x, s, z = self.place
        landing = self.slots.at[down]
        return pltpu.make_async_remote_copy(
            src_ref=landing if source is None else source,
            dst_ref=landing,
            send_sem=self.send.at[down],
            recv_sem=self.recv.at[down],
            device_id=(x, s, (z + 3) % 4 if down else (z + 1) % 4),
            device_id_type=MESH,
        )

    def sends(self, down):
        z = self.place[2]
        return z > self.root if down else z < self.root

    def start(self):
        for down in (0, 1):

            @pl.when((self.place[2] == 3 * down) & self.sends(down))
            def _():
                self.copy(down, self.own).start()

    def relay(self, down, at):
        @pl.when((self.place[2] == at) & self.sends(down))
        def _():
            self.copy(down).wait_recv()
            self.slots[down] = (self.slots[down].astype(F32) + self.own[...].astype(F32)).astype(BF)
            self.copy(down).start()

    def hop(self, number):
        self.relay(0, number)
        self.relay(1, 3 - number)

    def finish(self):
        z = self.place[2]
        self.out[...] = self.own[...]
        for down in (0, 1):

            @pl.when((z == self.root) & (z < 3 if down else z > 0))
            def _():
                self.copy(down).wait_recv()
                self.out[...] = (self.out[...].astype(F32) + self.slots[down].astype(F32)).astype(BF)

            @pl.when(self.sends(down))
            def _():
                self.copy(down).wait_send()


def meet(column=False):
    place = here()
    x, s, z = place
    others = [peer(place, chip, chip == 0) for chip in range(4)]
    if column:
        others += [(x, s, (z + 1) % 4), (x, s, (z + 3) % 4)]
    barrier = pltpu.get_barrier_semaphore()
    for other in others:
        pl.semaphore_signal(barrier, inc=1, device_id=other, device_id_type=MESH)
    pl.semaphore_wait(barrier, len(others))


def nn(left, right):
    return jnp.dot(left, right, preferred_element_type=F32)


def nt(left, right):
    return lax.dot_general(left, right, (((1,), (1,)), ((), ())), preferred_element_type=F32)


def tn(left, right):
    return lax.dot_general(left, right, (((0,), (0,)), ((), ())), preferred_element_type=F32)


def flat(ref):
    value = ref[...]
    return value.reshape(-1, value.shape[-1])


def in_blocks(length, size, body):
    def step(index, carry):
        body(pl.ds(pl.multiple_of(index * size, size), size), index * size)
        return carry

    lax.fori_loop(0, length // size, step, 0)


def weights_of_scores(query, keys, pkeys, seg_rows, seg_cols, begin, rate):
    scale = 1.0 / math.sqrt(HD)
    inner = nt(query, keys)
    per_scores = nt(query, pkeys) * scale
    row_places = begin + lax.broadcasted_iota(jnp.int32, inner.shape, 0)
    col_places = lax.broadcasted_iota(jnp.int32, inner.shape, 1)
    allowed = (seg_rows == seg_cols) & (col_places <= row_places)
    distance = jnp.maximum(row_places - col_places, 0).astype(F32)
    decay_w = jnp.where(allowed, jnp.exp(-rate * distance) * (1.0 / HD), 0.0)
    seq_scores = jnp.where(allowed, inner * scale, -jnp.inf)
    top = jnp.maximum(
        jnp.max(per_scores, axis=1, keepdims=True), jnp.max(seq_scores, axis=1, keepdims=True)
    )
    per_exp = jnp.exp(per_scores - top)
    seq_exp = jnp.exp(seq_scores - top)
    denom = jnp.sum(per_exp, axis=1, keepdims=True) + jnp.sum(seq_exp, axis=1, keepdims=True)
    share = 1.0 / denom
    return inner, decay_w, distance, seq_exp * share, per_exp * share


class SetupIn(NamedTuple):
    inputs: Any
    small: Any
    gain_rows: Any
    w_mix: Any
    w_out: Any
    w_gu: Any
    w_down: Any


class SetupOut(NamedTuple):
    rows: Any
    normed: Any
    gains: Any
    persist: Any
    rates: Any
    mix: Any
    mix_next: Any
    out: Any
    out_next: Any
    gu: Any
    gu_next: Any
    down: Any
    down_next: Any


class SetupScratch(NamedTuple):
    gain_all: Any
    small_all: Any
    mix_away: Any
    gu_away: Any
    down_away: Any
    zsend: Any
    zrecv: Any
    psend: Any
    precv: Any
    xsend: Any
    xrecv: Any
    gsend: Any
    grecv: Any
    csend: Any
    crecv: Any
    rsend: Any
    rrecv: Any


class ForwardIn(NamedTuple):
    normed: Any
    rows: Any
    gu_block: Any
    down_block: Any
    gains: Any
    mix: Any
    out: Any
    persist: Any
    rates: Any
    seg_rows: Any
    seg_cols: Any


class ForwardOut(NamedTuple):
    qkv: Any
    gate: Any
    recalled: Any
    combined: Any
    mid: Any
    normed_two: Any
    gate_up: Any
    hidden: Any
    gu: Any
    down: Any
    out_rows: Any
    normed_next: Any


class ForwardScratch(NamedTuple):
    csend: Any
    crecv: Any


class NextIn(NamedTuple):
    mix_block: Any
    out_block: Any


class NextWeights(NamedTuple):
    mix_next: Any
    out_next: Any


class NextScratch(NamedTuple):
    rsend: Any
    rrecv: Any


class BackwardIn(NamedTuple):
    grad_full: Any
    grad_rows: Any
    rows: Any
    normed: Any
    gu: Any
    down: Any
    gains: Any
    mix: Any
    out: Any
    persist: Any
    rates: Any
    seg_rows: Any
    seg_cols: Any
    qkv: Any
    gate: Any
    recalled: Any
    combined: Any
    mid: Any
    normed_two: Any
    gate_up: Any
    hidden: Any


class BackwardOut(NamedTuple):
    grad_mix: Any
    grad_out: Any
    gain_sums: Any
    grad_persist: Any
    grad_rate: Any
    gu_sum: Any
    down_sum: Any
    grad_h: Any


class PlaneScratch(NamedTuple):
    part: Any
    pair: Any
    away: Any
    near: Any
    ssend: Any
    srecv: Any
    gsend: Any
    grecv: Any


class BackwardScratch(NamedTuple):
    grad_gu: Any
    grad_proj: Any
    grad_keys: Any
    grad_values: Any
    own_gu: Any
    own_down: Any
    branch: Any
    grad_mid: Any
    gu_slots: Any
    down_slots: Any
    csend: Any
    crecv: Any


class EarlyIn(NamedTuple):
    early_mix: Any
    early_out: Any


class EarlyOut(NamedTuple):
    mix_sum: Any
    out_sum: Any


class EarlyScratch(NamedTuple):
    mix_slots: Any
    root_slots: Any
    rsend: Any
    rrecv: Any


class NextOut(NamedTuple):
    grad_next: Any


def fields(*kinds):
    return tuple(name for kind in kinds for name in kind._fields)


def named(names, refs):
    return types.SimpleNamespace(**dict(zip(names, refs, strict=True)))


def remote(source, landing, sems, index, target):
    return pltpu.make_async_remote_copy(
        src_ref=source,
        dst_ref=landing,
        send_sem=sems[0].at[index],
        recv_sem=sems[1].at[index],
        device_id=target,
        device_id_type=MESH,
    )


class ColumnGather:
    def __init__(self, full, send, recv, index):
        self.place = here()
        self.full, self.send, self.recv, self.index = full, send, recv, index

    def copy(self, block, down):
        x, s, z = self.place
        return pltpu.make_async_remote_copy(
            src_ref=self.full.at[block],
            dst_ref=self.full.at[block],
            send_sem=self.send.at[self.index, down, block],
            recv_sem=self.recv.at[self.index, block],
            device_id=(x, s, (z + 3) % 4 if down else (z + 1) % 4),
            device_id_type=MESH,
        )

    def at_each(self, body):
        for at in range(4):

            @pl.when(self.place[2] == at)
            def _():
                body(at)

    def start(self):
        def body(at):
            for down in (0, 1):
                if at != 3 * (1 - down):
                    self.copy(at, down).start()

        self.at_each(body)

    def hop(self, number):
        def body(at):
            if at - number >= 0:
                self.copy(at - number, 0).wait_recv()
                if at < 3:
                    self.copy(at - number, 0).start()
            if at + number <= 3:
                self.copy(at + number, 1).wait_recv()
                if at > 0:
                    self.copy(at + number, 1).start()

        self.at_each(body)

    def finish(self):
        self.hop(3)

        def body(at):
            for block in range(4):
                if block <= at < 3:
                    self.copy(block, 0).wait_send()
                if block >= at > 0:
                    self.copy(block, 1).wait_send()

        self.at_each(body)


class RootGather:
    def __init__(self, block, send, recv):
        self.place = here()
        x, s, z = self.place
        self.away = z - (2 * x + s // 2)
        self.block, self.send, self.recv = block, send, recv

    def copy(self, down):
        x, s, z = self.place
        return pltpu.make_async_remote_copy(
            src_ref=self.block,
            dst_ref=self.block,
            send_sem=self.send.at[down],
            recv_sem=self.recv.at[0],
            device_id=(x, s, (z + 3) % 4 if down else (z + 1) % 4),
            device_id_type=MESH,
        )

    def sends(self, down):
        z = self.place[2]
        return (self.away <= 0) & (z > 0) if down else (self.away >= 0) & (z < 3)

    def start(self):
        for down in (0, 1):

            @pl.when((self.away == 0) & self.sends(down))
            def _():
                self.copy(down).start()

    def hop(self, number):
        for down in (0, 1):

            @pl.when(self.away == (-number if down else number))
            def _():
                self.copy(down).wait_recv()

                @pl.when(self.sends(down))
                def _():
                    self.copy(down).start()

    def finish(self):
        self.hop(3)
        for down in (0, 1):

            @pl.when(self.sends(down))
            def _():
                self.copy(down).wait_send()


def setup_kernel(unit, *refs):
    r = named(fields(SetupIn, SetupOut, SetupScratch), refs)
    place = here()
    x, s, z = place
    size = r.rows.shape[1]
    partner = peer(place, 1, False)
    flips = [(dx, ds) for dx in (0, 1) for ds in range(4) if dx or ds]
    plane = [((x + dx) % 2, (s + ds) % 4, z) for dx, ds in flips]
    column = [(x, s, (z + dz) % 4) for dz in (1, 2, 3)]
    barrier = pltpu.get_barrier_semaphore()
    for other in plane + column:
        pl.semaphore_signal(barrier, inc=1, device_id=other, device_id_type=MESH)
    pl.semaphore_wait(barrier, len(plane) + len(column))

    zsems, psems, xsems = (r.zsend, r.zrecv), (r.psend, r.precv), (r.xsend, r.xrecv)
    for dz in (1, 2, 3):
        remote(r.gain_rows, r.gain_all.at[0, z], zsems, dz - 1, column[dz - 1]).start()
    r.gain_all[0, z] = r.gain_rows[...]
    for index in range(7):
        remote(r.small, r.small_all.at[x, s], psems, index, plane[index]).start()
    r.small_all[x, s] = r.small[...]

    mine, other = x * 4 + s, (1 - x) * 4 + s

    def mix_part(which):
        heads = [pl.ds(pl.multiple_of(kind * D + which * HD, HD), HD) for kind in range(4)]
        return jnp.concatenate([r.w_mix[0, :, cols] for cols in heads], 1)

    out_rows = pl.ds(pl.multiple_of(s % 2 * HD, HD), HD)
    root = z == 2 * x + s // 2
    rooted = z == 2 * (1 - x) + s // 2
    mixes = (r.mix.at[z], r.mix_next)
    outs = (r.out, r.out_next)
    gus = (r.gu, r.gu_next)
    downs = (r.down, r.down_next)
    for layer in (0, 1):

        @pl.when(x == layer)
        def _():
            r.mix_away[...] = mix_part(other)
            remote(r.mix_away, mixes[layer], xsems, 0, partner).start()
            mixes[layer][...] = mix_part(mine)

            @pl.when(rooted)
            def _():
                remote(r.w_out.at[0, out_rows], outs[layer], xsems, 1, partner).start()

            @pl.when(root)
            def _():
                outs[layer][...] = r.w_out[0, out_rows, :]

    for dz in (1, 2, 3):
        remote(r.gain_rows, r.gain_all.at[0, z], zsems, dz - 1, column[dz - 1]).wait_recv()
    remote(r.gain_all.at[0], r.gain_all.at[1], xsems, 4, partner).start()

    padded = r.down_away.shape[0]
    width = 8 * unit + 64

    def select(which, offset):
        begin = lax.broadcasted_iota(jnp.int32, (width, 128), 0) - offset
        col = lax.broadcasted_iota(jnp.int32, (width, 128), 1)
        return jnp.where((begin == which * unit + col) & (col < unit), 1.0, 0.0).astype(BF)

    def gu_part(which, out):
        for owner in range(4):
            base = owner * 8 * unit
            offset = base % 128
            chosen = select(which, offset)
            for side in range(2):
                begin = side * FF + base - offset
                part = nn(r.w_gu[0, :, begin : begin + width], chosen).astype(BF)
                at = side * 4 * padded + owner * padded
                out[:, at : at + padded] = part[:, :padded]

    def down_part(which, out):
        row = lax.broadcasted_iota(jnp.int32, (padded, 8 * unit), 0)
        col = lax.broadcasted_iota(jnp.int32, (padded, 8 * unit), 1)
        chosen = jnp.where((col == which * unit + row) & (row < unit), 1.0, 0.0).astype(BF)
        out[...] = nn(chosen, r.w_down[0]).astype(BF)

    gu_part(other, r.gu_away)
    down_part(other, r.down_away)
    for layer in (0, 1):

        @pl.when(x == layer)
        def _():
            remote(r.gu_away, gus[layer], xsems, 2, partner).start()
            remote(r.down_away, downs[layer], xsems, 3, partner).start()

    remote(r.gain_all.at[0], r.gain_all.at[1], xsems, 4, partner).wait_recv()
    for place_of, layer in ((0, x), (1, 1 - x)):
        for owner in range(4):
            for kind in range(2):
                for half in range(2):
                    begin = owner * 2 * HD + half * HD
                    row = 2 * kind + half
                    r.gains[layer, kind : kind + 1, begin : begin + HD] = r.gain_all[
                        place_of, owner, row : row + 1, :
                    ]
    gathers = [Gather(r.normed, batch, r.gsend, r.grecv) for batch in range(2)]
    for batch, gather in enumerate(gathers):
        rows = r.inputs[batch, 0, pl.ds(pl.multiple_of(x * size, size), size), :]
        r.rows[batch] = rows
        rows = rows.astype(F32)
        gather.start((rows * rms_scale(rows) * r.gains[0, 0:1, :]).astype(BF))

    remote(r.mix_away, r.mix_next, xsems, 0, partner).wait_recv()

    @pl.when(root)
    def _():
        remote(r.out, r.out_next, xsems, 1, partner).wait_recv()

    columns = [ColumnGather(r.mix, r.csend, r.crecv, 0), RootGather(r.out, r.rsend, r.rrecv)]
    for part in columns:
        part.start()
    for layer in (0, 1):

        @pl.when(x == layer)
        def _():
            gu_part(mine, gus[layer])
            down_part(mine, downs[layer])

    for part in columns:
        part.hop(1)
    for gather in gathers:
        gather.forward()
    for part in columns:
        part.hop(2)
    for index in range(7):
        dx, ds = flips[index]
        landing = r.small_all.at[(x + dx) % 2, (s + 4 - ds) % 4]
        remote(r.small, landing, psems, index, plane[index]).wait_recv()
    holder = 2 * x + s // 2
    for layer in range(2):
        begin = pl.multiple_of(s % 2 * 32, 32)
        rows = r.small_all[layer, holder, pl.ds(begin, 32), :]
        r.persist[layer] = rows.astype(BF).reshape(2, 16, HD)
        begin = pl.multiple_of(64 + s % 2 * 8, 8)
        r.rates[layer] = r.small_all[layer, holder, pl.ds(begin, 8), :]
    for gather in gathers:
        gather.finish()
    for part in columns:
        part.finish()
    remote(r.gu_away, r.gu_next, xsems, 2, partner).wait()
    remote(r.down_away, r.down_next, xsems, 3, partner).wait()
    remote(r.mix_away, r.mix_next, xsems, 0, partner).wait_send()
    remote(r.gain_all.at[0], r.gain_all.at[1], xsems, 4, partner).wait_send()

    @pl.when(rooted)
    def _():
        remote(r.out, r.out_next, xsems, 1, partner).wait_send()

    for dz in (1, 2, 3):
        remote(r.gain_rows, r.gain_all.at[0, z], zsems, dz - 1, column[dz - 1]).wait_send()
    for index in range(7):
        remote(r.small, r.small_all.at[x, s], psems, index, plane[index]).wait_send()


def forward_layer(layer, ins, outs, *refs):
    scratch = fields(PlaneScratch, ForwardScratch)
    last = len(ins) == len(ForwardIn._fields)
    if not last:
        scratch += NextScratch._fields
    r = named(ins + outs + scratch, refs)
    length = r.part.shape[1]
    z = lax.axis_index("shard")
    own = [
        ColumnGather(r.gu, r.csend, r.crecv, 0),
        ColumnGather(r.down, r.csend, r.crecv, 1),
    ]
    following = []
    if not last:
        following = [
            ColumnGather(r.mix_next, r.csend, r.crecv, 2),
            RootGather(r.out_next, r.rsend, r.rrecv),
        ]

    def each(parts, act):
        for part in parts:
            act(part)

    def project(batch):
        def block(rows, begin):
            proj = nn(r.normed[batch, rows, :], flat(r.mix))
            r.qkv[batch, rows, :] = proj[:, : 3 * HD].astype(BF)
            r.gate[batch, rows, :] = jax.nn.sigmoid(proj[:, 3 * HD :])

        in_blocks(length, 256, block)

    def mixer(batch):
        def block(rows, begin):
            values = r.qkv[batch, :, 2 * HD :]
            inner, decay_w, _, probs, per_probs = weights_of_scores(
                r.qkv[batch, rows, :HD],
                r.qkv[batch, :, HD : 2 * HD],
                r.persist[layer, 0],
                r.seg_rows[batch, rows, :],
                r.seg_cols[batch],
                begin,
                r.rates[layer, 0:1, 0:1],
            )
            attended = nn(probs.astype(BF), values) + nn(per_probs.astype(BF), r.persist[layer, 1])
            recalled = nn((inner * decay_w).astype(BF), values).astype(BF)
            r.recalled[batch, rows, :] = recalled
            combined = attended.astype(BF).astype(F32)
            combined = combined + r.gate[batch, rows, :] * recalled.astype(F32)
            combined = combined.astype(BF)
            r.combined[batch, rows, :] = combined
            r.part[batch, rows, :] = nn(combined, r.out[...]).astype(BF)

        in_blocks(length, 128, block)

    def feed(batch):
        def block(rows, begin):
            gate_up = nn(r.normed_two[batch, rows, :], flat(r.gu))
            r.gate_up[batch, rows, :] = gate_up
            half = gate_up.shape[1] // 2
            hidden = (jax.nn.silu(gate_up[:, :half]) * gate_up[:, half:]).astype(BF)
            r.hidden[batch, rows, :] = hidden
            r.part[batch, rows, :] = nn(hidden, flat(r.down)).astype(BF)

        in_blocks(length, 256, block)

    def scatter(batch):
        return Scatter(r.part, batch, r.pair, r.away, r.near, r.ssend, r.srecv)

    def send_normed(batch, own, gain, full):
        gather = Gather(full, batch, r.gsend, r.grecv)
        gather.start((own * rms_scale(own) * gain).astype(BF))
        return gather

    meet(True)
    r.gu[z] = r.gu_block[...]
    r.down[z] = r.down_block[...]
    each(own, lambda part: part.start())
    if not last:
        r.mix_next[z] = r.mix_block[...]

        @pl.when(following[1].away == 0)
        def _():
            r.out_next[...] = r.out_block[...]

    first, second = (scatter(batch) for batch in range(2))
    project(0)
    mixer(0)
    first.start()
    first.forward()
    project(1)
    mixer(1)
    second.start()
    second.forward()
    each(own, lambda part: part.hop(1))
    gathers = []
    for batch, part in enumerate((first, second)):
        mid = r.rows[batch].astype(F32) + part.finish()
        r.mid[batch] = mid
        gathers.append(send_normed(batch, mid, r.gains[layer, 1:2, :], r.normed_two))
    each(own, lambda part: part.hop(2))
    first, second = (scatter(batch) for batch in range(2))
    for batch, part in enumerate((first, second)):
        gathers[batch].forward()
        gathers[batch].finish()
        if batch == 0:
            each(own, lambda part: part.finish())
            each(following, lambda part: part.start())
        feed(batch)
        part.start()
        part.forward()
    each(following, lambda part: part.hop(1))
    gathers = []
    for batch, part in enumerate((first, second)):
        rows = (r.mid[batch] + part.finish()).astype(BF)
        r.out_rows[batch] = rows
        if not last:
            gain = r.gains[layer + 1, 0:1, :]
            gathers.append(send_normed(batch, rows.astype(F32), gain, r.normed_next))
    each(following, lambda part: part.hop(2))
    for gather in gathers:
        gather.forward()
    for gather in gathers:
        gather.finish()
    each(following, lambda part: part.finish())


def backward_layer(layer, ins, outs, *refs):
    scratch = fields(PlaneScratch, BackwardScratch)
    earlier = len(outs) == len(fields(BackwardOut, EarlyOut))
    if earlier:
        scratch += fields(EarlyScratch)
    r = named(ins + outs + scratch, refs)
    length = r.part.shape[1]
    last = not hasattr(r, "grad_next")
    sums = [
        ColumnSum(r.own_gu, r.gu_slots, r.gu_sum, r.csend, r.crecv, 0),
        ColumnSum(r.own_down, r.down_slots, r.down_sum, r.csend, r.crecv, 1),
    ]
    early = []
    if earlier:
        early = [
            ColumnSum(r.early_mix, r.mix_slots, r.mix_sum, r.csend, r.crecv, 2),
            RootSum(r.early_out, r.root_slots, r.out_sum, r.rsend, r.rrecv),
        ]

    def feed_back(batch):
        def block(rows, begin):
            grad_hidden = nt(r.grad_full[batch, rows, :], flat(r.down))
            half = grad_hidden.shape[1]
            gate_part = r.gate_up[batch, rows, :half]
            up_part = r.gate_up[batch, rows, half:]
            sig_part = jax.nn.sigmoid(gate_part)
            silu = gate_part * sig_part
            grad_gate = grad_hidden * up_part * (sig_part + silu * (1.0 - sig_part))
            r.grad_gu[batch, rows, :half] = grad_gate.astype(BF)
            r.grad_gu[batch, rows, half:] = (grad_hidden * silu).astype(BF)
            r.part[batch, rows, :] = nt(r.grad_gu[batch, rows, :], flat(r.gu)).astype(BF)

        in_blocks(length, 256, block)

    def feed_weights():
        def down(cols, begin):
            grad = tn(r.hidden[0], r.grad_full[0, :, cols])
            grad = grad + tn(r.hidden[1], r.grad_full[1, :, cols])
            grad = grad.reshape(4, grad.shape[0] // 4, grad.shape[1])
            r.own_down[:, :, cols] = grad.astype(BF)

        in_blocks(D, 256, down)
        product(r.own_gu, r.normed_two, r.grad_gu)

    def product(out, left, right):
        for owner in range(4):
            cols = slice(owner * (D // 4), (owner + 1) * (D // 4))
            grad = tn(left[0, :, cols], right[0]) + tn(left[1, :, cols], right[1])
            out[owner] = grad.astype(BF)

    def mixer_back(batch):
        scale = 1.0 / math.sqrt(HD)
        r.grad_keys[...] = jnp.zeros_like(r.grad_keys)
        r.grad_values[...] = jnp.zeros_like(r.grad_values)

        def block(rows, begin):
            grad_combined = nt(r.branch[batch, rows, :], r.out[...])
            gate = r.gate[batch, rows, :]
            recalled = r.recalled[batch, rows, :].astype(F32)
            attn_rows = grad_combined.astype(BF)
            memory_rows = (grad_combined * gate).astype(BF)
            grad_pre = grad_combined * recalled * gate * (1.0 - gate)
            r.grad_proj[batch, rows, 3 * HD :] = grad_pre.astype(BF)
            query = r.qkv[batch, rows, :HD]
            keys = r.qkv[batch, :, HD : 2 * HD]
            values = r.qkv[batch, :, 2 * HD :]
            inner, decay_w, distance, probs, per_probs = weights_of_scores(
                query,
                keys,
                r.persist[layer, 0],
                r.seg_rows[batch, rows, :],
                r.seg_cols[batch],
                begin,
                r.rates[layer, 0:1, 0:1],
            )
            per_dp = nt(attn_rows, r.persist[layer, 1])
            seq_dp = nt(attn_rows, values)
            delta = jnp.sum(per_probs * per_dp, axis=1, keepdims=True) + jnp.sum(
                probs * seq_dp, axis=1, keepdims=True
            )
            per_ds = (per_probs * (per_dp - delta)).astype(BF)
            seq_ds = (probs * (seq_dp - delta)).astype(BF)
            weighted = nt(memory_rows, values) * decay_w
            grad_inner = weighted.astype(BF)
            memory = inner * decay_w
            rate_terms = weighted * inner * distance
            r.grad_rate[...] -= jnp.sum(rate_terms, axis=0, keepdims=True)
            grad_query = (nn(per_ds, r.persist[layer, 0]) + nn(seq_ds, keys)) * scale
            grad_query = grad_query + nn(grad_inner, keys)
            r.grad_proj[batch, rows, :HD] = grad_query.astype(BF)
            r.grad_keys[...] += tn(seq_ds, query) * scale + tn(grad_inner, query)
            r.grad_values[...] += tn(probs.astype(BF), attn_rows) + tn(
                memory.astype(BF), memory_rows
            )
            r.grad_persist[0] += tn(per_ds, query) * scale
            r.grad_persist[1] += tn(per_probs.astype(BF), attn_rows)

        in_blocks(length, 128, block)
        r.grad_proj[batch, :, HD : 2 * HD] = r.grad_keys[...].astype(BF)
        r.grad_proj[batch, :, 2 * HD : 3 * HD] = r.grad_values[...].astype(BF)

        def back(rows, begin):
            r.part[batch, rows, :] = nt(r.grad_proj[batch, rows, :], flat(r.mix)).astype(BF)

        in_blocks(length, 256, back)

    def scatter(batch):
        return Scatter(r.part, batch, r.pair, r.away, r.near, r.ssend, r.srecv)

    def through_norm(batch, part, rows, gain):
        grad_normed = part.finish()
        inverse = rms_scale(rows)
        return norm_back(grad_normed, rows * inverse, inverse, gain)

    meet(True)
    r.grad_rate[...] = jnp.zeros_like(r.grad_rate)
    r.grad_persist[...] = jnp.zeros_like(r.grad_persist)
    for column in early:
        column.start()
    first, second = (scatter(batch) for batch in range(2))
    for batch, part in enumerate((first, second)):
        feed_back(batch)
        part.start()
        part.forward()
    feed_weights()
    gathers = []
    gain_sums = []
    for batch, part in enumerate((first, second)):
        grad_mid, gain_sum = through_norm(batch, part, r.mid[batch], r.gains[layer, 1:2, :])
        gain_sums.append(gain_sum[None])
        grad_mid = grad_mid + r.grad_rows[batch].astype(F32)
        r.grad_mid[batch] = grad_mid
        gather = Gather(r.branch, batch, r.gsend, r.grecv)
        gather.start(grad_mid.astype(BF))
        gathers.append(gather)
    r.gain_sums[1:2] = gain_sums[0] + gain_sums[1]
    for column in early:
        column.hop(1)
    for column in early:
        column.hop(2)
    for column in sums:
        column.start()
    first, second = (scatter(batch) for batch in range(2))
    for batch, part in enumerate((first, second)):
        gathers[batch].forward()
        gathers[batch].finish()
        mixer_back(batch)
        part.start()
        part.forward()
        if batch == 0:
            for column in early:
                column.finish()
            for column in sums:
                column.hop(1)
    product(r.grad_mix, r.normed, r.grad_proj)
    grad_out = tn(r.combined[0], r.branch[0]) + tn(r.combined[1], r.branch[1])
    r.grad_out[...] = grad_out.astype(BF)
    gathers = []
    gain_sums = []
    for batch, part in enumerate((first, second)):
        grad_h, gain_sum = through_norm(
            batch, part, r.rows[batch].astype(F32), r.gains[layer, 0:1, :]
        )
        gain_sums.append(gain_sum[None])
        grad_h = (grad_h + r.grad_mid[batch]).astype(BF)
        r.grad_h[batch] = grad_h
        if not last:
            gather = Gather(r.grad_next, batch, r.gsend, r.grecv)
            gather.start(grad_h)
            gathers.append(gather)
    r.gain_sums[0:1] = gain_sums[0] + gain_sums[1]
    for column in sums:
        column.hop(2)
    for gather in gathers:
        gather.forward()
    for gather in gathers:
        gather.finish()
    for column in sums:
        column.finish()


def final_kernel(*refs):
    place = here()
    x, s, z = place
    sibling, beside, partner = (peer(place, 0, True), peer(place, 2, False), peer(place, 1, False))
    across = peer(place, 3, False)
    by_layer = [list(refs[0:6]), list(refs[6:12])]
    small_ref = refs[12]
    bufs = refs[13:16]
    out_buf, rows_buf, grads_buf, plane_buf = refs[16:20]
    column_buf, mix_sum, out_sum, mix_slots, root_slots, *sems = refs[20:]
    psend, precv, osend, orecv, rsend, rrecv, zsend, zrecv, ssend, srecv, *sems = sems
    csend, crecv, hsend, hrecv = sems
    columns = [
        ColumnSum(by_layer[0][0], mix_slots, mix_sum, csend, crecv, 0),
        RootSum(by_layer[0][3], root_slots, out_sum, hsend, hrecv),
    ]
    by_layer[0][0], by_layer[0][3] = mix_sum, out_sum

    def copy(source, landing, sems, index, target):
        return pltpu.make_async_remote_copy(
            src_ref=source,
            dst_ref=landing,
            send_sem=sems[0].at[index],
            recv_sem=sems[1].at[index],
            device_id=target,
            device_id_type=MESH,
        )

    flips = [(dx, ds) for dx in (0, 1) for ds in range(4) if dx or ds]
    plane = [((x + dx) % 2, (s + ds) % 4, z) for dx, ds in flips]
    column = [(x, s, (z + dz) % 4) for dz in (1, 2, 3)]
    barrier = pltpu.get_barrier_semaphore()
    for other in plane + column:
        pl.semaphore_signal(barrier, inc=1, device_id=other, device_id_type=MESH)
    pl.semaphore_wait(barrier, len(plane) + len(column))

    def to_plane_of(dz):
        target = (z + dz) % 4
        return copy(
            small_ref.at[target], column_buf.at[dz - 1], (zsend, zrecv), dz - 1, (x, s, target)
        )

    def to_plane(index):
        slot = plane_buf.at[x * 4 + s]
        return copy(slot, slot, (ssend, srecv), index, plane[index])

    for dz in (1, 2, 3):
        to_plane_of(dz).start()

    psems = [(psend.at[i], precv.at[i]) for i in range(3)]

    def piece(index, kind, slot, target, source=None):
        landing = bufs[index].at[slot]
        return copy(landing if source is None else source, landing, psems[index], kind, target)

    mine = (x, s)
    turned = (1 - x, s)

    def send(indices):
        for layer in (0, 1):
            own, theirs = by_layer[layer], by_layer[1 - layer]

            @pl.when(x == layer)
            def _():
                for index in indices:
                    piece(index, 2, mine, partner, theirs[index]).start()
                    piece(index, 0, mine, beside, own[index]).start()
                    piece(index, 1, mine, sibling, own[index]).start()
                for index in indices:
                    bufs[index][mine] = own[index][...]

    def turn(indices):
        for index in indices:
            piece(index, 2, turned, partner).wait_recv()
            piece(index, 3, turned, beside).start()
            piece(index, 4, turned, sibling).start()

    for column in columns:
        column.start()
    send((1, 2))
    for layer in (0, 1):

        @pl.when(x == layer)
        def _():
            copy(by_layer[1 - layer][4], rows_buf, (rsend, rrecv), 0, partner).start()
            copy(by_layer[1 - layer][5], grads_buf, (rsend, rrecv), 1, partner).start()

    total = small_ref[z]
    for dz in (1, 2, 3):
        to_plane_of(dz).wait_recv()
        total = total + column_buf[dz - 1]
    plane_buf[x * 4 + s] = total
    for index in range(7):
        to_plane(index).start()
    for column in columns:
        column.hop(1)
    for column in columns:
        column.hop(2)
    turn((1, 2))
    for column in columns:
        column.finish()
    send((0,))

    core = s % 2
    root = z == 2 * x + s // 2
    of_root = (z // 2, 2 * (z % 2) + core)
    apart = 2 * ((x + of_root[0]) % 2) + (s // 2 + of_root[1] // 2) % 2

    def out_copy(index, target, source=None):
        landing = out_buf.at[core]
        return copy(landing if source is None else source, landing, (osend, orecv), index, target)

    for layer in (0, 1):

        @pl.when(root & (x == layer))
        def _():
            out_copy(1, beside, by_layer[layer][3]).start()
            out_copy(2, partner, by_layer[1 - layer][3]).start()
            out_copy(3, across, by_layer[1 - layer][3]).start()
            out_buf[core] = by_layer[layer][3][...]

    for apart_by in (1, 2, 3):

        @pl.when(apart == apart_by)
        def _():
            out_copy(apart_by, beside).wait_recv()

    out_copy(0, sibling).start()

    turn((0,))
    far = (x, (s + 2) % 4)
    far_turned = (1 - x, (s + 2) % 4)
    for index in (1, 2, 0):
        piece(index, 0, far, beside).wait_recv()
        piece(index, 5, far, sibling).start()
    for index in (1, 2, 0):
        piece(index, 3, far_turned, beside).wait_recv()
        piece(index, 6, far_turned, sibling).start()
    twin = sibling[1]
    far_twin = (twin + 2) % 4
    for index in range(3):
        piece(index, 1, (x, twin), sibling).wait_recv()
        piece(index, 4, (1 - x, twin), sibling).wait_recv()
        piece(index, 5, (x, far_twin), sibling).wait_recv()
        piece(index, 6, (1 - x, far_twin), sibling).wait_recv()
    other_out = out_buf.at[1 - core]
    copy(other_out, other_out, (osend, orecv), 0, sibling).wait_recv()
    for index in range(7):
        dx, ds = flips[index]
        slot = plane_buf.at[((x + dx) % 2) * 4 + (s + 4 - ds) % 4]
        copy(slot, slot, (ssend, srecv), index, plane[index]).wait_recv()
    for index in (0, 1):
        copy(rows_buf, rows_buf, (rsend, rrecv), index, partner).wait()
    for index in range(7):
        to_plane(index).wait_send()
    for dz in (1, 2, 3):
        to_plane_of(dz).wait_send()
    for index in range(3):
        for kind in range(7):
            piece(index, kind, mine, sibling).wait_send()
    out_copy(0, sibling).wait_send()

    @pl.when(root)
    def _():
        for index in (1, 2, 3):
            out_copy(index, sibling).wait_send()


def kernel_call(kernel, number, operands, outs, scratch):
    vmem = pl.BlockSpec(memory_space=pltpu.VMEM)
    return pl.pallas_call(
        kernel,
        out_shape=outs,
        in_specs=[vmem] * len(operands),
        out_specs=[vmem] * len(outs),
        scratch_shapes=scratch,
        compiler_params=pltpu.CompilerParams(
            collective_id=number, has_side_effects=True, vmem_limit_bytes=58 * 2**20
        ),
    )(*operands)


def pairs_of(*sizes):
    return [pltpu.SemaphoreType.DMA(size) for size in sizes for _ in range(2)]


def scatter_scratch(length):
    size = length // 8
    return [
        pltpu.VMEM((2, length, D), BF),
        pltpu.VMEM((2, 4, size, D), BF),
        pltpu.VMEM((2, 3, size, D), BF),
        pltpu.VMEM((2, 3, size, D), BF),
        *pairs_of((2, 7), (2, 7)),
    ]


def setup_call(number, inputs, small, gain_rows, w_mix, w_out, w_gu, w_down):
    count, _, tokens, _ = inputs.shape
    depth, length = w_mix.shape[1], 4 * tokens
    unit = w_down.shape[1] // 8
    padded = -(-unit // 32) * 32
    shape = jax.ShapeDtypeStruct
    outs = dict(
        rows=shape((count, length // 8, D), BF),
        normed=shape((count, length, D), BF),
        gains=shape((2, 2, D), F32),
        persist=shape((2, 2, 16, HD), BF),
        rates=shape((2, 8, HD), F32),
        mix=shape((4, depth, 4 * HD), BF),
        mix_next=shape((depth, 4 * HD), BF),
        out=shape((HD, D), BF),
        out_next=shape((HD, D), BF),
        gu=shape((depth, 8 * padded), BF),
        gu_next=shape((depth, 8 * padded), BF),
        down=shape((padded, D), BF),
        down_next=shape((padded, D), BF),
    )
    scratch = [
        pltpu.VMEM((2, 4, 8, HD), F32),
        pltpu.VMEM((2, 4) + small.shape, F32),
        pltpu.VMEM((depth, 4 * HD), BF),
        pltpu.VMEM((depth, 8 * padded), BF),
        pltpu.VMEM((padded, D), BF),
        *pairs_of((3,), (7,), (5,), (2, 7)),
        pltpu.SemaphoreType.DMA((1, 2, 4)),
        pltpu.SemaphoreType.DMA((1, 4)),
        pltpu.SemaphoreType.DMA((2,)),
        pltpu.SemaphoreType.DMA((1,)),
    ]
    operands = (inputs, small, gain_rows, w_mix, w_out, w_gu, w_down)
    kernel = functools.partial(setup_kernel, unit)
    return named(outs, kernel_call(kernel, number, operands, list(outs.values()), scratch))


def forward_call(number, layer, given):
    count, length, _ = given.normed.shape
    depth, half = D // 4, 4 * given.down_block.shape[0]
    last = layer == 1
    shape = jax.ShapeDtypeStruct
    outs = dict(
        qkv=shape((count, length, 3 * HD), BF),
        gate=shape((count, length, HD), F32),
        recalled=shape((count, length, HD), BF),
        combined=shape((count, length, HD), BF),
        mid=shape((count, length // 8, D), F32),
        normed_two=shape((count, length, D), BF),
        gate_up=shape((count, length, 2 * half), F32),
        hidden=shape((count, length, half), BF),
        gu=shape((4, depth, 2 * half), BF),
        down=shape((4, half // 4, D), BF),
        out_rows=shape((count, length // 8, D), BF),
        normed_next=shape((count, length, D), BF),
    )
    scratch = scatter_scratch(length)
    scratch += [pltpu.SemaphoreType.DMA((3, 2, 4)), pltpu.SemaphoreType.DMA((3, 4))]
    ins = ForwardIn._fields
    if last:
        del outs[ForwardOut._fields[-1]]
    else:
        ins += NextIn._fields
        outs |= dict(mix_next=shape((4, depth, 4 * HD), BF), out_next=shape((HD, D), BF))
        scratch += [pltpu.SemaphoreType.DMA((2,)), pltpu.SemaphoreType.DMA((1,))]
    operands = [getattr(given, name) for name in ins]
    kernel = functools.partial(forward_layer, layer, ins, tuple(outs))
    return named(outs, kernel_call(kernel, number, operands, list(outs.values()), scratch))


def backward_call(number, layer, given):
    count, length, _ = given.normed.shape
    half = 4 * given.down.shape[1]
    last = layer == 0
    depth = D // 4
    shape = jax.ShapeDtypeStruct
    outs = dict(
        grad_mix=shape((4, depth, 4 * HD), BF),
        grad_out=shape((HD, D), BF),
        gain_sums=shape((2, D), F32),
        grad_persist=shape(given.persist.shape[1:], F32),
        grad_rate=shape((1, length), F32),
        gu_sum=shape((depth, 2 * half), BF),
        down_sum=shape((half // 4, D), BF),
        grad_h=shape((count, length // 8, D), BF),
    )
    ins = BackwardIn._fields
    if last:
        ins += EarlyIn._fields
        outs |= dict(mix_sum=shape((depth, 4 * HD), BF), out_sum=shape((HD, D), BF))
    else:
        outs |= dict(grad_next=shape((count, length, D), BF))
    scratch = scatter_scratch(length) + [
        pltpu.VMEM((count, length, 2 * half), BF),
        pltpu.VMEM((count, length, 4 * HD), BF),
        pltpu.VMEM((length, HD), F32),
        pltpu.VMEM((length, HD), F32),
        pltpu.VMEM((4, depth, 2 * half), BF),
        pltpu.VMEM((4, half // 4, D), BF),
        pltpu.VMEM((count, length, D), BF),
        pltpu.VMEM((count, length // 8, D), F32),
        pltpu.VMEM((2, 3, depth, 2 * half), BF),
        pltpu.VMEM((2, 3, half // 4, D), BF),
        *pairs_of((3, 2, 3)),
    ]
    if last:
        scratch += [
            pltpu.VMEM((2, 3, depth, 4 * HD), BF),
            pltpu.VMEM((2, HD, D), BF),
            *pairs_of((2,)),
        ]
    kernel = functools.partial(backward_layer, layer, ins, tuple(outs))
    operands = [getattr(given, name) for name in ins]
    return named(outs, kernel_call(kernel, number, operands, list(outs.values()), scratch))


def final_call(number, by_layer, small):
    operands = (*by_layer[0], *by_layer[1], small)
    mix, gu, down, out, *rows = by_layer[1]
    outs = [jax.ShapeDtypeStruct((2, 4) + part.shape, BF) for part in (mix, gu, down)]
    outs.append(jax.ShapeDtypeStruct((2,) + out.shape, BF))
    outs += [jax.ShapeDtypeStruct(part.shape, BF) for part in rows]
    outs.append(jax.ShapeDtypeStruct((8,) + small.shape[1:], F32))
    scratch = [
        pltpu.VMEM((3,) + small.shape[1:], F32),
        pltpu.VMEM(mix.shape, BF),
        pltpu.VMEM(out.shape, BF),
        pltpu.VMEM((2, 3) + mix.shape, BF),
        pltpu.VMEM((2,) + out.shape, BF),
        *pairs_of((3, 7), (4,), (2,), (3,), (7,), (1, 2, 3), (2,)),
    ]
    return kernel_call(final_kernel, number, operands, outs, scratch)


def assemble_kernel(unit, mix_buf, gu_buf, down_buf, mix_ref, gu_ref, down_ref):
    padded = down_buf.shape[2]
    half = gu_buf.shape[3] // 2
    for which in range(8):
        slot = (which // 4, which % 4)
        mix = mix_buf[slot].astype(F32)
        for kind in range(4):
            begin = kind * D + which * HD
            mix_ref[0, :, begin : begin + HD] = mix[:, kind * HD : (kind + 1) * HD]
        part = gu_buf[slot].astype(F32)
        for side in range(2):
            for owner in range(half // padded):
                begin = side * FF + (owner * 8 + which) * unit
                source = side * half + owner * padded
                gu_ref[0, :, begin : begin + unit] = part[:, source : source + unit]
    for pair in range(2):
        down = down_buf[0, pair].astype(F32)
        down_ref[0, pair * unit : (pair + 1) * unit, :] = down[:unit]


def assemble_call(unit, mix_buf, gu_buf, down_buf):
    depth, padded = mix_buf.shape[2], down_buf.shape[2]
    rows = depth // 4
    return pl.pallas_call(
        functools.partial(assemble_kernel, unit),
        grid=(4,),
        out_shape=[
            jax.ShapeDtypeStruct((1, depth, 4 * D), F32),
            jax.ShapeDtypeStruct((1, depth, 2 * FF), F32),
            jax.ShapeDtypeStruct((1, 8 * unit, D), F32),
        ],
        in_specs=[
            pl.BlockSpec((2, 4, rows, 4 * HD), lambda i: (0, 0, i, 0)),
            pl.BlockSpec((2, 4, rows, gu_buf.shape[3]), lambda i: (0, 0, i, 0)),
            pl.BlockSpec((1, 2, padded, D), lambda i: (i // 2, i % 2, 0, 0)),
        ],
        out_specs=[
            pl.BlockSpec((1, rows, 4 * D), lambda i: (0, i, 0)),
            pl.BlockSpec((1, rows, 2 * FF), lambda i: (0, i, 0)),
            pl.BlockSpec((1, 2 * unit, D), lambda i: (0, i, 0)),
        ],
        compiler_params=pltpu.CompilerParams(vmem_limit_bytes=40 * 2**20),
    )(mix_buf, gu_buf, down_buf)


def tensor_parallel(
    inputs, segment_ids, cotangent, w_mix, w_out, w_gu, w_down, norm_gains, persist_kv, memory_decay
):
    x, s, z = here()
    nx, ns, nz = (lax.axis_size(a) for a in ("section", "seq", "shard"))
    width = nx * ns
    mine = x * ns + s
    other = (1 - x) * ns + s
    first = x == 0
    count, _, tokens, _ = inputs.shape
    length = tokens * ns
    size = length // width
    depth = w_mix.shape[1]
    unit = w_down.shape[1] // (nx * ns)

    def layers(own, got):
        return (jnp.where(first, own, got), jnp.where(first, got, own))

    small = persist_kv[0].reshape(-1, 2, HD).transpose(1, 0, 2).reshape(-1, HD).astype(F32)
    rates = jnp.broadcast_to(memory_decay[0][:, None, None], (2, 8, HD)).reshape(-1, HD)
    gain_rows = norm_gains[0].astype(F32).T.reshape(-1, HD)
    gain_rows = jnp.pad(gain_rows, ((0, 8 - gain_rows.shape[0]), (0, 0)))
    ready = setup_call(
        0, inputs, jnp.concatenate([small, rates], 0), gain_rows, w_mix, w_out, w_gu, w_down
    )
    shared = dict(
        gains=ready.gains,
        persist=ready.persist,
        rates=ready.rates,
        seg_rows=segment_ids[:, 0, :, None],
        seg_cols=segment_ids,
    )
    lower = dict(
        shared,
        normed=ready.normed,
        rows=ready.rows,
        mix=ready.mix,
        out=ready.out,
        gu_block=ready.gu,
        down_block=ready.down,
        mix_block=ready.mix_next,
        out_block=ready.out_next,
    )
    below = forward_call(1, 0, types.SimpleNamespace(**lower))
    upper = dict(
        shared,
        normed=below.normed_next,
        rows=below.out_rows,
        mix=below.mix_next,
        out=below.out_next,
        gu_block=ready.gu_next,
        down_block=ready.down_next,
    )
    above = forward_call(2, 1, types.SimpleNamespace(**upper))
    outputs = [below.out_rows, above.out_rows]
    cot_full = lax.all_gather(cotangent[:, 0], "seq", axis=1, tiled=True)
    cot_rows = lax.dynamic_slice_in_dim(cotangent[:, 0], x * size, size, 1)
    upper |= dict(vars(above), grad_full=cot_full, grad_rows=cot_rows)
    later = backward_call(3, 1, types.SimpleNamespace(**upper))
    lower |= dict(
        vars(below),
        grad_full=later.grad_next,
        grad_rows=later.grad_h,
        early_mix=later.grad_mix,
        early_out=later.grad_out,
    )
    earlier = backward_call(4, 0, types.SimpleNamespace(**lower))
    by_layer = [
        (earlier.grad_mix, earlier.gu_sum, earlier.down_sum, earlier.grad_out),
        (earlier.mix_sum, later.gu_sum, later.down_sum, earlier.out_sum),
    ]
    both = (earlier, later)
    grads = [found.grad_h for found in both]
    gain_sums = [found.gain_sums for found in both]

    memory_all = jnp.stack([found.grad_persist for found in both], 0).reshape(-1, HD)
    rate_all = jnp.stack([jnp.sum(found.grad_rate) for found in both])
    rate_all = jnp.pad(rate_all[None], ((0, 7), (0, HD - 2)))
    gain_all = jnp.stack(gain_sums, 0).reshape(4, nz, 2, HD).transpose(1, 0, 2, 3)
    memory_all = jnp.concatenate([memory_all, rate_all], 0)
    small = jnp.concatenate(
        [jnp.broadcast_to(memory_all[None], (nz,) + memory_all.shape), gain_all.reshape(nz, 8, HD)],
        1,
    )
    by_layer = [(*by_layer[layer], outputs[layer], grads[layer]) for layer in range(2)]
    mix_all, gu_all, down_all, out_all, rows_got, grads_got, plane_all = final_call(
        5, by_layer, small
    )

    def whole_rows(of_layer, got):
        both = layers(jnp.where(first, of_layer[0], of_layer[1]), got)
        return jnp.concatenate(both, 1)[None, :, None]

    section_out = whole_rows(outputs, rows_got)
    section_grad = whole_rows(grads, grads_got).astype(F32)
    grad_mix, grad_gu, grad_down = assemble_call(unit, mix_all, gu_all, down_all)
    grad_out = out_all.astype(F32).reshape(1, 2 * HD, D)

    heads_of = lax.dynamic_slice_in_dim(plane_all, 2 * s, 2, 0)
    of_section = lax.dynamic_index_in_dim(
        heads_of[:, :64].reshape(2, 2, 2, -1, HD), x, 1, keepdims=False
    )
    grad_persist = of_section.transpose(1, 2, 0, 3).reshape(1, 2, -1, 2 * HD)
    grad_rate = lax.dynamic_index_in_dim(heads_of[:, 64], x, 1, keepdims=False)[None]
    gain_all = jnp.sum(plane_all[:, 72:], 0).reshape(2, 2, depth)
    grad_gain = lax.dynamic_index_in_dim(gain_all, x, 0).transpose(0, 2, 1)
    return (
        section_out,
        section_grad,
        grad_mix,
        grad_out,
        grad_gu,
        grad_down,
        grad_gain,
        grad_persist,
        grad_rate,
    )


def solution(mesh):
    sizes = mesh.shape
    planar = (sizes["section"], sizes["seq"]) == (2, 4)
    placed = (
        P(None, "shard", "seq", None),
        P(None, "shard", None),
        P(None, "shard", "seq", None),
        P("section", "shard", None),
        P("section", "shard", None),
        P("section", "shard", None),
        P("section", "shard", None),
        P("section", "shard", None),
        P("section", None, None, "seq"),
        P("section", "seq"),
    )
    return jax.shard_map(
        tensor_parallel if planar else on_device,
        mesh=mesh,
        in_specs=placed,
        out_specs=(
            P("section", None, "shard", "seq", None),
            P("section", None, "shard", "seq", None),
            P("section", "shard", None),
            P("section", "shard", None),
            P("section", "shard", None),
            P("section", "shard", None),
            P("section", "shard", None),
            P("section", None, None, "seq"),
            P("section", "seq"),
        ),
        check_vma=False,
    )
```

```python
import functools
import math
import types
from typing import Any, NamedTuple

import jax
import jax.numpy as jnp
from jax import lax
from jax.experimental import pallas as pl
from jax.experimental.pallas import tpu as pltpu
from jax.sharding import PartitionSpec as P

D = 1024
H = 8
HD = 128
FF = 2816


def shifted(value, axis, by):
    size = lax.axis_size(axis)
    pairs = [(i, i + by) for i in range(size) if 0 <= i + by < size]
    return lax.ppermute(value, axis, pairs)


def as_sent(value):
    return jax.tree.map(lambda a: a.astype(jnp.bfloat16) if a.dtype == jnp.float32 else a, value)


def rms_scale(values):
    return lax.rsqrt(jnp.mean(values * values, axis=-1, keepdims=True) + 1e-06)


def norm_back(grad_normed, scaled, inverse, gain):
    grad_scaled = grad_normed * gain
    grad_rows = inverse * (
        grad_scaled - scaled * jnp.mean(grad_scaled * scaled, axis=-1, keepdims=True)
    )
    return (grad_rows, jnp.sum(grad_normed * scaled, axis=0))


def block_terms(query_rows, key_rows, seg_ids, begin, reach, rate):
    inner = jnp.dot(query_rows, key_rows.T, preferred_element_type=jnp.float32)
    row_places = begin + jnp.arange(reach - begin, dtype=jnp.int32)
    col_places = jnp.arange(reach, dtype=jnp.int32)
    allowed = (seg_ids[begin:reach][:, None] == seg_ids[:reach][None, :]) & (
        col_places[None, :] <= row_places[:, None]
    )
    distance = jnp.maximum(row_places[:, None] - col_places[None, :], 0).astype(jnp.float32)
    decay_w = jnp.where(allowed, jnp.exp(-rate * distance), jnp.float32(0.0))
    return (inner, allowed, decay_w, distance)


def head_forward(query, keys, values, pkeys, pvalues, rate, seg_ids):
    length, width = query.shape
    block = min(512, length)
    scale = 1.0 / math.sqrt(width)
    attn_parts, memory_parts, lse_parts = ([], [], [])
    for begin in range(0, length, block):
        reach = begin + block
        query_rows = query[begin:reach]
        inner, allowed, decay_w, distance = block_terms(
            query_rows, keys[:reach], seg_ids, begin, reach, rate
        )
        per_scores = jnp.dot(query_rows, pkeys.T, preferred_element_type=jnp.float32) * scale
        seq_scores = jnp.where(allowed, inner * scale, -jnp.inf)
        top = jnp.maximum(
            jnp.max(per_scores, axis=1, keepdims=True), jnp.max(seq_scores, axis=1, keepdims=True)
        )
        per_exp = jnp.exp(per_scores - top)
        seq_exp = jnp.exp(seq_scores - top)
        denom = jnp.sum(per_exp, axis=1, keepdims=True) + jnp.sum(seq_exp, axis=1, keepdims=True)
        attended = jnp.dot(
            (per_exp / denom).astype(jnp.bfloat16), pvalues, preferred_element_type=jnp.float32
        )
        attended = attended + jnp.dot(
            (seq_exp / denom).astype(jnp.bfloat16),
            values[:reach],
            preferred_element_type=jnp.float32,
        )
        memory_w = (inner * decay_w * (1.0 / width)).astype(jnp.bfloat16)
        recalled = jnp.dot(memory_w, values[:reach], preferred_element_type=jnp.float32)
        attn_parts.append(attended)
        memory_parts.append(recalled)
        lse_parts.append(top[:, 0] + jnp.log(denom[:, 0]))
    return (
        jnp.concatenate(attn_parts, 0),
        jnp.concatenate(memory_parts, 0),
        jnp.concatenate(lse_parts, 0),
    )


def head_backward(query, keys, values, pkeys, pvalues, rate, seg_ids, lse, grad_attn, grad_memory):
    length, width = query.shape
    block = min(512, length)
    scale = 1.0 / math.sqrt(width)
    query_grads = []
    grad_keys = jnp.zeros((length, width), jnp.float32)
    grad_values = jnp.zeros((length, width), jnp.float32)
    grad_pkeys = jnp.zeros(pkeys.shape, jnp.float32)
    grad_pvalues = jnp.zeros(pvalues.shape, jnp.float32)
    grad_rate = jnp.float32(0.0)
    for begin in range(0, length, block):
        reach = begin + block
        query_rows = query[begin:reach]
        key_rows = keys[:reach]
        value_rows = values[:reach]
        inner, allowed, decay_w, distance = block_terms(
            query_rows, key_rows, seg_ids, begin, reach, rate
        )
        per_scores = jnp.dot(query_rows, pkeys.T, preferred_element_type=jnp.float32) * scale
        seq_scores = jnp.where(allowed, inner * scale, -jnp.inf)
        row_lse = lse[begin:reach][:, None]
        per_prob = jnp.exp(per_scores - row_lse)
        seq_prob = jnp.exp(seq_scores - row_lse)
        attn_rows = grad_attn[begin:reach]
        memory_rows = grad_memory[begin:reach]
        per_dp = jnp.dot(attn_rows, pvalues.T, preferred_element_type=jnp.float32)
        seq_dp = jnp.dot(attn_rows, value_rows.T, preferred_element_type=jnp.float32)
        delta = jnp.sum(per_prob * per_dp, axis=1, keepdims=True) + jnp.sum(
            seq_prob * seq_dp, axis=1, keepdims=True
        )
        per_ds = (per_prob * (per_dp - delta)).astype(jnp.bfloat16)
        seq_ds = (seq_prob * (seq_dp - delta)).astype(jnp.bfloat16)
        rows_grad = (
            jnp.dot(per_ds, pkeys, preferred_element_type=jnp.float32)
            + jnp.dot(seq_ds, key_rows, preferred_element_type=jnp.float32)
        ) * scale
        grad_pkeys = (
            grad_pkeys
            + jnp.einsum("qk,qd->kd", per_ds, query_rows, preferred_element_type=jnp.float32)
            * scale
        )
        grad_pvalues = grad_pvalues + jnp.einsum(
            "qk,qd->kd",
            per_prob.astype(jnp.bfloat16),
            attn_rows,
            preferred_element_type=jnp.float32,
        )
        key_part = (
            jnp.einsum("qk,qd->kd", seq_ds, query_rows, preferred_element_type=jnp.float32) * scale
        )
        value_part = jnp.einsum(
            "qk,qd->kd",
            seq_prob.astype(jnp.bfloat16),
            attn_rows,
            preferred_element_type=jnp.float32,
        )
        memory_w = (inner * decay_w * (1.0 / width)).astype(jnp.bfloat16)
        grad_mw = jnp.dot(memory_rows, value_rows.T, preferred_element_type=jnp.float32)
        value_part = value_part + jnp.einsum(
            "qk,qd->kd", memory_w, memory_rows, preferred_element_type=jnp.float32
        )
        grad_inner = (grad_mw * decay_w * (1.0 / width)).astype(jnp.bfloat16)
        rows_grad = rows_grad + jnp.dot(grad_inner, key_rows, preferred_element_type=jnp.float32)
        key_part = key_part + jnp.einsum(
            "qk,qd->kd", grad_inner, query_rows, preferred_element_type=jnp.float32
        )
        grad_rate = grad_rate - jnp.sum(grad_mw * inner * decay_w * (1.0 / width) * distance)
        grad_keys = grad_keys.at[:reach].add(key_part)
        grad_values = grad_values.at[:reach].add(value_part)
        query_grads.append(rows_grad)
    return (
        jnp.concatenate(query_grads, 0),
        grad_keys,
        grad_values,
        grad_pkeys,
        grad_pvalues,
        grad_rate,
    )


def layer_forward(rows_in, seg_ids, full, pkv, rates):
    mix_w, out_w, gu_w, down_w, gains = full
    tokens = rows_in.shape[0]
    gain_one = gains[:, 0].astype(jnp.float32)
    gain_two = gains[:, 1].astype(jnp.float32)
    inverse_one = rms_scale(rows_in)
    scaled_one = rows_in * inverse_one
    normed = (scaled_one * gain_one).astype(jnp.bfloat16)
    proj = jnp.dot(normed, mix_w, preferred_element_type=jnp.float32)
    qkv = proj[:, : 3 * D].astype(jnp.bfloat16).reshape(tokens, 3, H, HD)
    gate = jax.nn.sigmoid(proj[:, 3 * D :])
    grouped = lax.all_to_all(qkv, "seq", split_axis=2, concat_axis=0, tiled=True)
    attn_heads, memory_heads, lse_heads = ([], [], [])
    for head in range(grouped.shape[2]):
        cols = slice(head * HD, (head + 1) * HD)
        attended, recalled, lse = head_forward(
            grouped[:, 0, head],
            grouped[:, 1, head],
            grouped[:, 2, head],
            pkv[0][:, cols],
            pkv[1][:, cols],
            rates[head],
            seg_ids,
        )
        attn_heads.append(attended)
        memory_heads.append(recalled)
        lse_heads.append(lse)
    mixed = jnp.stack([jnp.stack(attn_heads, 1), jnp.stack(memory_heads, 1)], 1).astype(
        jnp.bfloat16
    )
    returned = lax.all_to_all(mixed, "seq", split_axis=0, concat_axis=2, tiled=True)
    attended = returned[:, 0].reshape(tokens, D).astype(jnp.float32)
    recalled = returned[:, 1].reshape(tokens, D).astype(jnp.float32)
    combined = (attended + gate * recalled).astype(jnp.bfloat16)
    mid = rows_in + jnp.dot(combined, out_w, preferred_element_type=jnp.float32)
    inverse_two = rms_scale(mid)
    scaled_two = mid * inverse_two
    normed_two = (scaled_two * gain_two).astype(jnp.bfloat16)
    gate_up = jnp.dot(normed_two, gu_w, preferred_element_type=jnp.float32)
    hidden = (jax.nn.silu(gate_up[:, :FF]) * gate_up[:, FF:]).astype(jnp.bfloat16)
    result = mid + jnp.dot(hidden, down_w, preferred_element_type=jnp.float32)
    kept = (
        seg_ids,
        inverse_one,
        scaled_one,
        normed,
        grouped,
        jnp.stack(lse_heads, 1),
        gate,
        recalled,
        combined,
        inverse_two,
        scaled_two,
        normed_two,
        gate_up,
        hidden,
    )
    return (result, kept)


def layer_backward(grad_out, kept, full, pkv, rates):
    (
        seg_ids,
        inverse_one,
        scaled_one,
        normed,
        grouped,
        lse_all,
        gate,
        recalled,
        combined,
        inverse_two,
        scaled_two,
        normed_two,
        gate_up,
        hidden,
    ) = kept
    mix_w, out_w, gu_w, down_w, gains = full
    tokens = grad_out.shape[0]
    gain_one = gains[:, 0].astype(jnp.float32)
    gain_two = gains[:, 1].astype(jnp.float32)
    grad_f = grad_out.astype(jnp.bfloat16)
    grad_down = jnp.einsum("tf,td->fd", hidden, grad_f, preferred_element_type=jnp.float32)
    grad_hidden = jnp.dot(grad_f, down_w.T, preferred_element_type=jnp.float32)
    gate_part = gate_up[:, :FF]
    up_part = gate_up[:, FF:]
    sig_part = jax.nn.sigmoid(gate_part)
    grad_gate_part = grad_hidden * up_part * sig_part * (1.0 + gate_part * (1.0 - sig_part))
    grad_up_part = grad_hidden * gate_part * sig_part
    grad_gate_up = jnp.concatenate([grad_gate_part, grad_up_part], 1).astype(jnp.bfloat16)
    grad_gu = jnp.einsum("td,tf->df", normed_two, grad_gate_up, preferred_element_type=jnp.float32)
    grad_normed_two = jnp.dot(grad_gate_up, gu_w.T, preferred_element_type=jnp.float32)
    grad_mid_norm, grad_gain_two = norm_back(grad_normed_two, scaled_two, inverse_two, gain_two)
    grad_mid = grad_out + grad_mid_norm
    grad_branch = grad_mid.astype(jnp.bfloat16)
    grad_out_w = jnp.einsum("td,te->de", combined, grad_branch, preferred_element_type=jnp.float32)
    grad_combined = jnp.dot(grad_branch, out_w.T, preferred_element_type=jnp.float32)
    grad_attended = grad_combined.astype(jnp.bfloat16).reshape(tokens, H, HD)
    grad_recalled = (grad_combined * gate).astype(jnp.bfloat16).reshape(tokens, H, HD)
    grad_gate_pre = grad_combined * recalled * gate * (1.0 - gate)
    outgoing = jnp.stack([grad_attended, grad_recalled], 1)
    headward = lax.all_to_all(outgoing, "seq", split_axis=2, concat_axis=0, tiled=True)
    head_grads, pkey_grads, pvalue_grads, rate_grads = ([], [], [], [])
    for head in range(grouped.shape[2]):
        cols = slice(head * HD, (head + 1) * HD)
        dq, dk, dv, dpk, dpv, drate = head_backward(
            grouped[:, 0, head],
            grouped[:, 1, head],
            grouped[:, 2, head],
            pkv[0][:, cols],
            pkv[1][:, cols],
            rates[head],
            seg_ids,
            lse_all[:, head],
            headward[:, 0, head],
            headward[:, 1, head],
        )
        head_grads.append(jnp.stack([dq, dk, dv], 1))
        pkey_grads.append(dpk)
        pvalue_grads.append(dpv)
        rate_grads.append(drate)
    grads_heads = jnp.stack(head_grads, 2).astype(jnp.bfloat16)
    tokenward = lax.all_to_all(grads_heads, "seq", split_axis=0, concat_axis=2, tiled=True)
    grad_proj = jnp.concatenate(
        [tokenward.reshape(tokens, 3 * D), grad_gate_pre.astype(jnp.bfloat16)], 1
    )
    grad_mix = jnp.einsum("td,tf->df", normed, grad_proj, preferred_element_type=jnp.float32)
    grad_normed = jnp.dot(grad_proj, mix_w.T, preferred_element_type=jnp.float32)
    grad_in_norm, grad_gain_one = norm_back(grad_normed, scaled_one, inverse_one, gain_one)
    grad_rows = grad_mid + grad_in_norm
    weight_terms = (
        grad_mix,
        grad_out_w,
        grad_gu,
        grad_down,
        jnp.stack([grad_gain_one, grad_gain_two], 1),
    )
    memory_terms = (
        jnp.stack([jnp.concatenate(pkey_grads, 1), jnp.concatenate(pvalue_grads, 1)], 0),
        jnp.stack(rate_grads, 0),
    )
    return (weight_terms, memory_terms, grad_rows)


def on_device(
    inputs, segment_ids, cotangent, w_mix, w_out, w_gu, w_down, norm_gains, persist_kv, memory_decay
):
    first = lax.axis_index("section") == 0
    own_weights = (w_mix[0], w_out[0], w_gu[0], w_down[0], norm_gains[0])
    pkv = persist_kv[0]
    rates = memory_decay[0]
    count = inputs.shape[0]
    tokens = inputs.shape[2]
    zero_rows = jnp.zeros((tokens, D), jnp.float32)
    received = jnp.zeros((tokens, D), jnp.bfloat16)
    kept_ticks, out_ticks = ([], [])
    for tick in range(count + 1):
        own_rows = inputs[tick, 0].astype(jnp.float32) if tick < count else zero_rows
        layer_in = jnp.where(first, own_rows, received.astype(jnp.float32))
        seg_ids = jnp.where(
            first, segment_ids[min(tick, count - 1), 0], segment_ids[max(tick - 1, 0), 0]
        )
        full = (
            lax.all_gather(own_weights[0], "shard", axis=0, tiled=True),
            lax.all_gather(own_weights[1], "shard", axis=0, tiled=True),
            lax.all_gather(own_weights[2], "shard", axis=0, tiled=True),
            lax.all_gather(own_weights[3], "shard", axis=0, tiled=True),
            lax.all_gather(own_weights[4], "shard", axis=0, tiled=True),
        )
        result, kept = layer_forward(layer_in, seg_ids, full, pkv, rates)
        result_low = result.astype(jnp.bfloat16)
        out_ticks.append(result_low)
        kept_ticks.append(kept)
        if tick < count:
            received = shifted(result_low, "section", 1)
    grad_weights = (
        jnp.zeros((D, 4 * D), jnp.float32),
        jnp.zeros((D, D), jnp.float32),
        jnp.zeros((D, 2 * FF), jnp.float32),
        jnp.zeros((FF, D), jnp.float32),
        jnp.zeros((D, 2), jnp.float32),
    )
    grad_memory = (
        jnp.zeros((2,) + pkv.shape[1:], jnp.float32),
        jnp.zeros(rates.shape, jnp.float32),
    )
    back_received = jnp.zeros((tokens, D), jnp.bfloat16)
    grad_ticks = []
    for tick in range(count + 1):
        lower = max(tick - 1, 0)
        upper = min(tick + 1, count)
        kept = jax.tree.map(
            lambda early, late: jnp.where(first, early, late), kept_ticks[lower], kept_ticks[upper]
        )
        given = cotangent[tick, 0].astype(jnp.float32) if tick < count else zero_rows
        grad_out = jnp.where(first, back_received.astype(jnp.float32), given)
        full = (
            lax.all_gather(own_weights[0], "shard", axis=0, tiled=True),
            lax.all_gather(own_weights[1], "shard", axis=0, tiled=True),
            lax.all_gather(own_weights[2], "shard", axis=0, tiled=True),
            lax.all_gather(own_weights[3], "shard", axis=0, tiled=True),
            lax.all_gather(own_weights[4], "shard", axis=0, tiled=True),
        )
        weight_terms, memory_terms, grad_rows = layer_backward(grad_out, kept, full, pkv, rates)
        grad_weights = jax.tree.map(jnp.add, grad_weights, weight_terms)
        grad_memory = jax.tree.map(jnp.add, grad_memory, memory_terms)
        grad_ticks.append(grad_rows)
        if tick < count:
            back_received = shifted(grad_rows.astype(jnp.bfloat16), "section", -1)
    section_out = jnp.stack(
        [jnp.where(first, out_ticks[batch], out_ticks[batch + 1]) for batch in range(count)], 0
    )
    section_grad = jnp.stack(
        [
            jnp.where(
                first,
                grad_ticks[batch + 1],
                grad_ticks[batch].astype(jnp.bfloat16).astype(jnp.float32),
            )
            for batch in range(count)
        ],
        0,
    )
    shares = jax.tree.map(
        lambda part: part.astype(jnp.float32),
        lax.psum_scatter(as_sent(grad_weights), "shard", scatter_dimension=0, tiled=True),
    )
    shares = jax.tree.map(lambda part: part.astype(jnp.float32), lax.psum(as_sent(shares), "seq"))
    memory_sums = lax.psum(grad_memory, "shard")
    return (
        section_out.reshape(1, count, 1, tokens, D),
        section_grad.reshape(1, count, 1, tokens, D),
        shares[0][None],
        shares[1][None],
        shares[2][None],
        shares[3][None],
        shares[4][None],
        memory_sums[0][None],
        memory_sums[1][None],
    )


MESH = pl.DeviceIdType.MESH
BF = jnp.bfloat16
F32 = jnp.float32


def here():
    return (lax.axis_index("section"), lax.axis_index("seq"), lax.axis_index("shard"))


def peer(place, chip, flip):
    x, s, z = place
    if chip % 2:
        x = 1 - x
    if chip // 2:
        s = (s + 2) % 4
    if flip:
        s = s + 1 - 2 * (s % 2)
    return (x, s, z)


def rows_of(device, size):
    x, s, _ = device
    return pl.ds(pl.multiple_of((s * 2 + x) * size, size), size)


class Gather:
    def __init__(self, full, batch, send, recv):
        self.place = here()
        self.full, self.batch, self.send, self.recv = full, batch, send, recv
        self.size = full.shape[1] // 8

    def copy(self, owner, target, sem):
        block = self.full.at[self.batch, rows_of(owner, self.size)]
        return pltpu.make_async_remote_copy(
            src_ref=block,
            dst_ref=block,
            send_sem=self.send.at[self.batch, sem],
            recv_sem=self.recv.at[self.batch, sem],
            device_id=target,
            device_id_type=MESH,
        )

    def start(self, value):
        self.full[self.batch, rows_of(self.place, self.size), :] = value
        for chip in (3, 1, 2, 0):
            self.copy(self.place, peer(self.place, chip, chip == 0), chip).start()

    def forward(self):
        other = peer(self.place, 0, True)
        for chip in (1, 2, 3):
            owner = peer(self.place, chip, False)
            self.copy(owner, owner, chip).wait_recv()
            self.copy(owner, other, 3 + chip).start()

    def finish(self):
        other = peer(self.place, 0, True)
        self.copy(other, other, 0).wait_recv()
        for chip in (1, 2, 3):
            owner = peer(self.place, chip, True)
            self.copy(owner, other, 3 + chip).wait_recv()
        for chip in (0, 1, 2, 3):
            self.copy(self.place, peer(self.place, chip, chip == 0), chip).wait_send()
        for chip in (1, 2, 3):
            self.copy(peer(self.place, chip, False), other, 3 + chip).wait_send()


class Scatter:
    def __init__(self, part, batch, pair, away, near, send, recv):
        self.place = here()
        self.part, self.batch, self.pair, self.away, self.near = part, batch, pair, away, near
        self.send, self.recv = send, recv
        self.size = part.shape[1] // 8

    def to_pair(self, chip):
        return pltpu.make_async_remote_copy(
            src_ref=self.part.at[self.batch, rows_of(peer(self.place, chip, True), self.size)],
            dst_ref=self.pair.at[self.batch, chip],
            send_sem=self.send.at[self.batch, chip],
            recv_sem=self.recv.at[self.batch, chip],
            device_id=peer(self.place, 0, True),
            device_id_type=MESH,
        )

    def to_chip(self, chip):
        return pltpu.make_async_remote_copy(
            src_ref=self.away.at[self.batch, chip - 1],
            dst_ref=self.near.at[self.batch, chip - 1],
            send_sem=self.send.at[self.batch, 3 + chip],
            recv_sem=self.recv.at[self.batch, 3 + chip],
            device_id=peer(self.place, chip, False),
            device_id_type=MESH,
        )

    def start(self):
        for chip in (3, 1, 2, 0):
            self.to_pair(chip).start()

    def chip_sum(self, chip):
        self.to_pair(chip).wait_recv()
        own = self.part[self.batch, rows_of(peer(self.place, chip, False), self.size), :]
        return own.astype(F32) + self.pair[self.batch, chip].astype(F32)

    def forward(self):
        for chip in (3, 1, 2):
            self.away[self.batch, chip - 1] = self.chip_sum(chip).astype(BF)
            self.to_chip(chip).start()

    def finish(self):
        total = self.chip_sum(0)
        for chip in (1, 2, 3):
            self.to_chip(chip).wait_recv()
            total = total + self.near[self.batch, chip - 1].astype(F32)
        for chip in (0, 1, 2, 3):
            self.to_pair(chip).wait_send()
        for chip in (1, 2, 3):
            self.to_chip(chip).wait_send()
        return total


class Column:
    def __init__(self, send, recv):
        self.place = here()
        self.send, self.recv = send, recv

    def copy(self, source, landing, sent, received, plane):
        x, s, _ = self.place
        return pltpu.make_async_remote_copy(
            src_ref=source,
            dst_ref=landing,
            send_sem=self.send.at[sent],
            recv_sem=self.recv.at[received],
            device_id=(x, s, plane),
            device_id_type=MESH,
        )

    def at_each(self, body):
        for at in range(4):

            @pl.when(self.place[2] == at)
            def _():
                body(at)


class ColumnSum(Column):
    RELAYED = ((3, 1), None, None, (0, 2))
    DIRECT = ((2, 1), (2, 0), (1, 3), (1, 2))
    SOURCES = ((1, 2), (0, 2, 3), (0, 1, 3), (1, 2))

    def __init__(self, own, slots, out, send, recv):
        super().__init__(send, recv)
        self.own, self.slots, self.out = own, slots, out

    def first(self, at):
        block, plane = self.RELAYED[at]
        return self.copy(self.own.at[block], self.slots.at[plane], at, plane, plane)

    def direct(self, at, plane):
        return self.copy(self.own.at[plane], self.slots.at[at], plane, at, plane)

    def relayed(self, at):
        end = 3 if at == 1 else 0
        return self.copy(self.slots.at[at], self.slots.at[at], end, at, end)

    def start(self):
        def body(at):
            if self.RELAYED[at]:
                self.first(at).start()
            for plane in self.DIRECT[at]:
                self.direct(at, plane).start()

        self.at_each(body)

    def hop(self):
        for at, block in ((1, 3), (2, 0)):

            @pl.when(self.place[2] == at)
            def _():
                self.relayed(at).wait_recv()
                self.slots[at] = (
                    self.slots[at].astype(F32) + self.own[block].astype(F32)
                ).astype(BF)
                self.relayed(at).start()

    def finish(self):
        def body(at):
            total = self.own[at].astype(F32)
            for plane in self.SOURCES[at]:
                self.direct(plane, at).wait_recv()
                total = total + self.slots[plane].astype(F32)
            self.out[...] = total.astype(BF)
            if self.RELAYED[at]:
                self.first(at).wait_send()
            else:
                self.relayed(at).wait_send()
            for plane in self.DIRECT[at]:
                self.direct(at, plane).wait_send()

        self.at_each(body)


class ColumnGather(Column):
    TARGETS = ((2, 1), (3, 2, 0), (0, 1, 3), (1, 2))

    def __init__(self, full, send, recv):
        super().__init__(send, recv)
        self.full = full

    def block(self, at, plane):
        return self.copy(self.full.at[at], self.full.at[at], plane, at, plane)

    def relayed(self, at):
        block, plane = (3, 0) if at == 1 else (0, 3)
        return self.copy(self.full.at[block], self.full.at[block], at, block, plane)

    def start(self):
        def body(at):
            for plane in self.TARGETS[at]:
                self.block(at, plane).start()

        self.at_each(body)

    def hop(self):
        for at in (1, 2):

            @pl.when(self.place[2] == at)
            def _():
                self.relayed(at).wait_recv()
                self.relayed(at).start()

    def finish(self):
        def body(at):
            for plane in range(4):
                if plane != at and (at, plane) not in ((1, 3), (2, 0)):
                    self.block(plane, at).wait_recv()
            for plane in self.TARGETS[at]:
                self.block(at, plane).wait_send()
            if at in (1, 2):
                self.relayed(at).wait_send()

        self.at_each(body)


class Root(Column):
    def __init__(self, send, recv):
        super().__init__(send, recv)
        x, s, z = self.place
        self.root = 2 * x + s // 2
        self.low = self.root < 2
        self.between = jnp.where(self.low, 2, 1)
        self.end = jnp.where(self.low, 3, 0)
        self.is_root = z == self.root


class RootSum(Root):
    def __init__(self, own, slots, out, send, recv):
        super().__init__(send, recv)
        self.own, self.slots, self.out = own, slots, out

    def toward(self, slot, plane, source=None):
        landing = self.slots.at[slot]
        return self.copy(landing if source is None else source, landing, 0, slot, plane)

    def start(self):
        z = self.place[2]

        @pl.when(z == self.end)
        def _():
            self.toward(0, self.between, self.own).start()

        @pl.when((z != self.end) & (z != self.between) & (z != self.root))
        def _():
            self.toward(1, self.root, self.own).start()

    def hop(self):
        @pl.when(self.place[2] == self.between)
        def _():
            self.toward(0, self.root).wait_recv()
            self.slots[0] = (self.slots[0].astype(F32) + self.own[...].astype(F32)).astype(BF)
            self.toward(0, self.root).start()

    def finish(self):
        self.out[...] = self.own[...]

        @pl.when(self.is_root)
        def _():
            total = self.own[...].astype(F32)
            for slot in (0, 1):
                self.toward(slot, self.root).wait_recv()
                total = total + self.slots[slot].astype(F32)
            self.out[...] = total.astype(BF)

        @pl.when(jnp.logical_not(self.is_root))
        def _():
            self.toward(0, self.root).wait_send()


def meet(column=False):
    place = here()
    x, s, z = place
    others = [peer(place, chip, chip == 0) for chip in range(4)]
    if column:
        others += [(x, s, (z + dz) % 4) for dz in (1, 2, 3)]
    barrier = pltpu.get_barrier_semaphore()
    for other in others:
        pl.semaphore_signal(barrier, inc=1, device_id=other, device_id_type=MESH)
    pl.semaphore_wait(barrier, len(others))


def nn(left, right):
    return jnp.dot(left, right, preferred_element_type=F32)


def nt(left, right):
    return lax.dot_general(left, right, (((1,), (1,)), ((), ())), preferred_element_type=F32)


def tn(left, right):
    return lax.dot_general(left, right, (((0,), (0,)), ((), ())), preferred_element_type=F32)


def flat(ref):
    value = ref[...]
    return value.reshape(-1, value.shape[-1])


def in_blocks(length, size, body):
    def step(index, carry):
        body(pl.ds(pl.multiple_of(index * size, size), size), index * size)
        return carry

    lax.fori_loop(0, length // size, step, 0)


def weights_of_scores(query, keys, pkeys, seg_rows, seg_cols, begin, rate):
    scale = 1.0 / math.sqrt(HD)
    inner = nt(query, keys)
    per_scores = nt(query, pkeys) * scale
    row_places = begin + lax.broadcasted_iota(jnp.int32, inner.shape, 0)
    col_places = lax.broadcasted_iota(jnp.int32, inner.shape, 1)
    allowed = (seg_rows == seg_cols) & (col_places <= row_places)
    distance = jnp.maximum(row_places - col_places, 0).astype(F32)
    decay_w = jnp.where(allowed, jnp.exp(-rate * distance) * (1.0 / HD), 0.0)
    seq_scores = jnp.where(allowed, inner * scale, -jnp.inf)
    top = jnp.maximum(
        jnp.max(per_scores, axis=1, keepdims=True), jnp.max(seq_scores, axis=1, keepdims=True)
    )
    per_exp = jnp.exp(per_scores - top)
    seq_exp = jnp.exp(seq_scores - top)
    denom = jnp.sum(per_exp, axis=1, keepdims=True) + jnp.sum(seq_exp, axis=1, keepdims=True)
    share = 1.0 / denom
    return inner, decay_w, distance, seq_exp * share, per_exp * share


class BackwardIn(NamedTuple):
    grad_full: Any
    grad_rows: Any
    rows: Any
    normed: Any
    gu: Any
    down: Any
    gains: Any
    mix: Any
    out: Any
    persist: Any
    rates: Any
    seg_rows: Any
    seg_cols: Any
    qkv: Any
    gate: Any
    recalled: Any
    combined: Any
    mid: Any
    normed_two: Any
    gate_up: Any
    hidden: Any


class BackwardOut(NamedTuple):
    grad_mix: Any
    grad_out: Any
    gain_sums: Any
    grad_persist: Any
    grad_rate: Any
    gu_sum: Any
    down_sum: Any
    grad_h: Any


class PlaneScratch(NamedTuple):
    part: Any
    pair: Any
    away: Any
    near: Any
    ssend: Any
    srecv: Any
    gsend: Any
    grecv: Any


class BackwardScratch(NamedTuple):
    grad_gu: Any
    grad_proj: Any
    grad_keys: Any
    grad_values: Any
    own_gu: Any
    own_down: Any
    branch: Any
    grad_mid: Any
    gu_slots: Any
    down_slots: Any
    csend: Any
    crecv: Any


class EarlyIn(NamedTuple):
    early_mix: Any
    early_out: Any


class EarlyOut(NamedTuple):
    mix_sum: Any
    out_sum: Any


class EarlyScratch(NamedTuple):
    mix_slots: Any
    root_slots: Any
    rsend: Any
    rrecv: Any


class NextOut(NamedTuple):
    grad_next: Any


def fields(*kinds):
    return tuple(name for kind in kinds for name in kind._fields)


def named(names, refs):
    return types.SimpleNamespace(**dict(zip(names, refs, strict=True)))


def remote(source, landing, sems, index, target):
    return pltpu.make_async_remote_copy(
        src_ref=source,
        dst_ref=landing,
        send_sem=sems[0].at[index],
        recv_sem=sems[1].at[index],
        device_id=target,
        device_id_type=MESH,
    )


class RootGather(Root):
    def __init__(self, block, send, recv):
        super().__init__(send, recv)
        self.block = block

    def to(self, plane, sent):
        return self.copy(self.block, self.block, sent, 0, plane)

    def near(self):
        return jnp.where(self.low, 1 - self.root, 5 - self.root)

    def start(self):
        @pl.when(self.is_root)
        def _():
            self.to(self.between, 0).start()
            self.to(self.near(), 1).start()

    def hop(self):
        @pl.when(self.place[2] == self.between)
        def _():
            self.to(self.end, 0).wait_recv()
            self.to(self.end, 0).start()

    def finish(self):
        z = self.place[2]

        @pl.when((z != self.root) & (z != self.between))
        def _():
            self.to(self.end, 0).wait_recv()

        @pl.when((z == self.root) | (z == self.between))
        def _():
            self.to(self.end, 0).wait_send()

        @pl.when(self.is_root)
        def _():
            self.to(self.end, 1).wait_send()


class SeqGather:
    def __init__(self, full, batch, send, recv):
        self.place = here()
        self.full, self.batch, self.send, self.recv = full, batch, send, recv
        self.size = full.shape[1] // 4
        self.beside = peer(self.place, 2, False)
        self.sibling = peer(self.place, 0, True)

    def rows(self, owner):
        return pl.ds(pl.multiple_of(owner[1] * self.size, self.size), self.size)

    def copy(self, owner, target, sem):
        block = self.full.at[self.batch, self.rows(owner)]
        sems = (self.send.at[self.batch], self.recv.at[self.batch])
        return remote(block, block, sems, sem, target)

    def start(self, value):
        self.full[self.batch, self.rows(self.place), :] = value
        self.copy(self.place, self.beside, 0).start()
        self.copy(self.place, self.sibling, 1).start()

    def forward(self):
        self.copy(self.beside, self.beside, 0).wait_recv()
        self.copy(self.beside, self.sibling, 2).start()

    def finish(self):
        self.copy(self.sibling, self.sibling, 1).wait_recv()
        self.copy(peer(self.place, 2, True), self.sibling, 2).wait_recv()
        self.copy(self.place, self.beside, 0).wait_send()
        self.copy(self.place, self.sibling, 1).wait_send()
        self.copy(self.beside, self.sibling, 2).wait_send()


class ForwardIn(NamedTuple):
    inputs: Any
    small: Any
    gain_rows: Any
    w_mix: Any
    w_out: Any
    w_gu: Any
    w_down: Any
    seg_rows: Any
    seg_cols: Any


class ForwardOut(NamedTuple):
    rows: Any
    gains: Any
    persist: Any
    rates: Any


class Kept(NamedTuple):
    normed: Any
    mix: Any
    out: Any
    gu: Any
    down: Any
    qkv: Any
    gate: Any
    recalled: Any
    combined: Any
    mid: Any
    normed_two: Any
    gate_up: Any
    hidden: Any
    out_rows: Any


class ForwardScratch(NamedTuple):
    gain_all: Any
    small_all: Any
    mix_away: Any
    gu_away: Any
    down_away: Any
    zsend: Any
    zrecv: Any
    psend: Any
    precv: Any
    xsend: Any
    xrecv: Any
    gsend: Any
    grecv: Any
    csend: Any
    crecv: Any
    hsend: Any
    hrecv: Any
    saved: Any


def each(parts, act):
    for part in parts:
        act(part)


def forward_kernel(unit, *refs):
    count = len(Kept._fields)
    r, refs = refs[: len(ForwardIn._fields)], refs[len(ForwardIn._fields) :]
    given = vars(named(ForwardIn._fields, r))
    r, refs = refs[: len(ForwardOut._fields)], refs[len(ForwardOut._fields) :]
    given |= vars(named(ForwardOut._fields, r))
    in_hbm = [refs[:count], refs[count : 2 * count]]
    refs = refs[2 * count :]
    in_vmem = [refs[:count], refs[count : 2 * count]]
    refs = refs[2 * count :]
    scratch = PlaneScratch._fields[:6] + ForwardScratch._fields
    r = types.SimpleNamespace(**given, **vars(named(scratch, refs)))
    views = [types.SimpleNamespace(**vars(named(Kept._fields, part))) for part in in_vmem]
    views[0].rows, views[1].rows = r.rows, views[0].out_rows

    def save(layer, which):
        for name in which:
            index = Kept._fields.index(name)
            yield pltpu.make_async_copy(
                in_vmem[layer][index], in_hbm[layer][index], r.saved.at[layer, index]
            )

    place = here()
    x, s, z = place
    partner = peer(place, 1, False)
    flips = [(dx, ds) for dx in (0, 1) for ds in range(4) if dx or ds]
    plane = [((x + dx) % 2, (s + ds) % 4, z) for dx, ds in flips]
    column = [(x, s, (z + dz) % 4) for dz in (1, 2, 3)]
    column += [(1 - x, s, (z + dz) % 4) for dz in (1, 2, 3)]
    barrier = pltpu.get_barrier_semaphore()
    for other in plane + column:
        pl.semaphore_signal(barrier, inc=1, device_id=other, device_id_type=MESH)
    pl.semaphore_wait(barrier, len(plane) + len(column))

    zsems, psems, xsems = (r.zsend, r.zrecv), (r.psend, r.precv), (r.xsend, r.xrecv)
    holders = [*column, partner]

    def gains_to(index):
        return remote(r.gain_rows, r.gain_all.at[x, z], zsems, index, holders[index])

    for index in range(7):
        gains_to(index).start()
    r.gain_all[x, z] = r.gain_rows[...]

    mine, other = x * 4 + s, (1 - x) * 4 + s

    def mix_part(which):
        heads = [pl.ds(pl.multiple_of(kind * D + which * HD, HD), HD) for kind in range(4)]
        return jnp.concatenate([r.w_mix[0, :, cols] for cols in heads], 1)

    out_rows = pl.ds(pl.multiple_of(s % 2 * HD, HD), HD)
    root = z == 2 * x + s // 2
    rooted = z == 2 * (1 - x) + s // 2
    for layer in (0, 1):
        v = views[layer]

        @pl.when(x == layer)
        def _():
            r.mix_away[...] = mix_part(other)
            remote(r.mix_away, v.mix.at[z], xsems, 0, partner).start()
            v.mix[z] = mix_part(mine)

            @pl.when(rooted)
            def _():
                remote(r.w_out.at[0, out_rows], v.out, xsems, 1, partner).start()

            @pl.when(root)
            def _():
                v.out[...] = r.w_out[0, out_rows, :]

    for index in range(7):
        gains_to(index).wait_recv()
    for layer in range(2):
        for owner in range(4):
            for kind in range(2):
                for half in range(2):
                    begin = owner * 2 * HD + half * HD
                    row = 2 * kind + half
                    r.gains[layer, kind : kind + 1, begin : begin + HD] = r.gain_all[
                        layer, owner, row : row + 1, :
                    ]
    size = r.rows.shape[1]
    own_half = pl.ds(pl.multiple_of(x * size, size), size)
    arriving = [SeqGather(views[0].normed, batch, r.gsend, r.grecv) for batch in range(2)]
    for batch, gather in enumerate(arriving):
        rows = r.inputs[batch, 0].astype(F32)
        gather.start((rows * rms_scale(rows) * r.gains[0, 0:1, :]).astype(BF))
        r.rows[batch] = r.inputs[batch, 0, own_half, :]

    for index in range(7):
        remote(r.small, r.small_all.at[x, s], psems, index, plane[index]).start()
    r.small_all[x, s] = r.small[...]

    padded = r.down_away.shape[0]
    width = 8 * unit + 64

    def select(which, offset):
        begin = lax.broadcasted_iota(jnp.int32, (width, 128), 0) - offset
        col = lax.broadcasted_iota(jnp.int32, (width, 128), 1)
        return jnp.where((begin == which * unit + col) & (col < unit), 1.0, 0.0).astype(BF)

    def gu_part(which, out):
        for owner in range(4):
            base = owner * 8 * unit
            offset = base % 128
            chosen = select(which, offset)
            for side in range(2):
                begin = side * FF + base - offset
                part = nn(r.w_gu[0, :, begin : begin + width], chosen).astype(BF)
                at = side * 4 * padded + owner * padded
                out[:, at : at + padded] = part[:, :padded]

    def down_part(which, out):
        row = lax.broadcasted_iota(jnp.int32, (padded, 8 * unit), 0)
        col = lax.broadcasted_iota(jnp.int32, (padded, 8 * unit), 1)
        chosen = jnp.where((col == which * unit + row) & (row < unit), 1.0, 0.0).astype(BF)
        out[...] = nn(chosen, r.w_down[0]).astype(BF)

    gu_part(other, r.gu_away)
    down_part(other, r.down_away)
    for layer in (0, 1):
        v = views[layer]

        @pl.when(x == layer)
        def _():
            remote(r.gu_away, v.gu.at[z], xsems, 2, partner).start()
            remote(r.down_away, v.down.at[z], xsems, 3, partner).start()
            gu_part(mine, v.gu.at[z])
            down_part(mine, v.down.at[z])

    mixers, feeds = [], []
    for layer, v in enumerate(views):
        sems = [(r.csend.at[3 * layer + i], r.crecv.at[3 * layer + i]) for i in range(3)]
        mixers.append(
            [
                ColumnGather(v.mix, *sems[0]),
                RootGather(v.out, r.hsend.at[layer], r.hrecv.at[layer]),
            ]
        )
        feeds.append([ColumnGather(v.gu, *sems[1]), ColumnGather(v.down, *sems[2])])

    def swapped(layer, index):
        v = views[layer]
        landing = [v.mix.at[z], v.out, v.gu.at[z], v.down.at[z]][index]
        here_from = remote(landing, landing, xsems, index, partner)

        @pl.when((x != layer) & root if index == 1 else x != layer)
        def _():
            here_from.wait_recv()

    def start_mixer(layer):
        for index, part in enumerate(mixers[layer]):
            swapped(layer, index)
            part.start()

    def start_feed(layer):
        for index, part in enumerate(feeds[layer]):
            swapped(layer, 2 + index)
            part.start()

    start_mixer(0)
    arriving[0].forward()
    each(mixers[0], lambda part: part.hop())
    start_feed(0)
    arriving[1].forward()

    for index in range(7):
        dx, ds = flips[index]
        landing = r.small_all.at[(x + dx) % 2, (s + 4 - ds) % 4]
        remote(r.small, landing, psems, index, plane[index]).wait_recv()
    for layer in range(2):
        begin = pl.multiple_of(s % 2 * 32, 32)
        rows = r.small_all[layer, 2 * x + s // 2, pl.ds(begin, 32), :]
        r.persist[layer] = rows.astype(BF).reshape(2, 16, HD)
        begin = pl.multiple_of(64 + s % 2 * 8, 8)
        r.rates[layer] = r.small_all[layer, 2 * x + s // 2, pl.ds(begin, 8), :]

    length = r.part.shape[1]

    def project(layer, batch):
        v = views[layer]

        def block(rows, begin):
            proj = nn(v.normed[batch, rows, :], flat(v.mix))
            v.qkv[batch, rows, :] = proj[:, : 3 * HD].astype(BF)
            v.gate[batch, rows, :] = jax.nn.sigmoid(proj[:, 3 * HD :])

        in_blocks(length, 256, block)

    def mixer(layer, batch):
        v = views[layer]

        def block(rows, begin):
            values = v.qkv[batch, :, 2 * HD :]
            inner, decay_w, _, probs, per_probs = weights_of_scores(
                v.qkv[batch, rows, :HD],
                v.qkv[batch, :, HD : 2 * HD],
                r.persist[layer, 0],
                r.seg_rows[batch, rows, :],
                r.seg_cols[batch],
                begin,
                r.rates[layer, 0:1, 0:1],
            )
            attended = nn(probs.astype(BF), values) + nn(per_probs.astype(BF), r.persist[layer, 1])
            recalled = nn((inner * decay_w).astype(BF), values).astype(BF)
            v.recalled[batch, rows, :] = recalled
            combined = attended.astype(BF).astype(F32)
            combined = combined + v.gate[batch, rows, :] * recalled.astype(F32)
            combined = combined.astype(BF)
            v.combined[batch, rows, :] = combined
            r.part[batch, rows, :] = nn(combined, v.out[...]).astype(BF)

        in_blocks(length, 128, block)

    def feed(layer, batch):
        v = views[layer]

        def block(rows, begin):
            gate_up = nn(v.normed_two[batch, rows, :], flat(v.gu))
            v.gate_up[batch, rows, :] = gate_up
            half = gate_up.shape[1] // 2
            hidden = (jax.nn.silu(gate_up[:, :half]) * gate_up[:, half:]).astype(BF)
            v.hidden[batch, rows, :] = hidden
            r.part[batch, rows, :] = nn(hidden, flat(v.down)).astype(BF)

        in_blocks(length, 256, block)

    def scatter(batch):
        return Scatter(r.part, batch, r.pair, r.away, r.near, r.ssend, r.srecv)

    def send_normed(batch, own, gain, full):
        gather = Gather(full, batch, r.gsend, r.grecv)
        gather.start((own * rms_scale(own) * gain).astype(BF))
        return gather

    mixer_names = Kept._fields[:3] + Kept._fields[5:9]
    for layer, v in enumerate(views):
        parts = []
        for batch in range(2):
            if layer == 1:
                arriving[batch].forward()
            arriving[batch].finish()
            if batch == 0:
                each(mixers[layer], lambda part: part.finish())
            project(layer, batch)
            mixer(layer, batch)
            part = scatter(batch)
            part.start()
            part.forward()
            parts.append(part)
        each(save(layer, mixer_names), lambda copy: copy.start())
        gathers = []
        for batch, part in enumerate(parts):
            mid = v.rows[batch].astype(F32) + part.finish()
            v.mid[batch] = mid
            gathers.append(send_normed(batch, mid, r.gains[layer, 1:2, :], v.normed_two))
        each(feeds[layer], lambda part: part.hop())
        if layer == 0:
            start_mixer(1)
        parts = []
        for batch, gather in enumerate(gathers):
            gather.forward()
            gather.finish()
            if batch == 0:
                each(feeds[layer], lambda part: part.finish())
            feed(layer, batch)
            part = scatter(batch)
            part.start()
            part.forward()
            parts.append(part)
        if layer == 0:
            each(mixers[1], lambda part: part.hop())
            start_feed(1)
        each(save(layer, Kept._fields[3:5] + Kept._fields[9:13]), lambda copy: copy.start())
        arriving = []
        for batch, part in enumerate(parts):
            rows = (v.mid[batch] + part.finish()).astype(BF)
            v.out_rows[batch] = rows
            if layer == 0:
                gain = r.gains[1, 0:1, :]
                arriving.append(send_normed(batch, rows.astype(F32), gain, views[1].normed))
        each(save(layer, Kept._fields[13:]), lambda copy: copy.start())

    for layer in range(2):
        for copy in save(layer, Kept._fields):
            copy.wait()
    remote(r.mix_away, r.mix_away, xsems, 0, partner).wait_send()
    remote(r.gu_away, r.gu_away, xsems, 2, partner).wait_send()
    remote(r.down_away, r.down_away, xsems, 3, partner).wait_send()

    @pl.when(rooted)
    def _():
        remote(views[0].out, views[0].out, xsems, 1, partner).wait_send()

    for index in range(7):
        gains_to(index).wait_send()
        remote(r.small, r.small_all.at[x, s], psems, index, plane[index]).wait_send()


def backward_layer(layer, ins, outs, *refs):
    scratch = fields(PlaneScratch, BackwardScratch)
    earlier = len(outs) == len(fields(BackwardOut, EarlyOut))
    if earlier:
        scratch += fields(EarlyScratch)
    r = named(ins + outs + scratch, refs)
    length = r.part.shape[1]
    last = not hasattr(r, "grad_next")
    sums = [
        ColumnSum(r.own_gu, r.gu_slots, r.gu_sum, r.csend.at[0], r.crecv.at[0]),
        ColumnSum(r.own_down, r.down_slots, r.down_sum, r.csend.at[1], r.crecv.at[1]),
    ]
    early = []
    if earlier:
        early = [
            ColumnSum(r.early_mix, r.mix_slots, r.mix_sum, r.csend.at[2], r.crecv.at[2]),
            RootSum(r.early_out, r.root_slots, r.out_sum, r.rsend, r.rrecv),
        ]

    def feed_back(batch):
        def block(rows, begin):
            grad_hidden = nt(r.grad_full[batch, rows, :], flat(r.down))
            half = grad_hidden.shape[1]
            gate_part = r.gate_up[batch, rows, :half]
            up_part = r.gate_up[batch, rows, half:]
            sig_part = jax.nn.sigmoid(gate_part)
            silu = gate_part * sig_part
            grad_gate = grad_hidden * up_part * (sig_part + silu * (1.0 - sig_part))
            r.grad_gu[batch, rows, :half] = grad_gate.astype(BF)
            r.grad_gu[batch, rows, half:] = (grad_hidden * silu).astype(BF)
            r.part[batch, rows, :] = nt(r.grad_gu[batch, rows, :], flat(r.gu)).astype(BF)

        in_blocks(length, 256, block)

    def feed_weights():
        def down(cols, begin):
            grad = tn(r.hidden[0], r.grad_full[0, :, cols])
            grad = grad + tn(r.hidden[1], r.grad_full[1, :, cols])
            grad = grad.reshape(4, grad.shape[0] // 4, grad.shape[1])
            r.own_down[:, :, cols] = grad.astype(BF)

        in_blocks(D, 256, down)
        product(r.own_gu, r.normed_two, r.grad_gu)

    def product(out, left, right):
        for owner in range(4):
            cols = slice(owner * (D // 4), (owner + 1) * (D // 4))
            grad = tn(left[0, :, cols], right[0]) + tn(left[1, :, cols], right[1])
            out[owner] = grad.astype(BF)

    def mixer_back(batch):
        scale = 1.0 / math.sqrt(HD)
        r.grad_keys[...] = jnp.zeros_like(r.grad_keys)
        r.grad_values[...] = jnp.zeros_like(r.grad_values)

        def block(rows, begin):
            grad_combined = nt(r.branch[batch, rows, :], r.out[...])
            gate = r.gate[batch, rows, :]
            recalled = r.recalled[batch, rows, :].astype(F32)
            attn_rows = grad_combined.astype(BF)
            memory_rows = (grad_combined * gate).astype(BF)
            grad_pre = grad_combined * recalled * gate * (1.0 - gate)
            r.grad_proj[batch, rows, 3 * HD :] = grad_pre.astype(BF)
            query = r.qkv[batch, rows, :HD]
            keys = r.qkv[batch, :, HD : 2 * HD]
            values = r.qkv[batch, :, 2 * HD :]
            inner, decay_w, distance, probs, per_probs = weights_of_scores(
                query,
                keys,
                r.persist[layer, 0],
                r.seg_rows[batch, rows, :],
                r.seg_cols[batch],
                begin,
                r.rates[layer, 0:1, 0:1],
            )
            per_dp = nt(attn_rows, r.persist[layer, 1])
            seq_dp = nt(attn_rows, values)
            delta = jnp.sum(per_probs * per_dp, axis=1, keepdims=True) + jnp.sum(
                probs * seq_dp, axis=1, keepdims=True
            )
            per_ds = (per_probs * (per_dp - delta)).astype(BF)
            seq_ds = (probs * (seq_dp - delta)).astype(BF)
            weighted = nt(memory_rows, values) * decay_w
            grad_inner = weighted.astype(BF)
            memory = inner * decay_w
            rate_terms = weighted * inner * distance
            r.grad_rate[...] -= jnp.sum(rate_terms, axis=0, keepdims=True)
            grad_query = (nn(per_ds, r.persist[layer, 0]) + nn(seq_ds, keys)) * scale
            grad_query = grad_query + nn(grad_inner, keys)
            r.grad_proj[batch, rows, :HD] = grad_query.astype(BF)
            r.grad_keys[...] += tn(seq_ds, query) * scale + tn(grad_inner, query)
            r.grad_values[...] += tn(probs.astype(BF), attn_rows) + tn(
                memory.astype(BF), memory_rows
            )
            r.grad_persist[0] += tn(per_ds, query) * scale
            r.grad_persist[1] += tn(per_probs.astype(BF), attn_rows)

        in_blocks(length, 128, block)
        r.grad_proj[batch, :, HD : 2 * HD] = r.grad_keys[...].astype(BF)
        r.grad_proj[batch, :, 2 * HD : 3 * HD] = r.grad_values[...].astype(BF)

        def back(rows, begin):
            r.part[batch, rows, :] = nt(r.grad_proj[batch, rows, :], flat(r.mix)).astype(BF)

        in_blocks(length, 256, back)

    def scatter(batch):
        return Scatter(r.part, batch, r.pair, r.away, r.near, r.ssend, r.srecv)

    def through_norm(batch, part, rows, gain):
        grad_normed = part.finish()
        inverse = rms_scale(rows)
        return norm_back(grad_normed, rows * inverse, inverse, gain)

    meet(True)
    r.grad_rate[...] = jnp.zeros_like(r.grad_rate)
    r.grad_persist[...] = jnp.zeros_like(r.grad_persist)
    for column in early:
        column.start()
    first, second = (scatter(batch) for batch in range(2))
    for batch, part in enumerate((first, second)):
        feed_back(batch)
        part.start()
        part.forward()
    for column in early:
        column.hop()
    feed_weights()
    for column in sums:
        column.start()
    gathers = []
    gain_sums = []
    for batch, part in enumerate((first, second)):
        grad_mid, gain_sum = through_norm(batch, part, r.mid[batch], r.gains[layer, 1:2, :])
        gain_sums.append(gain_sum[None])
        grad_mid = grad_mid + r.grad_rows[batch].astype(F32)
        r.grad_mid[batch] = grad_mid
        gather = Gather(r.branch, batch, r.gsend, r.grecv)
        gather.start(grad_mid.astype(BF))
        gathers.append(gather)
    r.gain_sums[1:2] = gain_sums[0] + gain_sums[1]
    first, second = (scatter(batch) for batch in range(2))
    for batch, part in enumerate((first, second)):
        gathers[batch].forward()
        gathers[batch].finish()
        mixer_back(batch)
        part.start()
        part.forward()
        if batch == 0:
            for column in sums:
                column.hop()
    product(r.grad_mix, r.normed, r.grad_proj)
    grad_out = tn(r.combined[0], r.branch[0]) + tn(r.combined[1], r.branch[1])
    r.grad_out[...] = grad_out.astype(BF)
    gathers = []
    gain_sums = []
    for batch, part in enumerate((first, second)):
        grad_h, gain_sum = through_norm(
            batch, part, r.rows[batch].astype(F32), r.gains[layer, 0:1, :]
        )
        gain_sums.append(gain_sum[None])
        grad_h = (grad_h + r.grad_mid[batch]).astype(BF)
        r.grad_h[batch] = grad_h
        if not last:
            gather = Gather(r.grad_next, batch, r.gsend, r.grecv)
            gather.start(grad_h)
            gathers.append(gather)
    r.gain_sums[0:1] = gain_sums[0] + gain_sums[1]
    for gather in gathers:
        gather.forward()
    for gather in gathers:
        gather.finish()
    for column in early + sums:
        column.finish()


def final_kernel(*refs):
    place = here()
    x, s, z = place
    sibling, beside, partner = (peer(place, 0, True), peer(place, 2, False), peer(place, 1, False))
    across = peer(place, 3, False)
    by_layer = [list(refs[0:6]), list(refs[6:12])]
    small_ref = refs[12]
    bufs = refs[13:16]
    out_buf, rows_buf, grads_buf, plane_buf = refs[16:20]
    column_buf, mix_sum, out_sum, mix_slots, root_slots, *sems = refs[20:]
    psend, precv, osend, orecv, rsend, rrecv, zsend, zrecv, ssend, srecv, *sems = sems
    csend, crecv, hsend, hrecv = sems
    columns = [
        ColumnSum(by_layer[0][0], mix_slots, mix_sum, csend, crecv),
        RootSum(by_layer[0][3], root_slots, out_sum, hsend, hrecv),
    ]
    by_layer[0][0], by_layer[0][3] = mix_sum, out_sum

    def copy(source, landing, sems, index, target):
        return pltpu.make_async_remote_copy(
            src_ref=source,
            dst_ref=landing,
            send_sem=sems[0].at[index],
            recv_sem=sems[1].at[index],
            device_id=target,
            device_id_type=MESH,
        )

    flips = [(dx, ds) for dx in (0, 1) for ds in range(4) if dx or ds]
    plane = [((x + dx) % 2, (s + ds) % 4, z) for dx, ds in flips]
    column = [(x, s, (z + dz) % 4) for dz in (1, 2, 3)]
    barrier = pltpu.get_barrier_semaphore()
    for other in plane + column:
        pl.semaphore_signal(barrier, inc=1, device_id=other, device_id_type=MESH)
    pl.semaphore_wait(barrier, len(plane) + len(column))

    def to_plane_of(dz):
        target = (z + dz) % 4
        return copy(
            small_ref.at[target], column_buf.at[dz - 1], (zsend, zrecv), dz - 1, (x, s, target)
        )

    def to_plane(index):
        slot = plane_buf.at[x * 4 + s]
        return copy(slot, slot, (ssend, srecv), index, plane[index])

    for dz in (1, 2, 3):
        to_plane_of(dz).start()

    psems = [(psend.at[i], precv.at[i]) for i in range(3)]

    def piece(index, kind, slot, target, source=None):
        landing = bufs[index].at[slot]
        return copy(landing if source is None else source, landing, psems[index], kind, target)

    mine = (x, s)
    turned = (1 - x, s)

    def send(indices):
        for layer in (0, 1):
            own, theirs = by_layer[layer], by_layer[1 - layer]

            @pl.when(x == layer)
            def _():
                for index in indices:
                    piece(index, 2, mine, partner, theirs[index]).start()
                    piece(index, 0, mine, beside, own[index]).start()
                    piece(index, 1, mine, sibling, own[index]).start()
                for index in indices:
                    bufs[index][mine] = own[index][...]

    def turn(indices):
        for index in indices:
            piece(index, 2, turned, partner).wait_recv()
            piece(index, 3, turned, beside).start()
            piece(index, 4, turned, sibling).start()

    for column in columns:
        column.start()
    send((1, 2))
    for layer in (0, 1):

        @pl.when(x == layer)
        def _():
            copy(by_layer[1 - layer][4], rows_buf, (rsend, rrecv), 0, partner).start()
            copy(by_layer[1 - layer][5], grads_buf, (rsend, rrecv), 1, partner).start()

    total = small_ref[z]
    for dz in (1, 2, 3):
        to_plane_of(dz).wait_recv()
        total = total + column_buf[dz - 1]
    plane_buf[x * 4 + s] = total
    for index in range(7):
        to_plane(index).start()
    for column in columns:
        column.hop()
    turn((1, 2))
    for column in columns:
        column.finish()
    send((0,))

    core = s % 2
    root = z == 2 * x + s // 2
    of_root = (z // 2, 2 * (z % 2) + core)
    apart = 2 * ((x + of_root[0]) % 2) + (s // 2 + of_root[1] // 2) % 2

    def out_copy(index, target, source=None):
        landing = out_buf.at[core]
        return copy(landing if source is None else source, landing, (osend, orecv), index, target)

    for layer in (0, 1):

        @pl.when(root & (x == layer))
        def _():
            out_copy(1, beside, by_layer[layer][3]).start()
            out_copy(2, partner, by_layer[1 - layer][3]).start()
            out_copy(3, across, by_layer[1 - layer][3]).start()
            out_buf[core] = by_layer[layer][3][...]

    for apart_by in (1, 2, 3):

        @pl.when(apart == apart_by)
        def _():
            out_copy(apart_by, beside).wait_recv()

    out_copy(0, sibling).start()

    turn((0,))
    far = (x, (s + 2) % 4)
    far_turned = (1 - x, (s + 2) % 4)
    for index in (1, 2, 0):
        piece(index, 0, far, beside).wait_recv()
        piece(index, 5, far, sibling).start()
    for index in (1, 2, 0):
        piece(index, 3, far_turned, beside).wait_recv()
        piece(index, 6, far_turned, sibling).start()
    twin = sibling[1]
    far_twin = (twin + 2) % 4
    for index in range(3):
        piece(index, 1, (x, twin), sibling).wait_recv()
        piece(index, 4, (1 - x, twin), sibling).wait_recv()
        piece(index, 5, (x, far_twin), sibling).wait_recv()
        piece(index, 6, (1 - x, far_twin), sibling).wait_recv()
    other_out = out_buf.at[1 - core]
    copy(other_out, other_out, (osend, orecv), 0, sibling).wait_recv()
    for index in range(7):
        dx, ds = flips[index]
        slot = plane_buf.at[((x + dx) % 2) * 4 + (s + 4 - ds) % 4]
        copy(slot, slot, (ssend, srecv), index, plane[index]).wait_recv()
    for index in (0, 1):
        copy(rows_buf, rows_buf, (rsend, rrecv), index, partner).wait()
    for index in range(7):
        to_plane(index).wait_send()
    for dz in (1, 2, 3):
        to_plane_of(dz).wait_send()
    for index in range(3):
        for kind in range(7):
            piece(index, kind, mine, sibling).wait_send()
    out_copy(0, sibling).wait_send()

    @pl.when(root)
    def _():
        for index in (1, 2, 3):
            out_copy(index, sibling).wait_send()


def kernel_call(kernel, number, operands, outs, scratch, spaces=None):
    vmem = pl.BlockSpec(memory_space=pltpu.VMEM)
    spaces = spaces or [pltpu.VMEM] * len(outs)
    return pl.pallas_call(
        kernel,
        out_shape=outs,
        in_specs=[vmem] * len(operands),
        out_specs=[pl.BlockSpec(memory_space=space) for space in spaces],
        scratch_shapes=scratch,
        compiler_params=pltpu.CompilerParams(
            collective_id=number, has_side_effects=True, vmem_limit_bytes=58 * 2**20
        ),
    )(*operands)


def pairs_of(*sizes):
    return [pltpu.SemaphoreType.DMA(size) for size in sizes for _ in range(2)]


def scatter_scratch(length):
    size = length // 8
    return [
        pltpu.VMEM((2, length, D), BF),
        pltpu.VMEM((2, 4, size, D), BF),
        pltpu.VMEM((2, 3, size, D), BF),
        pltpu.VMEM((2, 3, size, D), BF),
        *pairs_of((2, 7), (2, 7)),
    ]


def forward_call(number, *operands):
    inputs, small, _, w_mix, _, _, w_down, *_ = operands
    count, _, tokens, _ = inputs.shape
    depth, length = w_mix.shape[1], 4 * tokens
    unit = w_down.shape[1] // 8
    padded = -(-unit // 32) * 32
    shape = jax.ShapeDtypeStruct
    outs = ForwardOut(
        rows=shape((count, length // 8, D), BF),
        gains=shape((2, 2, D), F32),
        persist=shape((2, 2, 16, HD), BF),
        rates=shape((2, 8, HD), F32),
    )
    kept = Kept(
        normed=shape((count, length, D), BF),
        mix=shape((4, depth, 4 * HD), BF),
        out=shape((HD, D), BF),
        gu=shape((4, depth, 8 * padded), BF),
        down=shape((4, padded, D), BF),
        qkv=shape((count, length, 3 * HD), BF),
        gate=shape((count, length, HD), F32),
        recalled=shape((count, length, HD), BF),
        combined=shape((count, length, HD), BF),
        mid=shape((count, length // 8, D), F32),
        normed_two=shape((count, length, D), BF),
        gate_up=shape((count, length, 8 * padded), F32),
        hidden=shape((count, length, 4 * padded), BF),
        out_rows=shape((count, length // 8, D), BF),
    )
    scratch = [pltpu.VMEM(part.shape, part.dtype) for part in (*kept, *kept)]
    scratch += scatter_scratch(length)[:6]
    scratch += [
        pltpu.VMEM((2, 4, 8, HD), F32),
        pltpu.VMEM((2, 4) + small.shape, F32),
        pltpu.VMEM((depth, 4 * HD), BF),
        pltpu.VMEM((depth, 8 * padded), BF),
        pltpu.VMEM((padded, D), BF),
        *pairs_of((7,), (7,), (4,), (2, 7), (6, 4), (2, 2)),
        pltpu.SemaphoreType.DMA((2, len(kept))),
    ]
    kernel = functools.partial(forward_kernel, unit)
    specs = [pltpu.VMEM] * len(outs) + [pl.ANY] * (2 * len(kept))
    found = kernel_call(kernel, number, operands, [*outs, *kept, *kept], scratch, specs)
    own, found = found[: len(outs)], found[len(outs) :]
    return (
        named(ForwardOut._fields, own),
        named(Kept._fields, found[: len(kept)]),
        named(Kept._fields, found[len(kept) :]),
    )


def backward_call(number, layer, given):
    count, length, _ = given.normed.shape
    half = 4 * given.down.shape[1]
    last = layer == 0
    depth = D // 4
    shape = jax.ShapeDtypeStruct
    outs = dict(
        grad_mix=shape((4, depth, 4 * HD), BF),
        grad_out=shape((HD, D), BF),
        gain_sums=shape((2, D), F32),
        grad_persist=shape(given.persist.shape[1:], F32),
        grad_rate=shape((1, length), F32),
        gu_sum=shape((depth, 2 * half), BF),
        down_sum=shape((half // 4, D), BF),
        grad_h=shape((count, length // 8, D), BF),
    )
    ins = BackwardIn._fields
    if last:
        ins += EarlyIn._fields
        outs |= dict(mix_sum=shape((depth, 4 * HD), BF), out_sum=shape((HD, D), BF))
    else:
        outs |= dict(grad_next=shape((count, length, D), BF))
    scratch = scatter_scratch(length) + [
        pltpu.VMEM((count, length, 2 * half), BF),
        pltpu.VMEM((count, length, 4 * HD), BF),
        pltpu.VMEM((length, HD), F32),
        pltpu.VMEM((length, HD), F32),
        pltpu.VMEM((4, depth, 2 * half), BF),
        pltpu.VMEM((4, half // 4, D), BF),
        pltpu.VMEM((count, length, D), BF),
        pltpu.VMEM((count, length // 8, D), F32),
        pltpu.VMEM((4, depth, 2 * half), BF),
        pltpu.VMEM((4, half // 4, D), BF),
        *pairs_of((3, 4)),
    ]
    if last:
        scratch += [
            pltpu.VMEM((4, depth, 4 * HD), BF),
            pltpu.VMEM((2, HD, D), BF),
            *pairs_of((2,)),
        ]
    kernel = functools.partial(backward_layer, layer, ins, tuple(outs))
    operands = [getattr(given, name) for name in ins]
    return named(outs, kernel_call(kernel, number, operands, list(outs.values()), scratch))


def final_call(number, by_layer, small):
    operands = (*by_layer[0], *by_layer[1], small)
    mix, gu, down, out, *rows = by_layer[1]
    outs = [jax.ShapeDtypeStruct((2, 4) + part.shape, BF) for part in (mix, gu, down)]
    outs.append(jax.ShapeDtypeStruct((2,) + out.shape, BF))
    outs += [jax.ShapeDtypeStruct(part.shape, BF) for part in rows]
    outs.append(jax.ShapeDtypeStruct((8,) + small.shape[1:], F32))
    scratch = [
        pltpu.VMEM((3,) + small.shape[1:], F32),
        pltpu.VMEM(mix.shape, BF),
        pltpu.VMEM(out.shape, BF),
        pltpu.VMEM((4,) + mix.shape, BF),
        pltpu.VMEM((2,) + out.shape, BF),
        *pairs_of((3, 7), (4,), (2,), (3,), (7,), (4,), (2,)),
    ]
    return kernel_call(final_kernel, number, operands, outs, scratch)


def assemble_kernel(unit, mix_buf, gu_buf, down_buf, mix_ref, gu_ref, down_ref):
    padded = down_buf.shape[2]
    half = gu_buf.shape[3] // 2
    for which in range(8):
        slot = (which // 4, which % 4)
        mix = mix_buf[slot].astype(F32)
        for kind in range(4):
            begin = kind * D + which * HD
            mix_ref[0, :, begin : begin + HD] = mix[:, kind * HD : (kind + 1) * HD]
        part = gu_buf[slot].astype(F32)
        for side in range(2):
            for owner in range(half // padded):
                begin = side * FF + (owner * 8 + which) * unit
                source = side * half + owner * padded
                gu_ref[0, :, begin : begin + unit] = part[:, source : source + unit]
    for pair in range(2):
        down = down_buf[0, pair].astype(F32)
        down_ref[0, pair * unit : (pair + 1) * unit, :] = down[:unit]


def assemble_call(unit, mix_buf, gu_buf, down_buf):
    depth, padded = mix_buf.shape[2], down_buf.shape[2]
    rows = depth // 4
    return pl.pallas_call(
        functools.partial(assemble_kernel, unit),
        grid=(4,),
        out_shape=[
            jax.ShapeDtypeStruct((1, depth, 4 * D), F32),
            jax.ShapeDtypeStruct((1, depth, 2 * FF), F32),
            jax.ShapeDtypeStruct((1, 8 * unit, D), F32),
        ],
        in_specs=[
            pl.BlockSpec((2, 4, rows, 4 * HD), lambda i: (0, 0, i, 0)),
            pl.BlockSpec((2, 4, rows, gu_buf.shape[3]), lambda i: (0, 0, i, 0)),
            pl.BlockSpec((1, 2, padded, D), lambda i: (i // 2, i % 2, 0, 0)),
        ],
        out_specs=[
            pl.BlockSpec((1, rows, 4 * D), lambda i: (0, i, 0)),
            pl.BlockSpec((1, rows, 2 * FF), lambda i: (0, i, 0)),
            pl.BlockSpec((1, 2 * unit, D), lambda i: (0, i, 0)),
        ],
        compiler_params=pltpu.CompilerParams(vmem_limit_bytes=40 * 2**20),
    )(mix_buf, gu_buf, down_buf)


def tensor_parallel(
    inputs, segment_ids, cotangent, w_mix, w_out, w_gu, w_down, norm_gains, persist_kv, memory_decay
):
    x, s, z = here()
    nx, ns, nz = (lax.axis_size(a) for a in ("section", "seq", "shard"))
    width = nx * ns
    mine = x * ns + s
    other = (1 - x) * ns + s
    first = x == 0
    count, _, tokens, _ = inputs.shape
    length = tokens * ns
    size = length // width
    depth = w_mix.shape[1]
    unit = w_down.shape[1] // (nx * ns)

    def layers(own, got):
        return (jnp.where(first, own, got), jnp.where(first, got, own))

    small = persist_kv[0].reshape(-1, 2, HD).transpose(1, 0, 2).reshape(-1, HD).astype(F32)
    rates = jnp.broadcast_to(memory_decay[0][:, None, None], (2, 8, HD)).reshape(-1, HD)
    gain_rows = norm_gains[0].astype(F32).T.reshape(-1, HD)
    gain_rows = jnp.pad(gain_rows, ((0, 8 - gain_rows.shape[0]), (0, 0)))
    small = jnp.concatenate([small, rates], 0)
    segments = (segment_ids[:, 0, :, None], segment_ids)
    ready, below, above = forward_call(
        1, inputs, small, gain_rows, w_mix, w_out, w_gu, w_down, *segments
    )
    shared = dict(
        gains=ready.gains,
        persist=ready.persist,
        rates=ready.rates,
        seg_rows=segments[0],
        seg_cols=segments[1],
    )
    lower = dict(shared, rows=ready.rows)
    upper = dict(shared, rows=below.out_rows)
    outputs = [below.out_rows, above.out_rows]
    cot_full = lax.all_gather(cotangent[:, 0], "seq", axis=1, tiled=True)
    cot_rows = lax.dynamic_slice_in_dim(cotangent[:, 0], x * size, size, 1)
    upper |= dict(vars(above), grad_full=cot_full, grad_rows=cot_rows)
    later = backward_call(3, 1, types.SimpleNamespace(**upper))
    lower |= dict(
        vars(below),
        grad_full=later.grad_next,
        grad_rows=later.grad_h,
        early_mix=later.grad_mix,
        early_out=later.grad_out,
    )
    earlier = backward_call(4, 0, types.SimpleNamespace(**lower))
    by_layer = [
        (earlier.grad_mix, earlier.gu_sum, earlier.down_sum, earlier.grad_out),
        (earlier.mix_sum, later.gu_sum, later.down_sum, earlier.out_sum),
    ]
    both = (earlier, later)
    grads = [found.grad_h for found in both]
    gain_sums = [found.gain_sums for found in both]

    memory_all = jnp.stack([found.grad_persist for found in both], 0).reshape(-1, HD)
    rate_all = jnp.stack([jnp.sum(found.grad_rate) for found in both])
    rate_all = jnp.pad(rate_all[None], ((0, 7), (0, HD - 2)))
    gain_all = jnp.stack(gain_sums, 0).reshape(4, nz, 2, HD).transpose(1, 0, 2, 3)
    memory_all = jnp.concatenate([memory_all, rate_all], 0)
    small = jnp.concatenate(
        [jnp.broadcast_to(memory_all[None], (nz,) + memory_all.shape), gain_all.reshape(nz, 8, HD)],
        1,
    )
    by_layer = [(*by_layer[layer], outputs[layer], grads[layer]) for layer in range(2)]
    mix_all, gu_all, down_all, out_all, rows_got, grads_got, plane_all = final_call(
        5, by_layer, small
    )

    def whole_rows(of_layer, got):
        both = layers(jnp.where(first, of_layer[0], of_layer[1]), got)
        return jnp.concatenate(both, 1)[None, :, None]

    section_out = whole_rows(outputs, rows_got)
    section_grad = whole_rows(grads, grads_got).astype(F32)
    grad_mix, grad_gu, grad_down = assemble_call(unit, mix_all, gu_all, down_all)
    grad_out = out_all.astype(F32).reshape(1, 2 * HD, D)

    heads_of = lax.dynamic_slice_in_dim(plane_all, 2 * s, 2, 0)
    of_section = lax.dynamic_index_in_dim(
        heads_of[:, :64].reshape(2, 2, 2, -1, HD), x, 1, keepdims=False
    )
    grad_persist = of_section.transpose(1, 2, 0, 3).reshape(1, 2, -1, 2 * HD)
    grad_rate = lax.dynamic_index_in_dim(heads_of[:, 64], x, 1, keepdims=False)[None]
    gain_all = jnp.sum(plane_all[:, 72:], 0).reshape(2, 2, depth)
    grad_gain = lax.dynamic_index_in_dim(gain_all, x, 0).transpose(0, 2, 1)
    return (
        section_out,
        section_grad,
        grad_mix,
        grad_out,
        grad_gu,
        grad_down,
        grad_gain,
        grad_persist,
        grad_rate,
    )


def solution(mesh):
    sizes = mesh.shape
    planar = (sizes["section"], sizes["seq"]) == (2, 4)
    placed = (
        P(None, "shard", "seq", None),
        P(None, "shard", None),
        P(None, "shard", "seq", None),
        P("section", "shard", None),
        P("section", "shard", None),
        P("section", "shard", None),
        P("section", "shard", None),
        P("section", "shard", None),
        P("section", None, None, "seq"),
        P("section", "seq"),
    )
    return jax.shard_map(
        tensor_parallel if planar else on_device,
        mesh=mesh,
        in_specs=placed,
        out_specs=(
            P("section", None, "shard", "seq", None),
            P("section", None, "shard", "seq", None),
            P("section", "shard", None),
            P("section", "shard", None),
            P("section", "shard", None),
            P("section", "shard", None),
            P("section", "shard", None),
            P("section", None, None, "seq"),
            P("section", "seq"),
        ),
        check_vma=False,
    )
```

```python
import functools
import math
import types
from typing import Any, NamedTuple

import jax
import jax.numpy as jnp
from jax import lax
from jax.experimental import pallas as pl
from jax.experimental.pallas import tpu as pltpu
from jax.sharding import PartitionSpec as P

D = 1024
H = 8
HD = 128
FF = 2816


def shifted(value, axis, by):
    size = lax.axis_size(axis)
    pairs = [(i, i + by) for i in range(size) if 0 <= i + by < size]
    return lax.ppermute(value, axis, pairs)


def as_sent(value):
    return jax.tree.map(lambda a: a.astype(jnp.bfloat16) if a.dtype == jnp.float32 else a, value)


def rms_scale(values):
    return lax.rsqrt(jnp.mean(values * values, axis=-1, keepdims=True) + 1e-06)


def norm_back(grad_normed, scaled, inverse, gain):
    grad_scaled = grad_normed * gain
    grad_rows = inverse * (
        grad_scaled - scaled * jnp.mean(grad_scaled * scaled, axis=-1, keepdims=True)
    )
    return (grad_rows, jnp.sum(grad_normed * scaled, axis=0))


def block_terms(query_rows, key_rows, seg_ids, begin, reach, rate):
    inner = jnp.dot(query_rows, key_rows.T, preferred_element_type=jnp.float32)
    row_places = begin + jnp.arange(reach - begin, dtype=jnp.int32)
    col_places = jnp.arange(reach, dtype=jnp.int32)
    allowed = (seg_ids[begin:reach][:, None] == seg_ids[:reach][None, :]) & (
        col_places[None, :] <= row_places[:, None]
    )
    distance = jnp.maximum(row_places[:, None] - col_places[None, :], 0).astype(jnp.float32)
    decay_w = jnp.where(allowed, jnp.exp(-rate * distance), jnp.float32(0.0))
    return (inner, allowed, decay_w, distance)


def head_forward(query, keys, values, pkeys, pvalues, rate, seg_ids):
    length, width = query.shape
    block = min(512, length)
    scale = 1.0 / math.sqrt(width)
    attn_parts, memory_parts, lse_parts = ([], [], [])
    for begin in range(0, length, block):
        reach = begin + block
        query_rows = query[begin:reach]
        inner, allowed, decay_w, distance = block_terms(
            query_rows, keys[:reach], seg_ids, begin, reach, rate
        )
        per_scores = jnp.dot(query_rows, pkeys.T, preferred_element_type=jnp.float32) * scale
        seq_scores = jnp.where(allowed, inner * scale, -jnp.inf)
        top = jnp.maximum(
            jnp.max(per_scores, axis=1, keepdims=True), jnp.max(seq_scores, axis=1, keepdims=True)
        )
        per_exp = jnp.exp(per_scores - top)
        seq_exp = jnp.exp(seq_scores - top)
        denom = jnp.sum(per_exp, axis=1, keepdims=True) + jnp.sum(seq_exp, axis=1, keepdims=True)
        attended = jnp.dot(
            (per_exp / denom).astype(jnp.bfloat16), pvalues, preferred_element_type=jnp.float32
        )
        attended = attended + jnp.dot(
            (seq_exp / denom).astype(jnp.bfloat16),
            values[:reach],
            preferred_element_type=jnp.float32,
        )
        memory_w = (inner * decay_w * (1.0 / width)).astype(jnp.bfloat16)
        recalled = jnp.dot(memory_w, values[:reach], preferred_element_type=jnp.float32)
        attn_parts.append(attended)
        memory_parts.append(recalled)
        lse_parts.append(top[:, 0] + jnp.log(denom[:, 0]))
    return (
        jnp.concatenate(attn_parts, 0),
        jnp.concatenate(memory_parts, 0),
        jnp.concatenate(lse_parts, 0),
    )


def head_backward(query, keys, values, pkeys, pvalues, rate, seg_ids, lse, grad_attn, grad_memory):
    length, width = query.shape
    block = min(512, length)
    scale = 1.0 / math.sqrt(width)
    query_grads = []
    grad_keys = jnp.zeros((length, width), jnp.float32)
    grad_values = jnp.zeros((length, width), jnp.float32)
    grad_pkeys = jnp.zeros(pkeys.shape, jnp.float32)
    grad_pvalues = jnp.zeros(pvalues.shape, jnp.float32)
    grad_rate = jnp.float32(0.0)
    for begin in range(0, length, block):
        reach = begin + block
        query_rows = query[begin:reach]
        key_rows = keys[:reach]
        value_rows = values[:reach]
        inner, allowed, decay_w, distance = block_terms(
            query_rows, key_rows, seg_ids, begin, reach, rate
        )
        per_scores = jnp.dot(query_rows, pkeys.T, preferred_element_type=jnp.float32) * scale
        seq_scores = jnp.where(allowed, inner * scale, -jnp.inf)
        row_lse = lse[begin:reach][:, None]
        per_prob = jnp.exp(per_scores - row_lse)
        seq_prob = jnp.exp(seq_scores - row_lse)
        attn_rows = grad_attn[begin:reach]
        memory_rows = grad_memory[begin:reach]
        per_dp = jnp.dot(attn_rows, pvalues.T, preferred_element_type=jnp.float32)
        seq_dp = jnp.dot(attn_rows, value_rows.T, preferred_element_type=jnp.float32)
        delta = jnp.sum(per_prob * per_dp, axis=1, keepdims=True) + jnp.sum(
            seq_prob * seq_dp, axis=1, keepdims=True
        )
        per_ds = (per_prob * (per_dp - delta)).astype(jnp.bfloat16)
        seq_ds = (seq_prob * (seq_dp - delta)).astype(jnp.bfloat16)
        rows_grad = (
            jnp.dot(per_ds, pkeys, preferred_element_type=jnp.float32)
            + jnp.dot(seq_ds, key_rows, preferred_element_type=jnp.float32)
        ) * scale
        grad_pkeys = (
            grad_pkeys
            + jnp.einsum("qk,qd->kd", per_ds, query_rows, preferred_element_type=jnp.float32)
            * scale
        )
        grad_pvalues = grad_pvalues + jnp.einsum(
            "qk,qd->kd",
            per_prob.astype(jnp.bfloat16),
            attn_rows,
            preferred_element_type=jnp.float32,
        )
        key_part = (
            jnp.einsum("qk,qd->kd", seq_ds, query_rows, preferred_element_type=jnp.float32) * scale
        )
        value_part = jnp.einsum(
            "qk,qd->kd",
            seq_prob.astype(jnp.bfloat16),
            attn_rows,
            preferred_element_type=jnp.float32,
        )
        memory_w = (inner * decay_w * (1.0 / width)).astype(jnp.bfloat16)
        grad_mw = jnp.dot(memory_rows, value_rows.T, preferred_element_type=jnp.float32)
        value_part = value_part + jnp.einsum(
            "qk,qd->kd", memory_w, memory_rows, preferred_element_type=jnp.float32
        )
        grad_inner = (grad_mw * decay_w * (1.0 / width)).astype(jnp.bfloat16)
        rows_grad = rows_grad + jnp.dot(grad_inner, key_rows, preferred_element_type=jnp.float32)
        key_part = key_part + jnp.einsum(
            "qk,qd->kd", grad_inner, query_rows, preferred_element_type=jnp.float32
        )
        grad_rate = grad_rate - jnp.sum(grad_mw * inner * decay_w * (1.0 / width) * distance)
        grad_keys = grad_keys.at[:reach].add(key_part)
        grad_values = grad_values.at[:reach].add(value_part)
        query_grads.append(rows_grad)
    return (
        jnp.concatenate(query_grads, 0),
        grad_keys,
        grad_values,
        grad_pkeys,
        grad_pvalues,
        grad_rate,
    )


def layer_forward(rows_in, seg_ids, full, pkv, rates):
    mix_w, out_w, gu_w, down_w, gains = full
    tokens = rows_in.shape[0]
    gain_one = gains[:, 0].astype(jnp.float32)
    gain_two = gains[:, 1].astype(jnp.float32)
    inverse_one = rms_scale(rows_in)
    scaled_one = rows_in * inverse_one
    normed = (scaled_one * gain_one).astype(jnp.bfloat16)
    proj = jnp.dot(normed, mix_w, preferred_element_type=jnp.float32)
    qkv = proj[:, : 3 * D].astype(jnp.bfloat16).reshape(tokens, 3, H, HD)
    gate = jax.nn.sigmoid(proj[:, 3 * D :])
    grouped = lax.all_to_all(qkv, "seq", split_axis=2, concat_axis=0, tiled=True)
    attn_heads, memory_heads, lse_heads = ([], [], [])
    for head in range(grouped.shape[2]):
        cols = slice(head * HD, (head + 1) * HD)
        attended, recalled, lse = head_forward(
            grouped[:, 0, head],
            grouped[:, 1, head],
            grouped[:, 2, head],
            pkv[0][:, cols],
            pkv[1][:, cols],
            rates[head],
            seg_ids,
        )
        attn_heads.append(attended)
        memory_heads.append(recalled)
        lse_heads.append(lse)
    mixed = jnp.stack([jnp.stack(attn_heads, 1), jnp.stack(memory_heads, 1)], 1).astype(
        jnp.bfloat16
    )
    returned = lax.all_to_all(mixed, "seq", split_axis=0, concat_axis=2, tiled=True)
    attended = returned[:, 0].reshape(tokens, D).astype(jnp.float32)
    recalled = returned[:, 1].reshape(tokens, D).astype(jnp.float32)
    combined = (attended + gate * recalled).astype(jnp.bfloat16)
    mid = rows_in + jnp.dot(combined, out_w, preferred_element_type=jnp.float32)
    inverse_two = rms_scale(mid)
    scaled_two = mid * inverse_two
    normed_two = (scaled_two * gain_two).astype(jnp.bfloat16)
    gate_up = jnp.dot(normed_two, gu_w, preferred_element_type=jnp.float32)
    hidden = (jax.nn.silu(gate_up[:, :FF]) * gate_up[:, FF:]).astype(jnp.bfloat16)
    result = mid + jnp.dot(hidden, down_w, preferred_element_type=jnp.float32)
    kept = (
        seg_ids,
        inverse_one,
        scaled_one,
        normed,
        grouped,
        jnp.stack(lse_heads, 1),
        gate,
        recalled,
        combined,
        inverse_two,
        scaled_two,
        normed_two,
        gate_up,
        hidden,
    )
    return (result, kept)


def layer_backward(grad_out, kept, full, pkv, rates):
    (
        seg_ids,
        inverse_one,
        scaled_one,
        normed,
        grouped,
        lse_all,
        gate,
        recalled,
        combined,
        inverse_two,
        scaled_two,
        normed_two,
        gate_up,
        hidden,
    ) = kept
    mix_w, out_w, gu_w, down_w, gains = full
    tokens = grad_out.shape[0]
    gain_one = gains[:, 0].astype(jnp.float32)
    gain_two = gains[:, 1].astype(jnp.float32)
    grad_f = grad_out.astype(jnp.bfloat16)
    grad_down = jnp.einsum("tf,td->fd", hidden, grad_f, preferred_element_type=jnp.float32)
    grad_hidden = jnp.dot(grad_f, down_w.T, preferred_element_type=jnp.float32)
    gate_part = gate_up[:, :FF]
    up_part = gate_up[:, FF:]
    sig_part = jax.nn.sigmoid(gate_part)
    grad_gate_part = grad_hidden * up_part * sig_part * (1.0 + gate_part * (1.0 - sig_part))
    grad_up_part = grad_hidden * gate_part * sig_part
    grad_gate_up = jnp.concatenate([grad_gate_part, grad_up_part], 1).astype(jnp.bfloat16)
    grad_gu = jnp.einsum("td,tf->df", normed_two, grad_gate_up, preferred_element_type=jnp.float32)
    grad_normed_two = jnp.dot(grad_gate_up, gu_w.T, preferred_element_type=jnp.float32)
    grad_mid_norm, grad_gain_two = norm_back(grad_normed_two, scaled_two, inverse_two, gain_two)
    grad_mid = grad_out + grad_mid_norm
    grad_branch = grad_mid.astype(jnp.bfloat16)
    grad_out_w = jnp.einsum("td,te->de", combined, grad_branch, preferred_element_type=jnp.float32)
    grad_combined = jnp.dot(grad_branch, out_w.T, preferred_element_type=jnp.float32)
    grad_attended = grad_combined.astype(jnp.bfloat16).reshape(tokens, H, HD)
    grad_recalled = (grad_combined * gate).astype(jnp.bfloat16).reshape(tokens, H, HD)
    grad_gate_pre = grad_combined * recalled * gate * (1.0 - gate)
    outgoing = jnp.stack([grad_attended, grad_recalled], 1)
    headward = lax.all_to_all(outgoing, "seq", split_axis=2, concat_axis=0, tiled=True)
    head_grads, pkey_grads, pvalue_grads, rate_grads = ([], [], [], [])
    for head in range(grouped.shape[2]):
        cols = slice(head * HD, (head + 1) * HD)
        dq, dk, dv, dpk, dpv, drate = head_backward(
            grouped[:, 0, head],
            grouped[:, 1, head],
            grouped[:, 2, head],
            pkv[0][:, cols],
            pkv[1][:, cols],
            rates[head],
            seg_ids,
            lse_all[:, head],
            headward[:, 0, head],
            headward[:, 1, head],
        )
        head_grads.append(jnp.stack([dq, dk, dv], 1))
        pkey_grads.append(dpk)
        pvalue_grads.append(dpv)
        rate_grads.append(drate)
    grads_heads = jnp.stack(head_grads, 2).astype(jnp.bfloat16)
    tokenward = lax.all_to_all(grads_heads, "seq", split_axis=0, concat_axis=2, tiled=True)
    grad_proj = jnp.concatenate(
        [tokenward.reshape(tokens, 3 * D), grad_gate_pre.astype(jnp.bfloat16)], 1
    )
    grad_mix = jnp.einsum("td,tf->df", normed, grad_proj, preferred_element_type=jnp.float32)
    grad_normed = jnp.dot(grad_proj, mix_w.T, preferred_element_type=jnp.float32)
    grad_in_norm, grad_gain_one = norm_back(grad_normed, scaled_one, inverse_one, gain_one)
    grad_rows = grad_mid + grad_in_norm
    weight_terms = (
        grad_mix,
        grad_out_w,
        grad_gu,
        grad_down,
        jnp.stack([grad_gain_one, grad_gain_two], 1),
    )
    memory_terms = (
        jnp.stack([jnp.concatenate(pkey_grads, 1), jnp.concatenate(pvalue_grads, 1)], 0),
        jnp.stack(rate_grads, 0),
    )
    return (weight_terms, memory_terms, grad_rows)


def on_device(
    inputs, segment_ids, cotangent, w_mix, w_out, w_gu, w_down, norm_gains, persist_kv, memory_decay
):
    first = lax.axis_index("section") == 0
    own_weights = (w_mix[0], w_out[0], w_gu[0], w_down[0], norm_gains[0])
    pkv = persist_kv[0]
    rates = memory_decay[0]
    count = inputs.shape[0]
    tokens = inputs.shape[2]
    zero_rows = jnp.zeros((tokens, D), jnp.float32)
    received = jnp.zeros((tokens, D), jnp.bfloat16)
    kept_ticks, out_ticks = ([], [])
    for tick in range(count + 1):
        own_rows = inputs[tick, 0].astype(jnp.float32) if tick < count else zero_rows
        layer_in = jnp.where(first, own_rows, received.astype(jnp.float32))
        seg_ids = jnp.where(
            first, segment_ids[min(tick, count - 1), 0], segment_ids[max(tick - 1, 0), 0]
        )
        full = (
            lax.all_gather(own_weights[0], "shard", axis=0, tiled=True),
            lax.all_gather(own_weights[1], "shard", axis=0, tiled=True),
            lax.all_gather(own_weights[2], "shard", axis=0, tiled=True),
            lax.all_gather(own_weights[3], "shard", axis=0, tiled=True),
            lax.all_gather(own_weights[4], "shard", axis=0, tiled=True),
        )
        result, kept = layer_forward(layer_in, seg_ids, full, pkv, rates)
        result_low = result.astype(jnp.bfloat16)
        out_ticks.append(result_low)
        kept_ticks.append(kept)
        if tick < count:
            received = shifted(result_low, "section", 1)
    grad_weights = (
        jnp.zeros((D, 4 * D), jnp.float32),
        jnp.zeros((D, D), jnp.float32),
        jnp.zeros((D, 2 * FF), jnp.float32),
        jnp.zeros((FF, D), jnp.float32),
        jnp.zeros((D, 2), jnp.float32),
    )
    grad_memory = (
        jnp.zeros((2,) + pkv.shape[1:], jnp.float32),
        jnp.zeros(rates.shape, jnp.float32),
    )
    back_received = jnp.zeros((tokens, D), jnp.bfloat16)
    grad_ticks = []
    for tick in range(count + 1):
        lower = max(tick - 1, 0)
        upper = min(tick + 1, count)
        kept = jax.tree.map(
            lambda early, late: jnp.where(first, early, late), kept_ticks[lower], kept_ticks[upper]
        )
        given = cotangent[tick, 0].astype(jnp.float32) if tick < count else zero_rows
        grad_out = jnp.where(first, back_received.astype(jnp.float32), given)
        full = (
            lax.all_gather(own_weights[0], "shard", axis=0, tiled=True),
            lax.all_gather(own_weights[1], "shard", axis=0, tiled=True),
            lax.all_gather(own_weights[2], "shard", axis=0, tiled=True),
            lax.all_gather(own_weights[3], "shard", axis=0, tiled=True),
            lax.all_gather(own_weights[4], "shard", axis=0, tiled=True),
        )
        weight_terms, memory_terms, grad_rows = layer_backward(grad_out, kept, full, pkv, rates)
        grad_weights = jax.tree.map(jnp.add, grad_weights, weight_terms)
        grad_memory = jax.tree.map(jnp.add, grad_memory, memory_terms)
        grad_ticks.append(grad_rows)
        if tick < count:
            back_received = shifted(grad_rows.astype(jnp.bfloat16), "section", -1)
    section_out = jnp.stack(
        [jnp.where(first, out_ticks[batch], out_ticks[batch + 1]) for batch in range(count)], 0
    )
    section_grad = jnp.stack(
        [
            jnp.where(
                first,
                grad_ticks[batch + 1],
                grad_ticks[batch].astype(jnp.bfloat16).astype(jnp.float32),
            )
            for batch in range(count)
        ],
        0,
    )
    shares = jax.tree.map(
        lambda part: part.astype(jnp.float32),
        lax.psum_scatter(as_sent(grad_weights), "shard", scatter_dimension=0, tiled=True),
    )
    shares = jax.tree.map(lambda part: part.astype(jnp.float32), lax.psum(as_sent(shares), "seq"))
    memory_sums = lax.psum(grad_memory, "shard")
    return (
        section_out.reshape(1, count, 1, tokens, D),
        section_grad.reshape(1, count, 1, tokens, D),
        shares[0][None],
        shares[1][None],
        shares[2][None],
        shares[3][None],
        shares[4][None],
        memory_sums[0][None],
        memory_sums[1][None],
    )


MESH = pl.DeviceIdType.MESH
BF = jnp.bfloat16
F32 = jnp.float32


def here():
    return (lax.axis_index("section"), lax.axis_index("seq"), lax.axis_index("shard"))


def peer(place, chip, flip):
    x, s, z = place
    if chip % 2:
        x = 1 - x
    if chip // 2:
        s = (s + 2) % 4
    if flip:
        s = s + 1 - 2 * (s % 2)
    return (x, s, z)


def rows_of(device, size):
    x, s, _ = device
    return pl.ds(pl.multiple_of((s * 2 + x) * size, size), size)


class Gather:
    def __init__(self, full, batch, send, recv):
        self.place = here()
        self.full, self.batch, self.send, self.recv = full, batch, send, recv
        self.size = full.shape[1] // 8

    def copy(self, owner, target, sem):
        block = self.full.at[self.batch, rows_of(owner, self.size)]
        return pltpu.make_async_remote_copy(
            src_ref=block,
            dst_ref=block,
            send_sem=self.send.at[self.batch, sem],
            recv_sem=self.recv.at[self.batch, sem],
            device_id=target,
            device_id_type=MESH,
        )

    def start(self, value):
        self.full[self.batch, rows_of(self.place, self.size), :] = value
        for chip in (3, 1, 2, 0):
            self.copy(self.place, peer(self.place, chip, chip == 0), chip).start()

    def forward(self):
        other = peer(self.place, 0, True)
        for chip in (1, 2, 3):
            owner = peer(self.place, chip, False)
            self.copy(owner, owner, chip).wait_recv()
            self.copy(owner, other, 3 + chip).start()

    def finish(self):
        other = peer(self.place, 0, True)
        self.copy(other, other, 0).wait_recv()
        for chip in (1, 2, 3):
            owner = peer(self.place, chip, True)
            self.copy(owner, other, 3 + chip).wait_recv()
        for chip in (0, 1, 2, 3):
            self.copy(self.place, peer(self.place, chip, chip == 0), chip).wait_send()
        for chip in (1, 2, 3):
            self.copy(peer(self.place, chip, False), other, 3 + chip).wait_send()


class Scatter:
    def __init__(self, part, batch, pair, away, near, send, recv):
        self.place = here()
        self.part, self.batch, self.pair, self.away, self.near = part, batch, pair, away, near
        self.send, self.recv = send, recv
        self.size = part.shape[1] // 8

    def to_pair(self, chip):
        return pltpu.make_async_remote_copy(
            src_ref=self.part.at[self.batch, rows_of(peer(self.place, chip, True), self.size)],
            dst_ref=self.pair.at[self.batch, chip],
            send_sem=self.send.at[self.batch, chip],
            recv_sem=self.recv.at[self.batch, chip],
            device_id=peer(self.place, 0, True),
            device_id_type=MESH,
        )

    def to_chip(self, chip):
        return pltpu.make_async_remote_copy(
            src_ref=self.away.at[self.batch, chip - 1],
            dst_ref=self.near.at[self.batch, chip - 1],
            send_sem=self.send.at[self.batch, 3 + chip],
            recv_sem=self.recv.at[self.batch, 3 + chip],
            device_id=peer(self.place, chip, False),
            device_id_type=MESH,
        )

    def start(self):
        for chip in (3, 1, 2, 0):
            self.to_pair(chip).start()

    def chip_sum(self, chip):
        self.to_pair(chip).wait_recv()
        own = self.part[self.batch, rows_of(peer(self.place, chip, False), self.size), :]
        return own.astype(F32) + self.pair[self.batch, chip].astype(F32)

    def forward(self):
        for chip in (3, 1, 2):
            self.away[self.batch, chip - 1] = self.chip_sum(chip).astype(BF)
            self.to_chip(chip).start()

    def finish(self):
        total = self.chip_sum(0)
        for chip in (1, 2, 3):
            self.to_chip(chip).wait_recv()
            total = total + self.near[self.batch, chip - 1].astype(F32)
        for chip in (0, 1, 2, 3):
            self.to_pair(chip).wait_send()
        for chip in (1, 2, 3):
            self.to_chip(chip).wait_send()
        return total


class Column:
    def __init__(self, send, recv):
        self.place = here()
        self.send, self.recv = send, recv

    def copy(self, source, landing, sent, received, plane):
        x, s, _ = self.place
        return pltpu.make_async_remote_copy(
            src_ref=source,
            dst_ref=landing,
            send_sem=self.send.at[sent],
            recv_sem=self.recv.at[received],
            device_id=(x, s, plane),
            device_id_type=MESH,
        )

    def at_each(self, body):
        for at in range(4):

            @pl.when(self.place[2] == at)
            def _():
                body(at)


class ColumnSum(Column):
    RELAYED = ((3, 1), None, None, (0, 2))
    DIRECT = ((2, 1), (2, 0), (1, 3), (1, 2))
    SOURCES = ((1, 2), (0, 2, 3), (0, 1, 3), (1, 2))

    def __init__(self, own, slots, out, send, recv):
        super().__init__(send, recv)
        self.own, self.slots, self.out = own, slots, out

    def first(self, at):
        block, plane = self.RELAYED[at]
        return self.copy(self.own.at[block], self.slots.at[plane], at, plane, plane)

    def direct(self, at, plane):
        return self.copy(self.own.at[plane], self.slots.at[at], plane, at, plane)

    def relayed(self, at):
        end = 3 if at == 1 else 0
        return self.copy(self.slots.at[at], self.slots.at[at], end, at, end)

    def start(self):
        def body(at):
            if self.RELAYED[at]:
                self.first(at).start()
            for plane in self.DIRECT[at]:
                self.direct(at, plane).start()

        self.at_each(body)

    def hop(self):
        for at, block in ((1, 3), (2, 0)):

            @pl.when(self.place[2] == at)
            def _():
                self.relayed(at).wait_recv()
                self.slots[at] = (
                    self.slots[at].astype(F32) + self.own[block].astype(F32)
                ).astype(BF)
                self.relayed(at).start()

    def finish(self):
        def body(at):
            total = self.own[at].astype(F32)
            for plane in self.SOURCES[at]:
                self.direct(plane, at).wait_recv()
                total = total + self.slots[plane].astype(F32)
            self.out[...] = total.astype(BF)
            if self.RELAYED[at]:
                self.first(at).wait_send()
            else:
                self.relayed(at).wait_send()
            for plane in self.DIRECT[at]:
                self.direct(at, plane).wait_send()

        self.at_each(body)


class ColumnGather(Column):
    TARGETS = ((2, 1), (3, 2, 0), (0, 1, 3), (1, 2))

    def __init__(self, full, send, recv):
        super().__init__(send, recv)
        self.full = full

    def block(self, at, plane):
        return self.copy(self.full.at[at], self.full.at[at], plane, at, plane)

    def relayed(self, at):
        block, plane = (3, 0) if at == 1 else (0, 3)
        return self.copy(self.full.at[block], self.full.at[block], at, block, plane)

    def start(self):
        def body(at):
            for plane in self.TARGETS[at]:
                self.block(at, plane).start()

        self.at_each(body)

    def hop(self):
        for at in (1, 2):

            @pl.when(self.place[2] == at)
            def _():
                self.relayed(at).wait_recv()
                self.relayed(at).start()

    def finish(self):
        def body(at):
            for plane in range(4):
                if plane != at and (at, plane) not in ((1, 3), (2, 0)):
                    self.block(plane, at).wait_recv()
            for plane in self.TARGETS[at]:
                self.block(at, plane).wait_send()
            if at in (1, 2):
                self.relayed(at).wait_send()

        self.at_each(body)


class Root(Column):
    def __init__(self, send, recv):
        super().__init__(send, recv)
        x, s, z = self.place
        self.root = 2 * x + s // 2
        self.low = self.root < 2
        self.between = jnp.where(self.low, 2, 1)
        self.end = jnp.where(self.low, 3, 0)
        self.is_root = z == self.root


class RootSum(Root):
    def __init__(self, own, slots, out, send, recv):
        super().__init__(send, recv)
        self.own, self.slots, self.out = own, slots, out

    def toward(self, slot, plane, source=None):
        landing = self.slots.at[slot]
        return self.copy(landing if source is None else source, landing, 0, slot, plane)

    def start(self):
        z = self.place[2]

        @pl.when(z == self.end)
        def _():
            self.toward(0, self.between, self.own).start()

        @pl.when((z != self.end) & (z != self.between) & (z != self.root))
        def _():
            self.toward(1, self.root, self.own).start()

    def hop(self):
        @pl.when(self.place[2] == self.between)
        def _():
            self.toward(0, self.root).wait_recv()
            self.slots[0] = (self.slots[0].astype(F32) + self.own[...].astype(F32)).astype(BF)
            self.toward(0, self.root).start()

    def finish(self):
        self.out[...] = self.own[...]

        @pl.when(self.is_root)
        def _():
            total = self.own[...].astype(F32)
            for slot in (0, 1):
                self.toward(slot, self.root).wait_recv()
                total = total + self.slots[slot].astype(F32)
            self.out[...] = total.astype(BF)

        @pl.when(jnp.logical_not(self.is_root))
        def _():
            self.toward(0, self.root).wait_send()


def nn(left, right):
    return jnp.dot(left, right, preferred_element_type=F32)


def nt(left, right):
    return lax.dot_general(left, right, (((1,), (1,)), ((), ())), preferred_element_type=F32)


def tn(left, right):
    return lax.dot_general(left, right, (((0,), (0,)), ((), ())), preferred_element_type=F32)


def flat(ref):
    value = ref[...]
    return value.reshape(-1, value.shape[-1])


def in_blocks(length, size, body):
    def step(index, carry):
        body(pl.ds(pl.multiple_of(index * size, size), size), index * size)
        return carry

    lax.fori_loop(0, length // size, step, 0)


def weights_of_scores(query, keys, pkeys, seg_rows, seg_cols, begin, rate):
    scale = 1.0 / math.sqrt(HD)
    inner = nt(query, keys)
    per_scores = nt(query, pkeys) * scale
    row_places = begin + lax.broadcasted_iota(jnp.int32, inner.shape, 0)
    col_places = lax.broadcasted_iota(jnp.int32, inner.shape, 1)
    allowed = (seg_rows == seg_cols) & (col_places <= row_places)
    distance = jnp.maximum(row_places - col_places, 0).astype(F32)
    decay_w = jnp.where(allowed, jnp.exp(-rate * distance) * (1.0 / HD), 0.0)
    seq_scores = jnp.where(allowed, inner * scale, -jnp.inf)
    top = jnp.maximum(
        jnp.max(per_scores, axis=1, keepdims=True), jnp.max(seq_scores, axis=1, keepdims=True)
    )
    per_exp = jnp.exp(per_scores - top)
    seq_exp = jnp.exp(seq_scores - top)
    denom = jnp.sum(per_exp, axis=1, keepdims=True) + jnp.sum(seq_exp, axis=1, keepdims=True)
    share = 1.0 / denom
    return inner, decay_w, distance, seq_exp * share, per_exp * share


class BackwardIn(NamedTuple):
    grad_full: Any
    grad_rows: Any
    rows: Any
    out_low: Any
    out_high: Any
    gains: Any
    persist: Any
    rates: Any
    seg_rows: Any
    seg_cols: Any


class BackwardOut(NamedTuple):
    mix_buf: Any
    gu_buf: Any
    down_buf: Any
    out_buf: Any
    rows_buf: Any
    grads_buf: Any
    plane_buf: Any
    grad_low: Any
    grad_high: Any


class PlaneScratch(NamedTuple):
    part: Any
    pair: Any
    away: Any
    near: Any
    ssend: Any
    srecv: Any
    gsend: Any
    grecv: Any


class BackwardScratch(NamedTuple):
    grad_gu: Any
    grad_proj: Any
    grad_keys: Any
    grad_values: Any
    branch: Any
    grad_mid: Any
    grad_next: Any
    grad_persist: Any
    grad_rate: Any
    gain_sums: Any
    small: Any
    column_buf: Any
    own_gu: Any
    own_down: Any
    grad_mix: Any
    grad_out: Any
    gu_slots: Any
    down_slots: Any
    mix_slots: Any
    root_slots: Any
    gu_sum: Any
    down_sum: Any
    mix_sum: Any
    out_sum: Any
    csend: Any
    crecv: Any
    hsend: Any
    hrecv: Any
    psend: Any
    precv: Any
    osend: Any
    orecv: Any
    rsend: Any
    rrecv: Any
    zsend: Any
    zrecv: Any
    qsend: Any
    qrecv: Any
    loaded: Any


def fields(*kinds):
    return tuple(name for kind in kinds for name in kind._fields)


def named(names, refs):
    return types.SimpleNamespace(**dict(zip(names, refs, strict=True)))


def remote(source, landing, sems, index, target):
    return pltpu.make_async_remote_copy(
        src_ref=source,
        dst_ref=landing,
        send_sem=sems[0].at[index],
        recv_sem=sems[1].at[index],
        device_id=target,
        device_id_type=MESH,
    )


class RootGather(Root):
    def __init__(self, block, send, recv):
        super().__init__(send, recv)
        self.block = block

    def to(self, plane, sent):
        return self.copy(self.block, self.block, sent, 0, plane)

    def near(self):
        return jnp.where(self.low, 1 - self.root, 5 - self.root)

    def start(self):
        @pl.when(self.is_root)
        def _():
            self.to(self.between, 0).start()
            self.to(self.near(), 1).start()

    def hop(self):
        @pl.when(self.place[2] == self.between)
        def _():
            self.to(self.end, 0).wait_recv()
            self.to(self.end, 0).start()

    def finish(self):
        z = self.place[2]

        @pl.when((z != self.root) & (z != self.between))
        def _():
            self.to(self.end, 0).wait_recv()

        @pl.when((z == self.root) | (z == self.between))
        def _():
            self.to(self.end, 0).wait_send()

        @pl.when(self.is_root)
        def _():
            self.to(self.end, 1).wait_send()


class SeqGather:
    def __init__(self, full, batch, send, recv):
        self.place = here()
        self.full, self.batch, self.send, self.recv = full, batch, send, recv
        self.size = full.shape[1] // 4
        self.beside = peer(self.place, 2, False)
        self.sibling = peer(self.place, 0, True)

    def rows(self, owner):
        return pl.ds(pl.multiple_of(owner[1] * self.size, self.size), self.size)

    def copy(self, owner, target, sem):
        block = self.full.at[self.batch, self.rows(owner)]
        sems = (self.send.at[self.batch], self.recv.at[self.batch])
        return remote(block, block, sems, sem, target)

    def start(self, value):
        self.full[self.batch, self.rows(self.place), :] = value
        self.copy(self.place, self.beside, 0).start()
        self.copy(self.place, self.sibling, 1).start()

    def forward(self):
        self.copy(self.beside, self.beside, 0).wait_recv()
        self.copy(self.beside, self.sibling, 2).start()

    def finish(self):
        self.copy(self.sibling, self.sibling, 1).wait_recv()
        self.copy(peer(self.place, 2, True), self.sibling, 2).wait_recv()
        self.copy(self.place, self.beside, 0).wait_send()
        self.copy(self.place, self.sibling, 1).wait_send()
        self.copy(self.beside, self.sibling, 2).wait_send()


class ForwardIn(NamedTuple):
    inputs: Any
    small: Any
    gain_rows: Any
    w_mix: Any
    w_out: Any
    w_gu: Any
    w_down: Any
    seg_rows: Any
    seg_cols: Any


class ForwardOut(NamedTuple):
    rows: Any
    gains: Any
    persist: Any
    rates: Any


class Kept(NamedTuple):
    normed: Any
    mix: Any
    out: Any
    gu: Any
    down: Any
    qkv: Any
    gate: Any
    recalled: Any
    combined: Any
    mid: Any
    normed_two: Any
    gate_up: Any
    hidden: Any
    out_rows: Any


class ForwardScratch(NamedTuple):
    gain_all: Any
    small_all: Any
    mix_away: Any
    gu_away: Any
    down_away: Any
    zsend: Any
    zrecv: Any
    psend: Any
    precv: Any
    xsend: Any
    xrecv: Any
    gsend: Any
    grecv: Any
    csend: Any
    crecv: Any
    hsend: Any
    hrecv: Any
    saved: Any


def each(parts, act):
    for part in parts:
        act(part)


def forward_kernel(unit, *refs):
    count = len(Kept._fields)
    r, refs = refs[: len(ForwardIn._fields)], refs[len(ForwardIn._fields) :]
    given = vars(named(ForwardIn._fields, r))
    r, refs = refs[: len(ForwardOut._fields)], refs[len(ForwardOut._fields) :]
    given |= vars(named(ForwardOut._fields, r))
    in_hbm = [refs[:count], refs[count : 2 * count]]
    refs = refs[2 * count :]
    in_vmem = [refs[:count], refs[count : 2 * count]]
    refs = refs[2 * count :]
    scratch = PlaneScratch._fields[:6] + ForwardScratch._fields
    r = types.SimpleNamespace(**given, **vars(named(scratch, refs)))
    views = [types.SimpleNamespace(**vars(named(Kept._fields, part))) for part in in_vmem]
    views[0].rows, views[1].rows = r.rows, views[0].out_rows

    def save(layer, which):
        for name in which:
            index = Kept._fields.index(name)
            yield pltpu.make_async_copy(
                in_vmem[layer][index], in_hbm[layer][index], r.saved.at[layer, index]
            )

    place = here()
    x, s, z = place
    partner = peer(place, 1, False)
    flips = [(dx, ds) for dx in (0, 1) for ds in range(4) if dx or ds]
    plane = [((x + dx) % 2, (s + ds) % 4, z) for dx, ds in flips]
    column = [(x, s, (z + dz) % 4) for dz in (1, 2, 3)]
    column += [(1 - x, s, (z + dz) % 4) for dz in (1, 2, 3)]
    barrier = pltpu.get_barrier_semaphore()
    for other in plane + column:
        pl.semaphore_signal(barrier, inc=1, device_id=other, device_id_type=MESH)
    pl.semaphore_wait(barrier, len(plane) + len(column))

    zsems, psems, xsems = (r.zsend, r.zrecv), (r.psend, r.precv), (r.xsend, r.xrecv)
    holders = [*column, partner]

    def gains_to(index):
        return remote(r.gain_rows, r.gain_all.at[x, z], zsems, index, holders[index])

    for index in range(7):
        gains_to(index).start()
    r.gain_all[x, z] = r.gain_rows[...]

    mine, other = x * 4 + s, (1 - x) * 4 + s

    def mix_part(which):
        heads = [pl.ds(pl.multiple_of(kind * D + which * HD, HD), HD) for kind in range(4)]
        return jnp.concatenate([r.w_mix[0, :, cols] for cols in heads], 1)

    out_rows = pl.ds(pl.multiple_of(s % 2 * HD, HD), HD)
    root = z == 2 * x + s // 2
    rooted = z == 2 * (1 - x) + s // 2
    for layer in (0, 1):
        v = views[layer]

        @pl.when(x == layer)
        def _():
            r.mix_away[...] = mix_part(other)
            remote(r.mix_away, v.mix.at[z], xsems, 0, partner).start()
            v.mix[z] = mix_part(mine)

            @pl.when(rooted)
            def _():
                remote(r.w_out.at[0, out_rows], v.out, xsems, 1, partner).start()

            @pl.when(root)
            def _():
                v.out[...] = r.w_out[0, out_rows, :]

    for index in range(7):
        gains_to(index).wait_recv()
    for layer in range(2):
        for owner in range(4):
            for kind in range(2):
                for half in range(2):
                    begin = owner * 2 * HD + half * HD
                    row = 2 * kind + half
                    r.gains[layer, kind : kind + 1, begin : begin + HD] = r.gain_all[
                        layer, owner, row : row + 1, :
                    ]
    size = r.rows.shape[1]
    own_half = pl.ds(pl.multiple_of(x * size, size), size)
    arriving = [SeqGather(views[0].normed, batch, r.gsend, r.grecv) for batch in range(2)]
    for batch, gather in enumerate(arriving):
        rows = r.inputs[batch, 0].astype(F32)
        gather.start((rows * rms_scale(rows) * r.gains[0, 0:1, :]).astype(BF))
        r.rows[batch] = r.inputs[batch, 0, own_half, :]

    for index in range(7):
        remote(r.small, r.small_all.at[x, s], psems, index, plane[index]).start()
    r.small_all[x, s] = r.small[...]

    padded = r.down_away.shape[0]
    width = 8 * unit + 64

    def select(which, offset):
        begin = lax.broadcasted_iota(jnp.int32, (width, 128), 0) - offset
        col = lax.broadcasted_iota(jnp.int32, (width, 128), 1)
        return jnp.where((begin == which * unit + col) & (col < unit), 1.0, 0.0).astype(BF)

    def gu_part(which, out):
        for owner in range(4):
            base = owner * 8 * unit
            offset = base % 128
            chosen = select(which, offset)
            for side in range(2):
                begin = side * FF + base - offset
                part = nn(r.w_gu[0, :, begin : begin + width], chosen).astype(BF)
                at = side * 4 * padded + owner * padded
                out[:, at : at + padded] = part[:, :padded]

    def down_part(which, out):
        row = lax.broadcasted_iota(jnp.int32, (padded, 8 * unit), 0)
        col = lax.broadcasted_iota(jnp.int32, (padded, 8 * unit), 1)
        chosen = jnp.where((col == which * unit + row) & (row < unit), 1.0, 0.0).astype(BF)
        out[...] = nn(chosen, r.w_down[0]).astype(BF)

    gu_part(other, r.gu_away)
    down_part(other, r.down_away)
    for layer in (0, 1):
        v = views[layer]

        @pl.when(x == layer)
        def _():
            remote(r.gu_away, v.gu.at[z], xsems, 2, partner).start()
            remote(r.down_away, v.down.at[z], xsems, 3, partner).start()
            gu_part(mine, v.gu.at[z])
            down_part(mine, v.down.at[z])

    mixers, feeds = [], []
    for layer, v in enumerate(views):
        sems = [(r.csend.at[3 * layer + i], r.crecv.at[3 * layer + i]) for i in range(3)]
        mixers.append(
            [
                ColumnGather(v.mix, *sems[0]),
                RootGather(v.out, r.hsend.at[layer], r.hrecv.at[layer]),
            ]
        )
        feeds.append([ColumnGather(v.gu, *sems[1]), ColumnGather(v.down, *sems[2])])

    def swapped(layer, index):
        v = views[layer]
        landing = [v.mix.at[z], v.out, v.gu.at[z], v.down.at[z]][index]
        here_from = remote(landing, landing, xsems, index, partner)

        @pl.when((x != layer) & root if index == 1 else x != layer)
        def _():
            here_from.wait_recv()

    def start_mixer(layer):
        for index, part in enumerate(mixers[layer]):
            swapped(layer, index)
            part.start()

    def start_feed(layer):
        for index, part in enumerate(feeds[layer]):
            swapped(layer, 2 + index)
            part.start()

    start_mixer(0)
    arriving[0].forward()
    each(mixers[0], lambda part: part.hop())
    start_feed(0)
    arriving[1].forward()

    for index in range(7):
        dx, ds = flips[index]
        landing = r.small_all.at[(x + dx) % 2, (s + 4 - ds) % 4]
        remote(r.small, landing, psems, index, plane[index]).wait_recv()
    for layer in range(2):
        begin = pl.multiple_of(s % 2 * 32, 32)
        rows = r.small_all[layer, 2 * x + s // 2, pl.ds(begin, 32), :]
        r.persist[layer] = rows.astype(BF).reshape(2, 16, HD)
        begin = pl.multiple_of(64 + s % 2 * 8, 8)
        r.rates[layer] = r.small_all[layer, 2 * x + s // 2, pl.ds(begin, 8), :]

    length = r.part.shape[1]

    def project(layer, batch):
        v = views[layer]

        def block(rows, begin):
            proj = nn(v.normed[batch, rows, :], flat(v.mix))
            v.qkv[batch, rows, :] = proj[:, : 3 * HD].astype(BF)
            v.gate[batch, rows, :] = jax.nn.sigmoid(proj[:, 3 * HD :])

        in_blocks(length, 256, block)

    def mixer(layer, batch):
        v = views[layer]

        def block(rows, begin):
            values = v.qkv[batch, :, 2 * HD :]
            inner, decay_w, _, probs, per_probs = weights_of_scores(
                v.qkv[batch, rows, :HD],
                v.qkv[batch, :, HD : 2 * HD],
                r.persist[layer, 0],
                r.seg_rows[batch, rows, :],
                r.seg_cols[batch],
                begin,
                r.rates[layer, 0:1, 0:1],
            )
            attended = nn(probs.astype(BF), values) + nn(per_probs.astype(BF), r.persist[layer, 1])
            recalled = nn((inner * decay_w).astype(BF), values).astype(BF)
            v.recalled[batch, rows, :] = recalled
            combined = attended.astype(BF).astype(F32)
            combined = combined + v.gate[batch, rows, :] * recalled.astype(F32)
            combined = combined.astype(BF)
            v.combined[batch, rows, :] = combined
            r.part[batch, rows, :] = nn(combined, v.out[...]).astype(BF)

        in_blocks(length, 128, block)

    def feed(layer, batch):
        v = views[layer]

        def block(rows, begin):
            gate_up = nn(v.normed_two[batch, rows, :], flat(v.gu))
            v.gate_up[batch, rows, :] = gate_up
            half = gate_up.shape[1] // 2
            hidden = (jax.nn.silu(gate_up[:, :half]) * gate_up[:, half:]).astype(BF)
            v.hidden[batch, rows, :] = hidden
            r.part[batch, rows, :] = nn(hidden, flat(v.down)).astype(BF)

        in_blocks(length, 256, block)

    def scatter(batch):
        return Scatter(r.part, batch, r.pair, r.away, r.near, r.ssend, r.srecv)

    def send_normed(batch, own, gain, full):
        gather = Gather(full, batch, r.gsend, r.grecv)
        gather.start((own * rms_scale(own) * gain).astype(BF))
        return gather

    mixer_names = Kept._fields[:3] + Kept._fields[5:9]
    for layer, v in enumerate(views):
        parts = []
        for batch in range(2):
            if layer == 1:
                arriving[batch].forward()
            arriving[batch].finish()
            if batch == 0:
                each(mixers[layer], lambda part: part.finish())
            project(layer, batch)
            mixer(layer, batch)
            part = scatter(batch)
            part.start()
            part.forward()
            parts.append(part)
        each(save(layer, mixer_names), lambda copy: copy.start())
        gathers = []
        for batch, part in enumerate(parts):
            mid = v.rows[batch].astype(F32) + part.finish()
            v.mid[batch] = mid
            gathers.append(send_normed(batch, mid, r.gains[layer, 1:2, :], v.normed_two))
        each(feeds[layer], lambda part: part.hop())
        if layer == 0:
            start_mixer(1)
        parts = []
        for batch, gather in enumerate(gathers):
            gather.forward()
            gather.finish()
            if batch == 0:
                each(feeds[layer], lambda part: part.finish())
            feed(layer, batch)
            part = scatter(batch)
            part.start()
            part.forward()
            parts.append(part)
        if layer == 0:
            each(mixers[1], lambda part: part.hop())
            start_feed(1)
        each(save(layer, Kept._fields[3:5] + Kept._fields[9:13]), lambda copy: copy.start())
        arriving = []
        for batch, part in enumerate(parts):
            rows = (v.mid[batch] + part.finish()).astype(BF)
            v.out_rows[batch] = rows
            if layer == 0:
                gain = r.gains[1, 0:1, :]
                arriving.append(send_normed(batch, rows.astype(F32), gain, views[1].normed))
        each(save(layer, Kept._fields[13:]), lambda copy: copy.start())

    for layer in range(2):
        for copy in save(layer, Kept._fields):
            copy.wait()
    remote(r.mix_away, r.mix_away, xsems, 0, partner).wait_send()
    remote(r.gu_away, r.gu_away, xsems, 2, partner).wait_send()
    remote(r.down_away, r.down_away, xsems, 3, partner).wait_send()

    @pl.when(rooted)
    def _():
        remote(views[0].out, views[0].out, xsems, 1, partner).wait_send()

    for index in range(7):
        gains_to(index).wait_send()
        remote(r.small, r.small_all.at[x, s], psems, index, plane[index]).wait_send()


def backward_kernel(*refs):
    saved_names = Kept._fields[:-1]
    count = len(saved_names)
    given = vars(named(BackwardIn._fields, refs[: len(BackwardIn._fields)]))
    refs = refs[len(BackwardIn._fields) :]
    in_hbm = [refs[:count], refs[count : 2 * count]]
    refs = refs[2 * count :]
    given |= vars(named(BackwardOut._fields, refs[: len(BackwardOut._fields)]))
    refs = refs[len(BackwardOut._fields) :]
    in_vmem = refs[:count]
    given |= vars(named(saved_names, in_vmem))
    scratch = fields(PlaneScratch, BackwardScratch)
    r = types.SimpleNamespace(**given, **vars(named(scratch, refs[count:])))
    length = r.part.shape[1]
    place = here()
    x, s, z = place

    def load(layer, which):
        for name in which:
            index = saved_names.index(name)
            yield pltpu.make_async_copy(in_hbm[layer][index], in_vmem[index], r.loaded.at[index])

    feed_names = saved_names[3:5] + saved_names[9:]
    mixer_names = saved_names[:3] + saved_names[5:9]
    for which in (feed_names, mixer_names):
        each(load(1, which), lambda copy: copy.start())
    feeds, mixers = [], []
    for layer in range(2):
        sems = [(r.csend.at[3 * layer + i], r.crecv.at[3 * layer + i]) for i in range(3)]
        feeds.append(
            [
                ColumnSum(r.own_gu, r.gu_slots.at[layer], r.gu_sum.at[layer], *sems[0]),
                ColumnSum(r.own_down, r.down_slots.at[layer], r.down_sum.at[layer], *sems[1]),
            ]
        )
        mixers.append(
            [
                ColumnSum(r.grad_mix, r.mix_slots.at[layer], r.mix_sum.at[layer], *sems[2]),
                RootSum(
                    r.grad_out,
                    r.root_slots.at[layer],
                    r.out_sum.at[layer],
                    r.hsend.at[layer],
                    r.hrecv.at[layer],
                ),
            ]
        )
    grads = (r.grad_low, r.grad_high)

    def feed_back(full, batch):
        def block(rows, begin):
            grad_hidden = nt(full[batch, rows, :], flat(r.down))
            half = grad_hidden.shape[1]
            gate_part = r.gate_up[batch, rows, :half]
            up_part = r.gate_up[batch, rows, half:]
            sig_part = jax.nn.sigmoid(gate_part)
            silu = gate_part * sig_part
            grad_gate = grad_hidden * up_part * (sig_part + silu * (1.0 - sig_part))
            r.grad_gu[batch, rows, :half] = grad_gate.astype(BF)
            r.grad_gu[batch, rows, half:] = (grad_hidden * silu).astype(BF)
            r.part[batch, rows, :] = nt(r.grad_gu[batch, rows, :], flat(r.gu)).astype(BF)

        in_blocks(length, 256, block)

    def feed_weights(full):
        def down(cols, begin):
            grad = tn(r.hidden[0], full[0, :, cols])
            grad = grad + tn(r.hidden[1], full[1, :, cols])
            grad = grad.reshape(4, grad.shape[0] // 4, grad.shape[1])
            r.own_down[:, :, cols] = grad.astype(BF)

        in_blocks(D, 256, down)
        product(r.own_gu, r.normed_two, r.grad_gu)

    def product(out, left, right):
        for owner in range(4):
            cols = slice(owner * (D // 4), (owner + 1) * (D // 4))
            grad = tn(left[0, :, cols], right[0]) + tn(left[1, :, cols], right[1])
            out[owner] = grad.astype(BF)

    def mixer_back(layer, batch):
        scale = 1.0 / math.sqrt(HD)
        r.grad_keys[...] = jnp.zeros_like(r.grad_keys)
        r.grad_values[...] = jnp.zeros_like(r.grad_values)

        def block(rows, begin):
            grad_combined = nt(r.branch[batch, rows, :], r.out[...])
            gate = r.gate[batch, rows, :]
            recalled = r.recalled[batch, rows, :].astype(F32)
            attn_rows = grad_combined.astype(BF)
            memory_rows = (grad_combined * gate).astype(BF)
            grad_pre = grad_combined * recalled * gate * (1.0 - gate)
            r.grad_proj[batch, rows, 3 * HD :] = grad_pre.astype(BF)
            query = r.qkv[batch, rows, :HD]
            keys = r.qkv[batch, :, HD : 2 * HD]
            values = r.qkv[batch, :, 2 * HD :]
            inner, decay_w, distance, probs, per_probs = weights_of_scores(
                query,
                keys,
                r.persist[layer, 0],
                r.seg_rows[batch, rows, :],
                r.seg_cols[batch],
                begin,
                r.rates[layer, 0:1, 0:1],
            )
            per_dp = nt(attn_rows, r.persist[layer, 1])
            seq_dp = nt(attn_rows, values)
            delta = jnp.sum(per_probs * per_dp, axis=1, keepdims=True) + jnp.sum(
                probs * seq_dp, axis=1, keepdims=True
            )
            per_ds = (per_probs * (per_dp - delta)).astype(BF)
            seq_ds = (probs * (seq_dp - delta)).astype(BF)
            weighted = nt(memory_rows, values) * decay_w
            grad_inner = weighted.astype(BF)
            memory = inner * decay_w
            rate_terms = weighted * inner * distance
            r.grad_rate[layer] -= jnp.sum(rate_terms, axis=0, keepdims=True)
            grad_query = (nn(per_ds, r.persist[layer, 0]) + nn(seq_ds, keys)) * scale
            grad_query = grad_query + nn(grad_inner, keys)
            r.grad_proj[batch, rows, :HD] = grad_query.astype(BF)
            r.grad_keys[...] += tn(seq_ds, query) * scale + tn(grad_inner, query)
            r.grad_values[...] += tn(probs.astype(BF), attn_rows) + tn(
                memory.astype(BF), memory_rows
            )
            r.grad_persist[layer, 0] += tn(per_ds, query) * scale
            r.grad_persist[layer, 1] += tn(per_probs.astype(BF), attn_rows)

        in_blocks(length, 128, block)
        r.grad_proj[batch, :, HD : 2 * HD] = r.grad_keys[...].astype(BF)
        r.grad_proj[batch, :, 2 * HD : 3 * HD] = r.grad_values[...].astype(BF)

        def back(rows, begin):
            r.part[batch, rows, :] = nt(r.grad_proj[batch, rows, :], flat(r.mix)).astype(BF)

        in_blocks(length, 256, back)

    def scatter(batch):
        return Scatter(r.part, batch, r.pair, r.away, r.near, r.ssend, r.srecv)

    def through_norm(batch, part, rows, gain):
        grad_normed = part.finish()
        inverse = rms_scale(rows)
        return norm_back(grad_normed, rows * inverse, inverse, gain)

    flips = [(dx, ds) for dx in (0, 1) for ds in range(4) if dx or ds]
    plane = [((x + dx) % 2, (s + ds) % 4, z) for dx, ds in flips]
    column = [(x, s, (z + dz) % 4) for dz in (1, 2, 3)]
    barrier = pltpu.get_barrier_semaphore()
    for other in plane + column:
        pl.semaphore_signal(barrier, inc=1, device_id=other, device_id_type=MESH)
    pl.semaphore_wait(barrier, len(plane) + len(column))
    r.grad_rate[...] = jnp.zeros_like(r.grad_rate)
    r.grad_persist[...] = jnp.zeros_like(r.grad_persist)
    arriving = None
    for layer in (1, 0):
        full = r.grad_next if arriving else r.grad_full
        above = grads[1] if arriving else r.grad_rows
        rows_in = r.out_low if layer else r.rows
        each(load(layer, feed_names), lambda copy: copy.wait())
        parts = []
        for batch in range(2):
            if arriving:
                arriving[batch].forward()
                arriving[batch].finish()
            feed_back(full, batch)
            part = scatter(batch)
            part.start()
            part.forward()
            parts.append(part)
        if layer == 0:
            each(mixers[1], lambda part: part.hop())
            each(feeds[1], lambda part: part.finish())
        feed_weights(full)
        each(feeds[layer], lambda part: part.start())
        gathers = []
        gain_sums = []
        for batch, part in enumerate(parts):
            grad_mid, gain_sum = through_norm(
                batch, part, r.mid[batch], r.gains[layer, 1:2, :]
            )
            gain_sums.append(gain_sum[None])
            grad_mid = grad_mid + above[batch].astype(F32)
            r.grad_mid[batch] = grad_mid
            gather = Gather(r.branch, batch, r.gsend, r.grecv)
            gather.start(grad_mid.astype(BF))
            gathers.append(gather)
        r.gain_sums[layer, 1:2] = gain_sums[0] + gain_sums[1]
        if layer == 1:
            each(load(0, feed_names), lambda copy: copy.start())
        each(load(layer, mixer_names), lambda copy: copy.wait())
        parts = []
        for batch, gather in enumerate(gathers):
            gather.forward()
            gather.finish()
            mixer_back(layer, batch)
            part = scatter(batch)
            part.start()
            part.forward()
            parts.append(part)
            if batch == 0:
                each(feeds[layer], lambda part: part.hop())
        if layer == 0:
            each(mixers[1], lambda part: part.finish())
        product(r.grad_mix, r.normed, r.grad_proj)
        grad_out = tn(r.combined[0], r.branch[0]) + tn(r.combined[1], r.branch[1])
        r.grad_out[...] = grad_out.astype(BF)
        each(mixers[layer], lambda part: part.start())
        if layer == 1:
            each(load(0, mixer_names), lambda copy: copy.start())
        arriving = []
        gain_sums = []
        for batch, part in enumerate(parts):
            grad_h, gain_sum = through_norm(
                batch, part, rows_in[batch].astype(F32), r.gains[layer, 0:1, :]
            )
            gain_sums.append(gain_sum[None])
            grad_h = (grad_h + r.grad_mid[batch]).astype(BF)
            grads[layer][batch] = grad_h
            if layer == 1:
                gather = Gather(r.grad_next, batch, r.gsend, r.grecv)
                gather.start(grad_h)
                arriving.append(gather)
        r.gain_sums[layer, 0:1] = gain_sums[0] + gain_sums[1]
    each(feeds[0], lambda part: part.finish())

    for layer in range(2):
        persist = r.grad_persist[layer].reshape(-1, HD)
        rate = r.grad_rate[layer]
        rate = sum(rate[:, begin : begin + HD] for begin in range(0, length, HD))
        for owner in range(4):
            r.small[owner, layer * 32 : (layer + 1) * 32, :] = persist
            r.small[owner, 64 + layer : 65 + layer, :] = rate
            for kind in range(2):
                for half in range(2):
                    row = 72 + 4 * layer + 2 * kind + half
                    begin = owner * 2 * HD + half * HD
                    r.small[owner, row : row + 1, :] = r.gain_sums[
                        layer, kind : kind + 1, begin : begin + HD
                    ]
    for owner in range(4):
        r.small[owner, 66:72, :] = jnp.zeros((6, HD), F32)

    sibling, beside, partner = (peer(place, 0, True), peer(place, 2, False), peer(place, 1, False))
    across = peer(place, 3, False)
    bufs = (r.mix_buf, r.gu_buf, r.down_buf)
    out_buf, rows_buf, grads_buf, plane_buf = r.out_buf, r.rows_buf, r.grads_buf, r.plane_buf
    by_layer = [
        [r.mix_sum.at[i], r.gu_sum.at[i], r.down_sum.at[i], r.out_sum.at[i]] for i in range(2)
    ]
    by_layer[0] += [r.out_low, r.grad_low]
    by_layer[1] += [r.out_high, r.grad_high]
    copy = remote

    def to_plane_of(dz):
        target = (z + dz) % 4
        return copy(
            r.small.at[target], r.column_buf.at[dz - 1], (r.zsend, r.zrecv), dz - 1, (x, s, target)
        )

    def to_plane(index):
        slot = plane_buf.at[x * 4 + s]
        return copy(slot, slot, (r.qsend, r.qrecv), index, plane[index])

    for dz in (1, 2, 3):
        to_plane_of(dz).start()

    psems = [(r.psend.at[i], r.precv.at[i]) for i in range(3)]

    def piece(index, kind, slot, target, source=None):
        landing = bufs[index].at[slot]
        return copy(landing if source is None else source, landing, psems[index], kind, target)

    mine = (x, s)
    turned = (1 - x, s)

    def send(indices):
        for layer in (0, 1):
            own, theirs = by_layer[layer], by_layer[1 - layer]

            @pl.when(x == layer)
            def _():
                for index in indices:
                    piece(index, 2, mine, partner, theirs[index]).start()
                    piece(index, 0, mine, beside, own[index]).start()
                    piece(index, 1, mine, sibling, own[index]).start()
                for index in indices:
                    bufs[index][mine] = own[index][...]

    def turn(indices):
        for index in indices:
            piece(index, 2, turned, partner).wait_recv()
            piece(index, 3, turned, beside).start()
            piece(index, 4, turned, sibling).start()

    send((1, 2))
    for layer in (0, 1):

        @pl.when(x == layer)
        def _():
            copy(by_layer[1 - layer][4], rows_buf, (r.rsend, r.rrecv), 0, partner).start()
            copy(by_layer[1 - layer][5], grads_buf, (r.rsend, r.rrecv), 1, partner).start()

    total = r.small[z]
    for dz in (1, 2, 3):
        to_plane_of(dz).wait_recv()
        total = total + r.column_buf[dz - 1]
    plane_buf[x * 4 + s] = total
    for index in range(7):
        to_plane(index).start()
    each(mixers[0], lambda part: part.hop())
    turn((1, 2))
    each(mixers[0], lambda part: part.finish())
    send((0,))

    core = s % 2
    root = z == 2 * x + s // 2
    of_root = (z // 2, 2 * (z % 2) + core)
    apart = 2 * ((x + of_root[0]) % 2) + (s // 2 + of_root[1] // 2) % 2

    def out_copy(index, target, source=None):
        landing = out_buf.at[core]
        return copy(landing if source is None else source, landing, (r.osend, r.orecv), index, target)

    for layer in (0, 1):

        @pl.when(root & (x == layer))
        def _():
            out_copy(1, beside, by_layer[layer][3]).start()
            out_copy(2, partner, by_layer[1 - layer][3]).start()
            out_copy(3, across, by_layer[1 - layer][3]).start()
            out_buf[core] = by_layer[layer][3][...]

    for apart_by in (1, 2, 3):

        @pl.when(apart == apart_by)
        def _():
            out_copy(apart_by, beside).wait_recv()

    out_copy(0, sibling).start()

    turn((0,))
    far = (x, (s + 2) % 4)
    far_turned = (1 - x, (s + 2) % 4)
    for index in (1, 2, 0):
        piece(index, 0, far, beside).wait_recv()
        piece(index, 5, far, sibling).start()
    for index in (1, 2, 0):
        piece(index, 3, far_turned, beside).wait_recv()
        piece(index, 6, far_turned, sibling).start()
    twin = sibling[1]
    far_twin = (twin + 2) % 4
    for index in range(3):
        piece(index, 1, (x, twin), sibling).wait_recv()
        piece(index, 4, (1 - x, twin), sibling).wait_recv()
        piece(index, 5, (x, far_twin), sibling).wait_recv()
        piece(index, 6, (1 - x, far_twin), sibling).wait_recv()
    other_out = out_buf.at[1 - core]
    copy(other_out, other_out, (r.osend, r.orecv), 0, sibling).wait_recv()
    for index in range(7):
        dx, ds = flips[index]
        slot = plane_buf.at[((x + dx) % 2) * 4 + (s + 4 - ds) % 4]
        copy(slot, slot, (r.qsend, r.qrecv), index, plane[index]).wait_recv()
    for index in (0, 1):
        copy(rows_buf, rows_buf, (r.rsend, r.rrecv), index, partner).wait()
    for index in range(7):
        to_plane(index).wait_send()
    for dz in (1, 2, 3):
        to_plane_of(dz).wait_send()
    for index in range(3):
        for kind in range(7):
            piece(index, kind, mine, sibling).wait_send()
    out_copy(0, sibling).wait_send()

    @pl.when(root)
    def _():
        for index in (1, 2, 3):
            out_copy(index, sibling).wait_send()


def kernel_call(kernel, number, operands, outs, scratch, spaces=None, places=None):
    spaces = spaces or [pltpu.VMEM] * len(outs)
    places = places or [pltpu.VMEM] * len(operands)
    return pl.pallas_call(
        kernel,
        out_shape=list(outs),
        in_specs=[pl.BlockSpec(memory_space=space) for space in places],
        out_specs=[pl.BlockSpec(memory_space=space) for space in spaces],
        scratch_shapes=scratch,
        compiler_params=pltpu.CompilerParams(
            collective_id=number, has_side_effects=True, vmem_limit_bytes=58 * 2**20
        ),
    )(*operands)


def pairs_of(*sizes):
    return [pltpu.SemaphoreType.DMA(size) for size in sizes for _ in range(2)]


def scatter_scratch(length):
    size = length // 8
    return [
        pltpu.VMEM((2, length, D), BF),
        pltpu.VMEM((2, 4, size, D), BF),
        pltpu.VMEM((2, 3, size, D), BF),
        pltpu.VMEM((2, 3, size, D), BF),
        *pairs_of((2, 7), (2, 7)),
    ]


def forward_call(number, *operands):
    inputs, small, _, w_mix, _, _, w_down, *_ = operands
    count, _, tokens, _ = inputs.shape
    depth, length = w_mix.shape[1], 4 * tokens
    unit = w_down.shape[1] // 8
    padded = -(-unit // 32) * 32
    shape = jax.ShapeDtypeStruct
    outs = ForwardOut(
        rows=shape((count, length // 8, D), BF),
        gains=shape((2, 2, D), F32),
        persist=shape((2, 2, 16, HD), BF),
        rates=shape((2, 8, HD), F32),
    )
    kept = Kept(
        normed=shape((count, length, D), BF),
        mix=shape((4, depth, 4 * HD), BF),
        out=shape((HD, D), BF),
        gu=shape((4, depth, 8 * padded), BF),
        down=shape((4, padded, D), BF),
        qkv=shape((count, length, 3 * HD), BF),
        gate=shape((count, length, HD), F32),
        recalled=shape((count, length, HD), BF),
        combined=shape((count, length, HD), BF),
        mid=shape((count, length // 8, D), F32),
        normed_two=shape((count, length, D), BF),
        gate_up=shape((count, length, 8 * padded), F32),
        hidden=shape((count, length, 4 * padded), BF),
        out_rows=shape((count, length // 8, D), BF),
    )
    scratch = [pltpu.VMEM(part.shape, part.dtype) for part in (*kept, *kept)]
    scratch += scatter_scratch(length)[:6]
    scratch += [
        pltpu.VMEM((2, 4, 8, HD), F32),
        pltpu.VMEM((2, 4) + small.shape, F32),
        pltpu.VMEM((depth, 4 * HD), BF),
        pltpu.VMEM((depth, 8 * padded), BF),
        pltpu.VMEM((padded, D), BF),
        *pairs_of((7,), (7,), (4,), (2, 7), (6, 4), (2, 2)),
        pltpu.SemaphoreType.DMA((2, len(kept))),
    ]
    kernel = functools.partial(forward_kernel, unit)
    specs = [pltpu.VMEM] * len(outs) + [pl.ANY] * (2 * len(kept))
    found = kernel_call(kernel, number, operands, [*outs, *kept, *kept], scratch, specs)
    own, found = found[: len(outs)], found[len(outs) :]
    return (
        named(ForwardOut._fields, own),
        named(Kept._fields, found[: len(kept)]),
        named(Kept._fields, found[len(kept) :]),
    )


def backward_call(number, given, below, above):
    saved = Kept._fields[:-1]
    kept = [getattr(part, name) for part in (below, above) for name in saved]
    count, length, _ = below.normed.shape
    depth, half, size = D // 4, 4 * below.down.shape[1], length // 8
    shape = jax.ShapeDtypeStruct
    outs = BackwardOut(
        mix_buf=shape((2, 4, depth, 4 * HD), BF),
        gu_buf=shape((2, 4, depth, 2 * half), BF),
        down_buf=shape((2, 4, half // 4, D), BF),
        out_buf=shape((2, HD, D), BF),
        rows_buf=shape((count, size, D), BF),
        grads_buf=shape((count, size, D), BF),
        plane_buf=shape((8, 80, HD), F32),
        grad_low=shape((count, size, D), BF),
        grad_high=shape((count, size, D), BF),
    )
    scratch = [pltpu.VMEM(part.shape, part.dtype) for part in kept[: len(saved)]]
    scratch += scatter_scratch(length) + [
        pltpu.VMEM((count, length, 2 * half), BF),
        pltpu.VMEM((count, length, 4 * HD), BF),
        pltpu.VMEM((length, HD), F32),
        pltpu.VMEM((length, HD), F32),
        pltpu.VMEM((count, length, D), BF),
        pltpu.VMEM((count, size, D), F32),
        pltpu.VMEM((count, length, D), BF),
        pltpu.VMEM((2, 2, 16, HD), F32),
        pltpu.VMEM((2, 1, length), F32),
        pltpu.VMEM((2, 2, D), F32),
        pltpu.VMEM((4, 80, HD), F32),
        pltpu.VMEM((3, 80, HD), F32),
        pltpu.VMEM((4, depth, 2 * half), BF),
        pltpu.VMEM((4, half // 4, D), BF),
        pltpu.VMEM((4, depth, 4 * HD), BF),
        pltpu.VMEM((HD, D), BF),
        pltpu.VMEM((2, 4, depth, 2 * half), BF),
        pltpu.VMEM((2, 4, half // 4, D), BF),
        pltpu.VMEM((2, 4, depth, 4 * HD), BF),
        pltpu.VMEM((2, 2, HD, D), BF),
        pltpu.VMEM((2, depth, 2 * half), BF),
        pltpu.VMEM((2, half // 4, D), BF),
        pltpu.VMEM((2, depth, 4 * HD), BF),
        pltpu.VMEM((2, HD, D), BF),
        *pairs_of((6, 4), (2, 2), (3, 7), (4,), (2,), (3,), (7,)),
        pltpu.SemaphoreType.DMA((len(saved),)),
    ]
    operands = [*(getattr(given, name) for name in BackwardIn._fields), *kept]
    spaces = [pltpu.VMEM] * len(BackwardIn._fields) + [pl.ANY] * len(kept)
    found = kernel_call(backward_kernel, number, operands, outs, scratch, None, spaces)
    return named(BackwardOut._fields, found)


def assemble_kernel(unit, mix_buf, gu_buf, down_buf, mix_ref, gu_ref, down_ref):
    padded = down_buf.shape[2]
    half = gu_buf.shape[3] // 2
    for which in range(8):
        slot = (which // 4, which % 4)
        mix = mix_buf[slot].astype(F32)
        for kind in range(4):
            begin = kind * D + which * HD
            mix_ref[0, :, begin : begin + HD] = mix[:, kind * HD : (kind + 1) * HD]
        part = gu_buf[slot].astype(F32)
        for side in range(2):
            for owner in range(half // padded):
                begin = side * FF + (owner * 8 + which) * unit
                source = side * half + owner * padded
                gu_ref[0, :, begin : begin + unit] = part[:, source : source + unit]
    for pair in range(2):
        down = down_buf[0, pair].astype(F32)
        down_ref[0, pair * unit : (pair + 1) * unit, :] = down[:unit]


def assemble_call(unit, mix_buf, gu_buf, down_buf):
    depth, padded = mix_buf.shape[2], down_buf.shape[2]
    rows = depth // 4
    return pl.pallas_call(
        functools.partial(assemble_kernel, unit),
        grid=(4,),
        out_shape=[
            jax.ShapeDtypeStruct((1, depth, 4 * D), F32),
            jax.ShapeDtypeStruct((1, depth, 2 * FF), F32),
            jax.ShapeDtypeStruct((1, 8 * unit, D), F32),
        ],
        in_specs=[
            pl.BlockSpec((2, 4, rows, 4 * HD), lambda i: (0, 0, i, 0)),
            pl.BlockSpec((2, 4, rows, gu_buf.shape[3]), lambda i: (0, 0, i, 0)),
            pl.BlockSpec((1, 2, padded, D), lambda i: (i // 2, i % 2, 0, 0)),
        ],
        out_specs=[
            pl.BlockSpec((1, rows, 4 * D), lambda i: (0, i, 0)),
            pl.BlockSpec((1, rows, 2 * FF), lambda i: (0, i, 0)),
            pl.BlockSpec((1, 2 * unit, D), lambda i: (0, i, 0)),
        ],
        compiler_params=pltpu.CompilerParams(vmem_limit_bytes=40 * 2**20),
    )(mix_buf, gu_buf, down_buf)


def tensor_parallel(
    inputs, segment_ids, cotangent, w_mix, w_out, w_gu, w_down, norm_gains, persist_kv, memory_decay
):
    x, s, z = here()
    nx, ns, nz = (lax.axis_size(a) for a in ("section", "seq", "shard"))
    width = nx * ns
    mine = x * ns + s
    other = (1 - x) * ns + s
    first = x == 0
    count, _, tokens, _ = inputs.shape
    length = tokens * ns
    size = length // width
    depth = w_mix.shape[1]
    unit = w_down.shape[1] // (nx * ns)

    def layers(own, got):
        return (jnp.where(first, own, got), jnp.where(first, got, own))

    small = persist_kv[0].reshape(-1, 2, HD).transpose(1, 0, 2).reshape(-1, HD).astype(F32)
    rates = jnp.broadcast_to(memory_decay[0][:, None, None], (2, 8, HD)).reshape(-1, HD)
    gain_rows = norm_gains[0].astype(F32).T.reshape(-1, HD)
    gain_rows = jnp.pad(gain_rows, ((0, 8 - gain_rows.shape[0]), (0, 0)))
    small = jnp.concatenate([small, rates], 0)
    segments = (segment_ids[:, 0, :, None], segment_ids)
    ready, below, above = forward_call(
        1, inputs, small, gain_rows, w_mix, w_out, w_gu, w_down, *segments
    )
    cot_full = lax.all_gather(cotangent[:, 0], "seq", axis=1, tiled=True)
    given = BackwardIn(
        grad_full=cot_full,
        grad_rows=lax.dynamic_slice_in_dim(cotangent[:, 0], x * size, size, 1),
        rows=ready.rows,
        out_low=below.out_rows,
        out_high=above.out_rows,
        gains=ready.gains,
        persist=ready.persist,
        rates=ready.rates,
        seg_rows=segments[0],
        seg_cols=segments[1],
    )
    found = backward_call(2, given, below, above)
    outputs = (below.out_rows, above.out_rows)
    grads = (found.grad_low, found.grad_high)

    def whole_rows(of_layer, got):
        both = layers(jnp.where(first, of_layer[0], of_layer[1]), got)
        return jnp.concatenate(both, 1)[None, :, None]

    section_out = whole_rows(outputs, found.rows_buf)
    section_grad = whole_rows(grads, found.grads_buf).astype(F32)
    grad_mix, grad_gu, grad_down = assemble_call(unit, found.mix_buf, found.gu_buf, found.down_buf)
    grad_out = found.out_buf.astype(F32).reshape(1, 2 * HD, D)

    plane_all = found.plane_buf
    heads_of = lax.dynamic_slice_in_dim(plane_all, 2 * s, 2, 0)
    of_section = lax.dynamic_index_in_dim(
        heads_of[:, :64].reshape(2, 2, 2, -1, HD), x, 1, keepdims=False
    )
    grad_persist = of_section.transpose(1, 2, 0, 3).reshape(1, 2, -1, 2 * HD)
    of_section = lax.dynamic_index_in_dim(heads_of[:, 64:66], x, 1, keepdims=False)
    grad_rate = jnp.sum(of_section, 1)[None]
    gain_all = jnp.sum(plane_all[:, 72:], 0).reshape(2, 2, depth)
    grad_gain = lax.dynamic_index_in_dim(gain_all, x, 0).transpose(0, 2, 1)
    return (
        section_out,
        section_grad,
        grad_mix,
        grad_out,
        grad_gu,
        grad_down,
        grad_gain,
        grad_persist,
        grad_rate,
    )


def solution(mesh):
    sizes = mesh.shape
    planar = (sizes["section"], sizes["seq"]) == (2, 4)
    placed = (
        P(None, "shard", "seq", None),
        P(None, "shard", None),
        P(None, "shard", "seq", None),
        P("section", "shard", None),
        P("section", "shard", None),
        P("section", "shard", None),
        P("section", "shard", None),
        P("section", "shard", None),
        P("section", None, None, "seq"),
        P("section", "seq"),
    )
    return jax.shard_map(
        tensor_parallel if planar else on_device,
        mesh=mesh,
        in_specs=placed,
        out_specs=(
            P("section", None, "shard", "seq", None),
            P("section", None, "shard", "seq", None),
            P("section", "shard", None),
            P("section", "shard", None),
            P("section", "shard", None),
            P("section", "shard", None),
            P("section", "shard", None),
            P("section", None, None, "seq"),
            P("section", "seq"),
        ),
        check_vma=False,
    )
```

```python
import functools
import math
import types
from typing import Any, NamedTuple

import jax
import jax.numpy as jnp
from jax import lax
from jax.experimental import pallas as pl
from jax.experimental.pallas import tpu as pltpu
from jax.sharding import PartitionSpec as P

D = 1024
H = 8
HD = 128
FF = 2816


def shifted(value, axis, by):
    size = lax.axis_size(axis)
    pairs = [(i, i + by) for i in range(size) if 0 <= i + by < size]
    return lax.ppermute(value, axis, pairs)


def as_sent(value):
    return jax.tree.map(lambda a: a.astype(jnp.bfloat16) if a.dtype == jnp.float32 else a, value)


def rms_scale(values):
    return lax.rsqrt(jnp.mean(values * values, axis=-1, keepdims=True) + 1e-06)


def norm_back(grad_normed, scaled, inverse, gain):
    grad_scaled = grad_normed * gain
    grad_rows = inverse * (
        grad_scaled - scaled * jnp.mean(grad_scaled * scaled, axis=-1, keepdims=True)
    )
    return (grad_rows, jnp.sum(grad_normed * scaled, axis=0))


def block_terms(query_rows, key_rows, seg_ids, begin, reach, rate):
    inner = jnp.dot(query_rows, key_rows.T, preferred_element_type=jnp.float32)
    row_places = begin + jnp.arange(reach - begin, dtype=jnp.int32)
    col_places = jnp.arange(reach, dtype=jnp.int32)
    allowed = (seg_ids[begin:reach][:, None] == seg_ids[:reach][None, :]) & (
        col_places[None, :] <= row_places[:, None]
    )
    distance = jnp.maximum(row_places[:, None] - col_places[None, :], 0).astype(jnp.float32)
    decay_w = jnp.where(allowed, jnp.exp(-rate * distance), jnp.float32(0.0))
    return (inner, allowed, decay_w, distance)


def head_forward(query, keys, values, pkeys, pvalues, rate, seg_ids):
    length, width = query.shape
    block = min(512, length)
    scale = 1.0 / math.sqrt(width)
    attn_parts, memory_parts, lse_parts = ([], [], [])
    for begin in range(0, length, block):
        reach = begin + block
        query_rows = query[begin:reach]
        inner, allowed, decay_w, distance = block_terms(
            query_rows, keys[:reach], seg_ids, begin, reach, rate
        )
        per_scores = jnp.dot(query_rows, pkeys.T, preferred_element_type=jnp.float32) * scale
        seq_scores = jnp.where(allowed, inner * scale, -jnp.inf)
        top = jnp.maximum(
            jnp.max(per_scores, axis=1, keepdims=True), jnp.max(seq_scores, axis=1, keepdims=True)
        )
        per_exp = jnp.exp(per_scores - top)
        seq_exp = jnp.exp(seq_scores - top)
        denom = jnp.sum(per_exp, axis=1, keepdims=True) + jnp.sum(seq_exp, axis=1, keepdims=True)
        attended = jnp.dot(
            (per_exp / denom).astype(jnp.bfloat16), pvalues, preferred_element_type=jnp.float32
        )
        attended = attended + jnp.dot(
            (seq_exp / denom).astype(jnp.bfloat16),
            values[:reach],
            preferred_element_type=jnp.float32,
        )
        memory_w = (inner * decay_w * (1.0 / width)).astype(jnp.bfloat16)
        recalled = jnp.dot(memory_w, values[:reach], preferred_element_type=jnp.float32)
        attn_parts.append(attended)
        memory_parts.append(recalled)
        lse_parts.append(top[:, 0] + jnp.log(denom[:, 0]))
    return (
        jnp.concatenate(attn_parts, 0),
        jnp.concatenate(memory_parts, 0),
        jnp.concatenate(lse_parts, 0),
    )


def head_backward(query, keys, values, pkeys, pvalues, rate, seg_ids, lse, grad_attn, grad_memory):
    length, width = query.shape
    block = min(512, length)
    scale = 1.0 / math.sqrt(width)
    query_grads = []
    grad_keys = jnp.zeros((length, width), jnp.float32)
    grad_values = jnp.zeros((length, width), jnp.float32)
    grad_pkeys = jnp.zeros(pkeys.shape, jnp.float32)
    grad_pvalues = jnp.zeros(pvalues.shape, jnp.float32)
    grad_rate = jnp.float32(0.0)
    for begin in range(0, length, block):
        reach = begin + block
        query_rows = query[begin:reach]
        key_rows = keys[:reach]
        value_rows = values[:reach]
        inner, allowed, decay_w, distance = block_terms(
            query_rows, key_rows, seg_ids, begin, reach, rate
        )
        per_scores = jnp.dot(query_rows, pkeys.T, preferred_element_type=jnp.float32) * scale
        seq_scores = jnp.where(allowed, inner * scale, -jnp.inf)
        row_lse = lse[begin:reach][:, None]
        per_prob = jnp.exp(per_scores - row_lse)
        seq_prob = jnp.exp(seq_scores - row_lse)
        attn_rows = grad_attn[begin:reach]
        memory_rows = grad_memory[begin:reach]
        per_dp = jnp.dot(attn_rows, pvalues.T, preferred_element_type=jnp.float32)
        seq_dp = jnp.dot(attn_rows, value_rows.T, preferred_element_type=jnp.float32)
        delta = jnp.sum(per_prob * per_dp, axis=1, keepdims=True) + jnp.sum(
            seq_prob * seq_dp, axis=1, keepdims=True
        )
        per_ds = (per_prob * (per_dp - delta)).astype(jnp.bfloat16)
        seq_ds = (seq_prob * (seq_dp - delta)).astype(jnp.bfloat16)
        rows_grad = (
            jnp.dot(per_ds, pkeys, preferred_element_type=jnp.float32)
            + jnp.dot(seq_ds, key_rows, preferred_element_type=jnp.float32)
        ) * scale
        grad_pkeys = (
            grad_pkeys
            + jnp.einsum("qk,qd->kd", per_ds, query_rows, preferred_element_type=jnp.float32)
            * scale
        )
        grad_pvalues = grad_pvalues + jnp.einsum(
            "qk,qd->kd",
            per_prob.astype(jnp.bfloat16),
            attn_rows,
            preferred_element_type=jnp.float32,
        )
        key_part = (
            jnp.einsum("qk,qd->kd", seq_ds, query_rows, preferred_element_type=jnp.float32) * scale
        )
        value_part = jnp.einsum(
            "qk,qd->kd",
            seq_prob.astype(jnp.bfloat16),
            attn_rows,
            preferred_element_type=jnp.float32,
        )
        memory_w = (inner * decay_w * (1.0 / width)).astype(jnp.bfloat16)
        grad_mw = jnp.dot(memory_rows, value_rows.T, preferred_element_type=jnp.float32)
        value_part = value_part + jnp.einsum(
            "qk,qd->kd", memory_w, memory_rows, preferred_element_type=jnp.float32
        )
        grad_inner = (grad_mw * decay_w * (1.0 / width)).astype(jnp.bfloat16)
        rows_grad = rows_grad + jnp.dot(grad_inner, key_rows, preferred_element_type=jnp.float32)
        key_part = key_part + jnp.einsum(
            "qk,qd->kd", grad_inner, query_rows, preferred_element_type=jnp.float32
        )
        grad_rate = grad_rate - jnp.sum(grad_mw * inner * decay_w * (1.0 / width) * distance)
        grad_keys = grad_keys.at[:reach].add(key_part)
        grad_values = grad_values.at[:reach].add(value_part)
        query_grads.append(rows_grad)
    return (
        jnp.concatenate(query_grads, 0),
        grad_keys,
        grad_values,
        grad_pkeys,
        grad_pvalues,
        grad_rate,
    )


def layer_forward(rows_in, seg_ids, full, pkv, rates):
    mix_w, out_w, gu_w, down_w, gains = full
    tokens = rows_in.shape[0]
    gain_one = gains[:, 0].astype(jnp.float32)
    gain_two = gains[:, 1].astype(jnp.float32)
    inverse_one = rms_scale(rows_in)
    scaled_one = rows_in * inverse_one
    normed = (scaled_one * gain_one).astype(jnp.bfloat16)
    proj = jnp.dot(normed, mix_w, preferred_element_type=jnp.float32)
    qkv = proj[:, : 3 * D].astype(jnp.bfloat16).reshape(tokens, 3, H, HD)
    gate = jax.nn.sigmoid(proj[:, 3 * D :])
    grouped = lax.all_to_all(qkv, "seq", split_axis=2, concat_axis=0, tiled=True)
    attn_heads, memory_heads, lse_heads = ([], [], [])
    for head in range(grouped.shape[2]):
        cols = slice(head * HD, (head + 1) * HD)
        attended, recalled, lse = head_forward(
            grouped[:, 0, head],
            grouped[:, 1, head],
            grouped[:, 2, head],
            pkv[0][:, cols],
            pkv[1][:, cols],
            rates[head],
            seg_ids,
        )
        attn_heads.append(attended)
        memory_heads.append(recalled)
        lse_heads.append(lse)
    mixed = jnp.stack([jnp.stack(attn_heads, 1), jnp.stack(memory_heads, 1)], 1).astype(
        jnp.bfloat16
    )
    returned = lax.all_to_all(mixed, "seq", split_axis=0, concat_axis=2, tiled=True)
    attended = returned[:, 0].reshape(tokens, D).astype(jnp.float32)
    recalled = returned[:, 1].reshape(tokens, D).astype(jnp.float32)
    combined = (attended + gate * recalled).astype(jnp.bfloat16)
    mid = rows_in + jnp.dot(combined, out_w, preferred_element_type=jnp.float32)
    inverse_two = rms_scale(mid)
    scaled_two = mid * inverse_two
    normed_two = (scaled_two * gain_two).astype(jnp.bfloat16)
    gate_up = jnp.dot(normed_two, gu_w, preferred_element_type=jnp.float32)
    hidden = (jax.nn.silu(gate_up[:, :FF]) * gate_up[:, FF:]).astype(jnp.bfloat16)
    result = mid + jnp.dot(hidden, down_w, preferred_element_type=jnp.float32)
    kept = (
        seg_ids,
        inverse_one,
        scaled_one,
        normed,
        grouped,
        jnp.stack(lse_heads, 1),
        gate,
        recalled,
        combined,
        inverse_two,
        scaled_two,
        normed_two,
        gate_up,
        hidden,
    )
    return (result, kept)


def layer_backward(grad_out, kept, full, pkv, rates):
    (
        seg_ids,
        inverse_one,
        scaled_one,
        normed,
        grouped,
        lse_all,
        gate,
        recalled,
        combined,
        inverse_two,
        scaled_two,
        normed_two,
        gate_up,
        hidden,
    ) = kept
    mix_w, out_w, gu_w, down_w, gains = full
    tokens = grad_out.shape[0]
    gain_one = gains[:, 0].astype(jnp.float32)
    gain_two = gains[:, 1].astype(jnp.float32)
    grad_f = grad_out.astype(jnp.bfloat16)
    grad_down = jnp.einsum("tf,td->fd", hidden, grad_f, preferred_element_type=jnp.float32)
    grad_hidden = jnp.dot(grad_f, down_w.T, preferred_element_type=jnp.float32)
    gate_part = gate_up[:, :FF]
    up_part = gate_up[:, FF:]
    sig_part = jax.nn.sigmoid(gate_part)
    grad_gate_part = grad_hidden * up_part * sig_part * (1.0 + gate_part * (1.0 - sig_part))
    grad_up_part = grad_hidden * gate_part * sig_part
    grad_gate_up = jnp.concatenate([grad_gate_part, grad_up_part], 1).astype(jnp.bfloat16)
    grad_gu = jnp.einsum("td,tf->df", normed_two, grad_gate_up, preferred_element_type=jnp.float32)
    grad_normed_two = jnp.dot(grad_gate_up, gu_w.T, preferred_element_type=jnp.float32)
    grad_mid_norm, grad_gain_two = norm_back(grad_normed_two, scaled_two, inverse_two, gain_two)
    grad_mid = grad_out + grad_mid_norm
    grad_branch = grad_mid.astype(jnp.bfloat16)
    grad_out_w = jnp.einsum("td,te->de", combined, grad_branch, preferred_element_type=jnp.float32)
    grad_combined = jnp.dot(grad_branch, out_w.T, preferred_element_type=jnp.float32)
    grad_attended = grad_combined.astype(jnp.bfloat16).reshape(tokens, H, HD)
    grad_recalled = (grad_combined * gate).astype(jnp.bfloat16).reshape(tokens, H, HD)
    grad_gate_pre = grad_combined * recalled * gate * (1.0 - gate)
    outgoing = jnp.stack([grad_attended, grad_recalled], 1)
    headward = lax.all_to_all(outgoing, "seq", split_axis=2, concat_axis=0, tiled=True)
    head_grads, pkey_grads, pvalue_grads, rate_grads = ([], [], [], [])
    for head in range(grouped.shape[2]):
        cols = slice(head * HD, (head + 1) * HD)
        dq, dk, dv, dpk, dpv, drate = head_backward(
            grouped[:, 0, head],
            grouped[:, 1, head],
            grouped[:, 2, head],
            pkv[0][:, cols],
            pkv[1][:, cols],
            rates[head],
            seg_ids,
            lse_all[:, head],
            headward[:, 0, head],
            headward[:, 1, head],
        )
        head_grads.append(jnp.stack([dq, dk, dv], 1))
        pkey_grads.append(dpk)
        pvalue_grads.append(dpv)
        rate_grads.append(drate)
    grads_heads = jnp.stack(head_grads, 2).astype(jnp.bfloat16)
    tokenward = lax.all_to_all(grads_heads, "seq", split_axis=0, concat_axis=2, tiled=True)
    grad_proj = jnp.concatenate(
        [tokenward.reshape(tokens, 3 * D), grad_gate_pre.astype(jnp.bfloat16)], 1
    )
    grad_mix = jnp.einsum("td,tf->df", normed, grad_proj, preferred_element_type=jnp.float32)
    grad_normed = jnp.dot(grad_proj, mix_w.T, preferred_element_type=jnp.float32)
    grad_in_norm, grad_gain_one = norm_back(grad_normed, scaled_one, inverse_one, gain_one)
    grad_rows = grad_mid + grad_in_norm
    weight_terms = (
        grad_mix,
        grad_out_w,
        grad_gu,
        grad_down,
        jnp.stack([grad_gain_one, grad_gain_two], 1),
    )
    memory_terms = (
        jnp.stack([jnp.concatenate(pkey_grads, 1), jnp.concatenate(pvalue_grads, 1)], 0),
        jnp.stack(rate_grads, 0),
    )
    return (weight_terms, memory_terms, grad_rows)


def on_device(
    inputs, segment_ids, cotangent, w_mix, w_out, w_gu, w_down, norm_gains, persist_kv, memory_decay
):
    first = lax.axis_index("section") == 0
    own_weights = (w_mix[0], w_out[0], w_gu[0], w_down[0], norm_gains[0])
    pkv = persist_kv[0]
    rates = memory_decay[0]
    count = inputs.shape[0]
    tokens = inputs.shape[2]
    zero_rows = jnp.zeros((tokens, D), jnp.float32)
    received = jnp.zeros((tokens, D), jnp.bfloat16)
    kept_ticks, out_ticks = ([], [])
    for tick in range(count + 1):
        own_rows = inputs[tick, 0].astype(jnp.float32) if tick < count else zero_rows
        layer_in = jnp.where(first, own_rows, received.astype(jnp.float32))
        seg_ids = jnp.where(
            first, segment_ids[min(tick, count - 1), 0], segment_ids[max(tick - 1, 0), 0]
        )
        full = (
            lax.all_gather(own_weights[0], "shard", axis=0, tiled=True),
            lax.all_gather(own_weights[1], "shard", axis=0, tiled=True),
            lax.all_gather(own_weights[2], "shard", axis=0, tiled=True),
            lax.all_gather(own_weights[3], "shard", axis=0, tiled=True),
            lax.all_gather(own_weights[4], "shard", axis=0, tiled=True),
        )
        result, kept = layer_forward(layer_in, seg_ids, full, pkv, rates)
        result_low = result.astype(jnp.bfloat16)
        out_ticks.append(result_low)
        kept_ticks.append(kept)
        if tick < count:
            received = shifted(result_low, "section", 1)
    grad_weights = (
        jnp.zeros((D, 4 * D), jnp.float32),
        jnp.zeros((D, D), jnp.float32),
        jnp.zeros((D, 2 * FF), jnp.float32),
        jnp.zeros((FF, D), jnp.float32),
        jnp.zeros((D, 2), jnp.float32),
    )
    grad_memory = (
        jnp.zeros((2,) + pkv.shape[1:], jnp.float32),
        jnp.zeros(rates.shape, jnp.float32),
    )
    back_received = jnp.zeros((tokens, D), jnp.bfloat16)
    grad_ticks = []
    for tick in range(count + 1):
        lower = max(tick - 1, 0)
        upper = min(tick + 1, count)
        kept = jax.tree.map(
            lambda early, late: jnp.where(first, early, late), kept_ticks[lower], kept_ticks[upper]
        )
        given = cotangent[tick, 0].astype(jnp.float32) if tick < count else zero_rows
        grad_out = jnp.where(first, back_received.astype(jnp.float32), given)
        full = (
            lax.all_gather(own_weights[0], "shard", axis=0, tiled=True),
            lax.all_gather(own_weights[1], "shard", axis=0, tiled=True),
            lax.all_gather(own_weights[2], "shard", axis=0, tiled=True),
            lax.all_gather(own_weights[3], "shard", axis=0, tiled=True),
            lax.all_gather(own_weights[4], "shard", axis=0, tiled=True),
        )
        weight_terms, memory_terms, grad_rows = layer_backward(grad_out, kept, full, pkv, rates)
        grad_weights = jax.tree.map(jnp.add, grad_weights, weight_terms)
        grad_memory = jax.tree.map(jnp.add, grad_memory, memory_terms)
        grad_ticks.append(grad_rows)
        if tick < count:
            back_received = shifted(grad_rows.astype(jnp.bfloat16), "section", -1)
    section_out = jnp.stack(
        [jnp.where(first, out_ticks[batch], out_ticks[batch + 1]) for batch in range(count)], 0
    )
    section_grad = jnp.stack(
        [
            jnp.where(
                first,
                grad_ticks[batch + 1],
                grad_ticks[batch].astype(jnp.bfloat16).astype(jnp.float32),
            )
            for batch in range(count)
        ],
        0,
    )
    shares = jax.tree.map(
        lambda part: part.astype(jnp.float32),
        lax.psum_scatter(as_sent(grad_weights), "shard", scatter_dimension=0, tiled=True),
    )
    shares = jax.tree.map(lambda part: part.astype(jnp.float32), lax.psum(as_sent(shares), "seq"))
    memory_sums = lax.psum(grad_memory, "shard")
    return (
        section_out.reshape(1, count, 1, tokens, D),
        section_grad.reshape(1, count, 1, tokens, D),
        shares[0][None],
        shares[1][None],
        shares[2][None],
        shares[3][None],
        shares[4][None],
        memory_sums[0][None],
        memory_sums[1][None],
    )


MESH = pl.DeviceIdType.MESH
BF = jnp.bfloat16
F32 = jnp.float32


def here():
    return (lax.axis_index("section"), lax.axis_index("seq"), lax.axis_index("shard"))


def peer(place, chip, flip):
    x, s, z = place
    if chip % 2:
        x = 1 - x
    if chip // 2:
        s = (s + 2) % 4
    if flip:
        s = s + 1 - 2 * (s % 2)
    return (x, s, z)


def rows_of(device, size):
    x, s, _ = device
    return pl.ds(pl.multiple_of((s * 2 + x) * size, size), size)


class Gather:
    def __init__(self, full, batch, send, recv):
        self.place = here()
        self.full, self.batch, self.send, self.recv = full, batch, send, recv
        self.size = full.shape[1] // 8

    def copy(self, owner, target, sem):
        block = self.full.at[self.batch, rows_of(owner, self.size)]
        return pltpu.make_async_remote_copy(
            src_ref=block,
            dst_ref=block,
            send_sem=self.send.at[self.batch, sem],
            recv_sem=self.recv.at[self.batch, sem],
            device_id=target,
            device_id_type=MESH,
        )

    def start(self, value):
        self.full[self.batch, rows_of(self.place, self.size), :] = value
        for chip in (3, 1, 2, 0):
            self.copy(self.place, peer(self.place, chip, chip == 0), chip).start()

    def forward(self):
        other = peer(self.place, 0, True)
        for chip in (1, 2, 3):
            owner = peer(self.place, chip, False)
            self.copy(owner, owner, chip).wait_recv()
            self.copy(owner, other, 3 + chip).start()

    def finish(self):
        other = peer(self.place, 0, True)
        self.copy(other, other, 0).wait_recv()
        for chip in (1, 2, 3):
            owner = peer(self.place, chip, True)
            self.copy(owner, other, 3 + chip).wait_recv()
        for chip in (0, 1, 2, 3):
            self.copy(self.place, peer(self.place, chip, chip == 0), chip).wait_send()
        for chip in (1, 2, 3):
            self.copy(peer(self.place, chip, False), other, 3 + chip).wait_send()


class Scatter:
    def __init__(self, part, batch, pair, away, near, send, recv):
        self.place = here()
        self.part, self.batch, self.pair, self.away, self.near = part, batch, pair, away, near
        self.send, self.recv = send, recv
        self.size = part.shape[1] // 8

    def to_pair(self, chip):
        return pltpu.make_async_remote_copy(
            src_ref=self.part.at[self.batch, rows_of(peer(self.place, chip, True), self.size)],
            dst_ref=self.pair.at[self.batch, chip],
            send_sem=self.send.at[self.batch, chip],
            recv_sem=self.recv.at[self.batch, chip],
            device_id=peer(self.place, 0, True),
            device_id_type=MESH,
        )

    def to_chip(self, chip):
        return pltpu.make_async_remote_copy(
            src_ref=self.away.at[self.batch, chip - 1],
            dst_ref=self.near.at[self.batch, chip - 1],
            send_sem=self.send.at[self.batch, 3 + chip],
            recv_sem=self.recv.at[self.batch, 3 + chip],
            device_id=peer(self.place, chip, False),
            device_id_type=MESH,
        )

    def start(self):
        for chip in (3, 1, 2, 0):
            self.to_pair(chip).start()

    def chip_sum(self, chip):
        self.to_pair(chip).wait_recv()
        own = self.part[self.batch, rows_of(peer(self.place, chip, False), self.size), :]
        return own.astype(F32) + self.pair[self.batch, chip].astype(F32)

    def forward(self):
        for chip in (3, 1, 2):
            self.away[self.batch, chip - 1] = self.chip_sum(chip).astype(BF)
            self.to_chip(chip).start()

    def finish(self):
        total = self.chip_sum(0)
        for chip in (1, 2, 3):
            self.to_chip(chip).wait_recv()
            total = total + self.near[self.batch, chip - 1].astype(F32)
        for chip in (0, 1, 2, 3):
            self.to_pair(chip).wait_send()
        for chip in (1, 2, 3):
            self.to_chip(chip).wait_send()
        return total


class Column:
    def __init__(self, send, recv):
        self.place = here()
        self.send, self.recv = send, recv

    def copy(self, source, landing, sent, received, plane):
        x, s, _ = self.place
        return pltpu.make_async_remote_copy(
            src_ref=source,
            dst_ref=landing,
            send_sem=self.send.at[sent],
            recv_sem=self.recv.at[received],
            device_id=(x, s, plane),
            device_id_type=MESH,
        )

    def at_each(self, body):
        for at in range(4):

            @pl.when(self.place[2] == at)
            def _():
                body(at)


class ColumnSum(Column):
    RELAYED = ((3, 1), None, None, (0, 2))
    DIRECT = ((2, 1), (2, 0), (1, 3), (1, 2))
    SOURCES = ((1, 2), (0, 2, 3), (0, 1, 3), (1, 2))

    def __init__(self, own, slots, out, send, recv):
        super().__init__(send, recv)
        self.own, self.slots, self.out = own, slots, out

    def first(self, at):
        block, plane = self.RELAYED[at]
        return self.copy(self.own.at[block], self.slots.at[plane], at, plane, plane)

    def direct(self, at, plane):
        return self.copy(self.own.at[plane], self.slots.at[at], plane, at, plane)

    def relayed(self, at):
        end = 3 if at == 1 else 0
        return self.copy(self.slots.at[at], self.slots.at[at], end, at, end)

    def start(self):
        def body(at):
            if self.RELAYED[at]:
                self.first(at).start()
            for plane in self.DIRECT[at]:
                self.direct(at, plane).start()

        self.at_each(body)

    def hop(self):
        for at, block in ((1, 3), (2, 0)):

            @pl.when(self.place[2] == at)
            def _():
                self.relayed(at).wait_recv()
                self.slots[at] = (
                    self.slots[at].astype(F32) + self.own[block].astype(F32)
                ).astype(BF)
                self.relayed(at).start()

    def finish(self):
        def body(at):
            total = self.own[at].astype(F32)
            for plane in self.SOURCES[at]:
                self.direct(plane, at).wait_recv()
                total = total + self.slots[plane].astype(F32)
            self.out[...] = total.astype(BF)
            if self.RELAYED[at]:
                self.first(at).wait_send()
            else:
                self.relayed(at).wait_send()
            for plane in self.DIRECT[at]:
                self.direct(at, plane).wait_send()

        self.at_each(body)


class ColumnGather(Column):
    TARGETS = ((2, 1), (3, 2, 0), (0, 1, 3), (1, 2))

    def __init__(self, full, send, recv):
        super().__init__(send, recv)
        self.full = full

    def block(self, at, plane):
        return self.copy(self.full.at[at], self.full.at[at], plane, at, plane)

    def relayed(self, at):
        block, plane = (3, 0) if at == 1 else (0, 3)
        return self.copy(self.full.at[block], self.full.at[block], at, block, plane)

    def start(self):
        def body(at):
            for plane in self.TARGETS[at]:
                self.block(at, plane).start()

        self.at_each(body)

    def hop(self):
        for at in (1, 2):

            @pl.when(self.place[2] == at)
            def _():
                self.relayed(at).wait_recv()
                self.relayed(at).start()

    def finish(self):
        def body(at):
            for plane in range(4):
                if plane != at and (at, plane) not in ((1, 3), (2, 0)):
                    self.block(plane, at).wait_recv()
            for plane in self.TARGETS[at]:
                self.block(at, plane).wait_send()
            if at in (1, 2):
                self.relayed(at).wait_send()

        self.at_each(body)


class Root(Column):
    def __init__(self, send, recv):
        super().__init__(send, recv)
        x, s, z = self.place
        self.root = 2 * x + s // 2
        self.low = self.root < 2
        self.between = jnp.where(self.low, 2, 1)
        self.end = jnp.where(self.low, 3, 0)
        self.is_root = z == self.root


class RootSum(Root):
    def __init__(self, own, slots, out, send, recv):
        super().__init__(send, recv)
        self.own, self.slots, self.out = own, slots, out

    def toward(self, slot, plane, source=None):
        landing = self.slots.at[slot]
        return self.copy(landing if source is None else source, landing, 0, slot, plane)

    def start(self):
        z = self.place[2]

        @pl.when(z == self.end)
        def _():
            self.toward(0, self.between, self.own).start()

        @pl.when((z != self.end) & (z != self.between) & (z != self.root))
        def _():
            self.toward(1, self.root, self.own).start()

    def hop(self):
        @pl.when(self.place[2] == self.between)
        def _():
            self.toward(0, self.root).wait_recv()
            self.slots[0] = (self.slots[0].astype(F32) + self.own[...].astype(F32)).astype(BF)
            self.toward(0, self.root).start()

    def finish(self):
        self.out[...] = self.own[...]

        @pl.when(self.is_root)
        def _():
            total = self.own[...].astype(F32)
            for slot in (0, 1):
                self.toward(slot, self.root).wait_recv()
                total = total + self.slots[slot].astype(F32)
            self.out[...] = total.astype(BF)

        @pl.when(jnp.logical_not(self.is_root))
        def _():
            self.toward(0, self.root).wait_send()


def nn(left, right):
    return jnp.dot(left, right, preferred_element_type=F32)


def nt(left, right):
    return lax.dot_general(left, right, (((1,), (1,)), ((), ())), preferred_element_type=F32)


def tn(left, right):
    return lax.dot_general(left, right, (((0,), (0,)), ((), ())), preferred_element_type=F32)


def flat(ref):
    value = ref[...]
    return value.reshape(-1, value.shape[-1])


def in_blocks(length, size, body):
    def step(index, carry):
        body(pl.ds(pl.multiple_of(index * size, size), size), index * size)
        return carry

    lax.fori_loop(0, length // size, step, 0)


def weights_of_scores(query, keys, pkeys, seg_rows, seg_cols, begin, rate):
    scale = 1.0 / math.sqrt(HD)
    inner = nt(query, keys)
    per_scores = nt(query, pkeys) * scale
    row_places = begin + lax.broadcasted_iota(jnp.int32, inner.shape, 0)
    col_places = lax.broadcasted_iota(jnp.int32, inner.shape, 1)
    allowed = (seg_rows == seg_cols) & (col_places <= row_places)
    distance = jnp.maximum(row_places - col_places, 0).astype(F32)
    decay_w = jnp.where(allowed, jnp.exp(-rate * distance) * (1.0 / HD), 0.0)
    seq_scores = jnp.where(allowed, inner * scale, -jnp.inf)
    top = jnp.maximum(
        jnp.max(per_scores, axis=1, keepdims=True), jnp.max(seq_scores, axis=1, keepdims=True)
    )
    per_exp = jnp.exp(per_scores - top)
    seq_exp = jnp.exp(seq_scores - top)
    denom = jnp.sum(per_exp, axis=1, keepdims=True) + jnp.sum(seq_exp, axis=1, keepdims=True)
    share = 1.0 / denom
    return inner, decay_w, distance, seq_exp * share, per_exp * share


class BackwardIn(NamedTuple):
    grad_full: Any
    grad_rows: Any
    rows: Any
    out_low: Any
    out_high: Any
    gains: Any
    persist: Any
    rates: Any
    seg_rows: Any
    seg_cols: Any


class BackwardOut(NamedTuple):
    mix_buf: Any
    gu_buf: Any
    down_buf: Any
    out_buf: Any
    rows_buf: Any
    grads_buf: Any
    plane_buf: Any
    grad_low: Any
    grad_high: Any


class PlaneScratch(NamedTuple):
    part: Any
    pair: Any
    away: Any
    near: Any
    ssend: Any
    srecv: Any
    gsend: Any
    grecv: Any


class BackwardScratch(NamedTuple):
    grad_gu: Any
    grad_proj: Any
    grad_keys: Any
    grad_values: Any
    branch: Any
    grad_mid: Any
    grad_next: Any
    grad_persist: Any
    grad_rate: Any
    gain_sums: Any
    small: Any
    column_buf: Any
    own_gu: Any
    own_down: Any
    grad_mix: Any
    grad_out: Any
    gu_slots: Any
    down_slots: Any
    mix_slots: Any
    root_slots: Any
    gu_sum: Any
    down_sum: Any
    mix_sum: Any
    out_sum: Any
    csend: Any
    crecv: Any
    hsend: Any
    hrecv: Any
    psend: Any
    precv: Any
    osend: Any
    orecv: Any
    rsend: Any
    rrecv: Any
    zsend: Any
    zrecv: Any
    qsend: Any
    qrecv: Any
    loaded: Any


def fields(*kinds):
    return tuple(name for kind in kinds for name in kind._fields)


def named(names, refs):
    return types.SimpleNamespace(**dict(zip(names, refs, strict=True)))


def remote(source, landing, sems, index, target):
    return pltpu.make_async_remote_copy(
        src_ref=source,
        dst_ref=landing,
        send_sem=sems[0].at[index],
        recv_sem=sems[1].at[index],
        device_id=target,
        device_id_type=MESH,
    )


class RootGather(Root):
    def __init__(self, block, send, recv):
        super().__init__(send, recv)
        self.block = block

    def to(self, plane, sent):
        return self.copy(self.block, self.block, sent, 0, plane)

    def near(self):
        return jnp.where(self.low, 1 - self.root, 5 - self.root)

    def start(self):
        @pl.when(self.is_root)
        def _():
            self.to(self.between, 0).start()
            self.to(self.near(), 1).start()

    def hop(self):
        @pl.when(self.place[2] == self.between)
        def _():
            self.to(self.end, 0).wait_recv()
            self.to(self.end, 0).start()

    def finish(self):
        z = self.place[2]

        @pl.when((z != self.root) & (z != self.between))
        def _():
            self.to(self.end, 0).wait_recv()

        @pl.when((z == self.root) | (z == self.between))
        def _():
            self.to(self.end, 0).wait_send()

        @pl.when(self.is_root)
        def _():
            self.to(self.end, 1).wait_send()


class SeqGather:
    def __init__(self, full, batch, send, recv):
        self.place = here()
        self.full, self.batch, self.send, self.recv = full, batch, send, recv
        self.size = full.shape[1] // 4
        self.beside = peer(self.place, 2, False)
        self.sibling = peer(self.place, 0, True)

    def rows(self, owner):
        return pl.ds(pl.multiple_of(owner[1] * self.size, self.size), self.size)

    def copy(self, owner, target, sem):
        block = self.full.at[self.batch, self.rows(owner)]
        sems = (self.send.at[self.batch], self.recv.at[self.batch])
        return remote(block, block, sems, sem, target)

    def start(self, value):
        self.full[self.batch, self.rows(self.place), :] = value
        self.copy(self.place, self.beside, 0).start()
        self.copy(self.place, self.sibling, 1).start()

    def forward(self):
        self.copy(self.beside, self.beside, 0).wait_recv()
        self.copy(self.beside, self.sibling, 2).start()

    def finish(self):
        self.copy(self.sibling, self.sibling, 1).wait_recv()
        self.copy(peer(self.place, 2, True), self.sibling, 2).wait_recv()
        self.copy(self.place, self.beside, 0).wait_send()
        self.copy(self.place, self.sibling, 1).wait_send()
        self.copy(self.beside, self.sibling, 2).wait_send()


class ForwardIn(NamedTuple):
    inputs: Any
    small: Any
    gain_rows: Any
    w_mix: Any
    w_out: Any
    w_gu: Any
    w_down: Any
    seg_rows: Any
    seg_cols: Any


class ForwardOut(NamedTuple):
    rows: Any
    gains: Any
    persist: Any
    rates: Any


class Kept(NamedTuple):
    normed: Any
    mix: Any
    out: Any
    gu: Any
    down: Any
    qkv: Any
    gate: Any
    recalled: Any
    combined: Any
    mid: Any
    normed_two: Any
    gate_up: Any
    hidden: Any
    out_rows: Any


class ForwardScratch(NamedTuple):
    gain_all: Any
    small_all: Any
    mix_away: Any
    gu_away: Any
    down_away: Any
    zsend: Any
    zrecv: Any
    psend: Any
    precv: Any
    xsend: Any
    xrecv: Any
    gsend: Any
    grecv: Any
    csend: Any
    crecv: Any
    hsend: Any
    hrecv: Any
    saved: Any


def each(parts, act):
    for part in parts:
        act(part)


def forward_kernel(unit, *refs):
    count = len(Kept._fields)
    r, refs = refs[: len(ForwardIn._fields)], refs[len(ForwardIn._fields) :]
    given = vars(named(ForwardIn._fields, r))
    r, refs = refs[: len(ForwardOut._fields)], refs[len(ForwardOut._fields) :]
    given |= vars(named(ForwardOut._fields, r))
    in_hbm = [refs[:count], refs[count : 2 * count]]
    refs = refs[2 * count :]
    in_vmem = [refs[:count], refs[count : 2 * count]]
    refs = refs[2 * count :]
    scratch = PlaneScratch._fields[:6] + ForwardScratch._fields
    r = types.SimpleNamespace(**given, **vars(named(scratch, refs)))
    views = [types.SimpleNamespace(**vars(named(Kept._fields, part))) for part in in_vmem]
    views[0].rows, views[1].rows = r.rows, views[0].out_rows

    def save(layer, which):
        for name in which:
            index = Kept._fields.index(name)
            yield pltpu.make_async_copy(
                in_vmem[layer][index], in_hbm[layer][index], r.saved.at[layer, index]
            )

    place = here()
    x, s, z = place
    partner = peer(place, 1, False)
    flips = [(dx, ds) for dx in (0, 1) for ds in range(4) if dx or ds]
    plane = [((x + dx) % 2, (s + ds) % 4, z) for dx, ds in flips]
    column = [(x, s, (z + dz) % 4) for dz in (1, 2, 3)]
    column += [(1 - x, s, (z + dz) % 4) for dz in (1, 2, 3)]
    barrier = pltpu.get_barrier_semaphore()
    for other in plane + column:
        pl.semaphore_signal(barrier, inc=1, device_id=other, device_id_type=MESH)
    pl.semaphore_wait(barrier, len(plane) + len(column))

    zsems, psems, xsems = (r.zsend, r.zrecv), (r.psend, r.precv), (r.xsend, r.xrecv)
    holders = [*column, partner]

    def gains_to(index):
        return remote(r.gain_rows, r.gain_all.at[x, z], zsems, index, holders[index])

    for index in range(7):
        gains_to(index).start()
    r.gain_all[x, z] = r.gain_rows[...]

    mine, other = x * 4 + s, (1 - x) * 4 + s

    def mix_part(which):
        heads = [pl.ds(pl.multiple_of(kind * D + which * HD, HD), HD) for kind in range(4)]
        return jnp.concatenate([r.w_mix[0, :, cols] for cols in heads], 1)

    out_rows = pl.ds(pl.multiple_of(s % 2 * HD, HD), HD)
    root = z == 2 * x + s // 2
    rooted = z == 2 * (1 - x) + s // 2
    for layer in (0, 1):
        v = views[layer]

        @pl.when(x == layer)
        def _():
            r.mix_away[...] = mix_part(other)
            remote(r.mix_away, v.mix.at[z], xsems, 0, partner).start()
            v.mix[z] = mix_part(mine)

            @pl.when(rooted)
            def _():
                remote(r.w_out.at[0, out_rows], v.out, xsems, 1, partner).start()

            @pl.when(root)
            def _():
                v.out[...] = r.w_out[0, out_rows, :]

    for index in range(7):
        gains_to(index).wait_recv()
    for layer in range(2):
        for owner in range(4):
            for kind in range(2):
                for half in range(2):
                    begin = owner * 2 * HD + half * HD
                    row = 2 * kind + half
                    r.gains[layer, kind : kind + 1, begin : begin + HD] = r.gain_all[
                        layer, owner, row : row + 1, :
                    ]
    size = r.rows.shape[1]
    own_half = pl.ds(pl.multiple_of(x * size, size), size)
    arriving = [SeqGather(views[0].normed, batch, r.gsend, r.grecv) for batch in range(2)]
    for batch, gather in enumerate(arriving):
        rows = r.inputs[batch, 0].astype(F32)
        gather.start((rows * rms_scale(rows) * r.gains[0, 0:1, :]).astype(BF))
        r.rows[batch] = r.inputs[batch, 0, own_half, :]

    for index in range(7):
        remote(r.small, r.small_all.at[x, s], psems, index, plane[index]).start()
    r.small_all[x, s] = r.small[...]

    padded = r.down_away.shape[0]
    width = 8 * unit + 64

    def select(which, offset):
        begin = lax.broadcasted_iota(jnp.int32, (width, 128), 0) - offset
        col = lax.broadcasted_iota(jnp.int32, (width, 128), 1)
        return jnp.where((begin == which * unit + col) & (col < unit), 1.0, 0.0).astype(BF)

    def gu_part(which, out):
        for owner in range(4):
            base = owner * 8 * unit
            offset = base % 128
            chosen = select(which, offset)
            for side in range(2):
                begin = side * FF + base - offset
                part = nn(r.w_gu[0, :, begin : begin + width], chosen).astype(BF)
                at = side * 4 * padded + owner * padded
                out[:, at : at + padded] = part[:, :padded]

    def down_part(which, out):
        row = lax.broadcasted_iota(jnp.int32, (padded, 8 * unit), 0)
        col = lax.broadcasted_iota(jnp.int32, (padded, 8 * unit), 1)
        chosen = jnp.where((col == which * unit + row) & (row < unit), 1.0, 0.0).astype(BF)
        out[...] = nn(chosen, r.w_down[0]).astype(BF)

    gu_part(other, r.gu_away)
    down_part(other, r.down_away)
    for layer in (0, 1):
        v = views[layer]

        @pl.when(x == layer)
        def _():
            remote(r.gu_away, v.gu.at[z], xsems, 2, partner).start()
            remote(r.down_away, v.down.at[z], xsems, 3, partner).start()

    mixers, feeds = [], []
    for layer, v in enumerate(views):
        sems = [(r.csend.at[3 * layer + i], r.crecv.at[3 * layer + i]) for i in range(3)]
        mixers.append(
            [
                ColumnGather(v.mix, *sems[0]),
                RootGather(v.out, r.hsend.at[layer], r.hrecv.at[layer]),
            ]
        )
        feeds.append([ColumnGather(v.gu, *sems[1]), ColumnGather(v.down, *sems[2])])

    def swapped(layer, index):
        v = views[layer]
        landing = [v.mix.at[z], v.out, v.gu.at[z], v.down.at[z]][index]
        here_from = remote(landing, landing, xsems, index, partner)

        @pl.when((x != layer) & root if index == 1 else x != layer)
        def _():
            here_from.wait_recv()

    def start_mixer(layer):
        for index, part in enumerate(mixers[layer]):
            swapped(layer, index)
            part.start()

    def start_feed(layer):
        for index, part in enumerate(feeds[layer]):
            swapped(layer, 2 + index)
            part.start()

    start_mixer(0)
    for layer, v in enumerate(views):

        @pl.when(x == layer)
        def _():
            gu_part(mine, v.gu.at[z])
            down_part(mine, v.down.at[z])

    start_feed(0)
    arriving[0].forward()
    each(mixers[0], lambda part: part.hop())
    arriving[1].forward()

    for index in range(7):
        dx, ds = flips[index]
        landing = r.small_all.at[(x + dx) % 2, (s + 4 - ds) % 4]
        remote(r.small, landing, psems, index, plane[index]).wait_recv()
    for layer in range(2):
        begin = pl.multiple_of(s % 2 * 32, 32)
        rows = r.small_all[layer, 2 * x + s // 2, pl.ds(begin, 32), :]
        r.persist[layer] = rows.astype(BF).reshape(2, 16, HD)
        begin = pl.multiple_of(64 + s % 2 * 8, 8)
        r.rates[layer] = r.small_all[layer, 2 * x + s // 2, pl.ds(begin, 8), :]

    length = r.part.shape[1]

    def project(layer, batch):
        v = views[layer]

        def block(rows, begin):
            proj = nn(v.normed[batch, rows, :], flat(v.mix))
            v.qkv[batch, rows, :] = proj[:, : 3 * HD].astype(BF)
            v.gate[batch, rows, :] = jax.nn.sigmoid(proj[:, 3 * HD :])

        in_blocks(length, 256, block)

    def mixer(layer, batch):
        v = views[layer]

        def block(rows, begin):
            values = v.qkv[batch, :, 2 * HD :]
            inner, decay_w, _, probs, per_probs = weights_of_scores(
                v.qkv[batch, rows, :HD],
                v.qkv[batch, :, HD : 2 * HD],
                r.persist[layer, 0],
                r.seg_rows[batch, rows, :],
                r.seg_cols[batch],
                begin,
                r.rates[layer, 0:1, 0:1],
            )
            attended = nn(probs.astype(BF), values) + nn(per_probs.astype(BF), r.persist[layer, 1])
            recalled = nn((inner * decay_w).astype(BF), values).astype(BF)
            v.recalled[batch, rows, :] = recalled
            combined = attended.astype(BF).astype(F32)
            combined = combined + v.gate[batch, rows, :] * recalled.astype(F32)
            combined = combined.astype(BF)
            v.combined[batch, rows, :] = combined
            r.part[batch, rows, :] = nn(combined, v.out[...]).astype(BF)

        in_blocks(length, 128, block)

    def feed(layer, batch):
        v = views[layer]

        def block(rows, begin):
            gate_up = nn(v.normed_two[batch, rows, :], flat(v.gu))
            v.gate_up[batch, rows, :] = gate_up
            half = gate_up.shape[1] // 2
            hidden = (jax.nn.silu(gate_up[:, :half]) * gate_up[:, half:]).astype(BF)
            v.hidden[batch, rows, :] = hidden
            r.part[batch, rows, :] = nn(hidden, flat(v.down)).astype(BF)

        in_blocks(length, 256, block)

    def scatter(batch):
        return Scatter(r.part, batch, r.pair, r.away, r.near, r.ssend, r.srecv)

    def send_normed(batch, own, gain, full):
        gather = Gather(full, batch, r.gsend, r.grecv)
        gather.start((own * rms_scale(own) * gain).astype(BF))
        return gather

    mixer_names = Kept._fields[:3] + Kept._fields[5:9]
    for layer, v in enumerate(views):
        parts = []
        for batch in range(2):
            if layer == 1:
                arriving[batch].forward()
            arriving[batch].finish()
            if batch == 0:
                each(mixers[layer], lambda part: part.finish())
            project(layer, batch)
            mixer(layer, batch)
            part = scatter(batch)
            part.start()
            part.forward()
            parts.append(part)
        each(save(layer, mixer_names), lambda copy: copy.start())
        if layer == 0:
            start_mixer(1)
        gathers = []
        for batch, part in enumerate(parts):
            mid = v.rows[batch].astype(F32) + part.finish()
            v.mid[batch] = mid
            gathers.append(send_normed(batch, mid, r.gains[layer, 1:2, :], v.normed_two))
        each(feeds[layer], lambda part: part.hop())
        parts = []
        for batch, gather in enumerate(gathers):
            gather.forward()
            gather.finish()
            if batch == 0:
                each(feeds[layer], lambda part: part.finish())
            feed(layer, batch)
            part = scatter(batch)
            part.start()
            part.forward()
            parts.append(part)
        if layer == 0:
            each(mixers[1], lambda part: part.hop())
            start_feed(1)
        each(save(layer, Kept._fields[3:5] + Kept._fields[9:13]), lambda copy: copy.start())
        arriving = []
        for batch, part in enumerate(parts):
            rows = (v.mid[batch] + part.finish()).astype(BF)
            v.out_rows[batch] = rows
            if layer == 0:
                gain = r.gains[1, 0:1, :]
                arriving.append(send_normed(batch, rows.astype(F32), gain, views[1].normed))
        each(save(layer, Kept._fields[13:]), lambda copy: copy.start())

    for layer in range(2):
        for copy in save(layer, Kept._fields):
            copy.wait()
    remote(r.mix_away, r.mix_away, xsems, 0, partner).wait_send()
    remote(r.gu_away, r.gu_away, xsems, 2, partner).wait_send()
    remote(r.down_away, r.down_away, xsems, 3, partner).wait_send()

    @pl.when(rooted)
    def _():
        remote(views[0].out, views[0].out, xsems, 1, partner).wait_send()

    for index in range(7):
        gains_to(index).wait_send()
        remote(r.small, r.small_all.at[x, s], psems, index, plane[index]).wait_send()


def backward_kernel(*refs):
    saved_names = Kept._fields[:-1]
    count = len(saved_names)
    given = vars(named(BackwardIn._fields, refs[: len(BackwardIn._fields)]))
    refs = refs[len(BackwardIn._fields) :]
    in_hbm = [refs[:count], refs[count : 2 * count]]
    refs = refs[2 * count :]
    given |= vars(named(BackwardOut._fields, refs[: len(BackwardOut._fields)]))
    refs = refs[len(BackwardOut._fields) :]
    in_vmem = refs[:count]
    given |= vars(named(saved_names, in_vmem))
    scratch = fields(PlaneScratch, BackwardScratch)
    r = types.SimpleNamespace(**given, **vars(named(scratch, refs[count:])))
    length = r.part.shape[1]
    place = here()
    x, s, z = place

    def load(layer, which):
        for name in which:
            index = saved_names.index(name)
            yield pltpu.make_async_copy(in_hbm[layer][index], in_vmem[index], r.loaded.at[index])

    feed_names = saved_names[3:5] + saved_names[9:]
    mixer_names = saved_names[:3] + saved_names[5:9]
    for which in (feed_names, mixer_names):
        each(load(1, which), lambda copy: copy.start())
    feeds, mixers = [], []
    for layer in range(2):
        sems = [(r.csend.at[3 * layer + i], r.crecv.at[3 * layer + i]) for i in range(3)]
        feeds.append(
            [
                ColumnSum(r.own_gu, r.gu_slots.at[layer], r.gu_sum.at[layer], *sems[0]),
                ColumnSum(r.own_down, r.down_slots.at[layer], r.down_sum.at[layer], *sems[1]),
            ]
        )
        mixers.append(
            [
                ColumnSum(r.grad_mix, r.mix_slots.at[layer], r.mix_sum.at[layer], *sems[2]),
                RootSum(
                    r.grad_out,
                    r.root_slots.at[layer],
                    r.out_sum.at[layer],
                    r.hsend.at[layer],
                    r.hrecv.at[layer],
                ),
            ]
        )
    grads = (r.grad_low, r.grad_high)

    def feed_back(full, batch):
        def block(rows, begin):
            grad_hidden = nt(full[batch, rows, :], flat(r.down))
            half = grad_hidden.shape[1]
            gate_part = r.gate_up[batch, rows, :half]
            up_part = r.gate_up[batch, rows, half:]
            sig_part = jax.nn.sigmoid(gate_part)
            silu = gate_part * sig_part
            grad_gate = grad_hidden * up_part * (sig_part + silu * (1.0 - sig_part))
            r.grad_gu[batch, rows, :half] = grad_gate.astype(BF)
            r.grad_gu[batch, rows, half:] = (grad_hidden * silu).astype(BF)
            r.part[batch, rows, :] = nt(r.grad_gu[batch, rows, :], flat(r.gu)).astype(BF)

        in_blocks(length, 256, block)

    def down_weights(full):
        def down(cols, begin):
            grad = tn(r.hidden[0], full[0, :, cols])
            grad = grad + tn(r.hidden[1], full[1, :, cols])
            grad = grad.reshape(4, grad.shape[0] // 4, grad.shape[1])
            r.own_down[:, :, cols] = grad.astype(BF)

        in_blocks(D, 256, down)

    def product(out, left, right):
        for owner in range(4):
            cols = slice(owner * (D // 4), (owner + 1) * (D // 4))
            grad = tn(left[0, :, cols], right[0]) + tn(left[1, :, cols], right[1])
            out[owner] = grad.astype(BF)

    def mixer_back(layer, batch):
        scale = 1.0 / math.sqrt(HD)
        r.grad_keys[...] = jnp.zeros_like(r.grad_keys)
        r.grad_values[...] = jnp.zeros_like(r.grad_values)

        def block(rows, begin):
            grad_combined = nt(r.branch[batch, rows, :], r.out[...])
            gate = r.gate[batch, rows, :]
            recalled = r.recalled[batch, rows, :].astype(F32)
            attn_rows = grad_combined.astype(BF)
            memory_rows = (grad_combined * gate).astype(BF)
            grad_pre = grad_combined * recalled * gate * (1.0 - gate)
            r.grad_proj[batch, rows, 3 * HD :] = grad_pre.astype(BF)
            query = r.qkv[batch, rows, :HD]
            keys = r.qkv[batch, :, HD : 2 * HD]
            values = r.qkv[batch, :, 2 * HD :]
            inner, decay_w, distance, probs, per_probs = weights_of_scores(
                query,
                keys,
                r.persist[layer, 0],
                r.seg_rows[batch, rows, :],
                r.seg_cols[batch],
                begin,
                r.rates[layer, 0:1, 0:1],
            )
            per_dp = nt(attn_rows, r.persist[layer, 1])
            seq_dp = nt(attn_rows, values)
            delta = jnp.sum(per_probs * per_dp, axis=1, keepdims=True) + jnp.sum(
                probs * seq_dp, axis=1, keepdims=True
            )
            per_ds = (per_probs * (per_dp - delta)).astype(BF)
            seq_ds = (probs * (seq_dp - delta)).astype(BF)
            weighted = nt(memory_rows, values) * decay_w
            grad_inner = weighted.astype(BF)
            memory = inner * decay_w
            rate_terms = weighted * inner * distance
            r.grad_rate[layer] -= jnp.sum(rate_terms, axis=0, keepdims=True)
            grad_query = (nn(per_ds, r.persist[layer, 0]) + nn(seq_ds, keys)) * scale
            grad_query = grad_query + nn(grad_inner, keys)
            r.grad_proj[batch, rows, :HD] = grad_query.astype(BF)
            r.grad_keys[...] += tn(seq_ds, query) * scale + tn(grad_inner, query)
            r.grad_values[...] += tn(probs.astype(BF), attn_rows) + tn(
                memory.astype(BF), memory_rows
            )
            r.grad_persist[layer, 0] += tn(per_ds, query) * scale
            r.grad_persist[layer, 1] += tn(per_probs.astype(BF), attn_rows)

        in_blocks(length, 128, block)
        r.grad_proj[batch, :, HD : 2 * HD] = r.grad_keys[...].astype(BF)
        r.grad_proj[batch, :, 2 * HD : 3 * HD] = r.grad_values[...].astype(BF)

        def back(rows, begin):
            r.part[batch, rows, :] = nt(r.grad_proj[batch, rows, :], flat(r.mix)).astype(BF)

        in_blocks(length, 256, back)

    def scatter(batch):
        return Scatter(r.part, batch, r.pair, r.away, r.near, r.ssend, r.srecv)

    def through_norm(batch, part, rows, gain):
        grad_normed = part.finish()
        inverse = rms_scale(rows)
        return norm_back(grad_normed, rows * inverse, inverse, gain)

    flips = [(dx, ds) for dx in (0, 1) for ds in range(4) if dx or ds]
    plane = [((x + dx) % 2, (s + ds) % 4, z) for dx, ds in flips]
    column = [(x, s, (z + dz) % 4) for dz in (1, 2, 3)]
    barrier = pltpu.get_barrier_semaphore()
    for other in plane + column:
        pl.semaphore_signal(barrier, inc=1, device_id=other, device_id_type=MESH)
    pl.semaphore_wait(barrier, len(plane) + len(column))
    r.grad_rate[...] = jnp.zeros_like(r.grad_rate)
    r.grad_persist[...] = jnp.zeros_like(r.grad_persist)
    arriving = None
    for layer in (1, 0):
        full = r.grad_next if arriving else r.grad_full
        above = grads[1] if arriving else r.grad_rows
        rows_in = r.out_low if layer else r.rows
        each(load(layer, feed_names), lambda copy: copy.wait())
        parts = []
        for batch in range(2):
            if arriving:
                arriving[batch].forward()
                arriving[batch].finish()
            if batch == 1 - layer:
                if layer == 0:
                    feeds[1][1].finish()
                down_weights(full)
                feeds[layer][1].start()
            feed_back(full, batch)
            part = scatter(batch)
            part.start()
            part.forward()
            parts.append(part)
        if layer == 0:
            each(mixers[1], lambda part: part.hop())
            feeds[1][0].finish()
        else:
            feeds[1][1].hop()
        product(r.own_gu, r.normed_two, r.grad_gu)
        feeds[layer][0].start()
        gathers = []
        gain_sums = []
        for batch, part in enumerate(parts):
            grad_mid, gain_sum = through_norm(
                batch, part, r.mid[batch], r.gains[layer, 1:2, :]
            )
            gain_sums.append(gain_sum[None])
            grad_mid = grad_mid + above[batch].astype(F32)
            r.grad_mid[batch] = grad_mid
            gather = Gather(r.branch, batch, r.gsend, r.grecv)
            gather.start(grad_mid.astype(BF))
            gathers.append(gather)
        r.gain_sums[layer, 1:2] = gain_sums[0] + gain_sums[1]
        if layer == 1:
            each(load(0, feed_names), lambda copy: copy.start())
        each(load(layer, mixer_names), lambda copy: copy.wait())
        parts = []
        for batch, gather in enumerate(gathers):
            gather.forward()
            gather.finish()
            if batch == 1:
                if layer == 0:
                    mixers[1][1].finish()
                grad_out = tn(r.combined[0], r.branch[0]) + tn(r.combined[1], r.branch[1])
                r.grad_out[...] = grad_out.astype(BF)
                mixers[layer][1].start()
            mixer_back(layer, batch)
            part = scatter(batch)
            part.start()
            part.forward()
            parts.append(part)
            if batch == 0:
                each(feeds[layer][: 2 - layer], lambda part: part.hop())
        if layer == 0:
            mixers[1][0].finish()
        product(r.grad_mix, r.normed, r.grad_proj)
        mixers[layer][0].start()
        if layer == 1:
            each(load(0, mixer_names), lambda copy: copy.start())
        arriving = []
        gain_sums = []
        for batch, part in enumerate(parts):
            grad_h, gain_sum = through_norm(
                batch, part, rows_in[batch].astype(F32), r.gains[layer, 0:1, :]
            )
            gain_sums.append(gain_sum[None])
            grad_h = (grad_h + r.grad_mid[batch]).astype(BF)
            grads[layer][batch] = grad_h
            if layer == 1:
                gather = Gather(r.grad_next, batch, r.gsend, r.grecv)
                gather.start(grad_h)
                arriving.append(gather)
        r.gain_sums[layer, 0:1] = gain_sums[0] + gain_sums[1]
    each(feeds[0], lambda part: part.finish())

    for layer in range(2):
        persist = r.grad_persist[layer].reshape(-1, HD)
        rate = r.grad_rate[layer]
        rate = sum(rate[:, begin : begin + HD] for begin in range(0, length, HD))
        for owner in range(4):
            r.small[owner, layer * 32 : (layer + 1) * 32, :] = persist
            r.small[owner, 64 + layer : 65 + layer, :] = rate
            for kind in range(2):
                for half in range(2):
                    row = 72 + 4 * layer + 2 * kind + half
                    begin = owner * 2 * HD + half * HD
                    r.small[owner, row : row + 1, :] = r.gain_sums[
                        layer, kind : kind + 1, begin : begin + HD
                    ]
    for owner in range(4):
        r.small[owner, 66:72, :] = jnp.zeros((6, HD), F32)

    sibling, beside, partner = (peer(place, 0, True), peer(place, 2, False), peer(place, 1, False))
    across = peer(place, 3, False)
    bufs = (r.mix_buf, r.gu_buf, r.down_buf)
    out_buf, rows_buf, grads_buf, plane_buf = r.out_buf, r.rows_buf, r.grads_buf, r.plane_buf
    by_layer = [
        [r.mix_sum.at[i], r.gu_sum.at[i], r.down_sum.at[i], r.out_sum.at[i]] for i in range(2)
    ]
    by_layer[0] += [r.out_low, r.grad_low]
    by_layer[1] += [r.out_high, r.grad_high]
    copy = remote

    def to_plane_of(dz):
        target = (z + dz) % 4
        return copy(
            r.small.at[target], r.column_buf.at[dz - 1], (r.zsend, r.zrecv), dz - 1, (x, s, target)
        )

    def to_plane(index):
        slot = plane_buf.at[x * 4 + s]
        return copy(slot, slot, (r.qsend, r.qrecv), index, plane[index])

    for dz in (1, 2, 3):
        to_plane_of(dz).start()

    psems = [(r.psend.at[i], r.precv.at[i]) for i in range(3)]

    def piece(index, kind, slot, target, source=None):
        landing = bufs[index].at[slot]
        return copy(landing if source is None else source, landing, psems[index], kind, target)

    mine = (x, s)
    turned = (1 - x, s)

    def send(indices):
        for layer in (0, 1):
            own, theirs = by_layer[layer], by_layer[1 - layer]

            @pl.when(x == layer)
            def _():
                for index in indices:
                    piece(index, 2, mine, partner, theirs[index]).start()
                    piece(index, 0, mine, beside, own[index]).start()
                    piece(index, 1, mine, sibling, own[index]).start()
                for index in indices:
                    bufs[index][mine] = own[index][...]

    def turn(indices):
        for index in indices:
            piece(index, 2, turned, partner).wait_recv()
            piece(index, 3, turned, beside).start()
            piece(index, 4, turned, sibling).start()

    send((1, 2))
    for layer in (0, 1):

        @pl.when(x == layer)
        def _():
            copy(by_layer[1 - layer][4], rows_buf, (r.rsend, r.rrecv), 0, partner).start()
            copy(by_layer[1 - layer][5], grads_buf, (r.rsend, r.rrecv), 1, partner).start()

    total = r.small[z]
    for dz in (1, 2, 3):
        to_plane_of(dz).wait_recv()
        total = total + r.column_buf[dz - 1]
    plane_buf[x * 4 + s] = total
    for index in range(7):
        to_plane(index).start()
    each(mixers[0], lambda part: part.hop())
    turn((1, 2))
    each(mixers[0], lambda part: part.finish())
    send((0,))

    core = s % 2
    root = z == 2 * x + s // 2
    of_root = (z // 2, 2 * (z % 2) + core)
    apart = 2 * ((x + of_root[0]) % 2) + (s // 2 + of_root[1] // 2) % 2

    def out_copy(index, target, source=None):
        landing = out_buf.at[core]
        return copy(landing if source is None else source, landing, (r.osend, r.orecv), index, target)

    for layer in (0, 1):

        @pl.when(root & (x == layer))
        def _():
            out_copy(1, beside, by_layer[layer][3]).start()
            out_copy(2, partner, by_layer[1 - layer][3]).start()
            out_copy(3, across, by_layer[1 - layer][3]).start()
            out_buf[core] = by_layer[layer][3][...]

    for apart_by in (1, 2, 3):

        @pl.when(apart == apart_by)
        def _():
            out_copy(apart_by, beside).wait_recv()

    out_copy(0, sibling).start()

    turn((0,))
    far = (x, (s + 2) % 4)
    far_turned = (1 - x, (s + 2) % 4)
    for index in (1, 2, 0):
        piece(index, 0, far, beside).wait_recv()
        piece(index, 5, far, sibling).start()
    for index in (1, 2, 0):
        piece(index, 3, far_turned, beside).wait_recv()
        piece(index, 6, far_turned, sibling).start()
    twin = sibling[1]
    far_twin = (twin + 2) % 4
    for index in range(3):
        piece(index, 1, (x, twin), sibling).wait_recv()
        piece(index, 4, (1 - x, twin), sibling).wait_recv()
        piece(index, 5, (x, far_twin), sibling).wait_recv()
        piece(index, 6, (1 - x, far_twin), sibling).wait_recv()
    other_out = out_buf.at[1 - core]
    copy(other_out, other_out, (r.osend, r.orecv), 0, sibling).wait_recv()
    for index in range(7):
        dx, ds = flips[index]
        slot = plane_buf.at[((x + dx) % 2) * 4 + (s + 4 - ds) % 4]
        copy(slot, slot, (r.qsend, r.qrecv), index, plane[index]).wait_recv()
    for index in (0, 1):
        copy(rows_buf, rows_buf, (r.rsend, r.rrecv), index, partner).wait()
    for index in range(7):
        to_plane(index).wait_send()
    for dz in (1, 2, 3):
        to_plane_of(dz).wait_send()
    for index in range(3):
        for kind in range(7):
            piece(index, kind, mine, sibling).wait_send()
    out_copy(0, sibling).wait_send()

    @pl.when(root)
    def _():
        for index in (1, 2, 3):
            out_copy(index, sibling).wait_send()


def kernel_call(kernel, number, operands, outs, scratch, spaces=None, places=None):
    spaces = spaces or [pltpu.VMEM] * len(outs)
    places = places or [pltpu.VMEM] * len(operands)
    return pl.pallas_call(
        kernel,
        out_shape=list(outs),
        in_specs=[pl.BlockSpec(memory_space=space) for space in places],
        out_specs=[pl.BlockSpec(memory_space=space) for space in spaces],
        scratch_shapes=scratch,
        compiler_params=pltpu.CompilerParams(
            collective_id=number, has_side_effects=True, vmem_limit_bytes=58 * 2**20
        ),
    )(*operands)


def pairs_of(*sizes):
    return [pltpu.SemaphoreType.DMA(size) for size in sizes for _ in range(2)]


def scatter_scratch(length):
    size = length // 8
    return [
        pltpu.VMEM((2, length, D), BF),
        pltpu.VMEM((2, 4, size, D), BF),
        pltpu.VMEM((2, 3, size, D), BF),
        pltpu.VMEM((2, 3, size, D), BF),
        *pairs_of((2, 8), (2, 8)),
    ]


def forward_call(number, *operands):
    inputs, small, _, w_mix, _, _, w_down, *_ = operands
    count, _, tokens, _ = inputs.shape
    depth, length = w_mix.shape[1], 4 * tokens
    unit = w_down.shape[1] // 8
    padded = -(-unit // 32) * 32
    shape = jax.ShapeDtypeStruct
    outs = ForwardOut(
        rows=shape((count, length // 8, D), BF),
        gains=shape((2, 2, D), F32),
        persist=shape((2, 2, 16, HD), BF),
        rates=shape((2, 8, HD), F32),
    )
    kept = Kept(
        normed=shape((count, length, D), BF),
        mix=shape((4, depth, 4 * HD), BF),
        out=shape((HD, D), BF),
        gu=shape((4, depth, 8 * padded), BF),
        down=shape((4, padded, D), BF),
        qkv=shape((count, length, 3 * HD), BF),
        gate=shape((count, length, HD), F32),
        recalled=shape((count, length, HD), BF),
        combined=shape((count, length, HD), BF),
        mid=shape((count, length // 8, D), F32),
        normed_two=shape((count, length, D), BF),
        gate_up=shape((count, length, 8 * padded), F32),
        hidden=shape((count, length, 4 * padded), BF),
        out_rows=shape((count, length // 8, D), BF),
    )
    scratch = [pltpu.VMEM(part.shape, part.dtype) for part in (*kept, *kept)]
    scratch += scatter_scratch(length)[:6]
    scratch += [
        pltpu.VMEM((2, 4, 8, HD), F32),
        pltpu.VMEM((2, 4) + small.shape, F32),
        pltpu.VMEM((depth, 4 * HD), BF),
        pltpu.VMEM((depth, 8 * padded), BF),
        pltpu.VMEM((padded, D), BF),
        *pairs_of((7,), (7,), (4,), (2, 8), (6, 4), (2, 2)),
        pltpu.SemaphoreType.DMA((2, len(kept))),
    ]
    kernel = functools.partial(forward_kernel, unit)
    specs = [pltpu.VMEM] * len(outs) + [pl.ANY] * (2 * len(kept))
    found = kernel_call(kernel, number, operands, [*outs, *kept, *kept], scratch, specs)
    own, found = found[: len(outs)], found[len(outs) :]
    return (
        named(ForwardOut._fields, own),
        named(Kept._fields, found[: len(kept)]),
        named(Kept._fields, found[len(kept) :]),
    )


def backward_call(number, given, below, above):
    saved = Kept._fields[:-1]
    kept = [getattr(part, name) for part in (below, above) for name in saved]
    count, length, _ = below.normed.shape
    depth, half, size = D // 4, 4 * below.down.shape[1], length // 8
    shape = jax.ShapeDtypeStruct
    outs = BackwardOut(
        mix_buf=shape((2, 4, depth, 4 * HD), BF),
        gu_buf=shape((2, 4, depth, 2 * half), BF),
        down_buf=shape((2, 4, half // 4, D), BF),
        out_buf=shape((2, HD, D), BF),
        rows_buf=shape((count, size, D), BF),
        grads_buf=shape((count, size, D), BF),
        plane_buf=shape((8, 80, HD), F32),
        grad_low=shape((count, size, D), BF),
        grad_high=shape((count, size, D), BF),
    )
    scratch = [pltpu.VMEM(part.shape, part.dtype) for part in kept[: len(saved)]]
    scratch += scatter_scratch(length) + [
        pltpu.VMEM((count, length, 2 * half), BF),
        pltpu.VMEM((count, length, 4 * HD), BF),
        pltpu.VMEM((length, HD), F32),
        pltpu.VMEM((length, HD), F32),
        pltpu.VMEM((count, length, D), BF),
        pltpu.VMEM((count, size, D), F32),
        pltpu.VMEM((count, length, D), BF),
        pltpu.VMEM((2, 2, 16, HD), F32),
        pltpu.VMEM((2, 1, length), F32),
        pltpu.VMEM((2, 2, D), F32),
        pltpu.VMEM((4, 80, HD), F32),
        pltpu.VMEM((3, 80, HD), F32),
        pltpu.VMEM((4, depth, 2 * half), BF),
        pltpu.VMEM((4, half // 4, D), BF),
        pltpu.VMEM((4, depth, 4 * HD), BF),
        pltpu.VMEM((HD, D), BF),
        pltpu.VMEM((2, 4, depth, 2 * half), BF),
        pltpu.VMEM((2, 4, half // 4, D), BF),
        pltpu.VMEM((2, 4, depth, 4 * HD), BF),
        pltpu.VMEM((2, 2, HD, D), BF),
        pltpu.VMEM((2, depth, 2 * half), BF),
        pltpu.VMEM((2, half // 4, D), BF),
        pltpu.VMEM((2, depth, 4 * HD), BF),
        pltpu.VMEM((2, HD, D), BF),
        *pairs_of((6, 4), (2, 2), (3, 7), (4,), (2,), (3,), (7,)),
        pltpu.SemaphoreType.DMA((len(saved),)),
    ]
    operands = [*(getattr(given, name) for name in BackwardIn._fields), *kept]
    spaces = [pltpu.VMEM] * len(BackwardIn._fields) + [pl.ANY] * len(kept)
    found = kernel_call(backward_kernel, number, operands, outs, scratch, None, spaces)
    return named(BackwardOut._fields, found)


def assemble_kernel(unit, mix_buf, gu_buf, down_buf, mix_ref, gu_ref, down_ref):
    padded = down_buf.shape[2]
    half = gu_buf.shape[3] // 2
    for which in range(8):
        slot = (which // 4, which % 4)
        mix = mix_buf[slot].astype(F32)
        for kind in range(4):
            begin = kind * D + which * HD
            mix_ref[0, :, begin : begin + HD] = mix[:, kind * HD : (kind + 1) * HD]
        part = gu_buf[slot].astype(F32)
        for side in range(2):
            for owner in range(half // padded):
                begin = side * FF + (owner * 8 + which) * unit
                source = side * half + owner * padded
                gu_ref[0, :, begin : begin + unit] = part[:, source : source + unit]
    for pair in range(2):
        down = down_buf[0, pair].astype(F32)
        down_ref[0, pair * unit : (pair + 1) * unit, :] = down[:unit]


def assemble_call(unit, mix_buf, gu_buf, down_buf):
    depth, padded = mix_buf.shape[2], down_buf.shape[2]
    rows = depth // 4
    return pl.pallas_call(
        functools.partial(assemble_kernel, unit),
        grid=(4,),
        out_shape=[
            jax.ShapeDtypeStruct((1, depth, 4 * D), F32),
            jax.ShapeDtypeStruct((1, depth, 2 * FF), F32),
            jax.ShapeDtypeStruct((1, 8 * unit, D), F32),
        ],
        in_specs=[
            pl.BlockSpec((2, 4, rows, 4 * HD), lambda i: (0, 0, i, 0)),
            pl.BlockSpec((2, 4, rows, gu_buf.shape[3]), lambda i: (0, 0, i, 0)),
            pl.BlockSpec((1, 2, padded, D), lambda i: (i // 2, i % 2, 0, 0)),
        ],
        out_specs=[
            pl.BlockSpec((1, rows, 4 * D), lambda i: (0, i, 0)),
            pl.BlockSpec((1, rows, 2 * FF), lambda i: (0, i, 0)),
            pl.BlockSpec((1, 2 * unit, D), lambda i: (0, i, 0)),
        ],
        compiler_params=pltpu.CompilerParams(vmem_limit_bytes=40 * 2**20),
    )(mix_buf, gu_buf, down_buf)


def tensor_parallel(
    inputs, segment_ids, cotangent, w_mix, w_out, w_gu, w_down, norm_gains, persist_kv, memory_decay
):
    x, s, z = here()
    nx, ns, nz = (lax.axis_size(a) for a in ("section", "seq", "shard"))
    width = nx * ns
    mine = x * ns + s
    other = (1 - x) * ns + s
    first = x == 0
    count, _, tokens, _ = inputs.shape
    length = tokens * ns
    size = length // width
    depth = w_mix.shape[1]
    unit = w_down.shape[1] // (nx * ns)

    def layers(own, got):
        return (jnp.where(first, own, got), jnp.where(first, got, own))

    small = persist_kv[0].reshape(-1, 2, HD).transpose(1, 0, 2).reshape(-1, HD).astype(F32)
    rates = jnp.broadcast_to(memory_decay[0][:, None, None], (2, 8, HD)).reshape(-1, HD)
    gain_rows = norm_gains[0].astype(F32).T.reshape(-1, HD)
    gain_rows = jnp.pad(gain_rows, ((0, 8 - gain_rows.shape[0]), (0, 0)))
    small = jnp.concatenate([small, rates], 0)
    segments = (segment_ids[:, 0, :, None], segment_ids)
    ready, below, above = forward_call(
        1, inputs, small, gain_rows, w_mix, w_out, w_gu, w_down, *segments
    )
    cot_full = lax.all_gather(cotangent[:, 0], "seq", axis=1, tiled=True)
    given = BackwardIn(
        grad_full=cot_full,
        grad_rows=lax.dynamic_slice_in_dim(cotangent[:, 0], x * size, size, 1),
        rows=ready.rows,
        out_low=below.out_rows,
        out_high=above.out_rows,
        gains=ready.gains,
        persist=ready.persist,
        rates=ready.rates,
        seg_rows=segments[0],
        seg_cols=segments[1],
    )
    found = backward_call(2, given, below, above)
    outputs = (below.out_rows, above.out_rows)
    grads = (found.grad_low, found.grad_high)

    def whole_rows(of_layer, got):
        both = layers(jnp.where(first, of_layer[0], of_layer[1]), got)
        return jnp.concatenate(both, 1)[None, :, None]

    section_out = whole_rows(outputs, found.rows_buf)
    section_grad = whole_rows(grads, found.grads_buf).astype(F32)
    grad_mix, grad_gu, grad_down = assemble_call(unit, found.mix_buf, found.gu_buf, found.down_buf)
    grad_out = found.out_buf.astype(F32).reshape(1, 2 * HD, D)

    plane_all = found.plane_buf
    heads_of = lax.dynamic_slice_in_dim(plane_all, 2 * s, 2, 0)
    of_section = lax.dynamic_index_in_dim(
        heads_of[:, :64].reshape(2, 2, 2, -1, HD), x, 1, keepdims=False
    )
    grad_persist = of_section.transpose(1, 2, 0, 3).reshape(1, 2, -1, 2 * HD)
    of_section = lax.dynamic_index_in_dim(heads_of[:, 64:66], x, 1, keepdims=False)
    grad_rate = jnp.sum(of_section, 1)[None]
    gain_all = jnp.sum(plane_all[:, 72:], 0).reshape(2, 2, depth)
    grad_gain = lax.dynamic_index_in_dim(gain_all, x, 0).transpose(0, 2, 1)
    return (
        section_out,
        section_grad,
        grad_mix,
        grad_out,
        grad_gu,
        grad_down,
        grad_gain,
        grad_persist,
        grad_rate,
    )


def solution(mesh):
    sizes = mesh.shape
    planar = (sizes["section"], sizes["seq"]) == (2, 4)
    placed = (
        P(None, "shard", "seq", None),
        P(None, "shard", None),
        P(None, "shard", "seq", None),
        P("section", "shard", None),
        P("section", "shard", None),
        P("section", "shard", None),
        P("section", "shard", None),
        P("section", "shard", None),
        P("section", None, None, "seq"),
        P("section", "seq"),
    )
    return jax.shard_map(
        tensor_parallel if planar else on_device,
        mesh=mesh,
        in_specs=placed,
        out_specs=(
            P("section", None, "shard", "seq", None),
            P("section", None, "shard", "seq", None),
            P("section", "shard", None),
            P("section", "shard", None),
            P("section", "shard", None),
            P("section", "shard", None),
            P("section", "shard", None),
            P("section", None, None, "seq"),
            P("section", "seq"),
        ),
        check_vma=False,
    )
```

```python
import functools
import math
import types
from typing import Any, NamedTuple

import jax
import jax.numpy as jnp
from jax import lax
from jax.experimental import pallas as pl
from jax.experimental.pallas import tpu as pltpu
from jax.sharding import PartitionSpec as P

D = 1024
H = 8
HD = 128
FF = 2816


def shifted(value, axis, by):
    size = lax.axis_size(axis)
    pairs = [(i, i + by) for i in range(size) if 0 <= i + by < size]
    return lax.ppermute(value, axis, pairs)


def as_sent(value):
    return jax.tree.map(lambda a: a.astype(jnp.bfloat16) if a.dtype == jnp.float32 else a, value)


def rms_scale(values):
    return lax.rsqrt(jnp.mean(values * values, axis=-1, keepdims=True) + 1e-06)


def norm_back(grad_normed, scaled, inverse, gain):
    grad_scaled = grad_normed * gain
    grad_rows = inverse * (
        grad_scaled - scaled * jnp.mean(grad_scaled * scaled, axis=-1, keepdims=True)
    )
    return (grad_rows, jnp.sum(grad_normed * scaled, axis=0))


def block_terms(query_rows, key_rows, seg_ids, begin, reach, rate):
    inner = jnp.dot(query_rows, key_rows.T, preferred_element_type=jnp.float32)
    row_places = begin + jnp.arange(reach - begin, dtype=jnp.int32)
    col_places = jnp.arange(reach, dtype=jnp.int32)
    allowed = (seg_ids[begin:reach][:, None] == seg_ids[:reach][None, :]) & (
        col_places[None, :] <= row_places[:, None]
    )
    distance = jnp.maximum(row_places[:, None] - col_places[None, :], 0).astype(jnp.float32)
    decay_w = jnp.where(allowed, jnp.exp(-rate * distance), jnp.float32(0.0))
    return (inner, allowed, decay_w, distance)


def head_forward(query, keys, values, pkeys, pvalues, rate, seg_ids):
    length, width = query.shape
    block = min(512, length)
    scale = 1.0 / math.sqrt(width)
    attn_parts, memory_parts, lse_parts = ([], [], [])
    for begin in range(0, length, block):
        reach = begin + block
        query_rows = query[begin:reach]
        inner, allowed, decay_w, distance = block_terms(
            query_rows, keys[:reach], seg_ids, begin, reach, rate
        )
        per_scores = jnp.dot(query_rows, pkeys.T, preferred_element_type=jnp.float32) * scale
        seq_scores = jnp.where(allowed, inner * scale, -jnp.inf)
        top = jnp.maximum(
            jnp.max(per_scores, axis=1, keepdims=True), jnp.max(seq_scores, axis=1, keepdims=True)
        )
        per_exp = jnp.exp(per_scores - top)
        seq_exp = jnp.exp(seq_scores - top)
        denom = jnp.sum(per_exp, axis=1, keepdims=True) + jnp.sum(seq_exp, axis=1, keepdims=True)
        attended = jnp.dot(
            (per_exp / denom).astype(jnp.bfloat16), pvalues, preferred_element_type=jnp.float32
        )
        attended = attended + jnp.dot(
            (seq_exp / denom).astype(jnp.bfloat16),
            values[:reach],
            preferred_element_type=jnp.float32,
        )
        memory_w = (inner * decay_w * (1.0 / width)).astype(jnp.bfloat16)
        recalled = jnp.dot(memory_w, values[:reach], preferred_element_type=jnp.float32)
        attn_parts.append(attended)
        memory_parts.append(recalled)
        lse_parts.append(top[:, 0] + jnp.log(denom[:, 0]))
    return (
        jnp.concatenate(attn_parts, 0),
        jnp.concatenate(memory_parts, 0),
        jnp.concatenate(lse_parts, 0),
    )


def head_backward(query, keys, values, pkeys, pvalues, rate, seg_ids, lse, grad_attn, grad_memory):
    length, width = query.shape
    block = min(512, length)
    scale = 1.0 / math.sqrt(width)
    query_grads = []
    grad_keys = jnp.zeros((length, width), jnp.float32)
    grad_values = jnp.zeros((length, width), jnp.float32)
    grad_pkeys = jnp.zeros(pkeys.shape, jnp.float32)
    grad_pvalues = jnp.zeros(pvalues.shape, jnp.float32)
    grad_rate = jnp.float32(0.0)
    for begin in range(0, length, block):
        reach = begin + block
        query_rows = query[begin:reach]
        key_rows = keys[:reach]
        value_rows = values[:reach]
        inner, allowed, decay_w, distance = block_terms(
            query_rows, key_rows, seg_ids, begin, reach, rate
        )
        per_scores = jnp.dot(query_rows, pkeys.T, preferred_element_type=jnp.float32) * scale
        seq_scores = jnp.where(allowed, inner * scale, -jnp.inf)
        row_lse = lse[begin:reach][:, None]
        per_prob = jnp.exp(per_scores - row_lse)
        seq_prob = jnp.exp(seq_scores - row_lse)
        attn_rows = grad_attn[begin:reach]
        memory_rows = grad_memory[begin:reach]
        per_dp = jnp.dot(attn_rows, pvalues.T, preferred_element_type=jnp.float32)
        seq_dp = jnp.dot(attn_rows, value_rows.T, preferred_element_type=jnp.float32)
        delta = jnp.sum(per_prob * per_dp, axis=1, keepdims=True) + jnp.sum(
            seq_prob * seq_dp, axis=1, keepdims=True
        )
        per_ds = (per_prob * (per_dp - delta)).astype(jnp.bfloat16)
        seq_ds = (seq_prob * (seq_dp - delta)).astype(jnp.bfloat16)
        rows_grad = (
            jnp.dot(per_ds, pkeys, preferred_element_type=jnp.float32)
            + jnp.dot(seq_ds, key_rows, preferred_element_type=jnp.float32)
        ) * scale
        grad_pkeys = (
            grad_pkeys
            + jnp.einsum("qk,qd->kd", per_ds, query_rows, preferred_element_type=jnp.float32)
            * scale
        )
        grad_pvalues = grad_pvalues + jnp.einsum(
            "qk,qd->kd",
            per_prob.astype(jnp.bfloat16),
            attn_rows,
            preferred_element_type=jnp.float32,
        )
        key_part = (
            jnp.einsum("qk,qd->kd", seq_ds, query_rows, preferred_element_type=jnp.float32) * scale
        )
        value_part = jnp.einsum(
            "qk,qd->kd",
            seq_prob.astype(jnp.bfloat16),
            attn_rows,
            preferred_element_type=jnp.float32,
        )
        memory_w = (inner * decay_w * (1.0 / width)).astype(jnp.bfloat16)
        grad_mw = jnp.dot(memory_rows, value_rows.T, preferred_element_type=jnp.float32)
        value_part = value_part + jnp.einsum(
            "qk,qd->kd", memory_w, memory_rows, preferred_element_type=jnp.float32
        )
        grad_inner = (grad_mw * decay_w * (1.0 / width)).astype(jnp.bfloat16)
        rows_grad = rows_grad + jnp.dot(grad_inner, key_rows, preferred_element_type=jnp.float32)
        key_part = key_part + jnp.einsum(
            "qk,qd->kd", grad_inner, query_rows, preferred_element_type=jnp.float32
        )
        grad_rate = grad_rate - jnp.sum(grad_mw * inner * decay_w * (1.0 / width) * distance)
        grad_keys = grad_keys.at[:reach].add(key_part)
        grad_values = grad_values.at[:reach].add(value_part)
        query_grads.append(rows_grad)
    return (
        jnp.concatenate(query_grads, 0),
        grad_keys,
        grad_values,
        grad_pkeys,
        grad_pvalues,
        grad_rate,
    )


def layer_forward(rows_in, seg_ids, full, pkv, rates):
    mix_w, out_w, gu_w, down_w, gains = full
    tokens = rows_in.shape[0]
    gain_one = gains[:, 0].astype(jnp.float32)
    gain_two = gains[:, 1].astype(jnp.float32)
    inverse_one = rms_scale(rows_in)
    scaled_one = rows_in * inverse_one
    normed = (scaled_one * gain_one).astype(jnp.bfloat16)
    proj = jnp.dot(normed, mix_w, preferred_element_type=jnp.float32)
    qkv = proj[:, : 3 * D].astype(jnp.bfloat16).reshape(tokens, 3, H, HD)
    gate = jax.nn.sigmoid(proj[:, 3 * D :])
    grouped = lax.all_to_all(qkv, "seq", split_axis=2, concat_axis=0, tiled=True)
    attn_heads, memory_heads, lse_heads = ([], [], [])
    for head in range(grouped.shape[2]):
        cols = slice(head * HD, (head + 1) * HD)
        attended, recalled, lse = head_forward(
            grouped[:, 0, head],
            grouped[:, 1, head],
            grouped[:, 2, head],
            pkv[0][:, cols],
            pkv[1][:, cols],
            rates[head],
            seg_ids,
        )
        attn_heads.append(attended)
        memory_heads.append(recalled)
        lse_heads.append(lse)
    mixed = jnp.stack([jnp.stack(attn_heads, 1), jnp.stack(memory_heads, 1)], 1).astype(
        jnp.bfloat16
    )
    returned = lax.all_to_all(mixed, "seq", split_axis=0, concat_axis=2, tiled=True)
    attended = returned[:, 0].reshape(tokens, D).astype(jnp.float32)
    recalled = returned[:, 1].reshape(tokens, D).astype(jnp.float32)
    combined = (attended + gate * recalled).astype(jnp.bfloat16)
    mid = rows_in + jnp.dot(combined, out_w, preferred_element_type=jnp.float32)
    inverse_two = rms_scale(mid)
    scaled_two = mid * inverse_two
    normed_two = (scaled_two * gain_two).astype(jnp.bfloat16)
    gate_up = jnp.dot(normed_two, gu_w, preferred_element_type=jnp.float32)
    hidden = (jax.nn.silu(gate_up[:, :FF]) * gate_up[:, FF:]).astype(jnp.bfloat16)
    result = mid + jnp.dot(hidden, down_w, preferred_element_type=jnp.float32)
    kept = (
        seg_ids,
        inverse_one,
        scaled_one,
        normed,
        grouped,
        jnp.stack(lse_heads, 1),
        gate,
        recalled,
        combined,
        inverse_two,
        scaled_two,
        normed_two,
        gate_up,
        hidden,
    )
    return (result, kept)


def layer_backward(grad_out, kept, full, pkv, rates):
    (
        seg_ids,
        inverse_one,
        scaled_one,
        normed,
        grouped,
        lse_all,
        gate,
        recalled,
        combined,
        inverse_two,
        scaled_two,
        normed_two,
        gate_up,
        hidden,
    ) = kept
    mix_w, out_w, gu_w, down_w, gains = full
    tokens = grad_out.shape[0]
    gain_one = gains[:, 0].astype(jnp.float32)
    gain_two = gains[:, 1].astype(jnp.float32)
    grad_f = grad_out.astype(jnp.bfloat16)
    grad_down = jnp.einsum("tf,td->fd", hidden, grad_f, preferred_element_type=jnp.float32)
    grad_hidden = jnp.dot(grad_f, down_w.T, preferred_element_type=jnp.float32)
    gate_part = gate_up[:, :FF]
    up_part = gate_up[:, FF:]
    sig_part = jax.nn.sigmoid(gate_part)
    grad_gate_part = grad_hidden * up_part * sig_part * (1.0 + gate_part * (1.0 - sig_part))
    grad_up_part = grad_hidden * gate_part * sig_part
    grad_gate_up = jnp.concatenate([grad_gate_part, grad_up_part], 1).astype(jnp.bfloat16)
    grad_gu = jnp.einsum("td,tf->df", normed_two, grad_gate_up, preferred_element_type=jnp.float32)
    grad_normed_two = jnp.dot(grad_gate_up, gu_w.T, preferred_element_type=jnp.float32)
    grad_mid_norm, grad_gain_two = norm_back(grad_normed_two, scaled_two, inverse_two, gain_two)
    grad_mid = grad_out + grad_mid_norm
    grad_branch = grad_mid.astype(jnp.bfloat16)
    grad_out_w = jnp.einsum("td,te->de", combined, grad_branch, preferred_element_type=jnp.float32)
    grad_combined = jnp.dot(grad_branch, out_w.T, preferred_element_type=jnp.float32)
    grad_attended = grad_combined.astype(jnp.bfloat16).reshape(tokens, H, HD)
    grad_recalled = (grad_combined * gate).astype(jnp.bfloat16).reshape(tokens, H, HD)
    grad_gate_pre = grad_combined * recalled * gate * (1.0 - gate)
    outgoing = jnp.stack([grad_attended, grad_recalled], 1)
    headward = lax.all_to_all(outgoing, "seq", split_axis=2, concat_axis=0, tiled=True)
    head_grads, pkey_grads, pvalue_grads, rate_grads = ([], [], [], [])
    for head in range(grouped.shape[2]):
        cols = slice(head * HD, (head + 1) * HD)
        dq, dk, dv, dpk, dpv, drate = head_backward(
            grouped[:, 0, head],
            grouped[:, 1, head],
            grouped[:, 2, head],
            pkv[0][:, cols],
            pkv[1][:, cols],
            rates[head],
            seg_ids,
            lse_all[:, head],
            headward[:, 0, head],
            headward[:, 1, head],
        )
        head_grads.append(jnp.stack([dq, dk, dv], 1))
        pkey_grads.append(dpk)
        pvalue_grads.append(dpv)
        rate_grads.append(drate)
    grads_heads = jnp.stack(head_grads, 2).astype(jnp.bfloat16)
    tokenward = lax.all_to_all(grads_heads, "seq", split_axis=0, concat_axis=2, tiled=True)
    grad_proj = jnp.concatenate(
        [tokenward.reshape(tokens, 3 * D), grad_gate_pre.astype(jnp.bfloat16)], 1
    )
    grad_mix = jnp.einsum("td,tf->df", normed, grad_proj, preferred_element_type=jnp.float32)
    grad_normed = jnp.dot(grad_proj, mix_w.T, preferred_element_type=jnp.float32)
    grad_in_norm, grad_gain_one = norm_back(grad_normed, scaled_one, inverse_one, gain_one)
    grad_rows = grad_mid + grad_in_norm
    weight_terms = (
        grad_mix,
        grad_out_w,
        grad_gu,
        grad_down,
        jnp.stack([grad_gain_one, grad_gain_two], 1),
    )
    memory_terms = (
        jnp.stack([jnp.concatenate(pkey_grads, 1), jnp.concatenate(pvalue_grads, 1)], 0),
        jnp.stack(rate_grads, 0),
    )
    return (weight_terms, memory_terms, grad_rows)


def on_device(
    inputs, segment_ids, cotangent, w_mix, w_out, w_gu, w_down, norm_gains, persist_kv, memory_decay
):
    first = lax.axis_index("section") == 0
    own_weights = (w_mix[0], w_out[0], w_gu[0], w_down[0], norm_gains[0])
    pkv = persist_kv[0]
    rates = memory_decay[0]
    count = inputs.shape[0]
    tokens = inputs.shape[2]
    zero_rows = jnp.zeros((tokens, D), jnp.float32)
    received = jnp.zeros((tokens, D), jnp.bfloat16)
    kept_ticks, out_ticks = ([], [])
    for tick in range(count + 1):
        own_rows = inputs[tick, 0].astype(jnp.float32) if tick < count else zero_rows
        layer_in = jnp.where(first, own_rows, received.astype(jnp.float32))
        seg_ids = jnp.where(
            first, segment_ids[min(tick, count - 1), 0], segment_ids[max(tick - 1, 0), 0]
        )
        full = (
            lax.all_gather(own_weights[0], "shard", axis=0, tiled=True),
            lax.all_gather(own_weights[1], "shard", axis=0, tiled=True),
            lax.all_gather(own_weights[2], "shard", axis=0, tiled=True),
            lax.all_gather(own_weights[3], "shard", axis=0, tiled=True),
            lax.all_gather(own_weights[4], "shard", axis=0, tiled=True),
        )
        result, kept = layer_forward(layer_in, seg_ids, full, pkv, rates)
        result_low = result.astype(jnp.bfloat16)
        out_ticks.append(result_low)
        kept_ticks.append(kept)
        if tick < count:
            received = shifted(result_low, "section", 1)
    grad_weights = (
        jnp.zeros((D, 4 * D), jnp.float32),
        jnp.zeros((D, D), jnp.float32),
        jnp.zeros((D, 2 * FF), jnp.float32),
        jnp.zeros((FF, D), jnp.float32),
        jnp.zeros((D, 2), jnp.float32),
    )
    grad_memory = (
        jnp.zeros((2,) + pkv.shape[1:], jnp.float32),
        jnp.zeros(rates.shape, jnp.float32),
    )
    back_received = jnp.zeros((tokens, D), jnp.bfloat16)
    grad_ticks = []
    for tick in range(count + 1):
        lower = max(tick - 1, 0)
        upper = min(tick + 1, count)
        kept = jax.tree.map(
            lambda early, late: jnp.where(first, early, late), kept_ticks[lower], kept_ticks[upper]
        )
        given = cotangent[tick, 0].astype(jnp.float32) if tick < count else zero_rows
        grad_out = jnp.where(first, back_received.astype(jnp.float32), given)
        full = (
            lax.all_gather(own_weights[0], "shard", axis=0, tiled=True),
            lax.all_gather(own_weights[1], "shard", axis=0, tiled=True),
            lax.all_gather(own_weights[2], "shard", axis=0, tiled=True),
            lax.all_gather(own_weights[3], "shard", axis=0, tiled=True),
            lax.all_gather(own_weights[4], "shard", axis=0, tiled=True),
        )
        weight_terms, memory_terms, grad_rows = layer_backward(grad_out, kept, full, pkv, rates)
        grad_weights = jax.tree.map(jnp.add, grad_weights, weight_terms)
        grad_memory = jax.tree.map(jnp.add, grad_memory, memory_terms)
        grad_ticks.append(grad_rows)
        if tick < count:
            back_received = shifted(grad_rows.astype(jnp.bfloat16), "section", -1)
    section_out = jnp.stack(
        [jnp.where(first, out_ticks[batch], out_ticks[batch + 1]) for batch in range(count)], 0
    )
    section_grad = jnp.stack(
        [
            jnp.where(
                first,
                grad_ticks[batch + 1],
                grad_ticks[batch].astype(jnp.bfloat16).astype(jnp.float32),
            )
            for batch in range(count)
        ],
        0,
    )
    shares = jax.tree.map(
        lambda part: part.astype(jnp.float32),
        lax.psum_scatter(as_sent(grad_weights), "shard", scatter_dimension=0, tiled=True),
    )
    shares = jax.tree.map(lambda part: part.astype(jnp.float32), lax.psum(as_sent(shares), "seq"))
    memory_sums = lax.psum(grad_memory, "shard")
    return (
        section_out.reshape(1, count, 1, tokens, D),
        section_grad.reshape(1, count, 1, tokens, D),
        shares[0][None],
        shares[1][None],
        shares[2][None],
        shares[3][None],
        shares[4][None],
        memory_sums[0][None],
        memory_sums[1][None],
    )


MESH = pl.DeviceIdType.MESH
BF = jnp.bfloat16
F32 = jnp.float32


def here():
    return (lax.axis_index("section"), lax.axis_index("seq"), lax.axis_index("shard"))


def peer(place, chip, flip):
    x, s, z = place
    if chip % 2:
        x = 1 - x
    if chip // 2:
        s = (s + 2) % 4
    if flip:
        s = s + 1 - 2 * (s % 2)
    return (x, s, z)


def rows_of(device, size):
    x, s, _ = device
    return pl.ds(pl.multiple_of((s * 2 + x) * size, size), size)


class Gather:
    def __init__(self, full, batch, send, recv):
        self.place = here()
        self.full, self.batch, self.send, self.recv = full, batch, send, recv
        self.size = full.shape[1] // 8

    def copy(self, owner, target, sem):
        block = self.full.at[self.batch, rows_of(owner, self.size)]
        return pltpu.make_async_remote_copy(
            src_ref=block,
            dst_ref=block,
            send_sem=self.send.at[self.batch, sem],
            recv_sem=self.recv.at[self.batch, sem],
            device_id=target,
            device_id_type=MESH,
        )

    def start(self, value):
        self.full[self.batch, rows_of(self.place, self.size), :] = value
        for chip in (3, 1, 2, 0):
            self.copy(self.place, peer(self.place, chip, chip == 0), chip).start()

    def forward(self):
        other = peer(self.place, 0, True)
        for chip in (1, 2, 3):
            owner = peer(self.place, chip, False)
            self.copy(owner, owner, chip).wait_recv()
            self.copy(owner, other, 3 + chip).start()

    def finish(self):
        other = peer(self.place, 0, True)
        self.copy(other, other, 0).wait_recv()
        for chip in (1, 2, 3):
            owner = peer(self.place, chip, True)
            self.copy(owner, other, 3 + chip).wait_recv()
        for chip in (0, 1, 2, 3):
            self.copy(self.place, peer(self.place, chip, chip == 0), chip).wait_send()
        for chip in (1, 2, 3):
            self.copy(peer(self.place, chip, False), other, 3 + chip).wait_send()


class Scatter:
    def __init__(self, part, batch, pair, away, near, send, recv):
        self.place = here()
        self.part, self.batch, self.pair, self.away, self.near = part, batch, pair, away, near
        self.send, self.recv = send, recv
        self.size = part.shape[1] // 8

    def to_pair(self, chip):
        return pltpu.make_async_remote_copy(
            src_ref=self.part.at[self.batch, rows_of(peer(self.place, chip, True), self.size)],
            dst_ref=self.pair.at[self.batch, chip],
            send_sem=self.send.at[self.batch, chip],
            recv_sem=self.recv.at[self.batch, chip],
            device_id=peer(self.place, 0, True),
            device_id_type=MESH,
        )

    def to_chip(self, chip):
        return pltpu.make_async_remote_copy(
            src_ref=self.away.at[self.batch, chip - 1],
            dst_ref=self.near.at[self.batch, chip - 1],
            send_sem=self.send.at[self.batch, 3 + chip],
            recv_sem=self.recv.at[self.batch, 3 + chip],
            device_id=peer(self.place, chip, False),
            device_id_type=MESH,
        )

    def start(self):
        for chip in (3, 1, 2, 0):
            self.to_pair(chip).start()

    def chip_sum(self, chip):
        self.to_pair(chip).wait_recv()
        own = self.part[self.batch, rows_of(peer(self.place, chip, False), self.size), :]
        return own.astype(F32) + self.pair[self.batch, chip].astype(F32)

    def forward(self):
        for chip in (3, 1, 2):
            self.away[self.batch, chip - 1] = self.chip_sum(chip).astype(BF)
            self.to_chip(chip).start()

    def finish(self):
        total = self.chip_sum(0)
        for chip in (1, 2, 3):
            self.to_chip(chip).wait_recv()
            total = total + self.near[self.batch, chip - 1].astype(F32)
        for chip in (0, 1, 2, 3):
            self.to_pair(chip).wait_send()
        for chip in (1, 2, 3):
            self.to_chip(chip).wait_send()
        return total


class Column:
    def __init__(self, send, recv):
        self.place = here()
        self.send, self.recv = send, recv

    def copy(self, source, landing, sent, received, plane):
        x, s, _ = self.place
        return pltpu.make_async_remote_copy(
            src_ref=source,
            dst_ref=landing,
            send_sem=self.send.at[sent],
            recv_sem=self.recv.at[received],
            device_id=(x, s, plane),
            device_id_type=MESH,
        )

    def at_each(self, body):
        for at in range(4):

            @pl.when(self.place[2] == at)
            def _():
                body(at)


class ColumnSum(Column):
    RELAYED = ((3, 1), None, None, (0, 2))
    DIRECT = ((2, 1), (2, 0), (1, 3), (1, 2))
    SOURCES = ((1, 2), (0, 2, 3), (0, 1, 3), (1, 2))

    def __init__(self, own, slots, out, send, recv):
        super().__init__(send, recv)
        self.own, self.slots, self.out = own, slots, out

    def first(self, at):
        block, plane = self.RELAYED[at]
        return self.copy(self.own.at[block], self.slots.at[plane], at, plane, plane)

    def direct(self, at, plane):
        return self.copy(self.own.at[plane], self.slots.at[at], plane, at, plane)

    def relayed(self, at):
        end = 3 if at == 1 else 0
        return self.copy(self.slots.at[at], self.slots.at[at], end, at, end)

    def start(self):
        def body(at):
            if self.RELAYED[at]:
                self.first(at).start()
            for plane in self.DIRECT[at]:
                self.direct(at, plane).start()

        self.at_each(body)

    def hop(self):
        for at, block in ((1, 3), (2, 0)):

            @pl.when(self.place[2] == at)
            def _():
                self.relayed(at).wait_recv()
                self.slots[at] = (
                    self.slots[at].astype(F32) + self.own[block].astype(F32)
                ).astype(BF)
                self.relayed(at).start()

    def finish(self):
        def body(at):
            total = self.own[at].astype(F32)
            for plane in self.SOURCES[at]:
                self.direct(plane, at).wait_recv()
                total = total + self.slots[plane].astype(F32)
            self.out[...] = total.astype(BF)
            if self.RELAYED[at]:
                self.first(at).wait_send()
            else:
                self.relayed(at).wait_send()
            for plane in self.DIRECT[at]:
                self.direct(at, plane).wait_send()

        self.at_each(body)


class ColumnGather(Column):
    TARGETS = ((2, 1), (3, 2, 0), (0, 1, 3), (1, 2))

    def __init__(self, full, send, recv):
        super().__init__(send, recv)
        self.full = full

    def block(self, at, plane):
        return self.copy(self.full.at[at], self.full.at[at], plane, at, plane)

    def relayed(self, at):
        block, plane = (3, 0) if at == 1 else (0, 3)
        return self.copy(self.full.at[block], self.full.at[block], at, block, plane)

    def start(self):
        def body(at):
            for plane in self.TARGETS[at]:
                self.block(at, plane).start()

        self.at_each(body)

    def hop(self):
        for at in (1, 2):

            @pl.when(self.place[2] == at)
            def _():
                self.relayed(at).wait_recv()
                self.relayed(at).start()

    def finish(self):
        def body(at):
            for plane in range(4):
                if plane != at and (at, plane) not in ((1, 3), (2, 0)):
                    self.block(plane, at).wait_recv()
            for plane in self.TARGETS[at]:
                self.block(at, plane).wait_send()
            if at in (1, 2):
                self.relayed(at).wait_send()

        self.at_each(body)


class Root(Column):
    def __init__(self, send, recv):
        super().__init__(send, recv)
        x, s, z = self.place
        self.root = 2 * x + s // 2
        self.low = self.root < 2
        self.between = jnp.where(self.low, 2, 1)
        self.end = jnp.where(self.low, 3, 0)
        self.is_root = z == self.root


class RootSum(Root):
    def __init__(self, own, slots, out, send, recv):
        super().__init__(send, recv)
        self.own, self.slots, self.out = own, slots, out

    def toward(self, slot, plane, source=None):
        landing = self.slots.at[slot]
        return self.copy(landing if source is None else source, landing, 0, slot, plane)

    def start(self):
        z = self.place[2]

        @pl.when(z == self.end)
        def _():
            self.toward(0, self.between, self.own).start()

        @pl.when((z != self.end) & (z != self.between) & (z != self.root))
        def _():
            self.toward(1, self.root, self.own).start()

    def hop(self):
        @pl.when(self.place[2] == self.between)
        def _():
            self.toward(0, self.root).wait_recv()
            self.slots[0] = (self.slots[0].astype(F32) + self.own[...].astype(F32)).astype(BF)
            self.toward(0, self.root).start()

    def finish(self):
        self.out[...] = self.own[...]

        @pl.when(self.is_root)
        def _():
            total = self.own[...].astype(F32)
            for slot in (0, 1):
                self.toward(slot, self.root).wait_recv()
                total = total + self.slots[slot].astype(F32)
            self.out[...] = total.astype(BF)

        @pl.when(jnp.logical_not(self.is_root))
        def _():
            self.toward(0, self.root).wait_send()


def nn(left, right):
    return jnp.dot(left, right, preferred_element_type=F32)


def nt(left, right):
    return lax.dot_general(left, right, (((1,), (1,)), ((), ())), preferred_element_type=F32)


def tn(left, right):
    return lax.dot_general(left, right, (((0,), (0,)), ((), ())), preferred_element_type=F32)


def flat(ref):
    value = ref[...]
    return value.reshape(-1, value.shape[-1])


def in_blocks(length, size, body):
    def step(index, carry):
        body(pl.ds(pl.multiple_of(index * size, size), size), index * size)
        return carry

    lax.fori_loop(0, length // size, step, 0)


def weights_of_scores(query, keys, pkeys, seg_rows, seg_cols, begin, rate):
    scale = 1.0 / math.sqrt(HD)
    inner = nt(query, keys)
    per_scores = nt(query, pkeys) * scale
    row_places = begin + lax.broadcasted_iota(jnp.int32, inner.shape, 0)
    col_places = lax.broadcasted_iota(jnp.int32, inner.shape, 1)
    allowed = (seg_rows == seg_cols) & (col_places <= row_places)
    distance = jnp.maximum(row_places - col_places, 0).astype(F32)
    decay_w = jnp.where(allowed, jnp.exp(-rate * distance) * (1.0 / HD), 0.0)
    seq_scores = jnp.where(allowed, inner * scale, -jnp.inf)
    top = jnp.maximum(
        jnp.max(per_scores, axis=1, keepdims=True), jnp.max(seq_scores, axis=1, keepdims=True)
    )
    per_exp = jnp.exp(per_scores - top)
    seq_exp = jnp.exp(seq_scores - top)
    denom = jnp.sum(per_exp, axis=1, keepdims=True) + jnp.sum(seq_exp, axis=1, keepdims=True)
    share = 1.0 / denom
    return inner, decay_w, distance, seq_exp * share, per_exp * share


class BackwardIn(NamedTuple):
    grad_full: Any
    grad_rows: Any
    rows: Any
    out_low: Any
    out_high: Any
    gains: Any
    persist: Any
    rates: Any
    seg_rows: Any
    seg_cols: Any


class BackwardOut(NamedTuple):
    mix_buf: Any
    gu_buf: Any
    down_buf: Any
    out_buf: Any
    rows_buf: Any
    grads_buf: Any
    plane_buf: Any
    grad_low: Any
    grad_high: Any


class PlaneScratch(NamedTuple):
    part: Any
    pair: Any
    away: Any
    near: Any
    ssend: Any
    srecv: Any
    gsend: Any
    grecv: Any


class BackwardScratch(NamedTuple):
    grad_gu: Any
    grad_proj: Any
    grad_keys: Any
    grad_values: Any
    branch: Any
    grad_mid: Any
    grad_next: Any
    grad_persist: Any
    grad_rate: Any
    gain_sums: Any
    small: Any
    column_buf: Any
    own_gu: Any
    own_down: Any
    grad_mix: Any
    grad_out: Any
    gu_slots: Any
    down_slots: Any
    mix_slots: Any
    root_slots: Any
    gu_sum: Any
    down_sum: Any
    mix_sum: Any
    out_sum: Any
    csend: Any
    crecv: Any
    hsend: Any
    hrecv: Any
    psend: Any
    precv: Any
    osend: Any
    orecv: Any
    rsend: Any
    rrecv: Any
    zsend: Any
    zrecv: Any
    qsend: Any
    qrecv: Any
    loaded: Any


def fields(*kinds):
    return tuple(name for kind in kinds for name in kind._fields)


def named(names, refs):
    return types.SimpleNamespace(**dict(zip(names, refs, strict=True)))


def remote(source, landing, sems, index, target):
    return pltpu.make_async_remote_copy(
        src_ref=source,
        dst_ref=landing,
        send_sem=sems[0].at[index],
        recv_sem=sems[1].at[index],
        device_id=target,
        device_id_type=MESH,
    )


class RootGather(Root):
    def __init__(self, block, send, recv):
        super().__init__(send, recv)
        self.block = block

    def to(self, plane, sent):
        return self.copy(self.block, self.block, sent, 0, plane)

    def near(self):
        return jnp.where(self.low, 1 - self.root, 5 - self.root)

    def start(self):
        @pl.when(self.is_root)
        def _():
            self.to(self.between, 0).start()
            self.to(self.near(), 1).start()

    def hop(self):
        @pl.when(self.place[2] == self.between)
        def _():
            self.to(self.end, 0).wait_recv()
            self.to(self.end, 0).start()

    def finish(self):
        z = self.place[2]

        @pl.when((z != self.root) & (z != self.between))
        def _():
            self.to(self.end, 0).wait_recv()

        @pl.when((z == self.root) | (z == self.between))
        def _():
            self.to(self.end, 0).wait_send()

        @pl.when(self.is_root)
        def _():
            self.to(self.end, 1).wait_send()


class SeqGather:
    def __init__(self, full, batch, send, recv):
        self.place = here()
        self.full, self.batch, self.send, self.recv = full, batch, send, recv
        self.size = full.shape[1] // 4
        self.beside = peer(self.place, 2, False)
        self.sibling = peer(self.place, 0, True)

    def rows(self, owner):
        return pl.ds(pl.multiple_of(owner[1] * self.size, self.size), self.size)

    def copy(self, owner, target, sem):
        block = self.full.at[self.batch, self.rows(owner)]
        sems = (self.send.at[self.batch], self.recv.at[self.batch])
        return remote(block, block, sems, sem, target)

    def start(self, value):
        self.full[self.batch, self.rows(self.place), :] = value
        self.copy(self.place, self.beside, 0).start()
        self.copy(self.place, self.sibling, 1).start()

    def forward(self):
        self.copy(self.beside, self.beside, 0).wait_recv()
        self.copy(self.beside, self.sibling, 2).start()

    def finish(self):
        self.copy(self.sibling, self.sibling, 1).wait_recv()
        self.copy(peer(self.place, 2, True), self.sibling, 2).wait_recv()
        self.copy(self.place, self.beside, 0).wait_send()
        self.copy(self.place, self.sibling, 1).wait_send()
        self.copy(self.beside, self.sibling, 2).wait_send()


class ForwardIn(NamedTuple):
    inputs: Any
    small: Any
    gain_rows: Any
    w_mix: Any
    w_out: Any
    w_gu: Any
    w_down: Any
    seg_rows: Any
    seg_cols: Any


class ForwardOut(NamedTuple):
    rows: Any
    gains: Any
    persist: Any
    rates: Any


class Kept(NamedTuple):
    normed: Any
    mix: Any
    out: Any
    gu: Any
    down: Any
    qkv: Any
    gate: Any
    recalled: Any
    combined: Any
    mid: Any
    normed_two: Any
    gate_up: Any
    hidden: Any
    out_rows: Any


class ForwardScratch(NamedTuple):
    gain_all: Any
    small_all: Any
    mix_away: Any
    gu_away: Any
    down_away: Any
    zsend: Any
    zrecv: Any
    psend: Any
    precv: Any
    xsend: Any
    xrecv: Any
    gsend: Any
    grecv: Any
    csend: Any
    crecv: Any
    hsend: Any
    hrecv: Any
    saved: Any


def each(parts, act):
    for part in parts:
        act(part)


def forward_kernel(unit, *refs):
    count = len(Kept._fields)
    r, refs = refs[: len(ForwardIn._fields)], refs[len(ForwardIn._fields) :]
    given = vars(named(ForwardIn._fields, r))
    r, refs = refs[: len(ForwardOut._fields)], refs[len(ForwardOut._fields) :]
    given |= vars(named(ForwardOut._fields, r))
    in_hbm = [refs[:count], refs[count : 2 * count]]
    refs = refs[2 * count :]
    in_vmem = [refs[:count], refs[count : 2 * count]]
    refs = refs[2 * count :]
    scratch = PlaneScratch._fields[:6] + ForwardScratch._fields
    r = types.SimpleNamespace(**given, **vars(named(scratch, refs)))
    views = [types.SimpleNamespace(**vars(named(Kept._fields, part))) for part in in_vmem]
    views[0].rows, views[1].rows = r.rows, views[0].out_rows

    def save(layer, which):
        for name in which:
            index = Kept._fields.index(name)
            yield pltpu.make_async_copy(
                in_vmem[layer][index], in_hbm[layer][index], r.saved.at[layer, index]
            )

    place = here()
    x, s, z = place
    partner = peer(place, 1, False)
    flips = [(dx, ds) for dx in (0, 1) for ds in range(4) if dx or ds]
    plane = [((x + dx) % 2, (s + ds) % 4, z) for dx, ds in flips]
    column = [(x, s, (z + dz) % 4) for dz in (1, 2, 3)]
    column += [(1 - x, s, (z + dz) % 4) for dz in (1, 2, 3)]
    barrier = pltpu.get_barrier_semaphore()
    for other in plane + column:
        pl.semaphore_signal(barrier, inc=1, device_id=other, device_id_type=MESH)
    pl.semaphore_wait(barrier, len(plane) + len(column))

    zsems, psems, xsems = (r.zsend, r.zrecv), (r.psend, r.precv), (r.xsend, r.xrecv)
    holders = [*column, partner]

    def gains_to(index):
        return remote(r.gain_rows, r.gain_all.at[x, z], zsems, index, holders[index])

    for index in range(7):
        gains_to(index).start()
    r.gain_all[x, z] = r.gain_rows[...]

    mine, other = x * 4 + s, (1 - x) * 4 + s

    def mix_part(which):
        heads = [pl.ds(pl.multiple_of(kind * D + which * HD, HD), HD) for kind in range(4)]
        return jnp.concatenate([r.w_mix[0, :, cols] for cols in heads], 1)

    out_rows = pl.ds(pl.multiple_of(s % 2 * HD, HD), HD)
    root = z == 2 * x + s // 2
    rooted = z == 2 * (1 - x) + s // 2
    for layer in (0, 1):
        v = views[layer]

        @pl.when(x == layer)
        def _():
            r.mix_away[...] = mix_part(other)
            remote(r.mix_away, v.mix.at[z], xsems, 0, partner).start()
            v.mix[z] = mix_part(mine)

            @pl.when(rooted)
            def _():
                remote(r.w_out.at[0, out_rows], v.out, xsems, 1, partner).start()

            @pl.when(root)
            def _():
                v.out[...] = r.w_out[0, out_rows, :]

    for index in range(7):
        gains_to(index).wait_recv()
    for layer in range(2):
        for owner in range(4):
            for kind in range(2):
                for half in range(2):
                    begin = owner * 2 * HD + half * HD
                    row = 2 * kind + half
                    r.gains[layer, kind : kind + 1, begin : begin + HD] = r.gain_all[
                        layer, owner, row : row + 1, :
                    ]
    size = r.rows.shape[1]
    own_half = pl.ds(pl.multiple_of(x * size, size), size)
    arriving = [SeqGather(views[0].normed, batch, r.gsend, r.grecv) for batch in range(2)]
    for batch, gather in enumerate(arriving):
        rows = r.inputs[batch, 0].astype(F32)
        gather.start((rows * rms_scale(rows) * r.gains[0, 0:1, :]).astype(BF))
        r.rows[batch] = r.inputs[batch, 0, own_half, :]

    for index in range(7):
        remote(r.small, r.small_all.at[x, s], psems, index, plane[index]).start()
    r.small_all[x, s] = r.small[...]

    padded = r.down_away.shape[0]
    width = 8 * unit + 64

    def select(which, offset):
        begin = lax.broadcasted_iota(jnp.int32, (width, 128), 0) - offset
        col = lax.broadcasted_iota(jnp.int32, (width, 128), 1)
        return jnp.where((begin == which * unit + col) & (col < unit), 1.0, 0.0).astype(BF)

    def gu_part(which, out):
        for owner in range(4):
            base = owner * 8 * unit
            offset = base % 128
            chosen = select(which, offset)
            for side in range(2):
                begin = side * FF + base - offset
                part = nn(r.w_gu[0, :, begin : begin + width], chosen).astype(BF)
                at = side * 4 * padded + owner * padded
                out[:, at : at + padded] = part[:, :padded]

    def down_part(which, out):
        row = lax.broadcasted_iota(jnp.int32, (padded, 8 * unit), 0)
        col = lax.broadcasted_iota(jnp.int32, (padded, 8 * unit), 1)
        chosen = jnp.where((col == which * unit + row) & (row < unit), 1.0, 0.0).astype(BF)
        out[...] = nn(chosen, r.w_down[0]).astype(BF)

    gu_part(other, r.gu_away)
    down_part(other, r.down_away)
    for layer in (0, 1):
        v = views[layer]

        @pl.when(x == layer)
        def _():
            remote(r.gu_away, v.gu.at[z], xsems, 2, partner).start()
            remote(r.down_away, v.down.at[z], xsems, 3, partner).start()

    mixers, feeds = [], []
    for layer, v in enumerate(views):
        sems = [(r.csend.at[3 * layer + i], r.crecv.at[3 * layer + i]) for i in range(3)]
        mixers.append(
            [
                ColumnGather(v.mix, *sems[0]),
                RootGather(v.out, r.hsend.at[layer], r.hrecv.at[layer]),
            ]
        )
        feeds.append([ColumnGather(v.gu, *sems[1]), ColumnGather(v.down, *sems[2])])

    def swapped(layer, index):
        v = views[layer]
        landing = [v.mix.at[z], v.out, v.gu.at[z], v.down.at[z]][index]
        here_from = remote(landing, landing, xsems, index, partner)

        @pl.when((x != layer) & root if index == 1 else x != layer)
        def _():
            here_from.wait_recv()

    def start_mixer(layer):
        for index, part in enumerate(mixers[layer]):
            swapped(layer, index)
            part.start()

    def start_feed(layer):
        for index, part in enumerate(feeds[layer]):
            swapped(layer, 2 + index)
            part.start()

    start_mixer(0)
    for layer, v in enumerate(views):

        @pl.when(x == layer)
        def _():
            gu_part(mine, v.gu.at[z])
            down_part(mine, v.down.at[z])

    start_feed(0)
    arriving[0].forward()
    each(mixers[0], lambda part: part.hop())
    arriving[1].forward()

    for index in range(7):
        dx, ds = flips[index]
        landing = r.small_all.at[(x + dx) % 2, (s + 4 - ds) % 4]
        remote(r.small, landing, psems, index, plane[index]).wait_recv()
    for layer in range(2):
        begin = pl.multiple_of(s % 2 * 32, 32)
        rows = r.small_all[layer, 2 * x + s // 2, pl.ds(begin, 32), :]
        r.persist[layer] = rows.astype(BF).reshape(2, 16, HD)
        begin = pl.multiple_of(64 + s % 2 * 8, 8)
        r.rates[layer] = r.small_all[layer, 2 * x + s // 2, pl.ds(begin, 8), :]

    length = r.part.shape[1]

    def project(layer, batch):
        v = views[layer]

        def block(rows, begin):
            proj = nn(v.normed[batch, rows, :], flat(v.mix))
            v.qkv[batch, rows, :] = proj[:, : 3 * HD].astype(BF)
            v.gate[batch, rows, :] = jax.nn.sigmoid(proj[:, 3 * HD :])

        in_blocks(length, 256, block)

    def mixer(layer, batch):
        v = views[layer]

        def block(rows, begin):
            values = v.qkv[batch, :, 2 * HD :]
            inner, decay_w, _, probs, per_probs = weights_of_scores(
                v.qkv[batch, rows, :HD],
                v.qkv[batch, :, HD : 2 * HD],
                r.persist[layer, 0],
                r.seg_rows[batch, rows, :],
                r.seg_cols[batch],
                begin,
                r.rates[layer, 0:1, 0:1],
            )
            attended = nn(probs.astype(BF), values) + nn(per_probs.astype(BF), r.persist[layer, 1])
            recalled = nn((inner * decay_w).astype(BF), values).astype(BF)
            v.recalled[batch, rows, :] = recalled
            combined = attended.astype(BF).astype(F32)
            combined = combined + v.gate[batch, rows, :] * recalled.astype(F32)
            combined = combined.astype(BF)
            v.combined[batch, rows, :] = combined
            r.part[batch, rows, :] = nn(combined, v.out[...]).astype(BF)

        in_blocks(length, 128, block)

    def feed(layer, batch):
        v = views[layer]

        def block(rows, begin):
            gate_up = nn(v.normed_two[batch, rows, :], flat(v.gu))
            v.gate_up[batch, rows, :] = gate_up
            half = gate_up.shape[1] // 2
            hidden = (jax.nn.silu(gate_up[:, :half]) * gate_up[:, half:]).astype(BF)
            v.hidden[batch, rows, :] = hidden
            r.part[batch, rows, :] = nn(hidden, flat(v.down)).astype(BF)

        in_blocks(length, 256, block)

    def scatter(batch):
        return Scatter(r.part, batch, r.pair, r.away, r.near, r.ssend, r.srecv)

    def send_normed(batch, own, gain, full):
        gather = Gather(full, batch, r.gsend, r.grecv)
        gather.start((own * rms_scale(own) * gain).astype(BF))
        return gather

    mixer_names = Kept._fields[:3] + Kept._fields[5:9]
    for layer, v in enumerate(views):
        parts = []
        for batch in range(2):
            if layer == 1:
                arriving[batch].forward()
            arriving[batch].finish()
            if batch == 0:
                each(mixers[layer], lambda part: part.finish())
            project(layer, batch)
            mixer(layer, batch)
            part = scatter(batch)
            part.start()
            part.forward()
            parts.append(part)
        each(save(layer, mixer_names), lambda copy: copy.start())
        if layer == 0:
            start_mixer(1)
        gathers = []
        for batch, part in enumerate(parts):
            mid = v.rows[batch].astype(F32) + part.finish()
            v.mid[batch] = mid
            gathers.append(send_normed(batch, mid, r.gains[layer, 1:2, :], v.normed_two))
        each(feeds[layer], lambda part: part.hop())
        parts = []
        for batch, gather in enumerate(gathers):
            gather.forward()
            gather.finish()
            if batch == 0:
                each(feeds[layer], lambda part: part.finish())
            feed(layer, batch)
            if layer == 0 and batch == 0:
                each(mixers[1], lambda part: part.hop())
                start_feed(1)
            part = scatter(batch)
            part.start()
            part.forward()
            parts.append(part)
        each(save(layer, Kept._fields[3:5] + Kept._fields[9:13]), lambda copy: copy.start())
        arriving = []
        for batch, part in enumerate(parts):
            rows = (v.mid[batch] + part.finish()).astype(BF)
            v.out_rows[batch] = rows
            if layer == 0:
                gain = r.gains[1, 0:1, :]
                arriving.append(send_normed(batch, rows.astype(F32), gain, views[1].normed))
        each(save(layer, Kept._fields[13:]), lambda copy: copy.start())

    for layer in range(2):
        for copy in save(layer, Kept._fields):
            copy.wait()
    remote(r.mix_away, r.mix_away, xsems, 0, partner).wait_send()
    remote(r.gu_away, r.gu_away, xsems, 2, partner).wait_send()
    remote(r.down_away, r.down_away, xsems, 3, partner).wait_send()

    @pl.when(rooted)
    def _():
        remote(views[0].out, views[0].out, xsems, 1, partner).wait_send()

    for index in range(7):
        gains_to(index).wait_send()
        remote(r.small, r.small_all.at[x, s], psems, index, plane[index]).wait_send()


def backward_kernel(*refs):
    saved_names = Kept._fields[:-1]
    count = len(saved_names)
    given = vars(named(BackwardIn._fields, refs[: len(BackwardIn._fields)]))
    refs = refs[len(BackwardIn._fields) :]
    in_hbm = [refs[:count], refs[count : 2 * count]]
    refs = refs[2 * count :]
    given |= vars(named(BackwardOut._fields, refs[: len(BackwardOut._fields)]))
    refs = refs[len(BackwardOut._fields) :]
    in_vmem = refs[:count]
    given |= vars(named(saved_names, in_vmem))
    scratch = fields(PlaneScratch, BackwardScratch)
    r = types.SimpleNamespace(**given, **vars(named(scratch, refs[count:])))
    length = r.part.shape[1]
    place = here()
    x, s, z = place

    def load(layer, which):
        for name in which:
            index = saved_names.index(name)
            yield pltpu.make_async_copy(in_hbm[layer][index], in_vmem[index], r.loaded.at[index])

    feed_names = saved_names[3:5] + saved_names[9:]
    mixer_names = saved_names[:3] + saved_names[5:9]
    for which in (feed_names, mixer_names):
        each(load(1, which), lambda copy: copy.start())
    feeds, mixers = [], []
    for layer in range(2):
        sems = [(r.csend.at[3 * layer + i], r.crecv.at[3 * layer + i]) for i in range(3)]
        feeds.append(
            [
                ColumnSum(r.own_gu, r.gu_slots.at[layer], r.gu_sum.at[layer], *sems[0]),
                ColumnSum(r.own_down, r.down_slots.at[layer], r.down_sum.at[layer], *sems[1]),
            ]
        )
        mixers.append(
            [
                ColumnSum(r.grad_mix, r.mix_slots.at[layer], r.mix_sum.at[layer], *sems[2]),
                RootSum(
                    r.grad_out,
                    r.root_slots.at[layer],
                    r.out_sum.at[layer],
                    r.hsend.at[layer],
                    r.hrecv.at[layer],
                ),
            ]
        )
    grads = (r.grad_low, r.grad_high)

    def feed_back(full, batch):
        def block(rows, begin):
            grad_hidden = nt(full[batch, rows, :], flat(r.down))
            half = grad_hidden.shape[1]
            gate_part = r.gate_up[batch, rows, :half]
            up_part = r.gate_up[batch, rows, half:]
            sig_part = jax.nn.sigmoid(gate_part)
            silu = gate_part * sig_part
            grad_gate = grad_hidden * up_part * (sig_part + silu * (1.0 - sig_part))
            r.grad_gu[batch, rows, :half] = grad_gate.astype(BF)
            r.grad_gu[batch, rows, half:] = (grad_hidden * silu).astype(BF)
            r.part[batch, rows, :] = nt(r.grad_gu[batch, rows, :], flat(r.gu)).astype(BF)

        in_blocks(length, 256, block)

    def down_weights(full):
        def down(cols, begin):
            grad = tn(r.hidden[0], full[0, :, cols])
            grad = grad + tn(r.hidden[1], full[1, :, cols])
            grad = grad.reshape(4, grad.shape[0] // 4, grad.shape[1])
            r.own_down[:, :, cols] = grad.astype(BF)

        in_blocks(D, 256, down)

    def product(out, left, right):
        for owner in range(4):
            cols = slice(owner * (D // 4), (owner + 1) * (D // 4))
            grad = tn(left[0, :, cols], right[0]) + tn(left[1, :, cols], right[1])
            out[owner] = grad.astype(BF)

    def mixer_back(layer, batch):
        scale = 1.0 / math.sqrt(HD)
        r.grad_keys[...] = jnp.zeros_like(r.grad_keys)
        r.grad_values[...] = jnp.zeros_like(r.grad_values)

        def block(rows, begin):
            grad_combined = nt(r.branch[batch, rows, :], r.out[...])
            gate = r.gate[batch, rows, :]
            recalled = r.recalled[batch, rows, :].astype(F32)
            attn_rows = grad_combined.astype(BF)
            memory_rows = (grad_combined * gate).astype(BF)
            grad_pre = grad_combined * recalled * gate * (1.0 - gate)
            r.grad_proj[batch, rows, 3 * HD :] = grad_pre.astype(BF)
            query = r.qkv[batch, rows, :HD]
            keys = r.qkv[batch, :, HD : 2 * HD]
            values = r.qkv[batch, :, 2 * HD :]
            inner, decay_w, distance, probs, per_probs = weights_of_scores(
                query,
                keys,
                r.persist[layer, 0],
                r.seg_rows[batch, rows, :],
                r.seg_cols[batch],
                begin,
                r.rates[layer, 0:1, 0:1],
            )
            per_dp = nt(attn_rows, r.persist[layer, 1])
            seq_dp = nt(attn_rows, values)
            delta = jnp.sum(per_probs * per_dp, axis=1, keepdims=True) + jnp.sum(
                probs * seq_dp, axis=1, keepdims=True
            )
            per_ds = (per_probs * (per_dp - delta)).astype(BF)
            seq_ds = (probs * (seq_dp - delta)).astype(BF)
            weighted = nt(memory_rows, values) * decay_w
            grad_inner = weighted.astype(BF)
            memory = inner * decay_w
            rate_terms = weighted * inner * distance
            r.grad_rate[layer] -= jnp.sum(rate_terms, axis=0, keepdims=True)
            grad_query = (nn(per_ds, r.persist[layer, 0]) + nn(seq_ds, keys)) * scale
            grad_query = grad_query + nn(grad_inner, keys)
            r.grad_proj[batch, rows, :HD] = grad_query.astype(BF)
            r.grad_keys[...] += tn(seq_ds, query) * scale + tn(grad_inner, query)
            r.grad_values[...] += tn(probs.astype(BF), attn_rows) + tn(
                memory.astype(BF), memory_rows
            )
            r.grad_persist[layer, 0] += tn(per_ds, query) * scale
            r.grad_persist[layer, 1] += tn(per_probs.astype(BF), attn_rows)

        in_blocks(length, 128, block)
        r.grad_proj[batch, :, HD : 2 * HD] = r.grad_keys[...].astype(BF)
        r.grad_proj[batch, :, 2 * HD : 3 * HD] = r.grad_values[...].astype(BF)

        def back(rows, begin):
            r.part[batch, rows, :] = nt(r.grad_proj[batch, rows, :], flat(r.mix)).astype(BF)

        in_blocks(length, 256, back)

    def scatter(batch):
        return Scatter(r.part, batch, r.pair, r.away, r.near, r.ssend, r.srecv)

    def through_norm(batch, part, rows, gain):
        grad_normed = part.finish()
        inverse = rms_scale(rows)
        return norm_back(grad_normed, rows * inverse, inverse, gain)

    flips = [(dx, ds) for dx in (0, 1) for ds in range(4) if dx or ds]
    plane = [((x + dx) % 2, (s + ds) % 4, z) for dx, ds in flips]
    column = [(x, s, (z + dz) % 4) for dz in (1, 2, 3)]
    barrier = pltpu.get_barrier_semaphore()
    for other in plane + column:
        pl.semaphore_signal(barrier, inc=1, device_id=other, device_id_type=MESH)
    pl.semaphore_wait(barrier, len(plane) + len(column))
    r.grad_rate[...] = jnp.zeros_like(r.grad_rate)
    r.grad_persist[...] = jnp.zeros_like(r.grad_persist)
    arriving = None
    for layer in (1, 0):
        full = r.grad_next if arriving else r.grad_full
        above = grads[1] if arriving else r.grad_rows
        rows_in = r.out_low if layer else r.rows
        each(load(layer, feed_names), lambda copy: copy.wait())
        parts = []
        for batch in range(2):
            if arriving:
                arriving[batch].forward()
                arriving[batch].finish()
            if batch == 1 - layer:
                if layer == 0:
                    feeds[1][1].finish()
                down_weights(full)
                feeds[layer][1].start()
            feed_back(full, batch)
            part = scatter(batch)
            part.start()
            part.forward()
            parts.append(part)
        if layer == 0:
            each(mixers[1], lambda part: part.hop())
            feeds[1][0].finish()
        else:
            feeds[1][1].hop()
        product(r.own_gu, r.normed_two, r.grad_gu)
        feeds[layer][0].start()
        gathers = []
        gain_sums = []
        for batch, part in enumerate(parts):
            grad_mid, gain_sum = through_norm(
                batch, part, r.mid[batch], r.gains[layer, 1:2, :]
            )
            gain_sums.append(gain_sum[None])
            grad_mid = grad_mid + above[batch].astype(F32)
            r.grad_mid[batch] = grad_mid
            gather = Gather(r.branch, batch, r.gsend, r.grecv)
            gather.start(grad_mid.astype(BF))
            gathers.append(gather)
        r.gain_sums[layer, 1:2] = gain_sums[0] + gain_sums[1]
        if layer == 1:
            each(load(0, feed_names), lambda copy: copy.start())
        each(load(layer, mixer_names), lambda copy: copy.wait())
        parts = []
        for batch, gather in enumerate(gathers):
            gather.forward()
            gather.finish()
            if batch == 1:
                if layer == 0:
                    mixers[1][1].finish()
                grad_out = tn(r.combined[0], r.branch[0]) + tn(r.combined[1], r.branch[1])
                r.grad_out[...] = grad_out.astype(BF)
                mixers[layer][1].start()
            mixer_back(layer, batch)
            part = scatter(batch)
            part.start()
            part.forward()
            parts.append(part)
            if batch == 0:
                each(feeds[layer][: 2 - layer], lambda part: part.hop())
        if layer == 0:
            mixers[1][0].finish()
        product(r.grad_mix, r.normed, r.grad_proj)
        mixers[layer][0].start()
        if layer == 1:
            each(load(0, mixer_names), lambda copy: copy.start())
        arriving = []
        gain_sums = []
        for batch, part in enumerate(parts):
            grad_h, gain_sum = through_norm(
                batch, part, rows_in[batch].astype(F32), r.gains[layer, 0:1, :]
            )
            gain_sums.append(gain_sum[None])
            grad_h = (grad_h + r.grad_mid[batch]).astype(BF)
            grads[layer][batch] = grad_h
            if layer == 1:
                gather = Gather(r.grad_next, batch, r.gsend, r.grecv)
                gather.start(grad_h)
                arriving.append(gather)
        r.gain_sums[layer, 0:1] = gain_sums[0] + gain_sums[1]
    each(feeds[0], lambda part: part.finish())

    for layer in range(2):
        persist = r.grad_persist[layer].reshape(-1, HD)
        rate = r.grad_rate[layer]
        rate = sum(rate[:, begin : begin + HD] for begin in range(0, length, HD))
        for owner in range(4):
            r.small[owner, layer * 32 : (layer + 1) * 32, :] = persist
            r.small[owner, 64 + layer : 65 + layer, :] = rate
            for kind in range(2):
                for half in range(2):
                    row = 72 + 4 * layer + 2 * kind + half
                    begin = owner * 2 * HD + half * HD
                    r.small[owner, row : row + 1, :] = r.gain_sums[
                        layer, kind : kind + 1, begin : begin + HD
                    ]
    for owner in range(4):
        r.small[owner, 66:72, :] = jnp.zeros((6, HD), F32)

    sibling, beside, partner = (peer(place, 0, True), peer(place, 2, False), peer(place, 1, False))
    across = peer(place, 3, False)
    bufs = (r.mix_buf, r.gu_buf, r.down_buf)
    out_buf, rows_buf, grads_buf, plane_buf = r.out_buf, r.rows_buf, r.grads_buf, r.plane_buf
    by_layer = [
        [r.mix_sum.at[i], r.gu_sum.at[i], r.down_sum.at[i], r.out_sum.at[i]] for i in range(2)
    ]
    by_layer[0] += [r.out_low, r.grad_low]
    by_layer[1] += [r.out_high, r.grad_high]
    copy = remote

    def to_plane_of(dz):
        target = (z + dz) % 4
        return copy(
            r.small.at[target], r.column_buf.at[dz - 1], (r.zsend, r.zrecv), dz - 1, (x, s, target)
        )

    def to_plane(index):
        slot = plane_buf.at[x * 4 + s]
        return copy(slot, slot, (r.qsend, r.qrecv), index, plane[index])

    for dz in (1, 2, 3):
        to_plane_of(dz).start()

    psems = [(r.psend.at[i], r.precv.at[i]) for i in range(3)]

    def piece(index, kind, slot, target, source=None):
        landing = bufs[index].at[slot]
        return copy(landing if source is None else source, landing, psems[index], kind, target)

    mine = (x, s)
    turned = (1 - x, s)

    def send(indices):
        for layer in (0, 1):
            own, theirs = by_layer[layer], by_layer[1 - layer]

            @pl.when(x == layer)
            def _():
                for index in indices:
                    piece(index, 2, mine, partner, theirs[index]).start()
                    piece(index, 0, mine, beside, own[index]).start()
                    piece(index, 1, mine, sibling, own[index]).start()
                for index in indices:
                    bufs[index][mine] = own[index][...]

    def turn(indices):
        for index in indices:
            piece(index, 2, turned, partner).wait_recv()
            piece(index, 3, turned, beside).start()
            piece(index, 4, turned, sibling).start()

    send((1, 2))
    for layer in (0, 1):

        @pl.when(x == layer)
        def _():
            copy(by_layer[1 - layer][4], rows_buf, (r.rsend, r.rrecv), 0, partner).start()
            copy(by_layer[1 - layer][5], grads_buf, (r.rsend, r.rrecv), 1, partner).start()

    total = r.small[z]
    for dz in (1, 2, 3):
        to_plane_of(dz).wait_recv()
        total = total + r.column_buf[dz - 1]
    plane_buf[x * 4 + s] = total
    for index in range(7):
        to_plane(index).start()
    each(mixers[0], lambda part: part.hop())
    turn((1, 2))
    each(mixers[0], lambda part: part.finish())
    send((0,))

    core = s % 2
    root = z == 2 * x + s // 2
    of_root = (z // 2, 2 * (z % 2) + core)
    apart = 2 * ((x + of_root[0]) % 2) + (s // 2 + of_root[1] // 2) % 2

    def out_copy(index, target, source=None):
        landing = out_buf.at[core]
        return copy(landing if source is None else source, landing, (r.osend, r.orecv), index, target)

    for layer in (0, 1):

        @pl.when(root & (x == layer))
        def _():
            out_copy(1, beside, by_layer[layer][3]).start()
            out_copy(2, partner, by_layer[1 - layer][3]).start()
            out_copy(3, across, by_layer[1 - layer][3]).start()
            out_buf[core] = by_layer[layer][3][...]

    for apart_by in (1, 2, 3):

        @pl.when(apart == apart_by)
        def _():
            out_copy(apart_by, beside).wait_recv()

    out_copy(0, sibling).start()

    turn((0,))
    far = (x, (s + 2) % 4)
    far_turned = (1 - x, (s + 2) % 4)
    for index in (1, 2, 0):
        piece(index, 0, far, beside).wait_recv()
        piece(index, 5, far, sibling).start()
    for index in (1, 2, 0):
        piece(index, 3, far_turned, beside).wait_recv()
        piece(index, 6, far_turned, sibling).start()
    twin = sibling[1]
    far_twin = (twin + 2) % 4
    for index in range(3):
        piece(index, 1, (x, twin), sibling).wait_recv()
        piece(index, 4, (1 - x, twin), sibling).wait_recv()
        piece(index, 5, (x, far_twin), sibling).wait_recv()
        piece(index, 6, (1 - x, far_twin), sibling).wait_recv()
    other_out = out_buf.at[1 - core]
    copy(other_out, other_out, (r.osend, r.orecv), 0, sibling).wait_recv()
    for index in range(7):
        dx, ds = flips[index]
        slot = plane_buf.at[((x + dx) % 2) * 4 + (s + 4 - ds) % 4]
        copy(slot, slot, (r.qsend, r.qrecv), index, plane[index]).wait_recv()
    for index in (0, 1):
        copy(rows_buf, rows_buf, (r.rsend, r.rrecv), index, partner).wait()
    for index in range(7):
        to_plane(index).wait_send()
    for dz in (1, 2, 3):
        to_plane_of(dz).wait_send()
    for index in range(3):
        for kind in range(7):
            piece(index, kind, mine, sibling).wait_send()
    out_copy(0, sibling).wait_send()

    @pl.when(root)
    def _():
        for index in (1, 2, 3):
            out_copy(index, sibling).wait_send()


def kernel_call(kernel, number, operands, outs, scratch, spaces=None, places=None):
    spaces = spaces or [pltpu.VMEM] * len(outs)
    places = places or [pltpu.VMEM] * len(operands)
    return pl.pallas_call(
        kernel,
        out_shape=list(outs),
        in_specs=[pl.BlockSpec(memory_space=space) for space in places],
        out_specs=[pl.BlockSpec(memory_space=space) for space in spaces],
        scratch_shapes=scratch,
        compiler_params=pltpu.CompilerParams(
            collective_id=number, has_side_effects=True, vmem_limit_bytes=58 * 2**20
        ),
    )(*operands)


def pairs_of(*sizes):
    return [pltpu.SemaphoreType.DMA(size) for size in sizes for _ in range(2)]


def scatter_scratch(length):
    size = length // 8
    return [
        pltpu.VMEM((2, length, D), BF),
        pltpu.VMEM((2, 4, size, D), BF),
        pltpu.VMEM((2, 3, size, D), BF),
        pltpu.VMEM((2, 3, size, D), BF),
        *pairs_of((2, 8), (2, 8)),
    ]


def forward_call(number, *operands):
    inputs, small, _, w_mix, _, _, w_down, *_ = operands
    count, _, tokens, _ = inputs.shape
    depth, length = w_mix.shape[1], 4 * tokens
    unit = w_down.shape[1] // 8
    padded = -(-unit // 32) * 32
    shape = jax.ShapeDtypeStruct
    outs = ForwardOut(
        rows=shape((count, length // 8, D), BF),
        gains=shape((2, 2, D), F32),
        persist=shape((2, 2, 16, HD), BF),
        rates=shape((2, 8, HD), F32),
    )
    kept = Kept(
        normed=shape((count, length, D), BF),
        mix=shape((4, depth, 4 * HD), BF),
        out=shape((HD, D), BF),
        gu=shape((4, depth, 8 * padded), BF),
        down=shape((4, padded, D), BF),
        qkv=shape((count, length, 3 * HD), BF),
        gate=shape((count, length, HD), F32),
        recalled=shape((count, length, HD), BF),
        combined=shape((count, length, HD), BF),
        mid=shape((count, length // 8, D), F32),
        normed_two=shape((count, length, D), BF),
        gate_up=shape((count, length, 8 * padded), F32),
        hidden=shape((count, length, 4 * padded), BF),
        out_rows=shape((count, length // 8, D), BF),
    )
    scratch = [pltpu.VMEM(part.shape, part.dtype) for part in (*kept, *kept)]
    scratch += scatter_scratch(length)[:6]
    scratch += [
        pltpu.VMEM((2, 4, 8, HD), F32),
        pltpu.VMEM((2, 4) + small.shape, F32),
        pltpu.VMEM((depth, 4 * HD), BF),
        pltpu.VMEM((depth, 8 * padded), BF),
        pltpu.VMEM((padded, D), BF),
        *pairs_of((7,), (7,), (4,), (2, 8), (6, 4), (2, 2)),
        pltpu.SemaphoreType.DMA((2, len(kept))),
    ]
    kernel = functools.partial(forward_kernel, unit)
    specs = [pltpu.VMEM] * len(outs) + [pl.ANY] * (2 * len(kept))
    found = kernel_call(kernel, number, operands, [*outs, *kept, *kept], scratch, specs)
    own, found = found[: len(outs)], found[len(outs) :]
    return (
        named(ForwardOut._fields, own),
        named(Kept._fields, found[: len(kept)]),
        named(Kept._fields, found[len(kept) :]),
    )


def backward_call(number, given, below, above):
    saved = Kept._fields[:-1]
    kept = [getattr(part, name) for part in (below, above) for name in saved]
    count, length, _ = below.normed.shape
    depth, half, size = D // 4, 4 * below.down.shape[1], length // 8
    shape = jax.ShapeDtypeStruct
    outs = BackwardOut(
        mix_buf=shape((2, 4, depth, 4 * HD), BF),
        gu_buf=shape((2, 4, depth, 2 * half), BF),
        down_buf=shape((2, 4, half // 4, D), BF),
        out_buf=shape((2, HD, D), BF),
        rows_buf=shape((count, size, D), BF),
        grads_buf=shape((count, size, D), BF),
        plane_buf=shape((8, 80, HD), F32),
        grad_low=shape((count, size, D), BF),
        grad_high=shape((count, size, D), BF),
    )
    scratch = [pltpu.VMEM(part.shape, part.dtype) for part in kept[: len(saved)]]
    scratch += scatter_scratch(length) + [
        pltpu.VMEM((count, length, 2 * half), BF),
        pltpu.VMEM((count, length, 4 * HD), BF),
        pltpu.VMEM((length, HD), F32),
        pltpu.VMEM((length, HD), F32),
        pltpu.VMEM((count, length, D), BF),
        pltpu.VMEM((count, size, D), F32),
        pltpu.VMEM((count, length, D), BF),
        pltpu.VMEM((2, 2, 16, HD), F32),
        pltpu.VMEM((2, 1, length), F32),
        pltpu.VMEM((2, 2, D), F32),
        pltpu.VMEM((4, 80, HD), F32),
        pltpu.VMEM((3, 80, HD), F32),
        pltpu.VMEM((4, depth, 2 * half), BF),
        pltpu.VMEM((4, half // 4, D), BF),
        pltpu.VMEM((4, depth, 4 * HD), BF),
        pltpu.VMEM((HD, D), BF),
        pltpu.VMEM((2, 4, depth, 2 * half), BF),
        pltpu.VMEM((2, 4, half // 4, D), BF),
        pltpu.VMEM((2, 4, depth, 4 * HD), BF),
        pltpu.VMEM((2, 2, HD, D), BF),
        pltpu.VMEM((2, depth, 2 * half), BF),
        pltpu.VMEM((2, half // 4, D), BF),
        pltpu.VMEM((2, depth, 4 * HD), BF),
        pltpu.VMEM((2, HD, D), BF),
        *pairs_of((6, 4), (2, 2), (3, 7), (4,), (2,), (3,), (7,)),
        pltpu.SemaphoreType.DMA((len(saved),)),
    ]
    operands = [*(getattr(given, name) for name in BackwardIn._fields), *kept]
    spaces = [pltpu.VMEM] * len(BackwardIn._fields) + [pl.ANY] * len(kept)
    found = kernel_call(backward_kernel, number, operands, outs, scratch, None, spaces)
    return named(BackwardOut._fields, found)


def assemble_kernel(unit, *refs):
    mix_buf, gu_buf, down_buf, out_buf, *rows, plane_buf = refs[:11]
    mix_ref, gu_ref, down_ref, out_ref, rows_ref, grads_ref, persist_ref, rate_ref = refs[11:]
    x, s, _ = here()

    @pl.when(pl.program_id(0) == 0)
    def _():
        size = rows[0].shape[1]
        own = pl.ds(pl.multiple_of(x * size, size), size)
        got = pl.ds(pl.multiple_of((1 - x) * size, size), size)
        for ref, (low, high, other) in ((rows_ref, rows[:3]), (grads_ref, rows[3:])):
            for layer, part in enumerate((low, high)):

                @pl.when(x == layer)
                def _():
                    for batch in range(2):
                        ref[0, batch, 0, own, :] = part[batch].astype(ref.dtype)

            for batch in range(2):
                ref[0, batch, 0, got, :] = other[batch].astype(ref.dtype)
        for head in range(2):
            out_ref[0, head * HD : (head + 1) * HD, :] = out_buf[head].astype(F32)
            for kind in range(2):
                begin = pl.multiple_of(x * 32 + kind * 16, 16)
                persist_ref[0, kind, :, head * HD : (head + 1) * HD] = plane_buf[
                    2 * s + head, pl.ds(begin, 16), :
                ]
            both = jnp.sum(plane_buf[2 * s + head, 64:72, :], axis=1, keepdims=True)
            rate_ref[0:1, head : head + 1] = jnp.where(x == 0, both[0:1], both[1:2])

    padded = down_buf.shape[2]
    half = gu_buf.shape[3] // 2
    for which in range(8):
        slot = (which // 4, which % 4)
        mix = mix_buf[slot].astype(F32)
        for kind in range(4):
            begin = kind * D + which * HD
            mix_ref[0, :, begin : begin + HD] = mix[:, kind * HD : (kind + 1) * HD]
        part = gu_buf[slot].astype(F32)
        for side in range(2):
            for owner in range(half // padded):
                begin = side * FF + (owner * 8 + which) * unit
                source = side * half + owner * padded
                gu_ref[0, :, begin : begin + unit] = part[:, source : source + unit]
    for pair in range(2):
        down = down_buf[0, pair].astype(F32)
        down_ref[0, pair * unit : (pair + 1) * unit, :] = down[:unit]


def assemble_call(unit, found, outputs, grads):
    mix_buf, gu_buf, down_buf = found.mix_buf, found.gu_buf, found.down_buf
    depth, padded = mix_buf.shape[2], down_buf.shape[2]
    rows = depth // 4
    count, size, _ = outputs[0].shape
    shape = jax.ShapeDtypeStruct
    outs = [
        shape((1, depth, 4 * D), F32),
        shape((1, depth, 2 * FF), F32),
        shape((1, 8 * unit, D), F32),
    ]
    once = [
        shape((1, 2 * HD, D), F32),
        shape((1, count, 1, 2 * size, D), BF),
        shape((1, count, 1, 2 * size, D), F32),
        shape((1, 2, 16, 2 * HD), F32),
        shape((1, 2), F32),
    ]
    given = (found.out_buf, *outputs, found.rows_buf, *grads, found.grads_buf, found.plane_buf)

    def whole(part):
        return pl.BlockSpec(part.shape, lambda i, zeros=(0,) * len(part.shape): zeros)

    return pl.pallas_call(
        functools.partial(assemble_kernel, unit),
        grid=(4,),
        out_shape=outs + once,
        in_specs=[
            pl.BlockSpec((2, 4, rows, 4 * HD), lambda i: (0, 0, i, 0)),
            pl.BlockSpec((2, 4, rows, gu_buf.shape[3]), lambda i: (0, 0, i, 0)),
            pl.BlockSpec((1, 2, padded, D), lambda i: (i // 2, i % 2, 0, 0)),
            *(whole(part) for part in given),
        ],
        out_specs=[
            pl.BlockSpec((1, rows, 4 * D), lambda i: (0, i, 0)),
            pl.BlockSpec((1, rows, 2 * FF), lambda i: (0, i, 0)),
            pl.BlockSpec((1, 2 * unit, D), lambda i: (0, i, 0)),
            *(whole(part) for part in once),
        ],
        compiler_params=pltpu.CompilerParams(vmem_limit_bytes=60 * 2**20),
    )(mix_buf, gu_buf, down_buf, *given)


def tensor_parallel(
    inputs, segment_ids, cotangent, w_mix, w_out, w_gu, w_down, norm_gains, persist_kv, memory_decay
):
    x, s, z = here()
    nx, ns, nz = (lax.axis_size(a) for a in ("section", "seq", "shard"))
    width = nx * ns
    count, _, tokens, _ = inputs.shape
    length = tokens * ns
    size = length // width
    depth = w_mix.shape[1]
    unit = w_down.shape[1] // (nx * ns)

    small = persist_kv[0].reshape(-1, 2, HD).transpose(1, 0, 2).reshape(-1, HD).astype(F32)
    rates = jnp.broadcast_to(memory_decay[0][:, None, None], (2, 8, HD)).reshape(-1, HD)
    gain_rows = norm_gains[0].astype(F32).T.reshape(-1, HD)
    gain_rows = jnp.pad(gain_rows, ((0, 8 - gain_rows.shape[0]), (0, 0)))
    small = jnp.concatenate([small, rates], 0)
    segments = (segment_ids[:, 0, :, None], segment_ids)
    ready, below, above = forward_call(
        1, inputs, small, gain_rows, w_mix, w_out, w_gu, w_down, *segments
    )
    cot_full = lax.all_gather(cotangent[:, 0], "seq", axis=1, tiled=True)
    given = BackwardIn(
        grad_full=cot_full,
        grad_rows=lax.dynamic_slice_in_dim(cotangent[:, 0], x * size, size, 1),
        rows=ready.rows,
        out_low=below.out_rows,
        out_high=above.out_rows,
        gains=ready.gains,
        persist=ready.persist,
        rates=ready.rates,
        seg_rows=segments[0],
        seg_cols=segments[1],
    )
    found = backward_call(2, given, below, above)
    outputs = (below.out_rows, above.out_rows)
    grads = (found.grad_low, found.grad_high)

    grad_mix, grad_gu, grad_down, grad_out, section_out, section_grad, grad_persist, grad_rate = (
        assemble_call(unit, found, outputs, grads)
    )
    gain_all = jnp.sum(found.plane_buf[:, 72:], 0).reshape(2, 2, depth)
    grad_gain = lax.dynamic_index_in_dim(gain_all, x, 0).transpose(0, 2, 1)
    return (
        section_out,
        section_grad,
        grad_mix,
        grad_out,
        grad_gu,
        grad_down,
        grad_gain,
        grad_persist,
        grad_rate,
    )


def solution(mesh):
    sizes = mesh.shape
    planar = (sizes["section"], sizes["seq"]) == (2, 4)
    placed = (
        P(None, "shard", "seq", None),
        P(None, "shard", None),
        P(None, "shard", "seq", None),
        P("section", "shard", None),
        P("section", "shard", None),
        P("section", "shard", None),
        P("section", "shard", None),
        P("section", "shard", None),
        P("section", None, None, "seq"),
        P("section", "seq"),
    )
    return jax.shard_map(
        tensor_parallel if planar else on_device,
        mesh=mesh,
        in_specs=placed,
        out_specs=(
            P("section", None, "shard", "seq", None),
            P("section", None, "shard", "seq", None),
            P("section", "shard", None),
            P("section", "shard", None),
            P("section", "shard", None),
            P("section", "shard", None),
            P("section", "shard", None),
            P("section", None, None, "seq"),
            P("section", "seq"),
        ),
        check_vma=False,
    )
```

```python
import functools
import math
import types
from typing import Any, NamedTuple

import jax
import jax.numpy as jnp
from jax import lax
from jax.experimental import pallas as pl
from jax.experimental.pallas import tpu as pltpu
from jax.sharding import PartitionSpec as P

D = 1024
H = 8
HD = 128
FF = 2816


def shifted(value, axis, by):
    size = lax.axis_size(axis)
    pairs = [(i, i + by) for i in range(size) if 0 <= i + by < size]
    return lax.ppermute(value, axis, pairs)


def as_sent(value):
    return jax.tree.map(lambda a: a.astype(jnp.bfloat16) if a.dtype == jnp.float32 else a, value)


def rms_scale(values):
    return lax.rsqrt(jnp.mean(values * values, axis=-1, keepdims=True) + 1e-06)


def norm_back(grad_normed, scaled, inverse, gain):
    grad_scaled = grad_normed * gain
    grad_rows = inverse * (
        grad_scaled - scaled * jnp.mean(grad_scaled * scaled, axis=-1, keepdims=True)
    )
    return (grad_rows, jnp.sum(grad_normed * scaled, axis=0))


def block_terms(query_rows, key_rows, seg_ids, begin, reach, rate):
    inner = jnp.dot(query_rows, key_rows.T, preferred_element_type=jnp.float32)
    row_places = begin + jnp.arange(reach - begin, dtype=jnp.int32)
    col_places = jnp.arange(reach, dtype=jnp.int32)
    allowed = (seg_ids[begin:reach][:, None] == seg_ids[:reach][None, :]) & (
        col_places[None, :] <= row_places[:, None]
    )
    distance = jnp.maximum(row_places[:, None] - col_places[None, :], 0).astype(jnp.float32)
    decay_w = jnp.where(allowed, jnp.exp(-rate * distance), jnp.float32(0.0))
    return (inner, allowed, decay_w, distance)


def head_forward(query, keys, values, pkeys, pvalues, rate, seg_ids):
    length, width = query.shape
    block = min(512, length)
    scale = 1.0 / math.sqrt(width)
    attn_parts, memory_parts, lse_parts = ([], [], [])
    for begin in range(0, length, block):
        reach = begin + block
        query_rows = query[begin:reach]
        inner, allowed, decay_w, distance = block_terms(
            query_rows, keys[:reach], seg_ids, begin, reach, rate
        )
        per_scores = jnp.dot(query_rows, pkeys.T, preferred_element_type=jnp.float32) * scale
        seq_scores = jnp.where(allowed, inner * scale, -jnp.inf)
        top = jnp.maximum(
            jnp.max(per_scores, axis=1, keepdims=True), jnp.max(seq_scores, axis=1, keepdims=True)
        )
        per_exp = jnp.exp(per_scores - top)
        seq_exp = jnp.exp(seq_scores - top)
        denom = jnp.sum(per_exp, axis=1, keepdims=True) + jnp.sum(seq_exp, axis=1, keepdims=True)
        attended = jnp.dot(
            (per_exp / denom).astype(jnp.bfloat16), pvalues, preferred_element_type=jnp.float32
        )
        attended = attended + jnp.dot(
            (seq_exp / denom).astype(jnp.bfloat16),
            values[:reach],
            preferred_element_type=jnp.float32,
        )
        memory_w = (inner * decay_w * (1.0 / width)).astype(jnp.bfloat16)
        recalled = jnp.dot(memory_w, values[:reach], preferred_element_type=jnp.float32)
        attn_parts.append(attended)
        memory_parts.append(recalled)
        lse_parts.append(top[:, 0] + jnp.log(denom[:, 0]))
    return (
        jnp.concatenate(attn_parts, 0),
        jnp.concatenate(memory_parts, 0),
        jnp.concatenate(lse_parts, 0),
    )


def head_backward(query, keys, values, pkeys, pvalues, rate, seg_ids, lse, grad_attn, grad_memory):
    length, width = query.shape
    block = min(512, length)
    scale = 1.0 / math.sqrt(width)
    query_grads = []
    grad_keys = jnp.zeros((length, width), jnp.float32)
    grad_values = jnp.zeros((length, width), jnp.float32)
    grad_pkeys = jnp.zeros(pkeys.shape, jnp.float32)
    grad_pvalues = jnp.zeros(pvalues.shape, jnp.float32)
    grad_rate = jnp.float32(0.0)
    for begin in range(0, length, block):
        reach = begin + block
        query_rows = query[begin:reach]
        key_rows = keys[:reach]
        value_rows = values[:reach]
        inner, allowed, decay_w, distance = block_terms(
            query_rows, key_rows, seg_ids, begin, reach, rate
        )
        per_scores = jnp.dot(query_rows, pkeys.T, preferred_element_type=jnp.float32) * scale
        seq_scores = jnp.where(allowed, inner * scale, -jnp.inf)
        row_lse = lse[begin:reach][:, None]
        per_prob = jnp.exp(per_scores - row_lse)
        seq_prob = jnp.exp(seq_scores - row_lse)
        attn_rows = grad_attn[begin:reach]
        memory_rows = grad_memory[begin:reach]
        per_dp = jnp.dot(attn_rows, pvalues.T, preferred_element_type=jnp.float32)
        seq_dp = jnp.dot(attn_rows, value_rows.T, preferred_element_type=jnp.float32)
        delta = jnp.sum(per_prob * per_dp, axis=1, keepdims=True) + jnp.sum(
            seq_prob * seq_dp, axis=1, keepdims=True
        )
        per_ds = (per_prob * (per_dp - delta)).astype(jnp.bfloat16)
        seq_ds = (seq_prob * (seq_dp - delta)).astype(jnp.bfloat16)
        rows_grad = (
            jnp.dot(per_ds, pkeys, preferred_element_type=jnp.float32)
            + jnp.dot(seq_ds, key_rows, preferred_element_type=jnp.float32)
        ) * scale
        grad_pkeys = (
            grad_pkeys
            + jnp.einsum("qk,qd->kd", per_ds, query_rows, preferred_element_type=jnp.float32)
            * scale
        )
        grad_pvalues = grad_pvalues + jnp.einsum(
            "qk,qd->kd",
            per_prob.astype(jnp.bfloat16),
            attn_rows,
            preferred_element_type=jnp.float32,
        )
        key_part = (
            jnp.einsum("qk,qd->kd", seq_ds, query_rows, preferred_element_type=jnp.float32) * scale
        )
        value_part = jnp.einsum(
            "qk,qd->kd",
            seq_prob.astype(jnp.bfloat16),
            attn_rows,
            preferred_element_type=jnp.float32,
        )
        memory_w = (inner * decay_w * (1.0 / width)).astype(jnp.bfloat16)
        grad_mw = jnp.dot(memory_rows, value_rows.T, preferred_element_type=jnp.float32)
        value_part = value_part + jnp.einsum(
            "qk,qd->kd", memory_w, memory_rows, preferred_element_type=jnp.float32
        )
        grad_inner = (grad_mw * decay_w * (1.0 / width)).astype(jnp.bfloat16)
        rows_grad = rows_grad + jnp.dot(grad_inner, key_rows, preferred_element_type=jnp.float32)
        key_part = key_part + jnp.einsum(
            "qk,qd->kd", grad_inner, query_rows, preferred_element_type=jnp.float32
        )
        grad_rate = grad_rate - jnp.sum(grad_mw * inner * decay_w * (1.0 / width) * distance)
        grad_keys = grad_keys.at[:reach].add(key_part)
        grad_values = grad_values.at[:reach].add(value_part)
        query_grads.append(rows_grad)
    return (
        jnp.concatenate(query_grads, 0),
        grad_keys,
        grad_values,
        grad_pkeys,
        grad_pvalues,
        grad_rate,
    )


def layer_forward(rows_in, seg_ids, full, pkv, rates):
    mix_w, out_w, gu_w, down_w, gains = full
    tokens = rows_in.shape[0]
    gain_one = gains[:, 0].astype(jnp.float32)
    gain_two = gains[:, 1].astype(jnp.float32)
    inverse_one = rms_scale(rows_in)
    scaled_one = rows_in * inverse_one
    normed = (scaled_one * gain_one).astype(jnp.bfloat16)
    proj = jnp.dot(normed, mix_w, preferred_element_type=jnp.float32)
    qkv = proj[:, : 3 * D].astype(jnp.bfloat16).reshape(tokens, 3, H, HD)
    gate = jax.nn.sigmoid(proj[:, 3 * D :])
    grouped = lax.all_to_all(qkv, "seq", split_axis=2, concat_axis=0, tiled=True)
    attn_heads, memory_heads, lse_heads = ([], [], [])
    for head in range(grouped.shape[2]):
        cols = slice(head * HD, (head + 1) * HD)
        attended, recalled, lse = head_forward(
            grouped[:, 0, head],
            grouped[:, 1, head],
            grouped[:, 2, head],
            pkv[0][:, cols],
            pkv[1][:, cols],
            rates[head],
            seg_ids,
        )
        attn_heads.append(attended)
        memory_heads.append(recalled)
        lse_heads.append(lse)
    mixed = jnp.stack([jnp.stack(attn_heads, 1), jnp.stack(memory_heads, 1)], 1).astype(
        jnp.bfloat16
    )
    returned = lax.all_to_all(mixed, "seq", split_axis=0, concat_axis=2, tiled=True)
    attended = returned[:, 0].reshape(tokens, D).astype(jnp.float32)
    recalled = returned[:, 1].reshape(tokens, D).astype(jnp.float32)
    combined = (attended + gate * recalled).astype(jnp.bfloat16)
    mid = rows_in + jnp.dot(combined, out_w, preferred_element_type=jnp.float32)
    inverse_two = rms_scale(mid)
    scaled_two = mid * inverse_two
    normed_two = (scaled_two * gain_two).astype(jnp.bfloat16)
    gate_up = jnp.dot(normed_two, gu_w, preferred_element_type=jnp.float32)
    hidden = (jax.nn.silu(gate_up[:, :FF]) * gate_up[:, FF:]).astype(jnp.bfloat16)
    result = mid + jnp.dot(hidden, down_w, preferred_element_type=jnp.float32)
    kept = (
        seg_ids,
        inverse_one,
        scaled_one,
        normed,
        grouped,
        jnp.stack(lse_heads, 1),
        gate,
        recalled,
        combined,
        inverse_two,
        scaled_two,
        normed_two,
        gate_up,
        hidden,
    )
    return (result, kept)


def layer_backward(grad_out, kept, full, pkv, rates):
    (
        seg_ids,
        inverse_one,
        scaled_one,
        normed,
        grouped,
        lse_all,
        gate,
        recalled,
        combined,
        inverse_two,
        scaled_two,
        normed_two,
        gate_up,
        hidden,
    ) = kept
    mix_w, out_w, gu_w, down_w, gains = full
    tokens = grad_out.shape[0]
    gain_one = gains[:, 0].astype(jnp.float32)
    gain_two = gains[:, 1].astype(jnp.float32)
    grad_f = grad_out.astype(jnp.bfloat16)
    grad_down = jnp.einsum("tf,td->fd", hidden, grad_f, preferred_element_type=jnp.float32)
    grad_hidden = jnp.dot(grad_f, down_w.T, preferred_element_type=jnp.float32)
    gate_part = gate_up[:, :FF]
    up_part = gate_up[:, FF:]
    sig_part = jax.nn.sigmoid(gate_part)
    grad_gate_part = grad_hidden * up_part * sig_part * (1.0 + gate_part * (1.0 - sig_part))
    grad_up_part = grad_hidden * gate_part * sig_part
    grad_gate_up = jnp.concatenate([grad_gate_part, grad_up_part], 1).astype(jnp.bfloat16)
    grad_gu = jnp.einsum("td,tf->df", normed_two, grad_gate_up, preferred_element_type=jnp.float32)
    grad_normed_two = jnp.dot(grad_gate_up, gu_w.T, preferred_element_type=jnp.float32)
    grad_mid_norm, grad_gain_two = norm_back(grad_normed_two, scaled_two, inverse_two, gain_two)
    grad_mid = grad_out + grad_mid_norm
    grad_branch = grad_mid.astype(jnp.bfloat16)
    grad_out_w = jnp.einsum("td,te->de", combined, grad_branch, preferred_element_type=jnp.float32)
    grad_combined = jnp.dot(grad_branch, out_w.T, preferred_element_type=jnp.float32)
    grad_attended = grad_combined.astype(jnp.bfloat16).reshape(tokens, H, HD)
    grad_recalled = (grad_combined * gate).astype(jnp.bfloat16).reshape(tokens, H, HD)
    grad_gate_pre = grad_combined * recalled * gate * (1.0 - gate)
    outgoing = jnp.stack([grad_attended, grad_recalled], 1)
    headward = lax.all_to_all(outgoing, "seq", split_axis=2, concat_axis=0, tiled=True)
    head_grads, pkey_grads, pvalue_grads, rate_grads = ([], [], [], [])
    for head in range(grouped.shape[2]):
        cols = slice(head * HD, (head + 1) * HD)
        dq, dk, dv, dpk, dpv, drate = head_backward(
            grouped[:, 0, head],
            grouped[:, 1, head],
            grouped[:, 2, head],
            pkv[0][:, cols],
            pkv[1][:, cols],
            rates[head],
            seg_ids,
            lse_all[:, head],
            headward[:, 0, head],
            headward[:, 1, head],
        )
        head_grads.append(jnp.stack([dq, dk, dv], 1))
        pkey_grads.append(dpk)
        pvalue_grads.append(dpv)
        rate_grads.append(drate)
    grads_heads = jnp.stack(head_grads, 2).astype(jnp.bfloat16)
    tokenward = lax.all_to_all(grads_heads, "seq", split_axis=0, concat_axis=2, tiled=True)
    grad_proj = jnp.concatenate(
        [tokenward.reshape(tokens, 3 * D), grad_gate_pre.astype(jnp.bfloat16)], 1
    )
    grad_mix = jnp.einsum("td,tf->df", normed, grad_proj, preferred_element_type=jnp.float32)
    grad_normed = jnp.dot(grad_proj, mix_w.T, preferred_element_type=jnp.float32)
    grad_in_norm, grad_gain_one = norm_back(grad_normed, scaled_one, inverse_one, gain_one)
    grad_rows = grad_mid + grad_in_norm
    weight_terms = (
        grad_mix,
        grad_out_w,
        grad_gu,
        grad_down,
        jnp.stack([grad_gain_one, grad_gain_two], 1),
    )
    memory_terms = (
        jnp.stack([jnp.concatenate(pkey_grads, 1), jnp.concatenate(pvalue_grads, 1)], 0),
        jnp.stack(rate_grads, 0),
    )
    return (weight_terms, memory_terms, grad_rows)


def on_device(
    inputs, segment_ids, cotangent, w_mix, w_out, w_gu, w_down, norm_gains, persist_kv, memory_decay
):
    first = lax.axis_index("section") == 0
    own_weights = (w_mix[0], w_out[0], w_gu[0], w_down[0], norm_gains[0])
    pkv = persist_kv[0]
    rates = memory_decay[0]
    count = inputs.shape[0]
    tokens = inputs.shape[2]
    zero_rows = jnp.zeros((tokens, D), jnp.float32)
    received = jnp.zeros((tokens, D), jnp.bfloat16)
    kept_ticks, out_ticks = ([], [])
    for tick in range(count + 1):
        own_rows = inputs[tick, 0].astype(jnp.float32) if tick < count else zero_rows
        layer_in = jnp.where(first, own_rows, received.astype(jnp.float32))
        seg_ids = jnp.where(
            first, segment_ids[min(tick, count - 1), 0], segment_ids[max(tick - 1, 0), 0]
        )
        full = (
            lax.all_gather(own_weights[0], "shard", axis=0, tiled=True),
            lax.all_gather(own_weights[1], "shard", axis=0, tiled=True),
            lax.all_gather(own_weights[2], "shard", axis=0, tiled=True),
            lax.all_gather(own_weights[3], "shard", axis=0, tiled=True),
            lax.all_gather(own_weights[4], "shard", axis=0, tiled=True),
        )
        result, kept = layer_forward(layer_in, seg_ids, full, pkv, rates)
        result_low = result.astype(jnp.bfloat16)
        out_ticks.append(result_low)
        kept_ticks.append(kept)
        if tick < count:
            received = shifted(result_low, "section", 1)
    grad_weights = (
        jnp.zeros((D, 4 * D), jnp.float32),
        jnp.zeros((D, D), jnp.float32),
        jnp.zeros((D, 2 * FF), jnp.float32),
        jnp.zeros((FF, D), jnp.float32),
        jnp.zeros((D, 2), jnp.float32),
    )
    grad_memory = (
        jnp.zeros((2,) + pkv.shape[1:], jnp.float32),
        jnp.zeros(rates.shape, jnp.float32),
    )
    back_received = jnp.zeros((tokens, D), jnp.bfloat16)
    grad_ticks = []
    for tick in range(count + 1):
        lower = max(tick - 1, 0)
        upper = min(tick + 1, count)
        kept = jax.tree.map(
            lambda early, late: jnp.where(first, early, late), kept_ticks[lower], kept_ticks[upper]
        )
        given = cotangent[tick, 0].astype(jnp.float32) if tick < count else zero_rows
        grad_out = jnp.where(first, back_received.astype(jnp.float32), given)
        full = (
            lax.all_gather(own_weights[0], "shard", axis=0, tiled=True),
            lax.all_gather(own_weights[1], "shard", axis=0, tiled=True),
            lax.all_gather(own_weights[2], "shard", axis=0, tiled=True),
            lax.all_gather(own_weights[3], "shard", axis=0, tiled=True),
            lax.all_gather(own_weights[4], "shard", axis=0, tiled=True),
        )
        weight_terms, memory_terms, grad_rows = layer_backward(grad_out, kept, full, pkv, rates)
        grad_weights = jax.tree.map(jnp.add, grad_weights, weight_terms)
        grad_memory = jax.tree.map(jnp.add, grad_memory, memory_terms)
        grad_ticks.append(grad_rows)
        if tick < count:
            back_received = shifted(grad_rows.astype(jnp.bfloat16), "section", -1)
    section_out = jnp.stack(
        [jnp.where(first, out_ticks[batch], out_ticks[batch + 1]) for batch in range(count)], 0
    )
    section_grad = jnp.stack(
        [
            jnp.where(
                first,
                grad_ticks[batch + 1],
                grad_ticks[batch].astype(jnp.bfloat16).astype(jnp.float32),
            )
            for batch in range(count)
        ],
        0,
    )
    shares = jax.tree.map(
        lambda part: part.astype(jnp.float32),
        lax.psum_scatter(as_sent(grad_weights), "shard", scatter_dimension=0, tiled=True),
    )
    shares = jax.tree.map(lambda part: part.astype(jnp.float32), lax.psum(as_sent(shares), "seq"))
    memory_sums = lax.psum(grad_memory, "shard")
    return (
        section_out.reshape(1, count, 1, tokens, D),
        section_grad.reshape(1, count, 1, tokens, D),
        shares[0][None],
        shares[1][None],
        shares[2][None],
        shares[3][None],
        shares[4][None],
        memory_sums[0][None],
        memory_sums[1][None],
    )


MESH = pl.DeviceIdType.MESH
BF = jnp.bfloat16
F32 = jnp.float32


def here():
    return (lax.axis_index("section"), lax.axis_index("seq"), lax.axis_index("shard"))


def peer(place, chip, flip):
    x, s, z = place
    if chip % 2:
        x = 1 - x
    if chip // 2:
        s = (s + 2) % 4
    if flip:
        s = s + 1 - 2 * (s % 2)
    return (x, s, z)


def rows_of(device, size):
    x, s, _ = device
    return pl.ds(pl.multiple_of((s * 2 + x) * size, size), size)


class Gather:
    def __init__(self, full, batch, send, recv):
        self.place = here()
        self.full, self.batch, self.send, self.recv = full, batch, send, recv
        self.size = full.shape[1] // 8

    def copy(self, owner, target, sem):
        block = self.full.at[self.batch, rows_of(owner, self.size)]
        return pltpu.make_async_remote_copy(
            src_ref=block,
            dst_ref=block,
            send_sem=self.send.at[self.batch, sem],
            recv_sem=self.recv.at[self.batch, sem],
            device_id=target,
            device_id_type=MESH,
        )

    def start(self, value):
        self.full[self.batch, rows_of(self.place, self.size), :] = value
        for chip in (3, 1, 2, 0):
            self.copy(self.place, peer(self.place, chip, chip == 0), chip).start()

    def forward(self):
        other = peer(self.place, 0, True)
        for chip in (1, 2, 3):
            owner = peer(self.place, chip, False)
            self.copy(owner, owner, chip).wait_recv()
            self.copy(owner, other, 3 + chip).start()

    def finish(self):
        other = peer(self.place, 0, True)
        self.copy(other, other, 0).wait_recv()
        for chip in (1, 2, 3):
            owner = peer(self.place, chip, True)
            self.copy(owner, other, 3 + chip).wait_recv()
        for chip in (0, 1, 2, 3):
            self.copy(self.place, peer(self.place, chip, chip == 0), chip).wait_send()
        for chip in (1, 2, 3):
            self.copy(peer(self.place, chip, False), other, 3 + chip).wait_send()


class Scatter:
    def __init__(self, part, batch, pair, away, near, send, recv):
        self.place = here()
        self.part, self.batch, self.pair, self.away, self.near = part, batch, pair, away, near
        self.send, self.recv = send, recv
        self.size = part.shape[1] // 8

    def to_pair(self, chip):
        return pltpu.make_async_remote_copy(
            src_ref=self.part.at[self.batch, rows_of(peer(self.place, chip, True), self.size)],
            dst_ref=self.pair.at[self.batch, chip],
            send_sem=self.send.at[self.batch, chip],
            recv_sem=self.recv.at[self.batch, chip],
            device_id=peer(self.place, 0, True),
            device_id_type=MESH,
        )

    def to_chip(self, chip):
        return pltpu.make_async_remote_copy(
            src_ref=self.away.at[self.batch, chip - 1],
            dst_ref=self.near.at[self.batch, chip - 1],
            send_sem=self.send.at[self.batch, 3 + chip],
            recv_sem=self.recv.at[self.batch, 3 + chip],
            device_id=peer(self.place, chip, False),
            device_id_type=MESH,
        )

    def start(self):
        for chip in (3, 1, 2, 0):
            self.to_pair(chip).start()

    def chip_sum(self, chip):
        self.to_pair(chip).wait_recv()
        own = self.part[self.batch, rows_of(peer(self.place, chip, False), self.size), :]
        return own.astype(F32) + self.pair[self.batch, chip].astype(F32)

    def forward(self):
        for chip in (3, 1, 2):
            self.away[self.batch, chip - 1] = self.chip_sum(chip).astype(BF)
            self.to_chip(chip).start()

    def finish(self):
        total = self.chip_sum(0)
        for chip in (1, 2, 3):
            self.to_chip(chip).wait_recv()
            total = total + self.near[self.batch, chip - 1].astype(F32)
        for chip in (0, 1, 2, 3):
            self.to_pair(chip).wait_send()
        for chip in (1, 2, 3):
            self.to_chip(chip).wait_send()
        return total


class Column:
    def __init__(self, send, recv):
        self.place = here()
        self.send, self.recv = send, recv

    def copy(self, source, landing, sent, received, plane):
        x, s, _ = self.place
        return pltpu.make_async_remote_copy(
            src_ref=source,
            dst_ref=landing,
            send_sem=self.send.at[sent],
            recv_sem=self.recv.at[received],
            device_id=(x, s, plane),
            device_id_type=MESH,
        )

    def at_each(self, body):
        for at in range(4):

            @pl.when(self.place[2] == at)
            def _():
                body(at)


class ColumnSum(Column):
    RELAYED = ((3, 1), None, None, (0, 2))
    DIRECT = ((2,), (2, 0), (1, 3), (1,))
    LATE = ((1,), (), (), (2,))
    SOURCES = ((1, 2), (0, 2, 3), (0, 1, 3), (1, 2))

    def __init__(self, own, slots, out, send, recv):
        super().__init__(send, recv)
        self.own, self.slots, self.out = own, slots, out

    def first(self, at):
        block, plane = self.RELAYED[at]
        return self.copy(self.own.at[block], self.slots.at[plane], at, plane, plane)

    def direct(self, at, plane):
        return self.copy(self.own.at[plane], self.slots.at[at], plane, at, plane)

    def relayed(self, at):
        end = 3 if at == 1 else 0
        return self.copy(self.slots.at[at], self.slots.at[at], end, at, end)

    def start(self):
        def body(at):
            if self.RELAYED[at]:
                self.first(at).start()
            for plane in self.DIRECT[at]:
                self.direct(at, plane).start()

        self.at_each(body)

    def hop(self):
        for at, block in ((1, 3), (2, 0)):

            @pl.when(self.place[2] == at)
            def _():
                self.relayed(at).wait_recv()
                self.slots[at] = (
                    self.slots[at].astype(F32) + self.own[block].astype(F32)
                ).astype(BF)
                self.relayed(at).start()

        for at in (0, 3):

            @pl.when(self.place[2] == at)
            def _():
                for plane in self.LATE[at]:
                    self.direct(at, plane).start()

    def finish(self):
        def body(at):
            total = self.own[at].astype(F32)
            for plane in self.SOURCES[at]:
                self.direct(plane, at).wait_recv()
                total = total + self.slots[plane].astype(F32)
            self.out[...] = total.astype(BF)
            if self.RELAYED[at]:
                self.first(at).wait_send()
            else:
                self.relayed(at).wait_send()
            for plane in self.DIRECT[at] + self.LATE[at]:
                self.direct(at, plane).wait_send()

        self.at_each(body)


class ColumnGather(Column):
    TARGETS = ((2, 1), (3, 2, 0), (0, 1, 3), (1, 2))

    def __init__(self, full, send, recv):
        super().__init__(send, recv)
        self.full = full

    def block(self, at, plane):
        return self.copy(self.full.at[at], self.full.at[at], plane, at, plane)

    def relayed(self, at):
        block, plane = (3, 0) if at == 1 else (0, 3)
        return self.copy(self.full.at[block], self.full.at[block], at, block, plane)

    def start(self):
        def body(at):
            for plane in self.TARGETS[at]:
                self.block(at, plane).start()

        self.at_each(body)

    def hop(self):
        for at in (1, 2):

            @pl.when(self.place[2] == at)
            def _():
                self.relayed(at).wait_recv()
                self.relayed(at).start()

    def finish(self):
        def body(at):
            for plane in range(4):
                if plane != at and (at, plane) not in ((1, 3), (2, 0)):
                    self.block(plane, at).wait_recv()
            for plane in self.TARGETS[at]:
                self.block(at, plane).wait_send()
            if at in (1, 2):
                self.relayed(at).wait_send()

        self.at_each(body)


class Root(Column):
    def __init__(self, send, recv):
        super().__init__(send, recv)
        x, s, z = self.place
        self.root = 2 * x + s // 2
        self.low = self.root < 2
        self.between = jnp.where(self.low, 2, 1)
        self.end = jnp.where(self.low, 3, 0)
        self.is_root = z == self.root


class RootSum(Root):
    def __init__(self, own, slots, out, send, recv):
        super().__init__(send, recv)
        self.own, self.slots, self.out = own, slots, out

    def toward(self, slot, plane, source=None):
        landing = self.slots.at[slot]
        return self.copy(landing if source is None else source, landing, 0, slot, plane)

    def start(self):
        z = self.place[2]

        @pl.when(z == self.end)
        def _():
            self.toward(0, self.between, self.own).start()

        @pl.when((z != self.end) & (z != self.between) & (z != self.root))
        def _():
            self.toward(1, self.root, self.own).start()

    def hop(self):
        @pl.when(self.place[2] == self.between)
        def _():
            self.toward(0, self.root).wait_recv()
            self.slots[0] = (self.slots[0].astype(F32) + self.own[...].astype(F32)).astype(BF)
            self.toward(0, self.root).start()

    def finish(self):
        self.out[...] = self.own[...]

        @pl.when(self.is_root)
        def _():
            total = self.own[...].astype(F32)
            for slot in (0, 1):
                self.toward(slot, self.root).wait_recv()
                total = total + self.slots[slot].astype(F32)
            self.out[...] = total.astype(BF)

        @pl.when(jnp.logical_not(self.is_root))
        def _():
            self.toward(0, self.root).wait_send()


def nn(left, right):
    return jnp.dot(left, right, preferred_element_type=F32)


def nt(left, right):
    return lax.dot_general(left, right, (((1,), (1,)), ((), ())), preferred_element_type=F32)


def tn(left, right):
    return lax.dot_general(left, right, (((0,), (0,)), ((), ())), preferred_element_type=F32)


def flat(ref):
    value = ref[...]
    return value.reshape(-1, value.shape[-1])


def in_blocks(length, size, body):
    def step(index, carry):
        body(pl.ds(pl.multiple_of(index * size, size), size), index * size)
        return carry

    lax.fori_loop(0, length // size, step, 0)


def weights_of_scores(query, keys, pkeys, seg_rows, seg_cols, begin, rate):
    scale = 1.0 / math.sqrt(HD)
    inner = nt(query, keys)
    per_scores = nt(query, pkeys) * scale
    row_places = begin + lax.broadcasted_iota(jnp.int32, inner.shape, 0)
    col_places = lax.broadcasted_iota(jnp.int32, inner.shape, 1)
    allowed = (seg_rows == seg_cols) & (col_places <= row_places)
    distance = jnp.maximum(row_places - col_places, 0).astype(F32)
    decay_w = jnp.where(allowed, jnp.exp(-rate * distance) * (1.0 / HD), 0.0)
    seq_scores = jnp.where(allowed, inner * scale, -jnp.inf)
    top = jnp.maximum(
        jnp.max(per_scores, axis=1, keepdims=True), jnp.max(seq_scores, axis=1, keepdims=True)
    )
    per_exp = jnp.exp(per_scores - top)
    seq_exp = jnp.exp(seq_scores - top)
    denom = jnp.sum(per_exp, axis=1, keepdims=True) + jnp.sum(seq_exp, axis=1, keepdims=True)
    share = 1.0 / denom
    return inner, decay_w, distance, seq_exp * share, per_exp * share


class BackwardIn(NamedTuple):
    grad_full: Any
    grad_rows: Any
    rows: Any
    out_low: Any
    out_high: Any
    gains: Any
    persist: Any
    rates: Any
    seg_rows: Any
    seg_cols: Any


class BackwardOut(NamedTuple):
    mix_buf: Any
    gu_buf: Any
    down_buf: Any
    out_buf: Any
    rows_buf: Any
    grads_buf: Any
    plane_buf: Any
    grad_low: Any
    grad_high: Any


class PlaneScratch(NamedTuple):
    part: Any
    pair: Any
    away: Any
    near: Any
    ssend: Any
    srecv: Any
    gsend: Any
    grecv: Any


class BackwardScratch(NamedTuple):
    grad_gu: Any
    grad_proj: Any
    grad_keys: Any
    grad_values: Any
    branch: Any
    grad_mid: Any
    grad_next: Any
    grad_persist: Any
    grad_rate: Any
    gain_sums: Any
    small: Any
    column_buf: Any
    own_gu: Any
    own_down: Any
    grad_mix: Any
    grad_out: Any
    gu_slots: Any
    down_slots: Any
    mix_slots: Any
    root_slots: Any
    gu_sum: Any
    down_sum: Any
    mix_sum: Any
    out_sum: Any
    csend: Any
    crecv: Any
    hsend: Any
    hrecv: Any
    psend: Any
    precv: Any
    osend: Any
    orecv: Any
    rsend: Any
    rrecv: Any
    zsend: Any
    zrecv: Any
    qsend: Any
    qrecv: Any
    loaded: Any


def fields(*kinds):
    return tuple(name for kind in kinds for name in kind._fields)


def named(names, refs):
    return types.SimpleNamespace(**dict(zip(names, refs, strict=True)))


def remote(source, landing, sems, index, target):
    return pltpu.make_async_remote_copy(
        src_ref=source,
        dst_ref=landing,
        send_sem=sems[0].at[index],
        recv_sem=sems[1].at[index],
        device_id=target,
        device_id_type=MESH,
    )


class RootGather(Root):
    def __init__(self, block, send, recv):
        super().__init__(send, recv)
        self.block = block

    def to(self, plane, sent):
        return self.copy(self.block, self.block, sent, 0, plane)

    def near(self):
        return jnp.where(self.low, 1 - self.root, 5 - self.root)

    def start(self):
        @pl.when(self.is_root)
        def _():
            self.to(self.between, 0).start()
            self.to(self.near(), 1).start()

    def hop(self):
        @pl.when(self.place[2] == self.between)
        def _():
            self.to(self.end, 0).wait_recv()
            self.to(self.end, 0).start()

    def finish(self):
        z = self.place[2]

        @pl.when((z != self.root) & (z != self.between))
        def _():
            self.to(self.end, 0).wait_recv()

        @pl.when((z == self.root) | (z == self.between))
        def _():
            self.to(self.end, 0).wait_send()

        @pl.when(self.is_root)
        def _():
            self.to(self.end, 1).wait_send()


class SeqGather:
    def __init__(self, full, batch, send, recv):
        self.place = here()
        self.full, self.batch, self.send, self.recv = full, batch, send, recv
        self.size = full.shape[1] // 4
        self.beside = peer(self.place, 2, False)
        self.sibling = peer(self.place, 0, True)

    def rows(self, owner):
        return pl.ds(pl.multiple_of(owner[1] * self.size, self.size), self.size)

    def copy(self, owner, target, sem):
        block = self.full.at[self.batch, self.rows(owner)]
        sems = (self.send.at[self.batch], self.recv.at[self.batch])
        return remote(block, block, sems, sem, target)

    def start(self, value):
        self.full[self.batch, self.rows(self.place), :] = value
        self.copy(self.place, self.beside, 0).start()
        self.copy(self.place, self.sibling, 1).start()

    def forward(self):
        self.copy(self.beside, self.beside, 0).wait_recv()
        self.copy(self.beside, self.sibling, 2).start()

    def finish(self):
        self.copy(self.sibling, self.sibling, 1).wait_recv()
        self.copy(peer(self.place, 2, True), self.sibling, 2).wait_recv()
        self.copy(self.place, self.beside, 0).wait_send()
        self.copy(self.place, self.sibling, 1).wait_send()
        self.copy(self.beside, self.sibling, 2).wait_send()


class ForwardIn(NamedTuple):
    inputs: Any
    small: Any
    gain_rows: Any
    w_mix: Any
    w_out: Any
    w_gu: Any
    w_down: Any
    seg_rows: Any
    seg_cols: Any


class ForwardOut(NamedTuple):
    rows: Any
    gains: Any
    persist: Any
    rates: Any


class Kept(NamedTuple):
    normed: Any
    mix: Any
    out: Any
    gu: Any
    down: Any
    qkv: Any
    gate: Any
    recalled: Any
    combined: Any
    mid: Any
    normed_two: Any
    gate_up: Any
    hidden: Any
    out_rows: Any


class ForwardScratch(NamedTuple):
    gain_all: Any
    small_all: Any
    mix_away: Any
    gu_away: Any
    down_away: Any
    zsend: Any
    zrecv: Any
    psend: Any
    precv: Any
    xsend: Any
    xrecv: Any
    gsend: Any
    grecv: Any
    csend: Any
    crecv: Any
    hsend: Any
    hrecv: Any
    saved: Any


def each(parts, act):
    for part in parts:
        act(part)


def forward_kernel(unit, *refs):
    count = len(Kept._fields)
    r, refs = refs[: len(ForwardIn._fields)], refs[len(ForwardIn._fields) :]
    given = vars(named(ForwardIn._fields, r))
    r, refs = refs[: len(ForwardOut._fields)], refs[len(ForwardOut._fields) :]
    given |= vars(named(ForwardOut._fields, r))
    in_hbm = [refs[:count], refs[count : 2 * count]]
    refs = refs[2 * count :]
    in_vmem = [refs[:count], refs[count : 2 * count]]
    refs = refs[2 * count :]
    scratch = PlaneScratch._fields[:6] + ForwardScratch._fields
    r = types.SimpleNamespace(**given, **vars(named(scratch, refs)))
    views = [types.SimpleNamespace(**vars(named(Kept._fields, part))) for part in in_vmem]
    views[0].rows, views[1].rows = r.rows, views[0].out_rows

    def save(layer, which):
        for name in which:
            index = Kept._fields.index(name)
            yield pltpu.make_async_copy(
                in_vmem[layer][index], in_hbm[layer][index], r.saved.at[layer, index]
            )

    place = here()
    x, s, z = place
    partner = peer(place, 1, False)
    flips = [(dx, ds) for dx in (0, 1) for ds in range(4) if dx or ds]
    plane = [((x + dx) % 2, (s + ds) % 4, z) for dx, ds in flips]
    column = [(x, s, (z + dz) % 4) for dz in (1, 2, 3)]
    column += [(1 - x, s, (z + dz) % 4) for dz in (1, 2, 3)]
    barrier = pltpu.get_barrier_semaphore()
    for other in plane + column:
        pl.semaphore_signal(barrier, inc=1, device_id=other, device_id_type=MESH)
    pl.semaphore_wait(barrier, len(plane) + len(column))

    zsems, psems, xsems = (r.zsend, r.zrecv), (r.psend, r.precv), (r.xsend, r.xrecv)
    holders = [*column, partner]

    def gains_to(index):
        return remote(r.gain_rows, r.gain_all.at[x, z], zsems, index, holders[index])

    for index in range(7):
        gains_to(index).start()
    r.gain_all[x, z] = r.gain_rows[...]

    mine, other = x * 4 + s, (1 - x) * 4 + s

    def mix_part(which):
        heads = [pl.ds(pl.multiple_of(kind * D + which * HD, HD), HD) for kind in range(4)]
        return jnp.concatenate([r.w_mix[0, :, cols] for cols in heads], 1)

    out_rows = pl.ds(pl.multiple_of(s % 2 * HD, HD), HD)
    root = z == 2 * x + s // 2
    rooted = z == 2 * (1 - x) + s // 2
    for layer in (0, 1):
        v = views[layer]

        @pl.when(x == layer)
        def _():
            r.mix_away[...] = mix_part(other)
            remote(r.mix_away, v.mix.at[z], xsems, 0, partner).start()
            v.mix[z] = mix_part(mine)

            @pl.when(rooted)
            def _():
                remote(r.w_out.at[0, out_rows], v.out, xsems, 1, partner).start()

            @pl.when(root)
            def _():
                v.out[...] = r.w_out[0, out_rows, :]

    for index in range(7):
        gains_to(index).wait_recv()
    for layer in range(2):
        for owner in range(4):
            for kind in range(2):
                for half in range(2):
                    begin = owner * 2 * HD + half * HD
                    row = 2 * kind + half
                    r.gains[layer, kind : kind + 1, begin : begin + HD] = r.gain_all[
                        layer, owner, row : row + 1, :
                    ]
    size = r.rows.shape[1]
    own_half = pl.ds(pl.multiple_of(x * size, size), size)
    arriving = [SeqGather(views[0].normed, batch, r.gsend, r.grecv) for batch in range(2)]
    for batch, gather in enumerate(arriving):
        rows = r.inputs[batch, 0].astype(F32)
        gather.start((rows * rms_scale(rows) * r.gains[0, 0:1, :]).astype(BF))
        r.rows[batch] = r.inputs[batch, 0, own_half, :]

    for index in range(7):
        remote(r.small, r.small_all.at[x, s], psems, index, plane[index]).start()
    r.small_all[x, s] = r.small[...]

    padded = r.down_away.shape[0]
    width = 8 * unit + 64

    def select(which, offset):
        begin = lax.broadcasted_iota(jnp.int32, (width, 128), 0) - offset
        col = lax.broadcasted_iota(jnp.int32, (width, 128), 1)
        return jnp.where((begin == which * unit + col) & (col < unit), 1.0, 0.0).astype(BF)

    def gu_part(which, out):
        for owner in range(4):
            base = owner * 8 * unit
            offset = base % 128
            chosen = select(which, offset)
            for side in range(2):
                begin = side * FF + base - offset
                part = nn(r.w_gu[0, :, begin : begin + width], chosen).astype(BF)
                at = side * 4 * padded + owner * padded
                out[:, at : at + padded] = part[:, :padded]

    def down_part(which, out):
        row = lax.broadcasted_iota(jnp.int32, (padded, 8 * unit), 0)
        col = lax.broadcasted_iota(jnp.int32, (padded, 8 * unit), 1)
        chosen = jnp.where((col == which * unit + row) & (row < unit), 1.0, 0.0).astype(BF)
        out[...] = nn(chosen, r.w_down[0]).astype(BF)

    gu_part(other, r.gu_away)
    down_part(other, r.down_away)
    for layer in (0, 1):
        v = views[layer]

        @pl.when(x == layer)
        def _():
            remote(r.gu_away, v.gu.at[z], xsems, 2, partner).start()
            remote(r.down_away, v.down.at[z], xsems, 3, partner).start()

    mixers, feeds = [], []
    for layer, v in enumerate(views):
        sems = [(r.csend.at[3 * layer + i], r.crecv.at[3 * layer + i]) for i in range(3)]
        mixers.append(
            [
                ColumnGather(v.mix, *sems[0]),
                RootGather(v.out, r.hsend.at[layer], r.hrecv.at[layer]),
            ]
        )
        feeds.append([ColumnGather(v.gu, *sems[1]), ColumnGather(v.down, *sems[2])])

    def swapped(layer, index):
        v = views[layer]
        landing = [v.mix.at[z], v.out, v.gu.at[z], v.down.at[z]][index]
        here_from = remote(landing, landing, xsems, index, partner)

        @pl.when((x != layer) & root if index == 1 else x != layer)
        def _():
            here_from.wait_recv()

    def start_mixer(layer):
        for index, part in enumerate(mixers[layer]):
            swapped(layer, index)
            part.start()

    def start_feed(layer):
        for index, part in enumerate(feeds[layer]):
            swapped(layer, 2 + index)
            part.start()

    start_mixer(0)
    for layer, v in enumerate(views):

        @pl.when(x == layer)
        def _():
            gu_part(mine, v.gu.at[z])
            down_part(mine, v.down.at[z])

    start_feed(0)
    arriving[0].forward()
    each(mixers[0], lambda part: part.hop())
    arriving[1].forward()

    for index in range(7):
        dx, ds = flips[index]
        landing = r.small_all.at[(x + dx) % 2, (s + 4 - ds) % 4]
        remote(r.small, landing, psems, index, plane[index]).wait_recv()
    for layer in range(2):
        begin = pl.multiple_of(s % 2 * 32, 32)
        rows = r.small_all[layer, 2 * x + s // 2, pl.ds(begin, 32), :]
        r.persist[layer] = rows.astype(BF).reshape(2, 16, HD)
        begin = pl.multiple_of(64 + s % 2 * 8, 8)
        r.rates[layer] = r.small_all[layer, 2 * x + s // 2, pl.ds(begin, 8), :]

    length = r.part.shape[1]

    def project(layer, batch):
        v = views[layer]

        def block(rows, begin):
            proj = nn(v.normed[batch, rows, :], flat(v.mix))
            v.qkv[batch, rows, :] = proj[:, : 3 * HD].astype(BF)
            v.gate[batch, rows, :] = jax.nn.sigmoid(proj[:, 3 * HD :])

        in_blocks(length, 256, block)

    def mixer(layer, batch):
        v = views[layer]

        def block(rows, begin):
            values = v.qkv[batch, :, 2 * HD :]
            inner, decay_w, _, probs, per_probs = weights_of_scores(
                v.qkv[batch, rows, :HD],
                v.qkv[batch, :, HD : 2 * HD],
                r.persist[layer, 0],
                r.seg_rows[batch, rows, :],
                r.seg_cols[batch],
                begin,
                r.rates[layer, 0:1, 0:1],
            )
            attended = nn(probs.astype(BF), values) + nn(per_probs.astype(BF), r.persist[layer, 1])
            recalled = nn((inner * decay_w).astype(BF), values).astype(BF)
            v.recalled[batch, rows, :] = recalled
            combined = attended.astype(BF).astype(F32)
            combined = combined + v.gate[batch, rows, :] * recalled.astype(F32)
            combined = combined.astype(BF)
            v.combined[batch, rows, :] = combined
            r.part[batch, rows, :] = nn(combined, v.out[...]).astype(BF)

        in_blocks(length, 128, block)

    def feed(layer, batch):
        v = views[layer]

        def block(rows, begin):
            gate_up = nn(v.normed_two[batch, rows, :], flat(v.gu))
            v.gate_up[batch, rows, :] = gate_up
            half = gate_up.shape[1] // 2
            hidden = (jax.nn.silu(gate_up[:, :half]) * gate_up[:, half:]).astype(BF)
            v.hidden[batch, rows, :] = hidden
            r.part[batch, rows, :] = nn(hidden, flat(v.down)).astype(BF)

        in_blocks(length, 256, block)

    def scatter(batch):
        return Scatter(r.part, batch, r.pair, r.away, r.near, r.ssend, r.srecv)

    def send_normed(batch, own, gain, full):
        gather = Gather(full, batch, r.gsend, r.grecv)
        gather.start((own * rms_scale(own) * gain).astype(BF))
        return gather

    mixer_names = Kept._fields[:3] + Kept._fields[5:9]
    for layer, v in enumerate(views):
        parts = []
        for batch in range(2):
            if layer == 1:
                arriving[batch].forward()
            arriving[batch].finish()
            if batch == 0:
                each(mixers[layer], lambda part: part.finish())
            project(layer, batch)
            mixer(layer, batch)
            part = scatter(batch)
            part.start()
            part.forward()
            if layer == 1 and batch == 0:
                each(feeds[1], lambda part: part.hop())
            parts.append(part)
        each(save(layer, mixer_names), lambda copy: copy.start())
        if layer == 0:
            start_mixer(1)
        gathers = []
        for batch, part in enumerate(parts):
            mid = v.rows[batch].astype(F32) + part.finish()
            v.mid[batch] = mid
            gathers.append(send_normed(batch, mid, r.gains[layer, 1:2, :], v.normed_two))
        if layer == 0:
            each(feeds[0], lambda part: part.hop())
        parts = []
        for batch, gather in enumerate(gathers):
            gather.forward()
            gather.finish()
            if batch == 0:
                each(feeds[layer], lambda part: part.finish())
            feed(layer, batch)
            if layer == 0 and batch == 0:
                each(mixers[1], lambda part: part.hop())
                start_feed(1)
            part = scatter(batch)
            part.start()
            part.forward()
            parts.append(part)
        each(save(layer, Kept._fields[3:5] + Kept._fields[9:13]), lambda copy: copy.start())
        arriving = []
        for batch, part in enumerate(parts):
            rows = (v.mid[batch] + part.finish()).astype(BF)
            v.out_rows[batch] = rows
            if layer == 0:
                gain = r.gains[1, 0:1, :]
                arriving.append(send_normed(batch, rows.astype(F32), gain, views[1].normed))
        each(save(layer, Kept._fields[13:]), lambda copy: copy.start())

    for layer in range(2):
        for copy in save(layer, Kept._fields):
            copy.wait()
    remote(r.mix_away, r.mix_away, xsems, 0, partner).wait_send()
    remote(r.gu_away, r.gu_away, xsems, 2, partner).wait_send()
    remote(r.down_away, r.down_away, xsems, 3, partner).wait_send()

    @pl.when(rooted)
    def _():
        remote(views[0].out, views[0].out, xsems, 1, partner).wait_send()

    for index in range(7):
        gains_to(index).wait_send()
        remote(r.small, r.small_all.at[x, s], psems, index, plane[index]).wait_send()


def backward_kernel(*refs):
    saved_names = Kept._fields[:-1]
    count = len(saved_names)
    given = vars(named(BackwardIn._fields, refs[: len(BackwardIn._fields)]))
    refs = refs[len(BackwardIn._fields) :]
    in_hbm = [refs[:count], refs[count : 2 * count]]
    refs = refs[2 * count :]
    given |= vars(named(BackwardOut._fields, refs[: len(BackwardOut._fields)]))
    refs = refs[len(BackwardOut._fields) :]
    in_vmem = refs[:count]
    given |= vars(named(saved_names, in_vmem))
    scratch = fields(PlaneScratch, BackwardScratch)
    r = types.SimpleNamespace(**given, **vars(named(scratch, refs[count:])))
    length = r.part.shape[1]
    place = here()
    x, s, z = place

    def load(layer, which):
        for name in which:
            index = saved_names.index(name)
            yield pltpu.make_async_copy(in_hbm[layer][index], in_vmem[index], r.loaded.at[index])

    feed_names = saved_names[3:5] + saved_names[9:]
    mixer_names = saved_names[:3] + saved_names[5:9]
    for which in (feed_names, mixer_names):
        each(load(1, which), lambda copy: copy.start())
    feeds, mixers = [], []
    for layer in range(2):
        sems = [(r.csend.at[3 * layer + i], r.crecv.at[3 * layer + i]) for i in range(3)]
        feeds.append(
            [
                ColumnSum(r.own_gu, r.gu_slots.at[layer], r.gu_sum.at[layer], *sems[0]),
                ColumnSum(r.own_down, r.down_slots.at[layer], r.down_sum.at[layer], *sems[1]),
            ]
        )
        mixers.append(
            [
                ColumnSum(r.grad_mix, r.mix_slots.at[layer], r.mix_sum.at[layer], *sems[2]),
                RootSum(
                    r.grad_out,
                    r.root_slots.at[layer],
                    r.out_sum.at[layer],
                    r.hsend.at[layer],
                    r.hrecv.at[layer],
                ),
            ]
        )
    grads = (r.grad_low, r.grad_high)

    def feed_back(full, batch):
        def block(rows, begin):
            grad_hidden = nt(full[batch, rows, :], flat(r.down))
            half = grad_hidden.shape[1]
            gate_part = r.gate_up[batch, rows, :half]
            up_part = r.gate_up[batch, rows, half:]
            sig_part = jax.nn.sigmoid(gate_part)
            silu = gate_part * sig_part
            grad_gate = grad_hidden * up_part * (sig_part + silu * (1.0 - sig_part))
            r.grad_gu[batch, rows, :half] = grad_gate.astype(BF)
            r.grad_gu[batch, rows, half:] = (grad_hidden * silu).astype(BF)
            r.part[batch, rows, :] = nt(r.grad_gu[batch, rows, :], flat(r.gu)).astype(BF)

        in_blocks(length, 256, block)

    def down_weights(full):
        def down(cols, begin):
            grad = tn(r.hidden[0], full[0, :, cols])
            grad = grad + tn(r.hidden[1], full[1, :, cols])
            grad = grad.reshape(4, grad.shape[0] // 4, grad.shape[1])
            r.own_down[:, :, cols] = grad.astype(BF)

        in_blocks(D, 256, down)

    def product(out, left, right):
        for owner in range(4):
            cols = slice(owner * (D // 4), (owner + 1) * (D // 4))
            grad = tn(left[0, :, cols], right[0]) + tn(left[1, :, cols], right[1])
            out[owner] = grad.astype(BF)

    def mixer_back(layer, batch):
        scale = 1.0 / math.sqrt(HD)
        r.grad_keys[...] = jnp.zeros_like(r.grad_keys)
        r.grad_values[...] = jnp.zeros_like(r.grad_values)

        def block(rows, begin):
            grad_combined = nt(r.branch[batch, rows, :], r.out[...])
            gate = r.gate[batch, rows, :]
            recalled = r.recalled[batch, rows, :].astype(F32)
            attn_rows = grad_combined.astype(BF)
            memory_rows = (grad_combined * gate).astype(BF)
            grad_pre = grad_combined * recalled * gate * (1.0 - gate)
            r.grad_proj[batch, rows, 3 * HD :] = grad_pre.astype(BF)
            query = r.qkv[batch, rows, :HD]
            keys = r.qkv[batch, :, HD : 2 * HD]
            values = r.qkv[batch, :, 2 * HD :]
            inner, decay_w, distance, probs, per_probs = weights_of_scores(
                query,
                keys,
                r.persist[layer, 0],
                r.seg_rows[batch, rows, :],
                r.seg_cols[batch],
                begin,
                r.rates[layer, 0:1, 0:1],
            )
            per_dp = nt(attn_rows, r.persist[layer, 1])
            seq_dp = nt(attn_rows, values)
            delta = jnp.sum(per_probs * per_dp, axis=1, keepdims=True) + jnp.sum(
                probs * seq_dp, axis=1, keepdims=True
            )
            per_ds = (per_probs * (per_dp - delta)).astype(BF)
            seq_ds = (probs * (seq_dp - delta)).astype(BF)
            weighted = nt(memory_rows, values) * decay_w
            grad_inner = weighted.astype(BF)
            memory = inner * decay_w
            rate_terms = weighted * inner * distance
            r.grad_rate[layer] -= jnp.sum(rate_terms, axis=0, keepdims=True)
            grad_query = (nn(per_ds, r.persist[layer, 0]) + nn(seq_ds, keys)) * scale
            grad_query = grad_query + nn(grad_inner, keys)
            r.grad_proj[batch, rows, :HD] = grad_query.astype(BF)
            r.grad_keys[...] += tn(seq_ds, query) * scale + tn(grad_inner, query)
            r.grad_values[...] += tn(probs.astype(BF), attn_rows) + tn(
                memory.astype(BF), memory_rows
            )
            r.grad_persist[layer, 0] += tn(per_ds, query) * scale
            r.grad_persist[layer, 1] += tn(per_probs.astype(BF), attn_rows)

        in_blocks(length, 128, block)
        r.grad_proj[batch, :, HD : 2 * HD] = r.grad_keys[...].astype(BF)
        r.grad_proj[batch, :, 2 * HD : 3 * HD] = r.grad_values[...].astype(BF)

        def back(rows, begin):
            r.part[batch, rows, :] = nt(r.grad_proj[batch, rows, :], flat(r.mix)).astype(BF)

        in_blocks(length, 256, back)

    def scatter(batch):
        return Scatter(r.part, batch, r.pair, r.away, r.near, r.ssend, r.srecv)

    def through_norm(batch, part, rows, gain):
        grad_normed = part.finish()
        inverse = rms_scale(rows)
        return norm_back(grad_normed, rows * inverse, inverse, gain)

    flips = [(dx, ds) for dx in (0, 1) for ds in range(4) if dx or ds]
    plane = [((x + dx) % 2, (s + ds) % 4, z) for dx, ds in flips]
    column = [(x, s, (z + dz) % 4) for dz in (1, 2, 3)]
    barrier = pltpu.get_barrier_semaphore()
    for other in plane + column:
        pl.semaphore_signal(barrier, inc=1, device_id=other, device_id_type=MESH)
    pl.semaphore_wait(barrier, len(plane) + len(column))
    r.grad_rate[...] = jnp.zeros_like(r.grad_rate)
    r.grad_persist[...] = jnp.zeros_like(r.grad_persist)
    arriving = None
    for layer in (1, 0):
        full = r.grad_next if arriving else r.grad_full
        above = grads[1] if arriving else r.grad_rows
        rows_in = r.out_low if layer else r.rows
        each(load(layer, feed_names), lambda copy: copy.wait())
        parts = []
        for batch in range(2):
            if arriving:
                arriving[batch].forward()
                arriving[batch].finish()
            if batch == 1 - layer:
                if layer == 0:
                    feeds[1][1].finish()
                down_weights(full)
                feeds[layer][1].start()
            feed_back(full, batch)
            part = scatter(batch)
            part.start()
            part.forward()
            parts.append(part)
        if layer == 0:
            each(mixers[1], lambda part: part.hop())
            feeds[1][0].finish()
        else:
            feeds[1][1].hop()
        product(r.own_gu, r.normed_two, r.grad_gu)
        feeds[layer][0].start()
        gathers = []
        gain_sums = []
        for batch, part in enumerate(parts):
            grad_mid, gain_sum = through_norm(
                batch, part, r.mid[batch], r.gains[layer, 1:2, :]
            )
            gain_sums.append(gain_sum[None])
            grad_mid = grad_mid + above[batch].astype(F32)
            r.grad_mid[batch] = grad_mid
            gather = Gather(r.branch, batch, r.gsend, r.grecv)
            gather.start(grad_mid.astype(BF))
            gathers.append(gather)
        r.gain_sums[layer, 1:2] = gain_sums[0] + gain_sums[1]
        if layer == 1:
            each(load(0, feed_names), lambda copy: copy.start())
        each(load(layer, mixer_names), lambda copy: copy.wait())
        parts = []
        for batch, gather in enumerate(gathers):
            gather.forward()
            gather.finish()
            if batch == 1:
                if layer == 0:
                    mixers[1][1].finish()
                grad_out = tn(r.combined[0], r.branch[0]) + tn(r.combined[1], r.branch[1])
                r.grad_out[...] = grad_out.astype(BF)
                mixers[layer][1].start()
            mixer_back(layer, batch)
            part = scatter(batch)
            part.start()
            part.forward()
            parts.append(part)
            if batch == 0:
                each(feeds[layer][: 2 - layer], lambda part: part.hop())
        if layer == 0:
            mixers[1][0].finish()
        product(r.grad_mix, r.normed, r.grad_proj)
        mixers[layer][0].start()
        if layer == 1:
            each(load(0, mixer_names), lambda copy: copy.start())
        arriving = []
        gain_sums = []
        for batch, part in enumerate(parts):
            grad_h, gain_sum = through_norm(
                batch, part, rows_in[batch].astype(F32), r.gains[layer, 0:1, :]
            )
            gain_sums.append(gain_sum[None])
            grad_h = (grad_h + r.grad_mid[batch]).astype(BF)
            grads[layer][batch] = grad_h
            if layer == 1:
                gather = Gather(r.grad_next, batch, r.gsend, r.grecv)
                gather.start(grad_h)
                arriving.append(gather)
        r.gain_sums[layer, 0:1] = gain_sums[0] + gain_sums[1]
    each(feeds[0], lambda part: part.finish())

    for layer in range(2):
        persist = r.grad_persist[layer].reshape(-1, HD)
        rate = r.grad_rate[layer]
        rate = sum(rate[:, begin : begin + HD] for begin in range(0, length, HD))
        for owner in range(4):
            r.small[owner, layer * 32 : (layer + 1) * 32, :] = persist
            r.small[owner, 64 + layer : 65 + layer, :] = rate
            for kind in range(2):
                for half in range(2):
                    row = 72 + 4 * layer + 2 * kind + half
                    begin = owner * 2 * HD + half * HD
                    r.small[owner, row : row + 1, :] = r.gain_sums[
                        layer, kind : kind + 1, begin : begin + HD
                    ]
    for owner in range(4):
        r.small[owner, 66:72, :] = jnp.zeros((6, HD), F32)

    sibling, beside, partner = (peer(place, 0, True), peer(place, 2, False), peer(place, 1, False))
    across = peer(place, 3, False)
    bufs = (r.mix_buf, r.gu_buf, r.down_buf)
    out_buf, rows_buf, grads_buf, plane_buf = r.out_buf, r.rows_buf, r.grads_buf, r.plane_buf
    by_layer = [
        [r.mix_sum.at[i], r.gu_sum.at[i], r.down_sum.at[i], r.out_sum.at[i]] for i in range(2)
    ]
    by_layer[0] += [r.out_low, r.grad_low]
    by_layer[1] += [r.out_high, r.grad_high]
    copy = remote

    def to_plane_of(dz):
        target = (z + dz) % 4
        return copy(
            r.small.at[target], r.column_buf.at[dz - 1], (r.zsend, r.zrecv), dz - 1, (x, s, target)
        )

    def to_plane(index):
        slot = plane_buf.at[x * 4 + s]
        return copy(slot, slot, (r.qsend, r.qrecv), index, plane[index])

    for dz in (1, 2, 3):
        to_plane_of(dz).start()

    psems = [(r.psend.at[i], r.precv.at[i]) for i in range(3)]

    def piece(index, kind, slot, target, source=None):
        landing = bufs[index].at[slot]
        return copy(landing if source is None else source, landing, psems[index], kind, target)

    mine = (x, s)
    turned = (1 - x, s)

    def send(indices):
        for layer in (0, 1):
            own, theirs = by_layer[layer], by_layer[1 - layer]

            @pl.when(x == layer)
            def _():
                for index in indices:
                    piece(index, 2, mine, partner, theirs[index]).start()
                    piece(index, 0, mine, beside, own[index]).start()
                    piece(index, 1, mine, sibling, own[index]).start()
                for index in indices:
                    bufs[index][mine] = own[index][...]

    def turn(indices):
        for index in indices:
            piece(index, 2, turned, partner).wait_recv()
            piece(index, 3, turned, beside).start()
            piece(index, 4, turned, sibling).start()

    send((1, 2))
    for layer in (0, 1):

        @pl.when(x == layer)
        def _():
            copy(by_layer[1 - layer][4], rows_buf, (r.rsend, r.rrecv), 0, partner).start()
            copy(by_layer[1 - layer][5], grads_buf, (r.rsend, r.rrecv), 1, partner).start()

    total = r.small[z]
    for dz in (1, 2, 3):
        to_plane_of(dz).wait_recv()
        total = total + r.column_buf[dz - 1]
    plane_buf[x * 4 + s] = total
    for index in range(7):
        to_plane(index).start()
    each(mixers[0], lambda part: part.hop())
    turn((1, 2))
    each(mixers[0], lambda part: part.finish())
    send((0,))

    core = s % 2
    root = z == 2 * x + s // 2
    of_root = (z // 2, 2 * (z % 2) + core)
    apart = 2 * ((x + of_root[0]) % 2) + (s // 2 + of_root[1] // 2) % 2

    def out_copy(index, target, source=None):
        landing = out_buf.at[core]
        return copy(landing if source is None else source, landing, (r.osend, r.orecv), index, target)

    for layer in (0, 1):

        @pl.when(root & (x == layer))
        def _():
            out_copy(1, beside, by_layer[layer][3]).start()
            out_copy(2, partner, by_layer[1 - layer][3]).start()
            out_copy(3, across, by_layer[1 - layer][3]).start()
            out_buf[core] = by_layer[layer][3][...]

    for apart_by in (1, 2, 3):

        @pl.when(apart == apart_by)
        def _():
            out_copy(apart_by, beside).wait_recv()

    out_copy(0, sibling).start()

    turn((0,))
    far = (x, (s + 2) % 4)
    far_turned = (1 - x, (s + 2) % 4)
    for index in (1, 2, 0):
        piece(index, 0, far, beside).wait_recv()
        piece(index, 5, far, sibling).start()
    for index in (1, 2, 0):
        piece(index, 3, far_turned, beside).wait_recv()
        piece(index, 6, far_turned, sibling).start()
    twin = sibling[1]
    far_twin = (twin + 2) % 4
    for index in range(3):
        piece(index, 1, (x, twin), sibling).wait_recv()
        piece(index, 4, (1 - x, twin), sibling).wait_recv()
        piece(index, 5, (x, far_twin), sibling).wait_recv()
        piece(index, 6, (1 - x, far_twin), sibling).wait_recv()
    other_out = out_buf.at[1 - core]
    copy(other_out, other_out, (r.osend, r.orecv), 0, sibling).wait_recv()
    for index in range(7):
        dx, ds = flips[index]
        slot = plane_buf.at[((x + dx) % 2) * 4 + (s + 4 - ds) % 4]
        copy(slot, slot, (r.qsend, r.qrecv), index, plane[index]).wait_recv()
    for index in (0, 1):
        copy(rows_buf, rows_buf, (r.rsend, r.rrecv), index, partner).wait()
    for index in range(7):
        to_plane(index).wait_send()
    for dz in (1, 2, 3):
        to_plane_of(dz).wait_send()
    for index in range(3):
        for kind in range(7):
            piece(index, kind, mine, sibling).wait_send()
    out_copy(0, sibling).wait_send()

    @pl.when(root)
    def _():
        for index in (1, 2, 3):
            out_copy(index, sibling).wait_send()


def kernel_call(kernel, number, operands, outs, scratch, spaces=None, places=None):
    spaces = spaces or [pltpu.VMEM] * len(outs)
    places = places or [pltpu.VMEM] * len(operands)
    return pl.pallas_call(
        kernel,
        out_shape=list(outs),
        in_specs=[pl.BlockSpec(memory_space=space) for space in places],
        out_specs=[pl.BlockSpec(memory_space=space) for space in spaces],
        scratch_shapes=scratch,
        compiler_params=pltpu.CompilerParams(
            collective_id=number, has_side_effects=True, vmem_limit_bytes=58 * 2**20
        ),
    )(*operands)


def pairs_of(*sizes):
    return [pltpu.SemaphoreType.DMA(size) for size in sizes for _ in range(2)]


def scatter_scratch(length):
    size = length // 8
    return [
        pltpu.VMEM((2, length, D), BF),
        pltpu.VMEM((2, 4, size, D), BF),
        pltpu.VMEM((2, 3, size, D), BF),
        pltpu.VMEM((2, 3, size, D), BF),
        *pairs_of((2, 8), (2, 8)),
    ]


def forward_call(number, *operands):
    inputs, small, _, w_mix, _, _, w_down, *_ = operands
    count, _, tokens, _ = inputs.shape
    depth, length = w_mix.shape[1], 4 * tokens
    unit = w_down.shape[1] // 8
    padded = -(-unit // 32) * 32
    shape = jax.ShapeDtypeStruct
    outs = ForwardOut(
        rows=shape((count, length // 8, D), BF),
        gains=shape((2, 2, D), F32),
        persist=shape((2, 2, 16, HD), BF),
        rates=shape((2, 8, HD), F32),
    )
    kept = Kept(
        normed=shape((count, length, D), BF),
        mix=shape((4, depth, 4 * HD), BF),
        out=shape((HD, D), BF),
        gu=shape((4, depth, 8 * padded), BF),
        down=shape((4, padded, D), BF),
        qkv=shape((count, length, 3 * HD), BF),
        gate=shape((count, length, HD), F32),
        recalled=shape((count, length, HD), BF),
        combined=shape((count, length, HD), BF),
        mid=shape((count, length // 8, D), F32),
        normed_two=shape((count, length, D), BF),
        gate_up=shape((count, length, 8 * padded), F32),
        hidden=shape((count, length, 4 * padded), BF),
        out_rows=shape((count, length // 8, D), BF),
    )
    scratch = [pltpu.VMEM(part.shape, part.dtype) for part in (*kept, *kept)]
    scratch += scatter_scratch(length)[:6]
    scratch += [
        pltpu.VMEM((2, 4, 8, HD), F32),
        pltpu.VMEM((2, 4) + small.shape, F32),
        pltpu.VMEM((depth, 4 * HD), BF),
        pltpu.VMEM((depth, 8 * padded), BF),
        pltpu.VMEM((padded, D), BF),
        *pairs_of((7,), (7,), (4,), (2, 8), (6, 4), (2, 2)),
        pltpu.SemaphoreType.DMA((2, len(kept))),
    ]
    kernel = functools.partial(forward_kernel, unit)
    specs = [pltpu.VMEM] * len(outs) + [pl.ANY] * (2 * len(kept))
    found = kernel_call(kernel, number, operands, [*outs, *kept, *kept], scratch, specs)
    own, found = found[: len(outs)], found[len(outs) :]
    return (
        named(ForwardOut._fields, own),
        named(Kept._fields, found[: len(kept)]),
        named(Kept._fields, found[len(kept) :]),
    )


def backward_call(number, given, below, above):
    saved = Kept._fields[:-1]
    kept = [getattr(part, name) for part in (below, above) for name in saved]
    count, length, _ = below.normed.shape
    depth, half, size = D // 4, 4 * below.down.shape[1], length // 8
    shape = jax.ShapeDtypeStruct
    outs = BackwardOut(
        mix_buf=shape((2, 4, depth, 4 * HD), BF),
        gu_buf=shape((2, 4, depth, 2 * half), BF),
        down_buf=shape((2, 4, half // 4, D), BF),
        out_buf=shape((2, HD, D), BF),
        rows_buf=shape((count, size, D), BF),
        grads_buf=shape((count, size, D), BF),
        plane_buf=shape((8, 80, HD), F32),
        grad_low=shape((count, size, D), BF),
        grad_high=shape((count, size, D), BF),
    )
    scratch = [pltpu.VMEM(part.shape, part.dtype) for part in kept[: len(saved)]]
    scratch += scatter_scratch(length) + [
        pltpu.VMEM((count, length, 2 * half), BF),
        pltpu.VMEM((count, length, 4 * HD), BF),
        pltpu.VMEM((length, HD), F32),
        pltpu.VMEM((length, HD), F32),
        pltpu.VMEM((count, length, D), BF),
        pltpu.VMEM((count, size, D), F32),
        pltpu.VMEM((count, length, D), BF),
        pltpu.VMEM((2, 2, 16, HD), F32),
        pltpu.VMEM((2, 1, length), F32),
        pltpu.VMEM((2, 2, D), F32),
        pltpu.VMEM((4, 80, HD), F32),
        pltpu.VMEM((3, 80, HD), F32),
        pltpu.VMEM((4, depth, 2 * half), BF),
        pltpu.VMEM((4, half // 4, D), BF),
        pltpu.VMEM((4, depth, 4 * HD), BF),
        pltpu.VMEM((HD, D), BF),
        pltpu.VMEM((2, 4, depth, 2 * half), BF),
        pltpu.VMEM((2, 4, half // 4, D), BF),
        pltpu.VMEM((2, 4, depth, 4 * HD), BF),
        pltpu.VMEM((2, 2, HD, D), BF),
        pltpu.VMEM((2, depth, 2 * half), BF),
        pltpu.VMEM((2, half // 4, D), BF),
        pltpu.VMEM((2, depth, 4 * HD), BF),
        pltpu.VMEM((2, HD, D), BF),
        *pairs_of((6, 4), (2, 2), (3, 7), (4,), (2,), (3,), (7,)),
        pltpu.SemaphoreType.DMA((len(saved),)),
    ]
    operands = [*(getattr(given, name) for name in BackwardIn._fields), *kept]
    spaces = [pltpu.VMEM] * len(BackwardIn._fields) + [pl.ANY] * len(kept)
    found = kernel_call(backward_kernel, number, operands, outs, scratch, None, spaces)
    return named(BackwardOut._fields, found)


def assemble_kernel(unit, *refs):
    mix_buf, gu_buf, down_buf, out_buf, *rows, plane_buf = refs[:11]
    mix_ref, gu_ref, down_ref, out_ref, rows_ref, grads_ref, persist_ref, rate_ref = refs[11:]
    x, s, _ = here()

    @pl.when(pl.program_id(0) == 0)
    def _():
        size = rows[0].shape[1]
        own = pl.ds(pl.multiple_of(x * size, size), size)
        got = pl.ds(pl.multiple_of((1 - x) * size, size), size)
        for ref, (low, high, other) in ((rows_ref, rows[:3]), (grads_ref, rows[3:])):
            for layer, part in enumerate((low, high)):

                @pl.when(x == layer)
                def _():
                    for batch in range(2):
                        ref[0, batch, 0, own, :] = part[batch].astype(ref.dtype)

            for batch in range(2):
                ref[0, batch, 0, got, :] = other[batch].astype(ref.dtype)
        for head in range(2):
            out_ref[0, head * HD : (head + 1) * HD, :] = out_buf[head].astype(F32)
            for kind in range(2):
                begin = pl.multiple_of(x * 32 + kind * 16, 16)
                persist_ref[0, kind, :, head * HD : (head + 1) * HD] = plane_buf[
                    2 * s + head, pl.ds(begin, 16), :
                ]
            both = jnp.sum(plane_buf[2 * s + head, 64:72, :], axis=1, keepdims=True)
            rate_ref[0:1, head : head + 1] = jnp.where(x == 0, both[0:1], both[1:2])

    padded = down_buf.shape[2]
    half = gu_buf.shape[3] // 2
    for which in range(8):
        slot = (which // 4, which % 4)
        mix = mix_buf[slot].astype(F32)
        for kind in range(4):
            begin = kind * D + which * HD
            mix_ref[0, :, begin : begin + HD] = mix[:, kind * HD : (kind + 1) * HD]
        part = gu_buf[slot].astype(F32)
        for side in range(2):
            for owner in range(half // padded):
                begin = side * FF + (owner * 8 + which) * unit
                source = side * half + owner * padded
                gu_ref[0, :, begin : begin + unit] = part[:, source : source + unit]
    for pair in range(2):
        down = down_buf[0, pair].astype(F32)
        down_ref[0, pair * unit : (pair + 1) * unit, :] = down[:unit]


def assemble_call(unit, found, outputs, grads):
    mix_buf, gu_buf, down_buf = found.mix_buf, found.gu_buf, found.down_buf
    depth, padded = mix_buf.shape[2], down_buf.shape[2]
    rows = depth // 4
    count, size, _ = outputs[0].shape
    shape = jax.ShapeDtypeStruct
    outs = [
        shape((1, depth, 4 * D), F32),
        shape((1, depth, 2 * FF), F32),
        shape((1, 8 * unit, D), F32),
    ]
    once = [
        shape((1, 2 * HD, D), F32),
        shape((1, count, 1, 2 * size, D), BF),
        shape((1, count, 1, 2 * size, D), F32),
        shape((1, 2, 16, 2 * HD), F32),
        shape((1, 2), F32),
    ]
    given = (found.out_buf, *outputs, found.rows_buf, *grads, found.grads_buf, found.plane_buf)

    def whole(part):
        return pl.BlockSpec(part.shape, lambda i, zeros=(0,) * len(part.shape): zeros)

    return pl.pallas_call(
        functools.partial(assemble_kernel, unit),
        grid=(4,),
        out_shape=outs + once,
        in_specs=[
            pl.BlockSpec((2, 4, rows, 4 * HD), lambda i: (0, 0, i, 0)),
            pl.BlockSpec((2, 4, rows, gu_buf.shape[3]), lambda i: (0, 0, i, 0)),
            pl.BlockSpec((1, 2, padded, D), lambda i: (i // 2, i % 2, 0, 0)),
            *(whole(part) for part in given),
        ],
        out_specs=[
            pl.BlockSpec((1, rows, 4 * D), lambda i: (0, i, 0)),
            pl.BlockSpec((1, rows, 2 * FF), lambda i: (0, i, 0)),
            pl.BlockSpec((1, 2 * unit, D), lambda i: (0, i, 0)),
            *(whole(part) for part in once),
        ],
        compiler_params=pltpu.CompilerParams(vmem_limit_bytes=60 * 2**20),
    )(mix_buf, gu_buf, down_buf, *given)


def tensor_parallel(
    inputs, segment_ids, cotangent, w_mix, w_out, w_gu, w_down, norm_gains, persist_kv, memory_decay
):
    x, s, z = here()
    nx, ns, nz = (lax.axis_size(a) for a in ("section", "seq", "shard"))
    width = nx * ns
    count, _, tokens, _ = inputs.shape
    length = tokens * ns
    size = length // width
    depth = w_mix.shape[1]
    unit = w_down.shape[1] // (nx * ns)

    small = persist_kv[0].reshape(-1, 2, HD).transpose(1, 0, 2).reshape(-1, HD).astype(F32)
    rates = jnp.broadcast_to(memory_decay[0][:, None, None], (2, 8, HD)).reshape(-1, HD)
    gain_rows = norm_gains[0].astype(F32).T.reshape(-1, HD)
    gain_rows = jnp.pad(gain_rows, ((0, 8 - gain_rows.shape[0]), (0, 0)))
    small = jnp.concatenate([small, rates], 0)
    segments = (segment_ids[:, 0, :, None], segment_ids)
    ready, below, above = forward_call(
        1, inputs, small, gain_rows, w_mix, w_out, w_gu, w_down, *segments
    )
    cot_full = lax.all_gather(cotangent[:, 0], "seq", axis=1, tiled=True)
    given = BackwardIn(
        grad_full=cot_full,
        grad_rows=lax.dynamic_slice_in_dim(cotangent[:, 0], x * size, size, 1),
        rows=ready.rows,
        out_low=below.out_rows,
        out_high=above.out_rows,
        gains=ready.gains,
        persist=ready.persist,
        rates=ready.rates,
        seg_rows=segments[0],
        seg_cols=segments[1],
    )
    found = backward_call(2, given, below, above)
    outputs = (below.out_rows, above.out_rows)
    grads = (found.grad_low, found.grad_high)

    grad_mix, grad_gu, grad_down, grad_out, section_out, section_grad, grad_persist, grad_rate = (
        assemble_call(unit, found, outputs, grads)
    )
    gain_all = jnp.sum(found.plane_buf[:, 72:], 0).reshape(2, 2, depth)
    grad_gain = lax.dynamic_index_in_dim(gain_all, x, 0).transpose(0, 2, 1)
    return (
        section_out,
        section_grad,
        grad_mix,
        grad_out,
        grad_gu,
        grad_down,
        grad_gain,
        grad_persist,
        grad_rate,
    )


def solution(mesh):
    sizes = mesh.shape
    planar = (sizes["section"], sizes["seq"]) == (2, 4)
    placed = (
        P(None, "shard", "seq", None),
        P(None, "shard", None),
        P(None, "shard", "seq", None),
        P("section", "shard", None),
        P("section", "shard", None),
        P("section", "shard", None),
        P("section", "shard", None),
        P("section", "shard", None),
        P("section", None, None, "seq"),
        P("section", "seq"),
    )
    return jax.shard_map(
        tensor_parallel if planar else on_device,
        mesh=mesh,
        in_specs=placed,
        out_specs=(
            P("section", None, "shard", "seq", None),
            P("section", None, "shard", "seq", None),
            P("section", "shard", None),
            P("section", "shard", None),
            P("section", "shard", None),
            P("section", "shard", None),
            P("section", "shard", None),
            P("section", None, None, "seq"),
            P("section", "seq"),
        ),
        check_vma=False,
    )
```
